32 devices in a mesh: dp: 8 (over z, x), seq: 4 (over y, core).
Axes of the slice: x: 2, y: 2, z: 4, core: 2. Of those that a mesh axis runs over, the one named last changes fastest.
Arguments:
- dec_states: bfloat16 [8, 1024, 768], P('dp', 'seq'), may hold values from -6 to 6
- enc_states: bfloat16 [8, 1024, 768], P('dp', 'seq'), may hold values from -6 to 6
- out_grad: bfloat16 [8, 1024, 768], P('dp', 'seq'), may hold values from -6 to 6
- dec_lengths: int32 [8, 4], P('dp'), may hold values from 1 to 1021, as said below
- enc_lengths: int32 [8, 4], P('dp'), may hold values from 1 to 1021, as said below
- self_query: bfloat16 [768, 768], replicated, may hold values from -0.109375 to 0.109375
- self_key: bfloat16 [768, 768], replicated, may hold values from -0.109375 to 0.109375
- self_value: bfloat16 [768, 768], replicated, may hold values from -0.21875 to 0.21875
- self_output: bfloat16 [768, 768], replicated, may hold values from -1.25 to 1.25
- cross_query: bfloat16 [768, 768], replicated, may hold values from -0.109375 to 0.109375
- cross_key: bfloat16 [768, 768], replicated, may hold values from -0.109375 to 0.109375
- cross_value: bfloat16 [768, 768], replicated, may hold values from -0.21875 to 0.21875
- cross_output: bfloat16 [768, 768], replicated, may hold values from -1.25 to 1.25
- ffn_in: bfloat16 [768, 3072], replicated, may hold values from -0.21875 to 0.21875
- ffn_out: bfloat16 [3072, 768], replicated, may hold values from -0.109375 to 0.109375
- gain_self: bfloat16 [768], replicated, may hold values from 0.099609375 to 1.8984375
- gain_cross: bfloat16 [768], replicated, may hold values from 0.099609375 to 1.8984375
- gain_ffn: bfloat16 [768], replicated, may hold values from 0.099609375 to 1.8984375
- position_bias: bfloat16 [32, 12], replicated, may hold values from -4 to 4
Outputs:
- layer_out: bfloat16 [8, 1024, 768], P('dp', 'seq')
- dec_grad: float32 [8, 1024, 768], P('dp', 'seq')
- enc_grad: float32 [8, 1024, 768], P('dp', 'seq')
- grad_self_query: float32 [768, 768], P('seq')
- grad_self_key: float32 [768, 768], P('seq')
- grad_self_value: float32 [768, 768], P('seq')
- grad_self_output: float32 [768, 768], P('seq')
- grad_cross_query: float32 [768, 768], P('seq')
- grad_cross_key: float32 [768, 768], P('seq')
- grad_cross_value: float32 [768, 768], P('seq')
- grad_cross_output: float32 [768, 768], P('seq')
- grad_ffn_in: float32 [768, 3072], P('seq')
- grad_ffn_out: float32 [3072, 768], P('seq')
- grad_gain_self: float32 [768], P('seq')
- grad_gain_cross: float32 [768], P('seq')
- grad_gain_ffn: float32 [768], P('seq')
- grad_position_bias: float32 [32, 12], P('seq')
The draws below stay inside these ranges and needn't reach their ends.
Inputs may be any that keep to these rules, and one draw needn't show every extreme that they name: `dec_lengths`: the 4 lengths of a row sum to 1024. In every row one item, the second or third, begins within the first 256 positions and ends within the last 256; each other item is shorter than 128. In one row of every draw the other items have length 1 each. `enc_lengths`: as for dec_lengths, drawn apart from them.
All inputs are finite; a program needn't handle non-finite values.
Results may differ from the reference program's by a relative error of at most 0.028.
The reference program's roundings to bfloat16 on the way count: a program that leaves them out, or rounds other values in their place, can miss the bound.
Values may be sent and summed in bfloat16 or wider, within the bound.
A program may use at most 192 MiB of HBM per device.

```python
import math
import jax
import jax.numpy as jnp
from jax import lax

D = 768
HEADS = 12
HEAD_DIM = 64
FF = 3072
BUCKETS = 32
TOK_DEV = 256
ITEMS = 4
BATCH = 8
SEQ_GRP = 1024


def packed_lengths(key):
    short_key, place_key, row_key = jax.random.split(key, 3)
    shorts = jax.random.randint(short_key, (BATCH, ITEMS - 1), 1, TOK_DEV // 2, dtype=jnp.int32)
    chosen = jax.random.randint(row_key, (), 0, BATCH, dtype=jnp.int32)
    rows = jnp.arange(BATCH, dtype=jnp.int32)[:, None]
    shorts = jnp.where(rows == chosen, 1, shorts).astype(jnp.int32)
    place = jax.random.randint(place_key, (BATCH, 1), 1, 3, dtype=jnp.int32)
    longest = SEQ_GRP - jnp.sum(shorts, axis=1, keepdims=True)
    slots = jnp.arange(ITEMS, dtype=jnp.int32)[None, :]
    padded = jnp.concatenate([shorts, jnp.zeros((BATCH, 1), jnp.int32)], axis=1)
    source = jnp.maximum(jnp.where(slots < place, slots, slots - 1), 0)
    picked = jnp.take_along_axis(padded, jnp.broadcast_to(source, (BATCH, ITEMS)), axis=1)
    return jnp.where(slots == place, longest, picked).astype(jnp.int32)


def draw_dec_lengths(key, part):
    key = jax.random.fold_in(key, 5)
    return packed_lengths(key)


def draw_enc_lengths(key, part):
    key = jax.random.fold_in(key, 9)
    return packed_lengths(key)


def shard_levels(key, shape, cuts, low, top_value):
    level, own = 1.0, jax.random.fold_in(key, 6)
    for axis_at, shards_of in cuts:
        heights = jnp.exp(jax.random.uniform(jax.random.fold_in(own, axis_at), (shards_of,), jnp.float32, low / len(cuts), top_value / len(cuts)))
        level = level * jnp.repeat(heights, shape[axis_at] // shards_of).reshape([-1 if axis == axis_at else 1 for axis in range(len(shape))])
    return level


def centred(stream_key, shape, scale, bound, cuts=(), kind=jnp.bfloat16):
    result = jax.random.normal(stream_key, shape, jnp.float32) * scale
    if len(cuts) > 0:
        result = shard_levels(stream_key, shape, cuts, -0.22, 0.18) * result
    return jnp.clip(result, min=-bound, max=bound).astype(kind)


def setup_inputs(seed: int = 0) -> dict:
    seeds = jax.random.split(jax.random.key(seed), 20)
    return {
        "dec_states": centred(seeds[0], (BATCH, SEQ_GRP, D), 1.0, 6.0, ((0, 8), (1, 4))),
        "enc_states": centred(seeds[1], (BATCH, SEQ_GRP, D), 1.0, 6.0, ((0, 8), (1, 4))),
        "out_grad": centred(seeds[2], (BATCH, SEQ_GRP, D), 1.0, 6.0, ((0, 8), (1, 4))),
        "dec_lengths": draw_dec_lengths(jax.random.fold_in(seeds[19], 71), 0),
        "enc_lengths": draw_enc_lengths(jax.random.fold_in(seeds[19], 71), 0),
        "self_query": centred(seeds[5], (D, D), (4 * D) ** -0.5, 0.109375),
        "self_key": centred(seeds[6], (D, D), (4 * D) ** -0.5, 0.109375),
        "self_value": centred(seeds[7], (D, D), D ** -0.5, 0.21875),
        "self_output": centred(seeds[8], (D, D), (D // 32) ** -0.5, 1.25),
        "cross_query": centred(seeds[9], (D, D), (4 * D) ** -0.5, 0.109375),
        "cross_key": centred(seeds[10], (D, D), (4 * D) ** -0.5, 0.109375),
        "cross_value": centred(seeds[11], (D, D), D ** -0.5, 0.21875),
        "cross_output": centred(seeds[12], (D, D), (D // 32) ** -0.5, 1.25),
        "ffn_in": centred(seeds[13], (D, FF), D ** -0.5, 0.21875),
        "ffn_out": centred(seeds[14], (FF, D), FF ** -0.5, 0.109375),
        "gain_self": jnp.clip(1.0 + 0.18 * jax.random.normal(seeds[15], (D,), jnp.float32), 0.099609375, 1.8984375).astype(jnp.bfloat16),
        "gain_cross": jnp.clip(1.0 + 0.18 * jax.random.normal(seeds[16], (D,), jnp.float32), 0.099609375, 1.8984375).astype(jnp.bfloat16),
        "gain_ffn": jnp.clip(1.0 + 0.18 * jax.random.normal(seeds[17], (D,), jnp.float32), 0.099609375, 1.8984375).astype(jnp.bfloat16),
        "position_bias": centred(seeds[18], (BUCKETS, HEADS), 1.0, 4.0),
    }


@jax.custom_vjp
def low(v):
    return lax.optimization_barrier(v.astype(jnp.bfloat16)).astype(jnp.float32)

@jax.custom_vjp
def low_back(v):
    return v

def low_keep(v):
    return (low(v), None)

def low_pass(kept, grad):
    return (grad,)

def back_keep(v):
    return (v, None)

def back_low(kept, grad):
    return (low(grad),)
low.defvjp(low_keep, low_pass)
low_back.defvjp(back_keep, back_low)
EPS = 1e-06
NEG = -1000000000.0
BEST = lax.Precision.HIGHEST

def narrow_both(values):
    return low_back(low(values))

def bucket_of(distance):
    farther = jnp.full(distance.shape, 16, jnp.int32)
    for level in range(1, 16):
        farther = farther + (distance >= math.ceil(16 * 8 ** (level / 16))).astype(jnp.int32)
    return jnp.where(distance < 16, distance, farther)

def item_ids(lengths, count):
    starts = jnp.cumsum(lengths) - lengths
    places = jnp.arange(count, dtype=jnp.int32)
    return lax.optimization_barrier(jnp.sum((places[:, None] >= starts[None, :]).astype(jnp.int32), axis=1)) - 1

def norm_rows(values, gain):
    return values * lax.rsqrt(lax.optimization_barrier(jnp.mean(values * values, axis=-1, keepdims=True)) + EPS) * gain

def matmul(left, right):
    return jnp.dot(left, right, precision=BEST, preferred_element_type=jnp.float32)

def attend(queries, keys, values, allowed, extra):
    count = queries.shape[0]
    total = keys.shape[0]
    query_heads = queries.reshape(count, HEADS, HEAD_DIM)
    key_heads = keys.reshape(total, HEADS, HEAD_DIM)
    value_heads = values.reshape(total, HEADS, HEAD_DIM)
    scores = low_back(jnp.einsum('shd,khd->hsk', query_heads, key_heads, precision=BEST) + extra)
    scores = jnp.where(allowed[None], scores, NEG)
    shifted = scores - lax.optimization_barrier(jnp.max(scores, axis=2, keepdims=True))
    weights = jnp.exp(shifted)
    probs = low(weights / lax.optimization_barrier(jnp.sum(weights, axis=2, keepdims=True)))
    context = jnp.einsum('hsk,khd->shd', probs, value_heads, precision=BEST)
    return context.reshape(count, HEADS * HEAD_DIM)

def layer_row(params, states, encoded, dec_len, enc_len):
    self_query, self_key, self_value, self_output, cross_query, cross_key, cross_value, cross_output, ffn_in, ffn_out, gain_self, gain_cross, gain_ffn, position_bias = params
    length = states.shape[0]
    dec_items = item_ids(dec_len, length)
    enc_items = item_ids(enc_len, encoded.shape[0])
    places = jnp.arange(length, dtype=jnp.int32)
    distance = jnp.maximum(places[:, None] - places[None, :], 0)
    causal = (dec_items[:, None] == dec_items[None, :]) & (places[None, :] <= places[:, None])
    bias_terms = jnp.transpose(jnp.take(position_bias, bucket_of(distance), axis=0), (2, 0, 1))
    normed = low(norm_rows(states, gain_self))
    queries = narrow_both(matmul(normed, self_query))
    keys = narrow_both(matmul(normed, self_key))
    values = narrow_both(matmul(normed, self_value))
    context = narrow_both(attend(queries, keys, values, causal, bias_terms))
    first = states + low_back(matmul(context, self_output))
    crossing = dec_items[:, None] == enc_items[None, :]
    normed_cross = low(norm_rows(first, gain_cross))
    cross_queries = narrow_both(matmul(normed_cross, cross_query))
    cross_keys = narrow_both(matmul(encoded, cross_key))
    cross_values = narrow_both(matmul(encoded, cross_value))
    cross_context = narrow_both(attend(cross_queries, cross_keys, cross_values, crossing, 0.0))
    second = first + low_back(matmul(cross_context, cross_output))
    normed_ffn = low(norm_rows(second, gain_ffn))
    inner = low(jax.nn.gelu(low_back(matmul(normed_ffn, ffn_in)), approximate=False))
    return second + low_back(matmul(inner, ffn_out))

def reference(dec_states, enc_states, out_grad, dec_lengths, enc_lengths, self_query, self_key, self_value, self_output, cross_query, cross_key, cross_value, cross_output, ffn_in, ffn_out, gain_self, gain_cross, gain_ffn, position_bias):
    params = tuple((weight.astype(jnp.float32) for weight in (self_query, self_key, self_value, self_output, cross_query, cross_key, cross_value, cross_output, ffn_in, ffn_out, gain_self, gain_cross, gain_ffn, position_bias)))

    def forward(weights, states, encoded):

        def one_row(inputs):
            return layer_row(weights, inputs[0], inputs[1], inputs[2], inputs[3])
        return lax.map(jax.checkpoint(one_row), (states, encoded, dec_lengths, enc_lengths))
    outputs, pullback = jax.vjp(forward, params, dec_states.astype(jnp.float32), enc_states.astype(jnp.float32))
    grads, state_grad, encoded_grad = pullback(out_grad.astype(jnp.float32))
    return (outputs.astype(jnp.bfloat16), state_grad, encoded_grad, grads[0], grads[1], grads[2], grads[3], grads[4], grads[5], grads[6], grads[7], grads[8], grads[9], grads[10], grads[11], grads[12], grads[13])
```

```python
import functools
import math

import jax
import jax.numpy as jnp
from jax import lax
from jax.experimental import pallas as pl
from jax.experimental.pallas import tpu as pltpu
from jax.sharding import PartitionSpec as P

EPS = 1e-06
NEG = -1000000000.0


def bucket_of(distance):
    farther = jnp.full(distance.shape, 16, jnp.int32)
    for level in range(1, 16):
        farther = farther + (distance >= math.ceil(16 * 8 ** (level / 16))).astype(jnp.int32)
    return jnp.where(distance < 16, distance, farther)


def item_ids(lengths, count):
    starts = jnp.cumsum(lengths) - lengths
    places = jnp.arange(count, dtype=jnp.int32)
    return jnp.sum((places[:, None] >= starts[None, :]).astype(jnp.int32), axis=1) - 1


def norm_rows(values, gain):
    return values * lax.rsqrt(jnp.mean(values * values, axis=-1, keepdims=True) + EPS) * gain


def matmul(left, right):
    return jnp.dot(left, right, preferred_element_type=jnp.float32)


def matmul_right_t(left, right):
    return lax.dot_general(
        left, right, (((1,), (1,)), ((), ())), preferred_element_type=jnp.float32
    )


def matmul_left_t(left, right):
    return lax.dot_general(
        left, right, (((0,), (0,)), ((), ())), preferred_element_type=jnp.float32
    )


def block_scores(query_heads, keys_all, start, span, allowed, position_terms, table):
    heads, head_dim = (query_heads.shape[1], query_heads.shape[2])
    key_block = keys_all[start : start + span].reshape(span, heads, head_dim)
    raw = jnp.einsum("shd,khd->hsk", query_heads, key_block, preferred_element_type=jnp.float32)
    if table is not None:
        raw = raw + jnp.einsum(
            "skb,bh->hsk", position_terms(start, span), table, preferred_element_type=jnp.float32
        )
    return (jnp.where(allowed(start, span)[None], raw, NEG), key_block)


def attention_forward(queries, keys_all, values_all, allowed, position_terms, table, heads):
    count, width = queries.shape
    total = keys_all.shape[0]
    span = min(512, total)
    head_dim = width // heads
    query_heads = queries.reshape(count, heads, head_dim)
    running = jnp.full((heads, count), -jnp.inf, jnp.float32)
    mass = jnp.zeros((heads, count), jnp.float32)
    for start in range(0, total, span):
        scores, _ = block_scores(query_heads, keys_all, start, span, allowed, position_terms, table)
        newer = jnp.maximum(running, jnp.max(scores, axis=2))
        mass = mass * jnp.exp(running - newer) + jnp.sum(
            jnp.exp(scores - newer[:, :, None]), axis=2
        )
        running = newer
    log_mass = running + jnp.log(mass)
    context = jnp.zeros((count, heads, head_dim), jnp.float32)
    for start in range(0, total, span):
        scores, _ = block_scores(query_heads, keys_all, start, span, allowed, position_terms, table)
        probs = jnp.exp(scores - log_mass[:, :, None]).astype(jnp.bfloat16)
        value_block = values_all[start : start + span].reshape(span, heads, head_dim)
        context = context + jnp.einsum(
            "hsk,khd->shd", probs, value_block, preferred_element_type=jnp.float32
        )
    return (context.reshape(count, width), log_mass)


def attention_backward(
    queries,
    keys_all,
    values_all,
    allowed,
    position_terms,
    table,
    heads,
    context,
    log_mass,
    context_grad,
):
    count, width = queries.shape
    total = keys_all.shape[0]
    span = min(512, total)
    head_dim = width // heads
    query_heads = queries.reshape(count, heads, head_dim)
    grad_heads = context_grad.reshape(count, heads, head_dim)
    row_terms = jnp.sum(
        grad_heads.astype(jnp.float32) * context.reshape(count, heads, head_dim), axis=2
    ).T
    query_grad = jnp.zeros((count, heads, head_dim), jnp.float32)
    key_parts = []
    value_parts = []
    table_grad = None
    if table is not None:
        table_grad = jnp.zeros(table.shape, jnp.float32)
    for start in range(0, total, span):
        scores, key_block = block_scores(
            query_heads, keys_all, start, span, allowed, position_terms, table
        )
        value_block = values_all[start : start + span].reshape(span, heads, head_dim)
        probs = jnp.exp(scores - log_mass[:, :, None])
        prob_grad = jnp.einsum(
            "shd,khd->hsk", grad_heads, value_block, preferred_element_type=jnp.float32
        )
        score_grad = (probs * (prob_grad - row_terms[:, :, None])).astype(jnp.bfloat16)
        query_grad = query_grad + jnp.einsum(
            "hsk,khd->shd", score_grad, key_block, preferred_element_type=jnp.float32
        )
        key_parts.append(
            jnp.einsum(
                "hsk,shd->khd", score_grad, query_heads, preferred_element_type=jnp.float32
            ).reshape(span, width)
        )
        value_parts.append(
            jnp.einsum(
                "hsk,shd->khd",
                probs.astype(jnp.bfloat16),
                grad_heads,
                preferred_element_type=jnp.float32,
            ).reshape(span, width)
        )
        if table is not None:
            table_grad = table_grad + jnp.einsum(
                "hsk,skb->bh",
                score_grad,
                position_terms(start, span),
                preferred_element_type=jnp.float32,
            )
    return (
        query_grad.reshape(count, width),
        jnp.concatenate(key_parts, axis=0),
        jnp.concatenate(value_parts, axis=0),
        table_grad,
    )


MESH = pl.DeviceIdType.MESH


def add_low(left, right):
    return (left.astype(jnp.float32) + right.astype(jnp.float32)).astype(jnp.bfloat16)


def reduce_kernel(
    planes,
    piece,
    chunks,
    big_hbm,
    small_in,
    fin,
    small_out,
    kept,
    core_recv,
    y_recv,
    x_recv,
    z_recv,
    small_a,
    small_c,
    small_y,
    small_x,
    small_z,
    load_sem,
    core_sem,
    y_sem,
    x_sem,
    z_sem,
    gz_sem,
    gx_sem,
    tiny_sem,
):
    row = lax.axis_index("dp")
    place = lax.axis_index("seq")
    side, core = place // 2, lax.rem(place, 2)
    plane, half = row // 2, lax.rem(row, 2)
    core_peer = (row, side * 2 + 1 - core)
    y_peer = (row, (1 - side) * 2 + core)
    x_peer = (plane * 2 + 1 - half, place)

    def z_peer(step):
        return (lax.rem(plane + step, planes) * 2 + half, place)

    half_rows = piece * planes
    chunk_rows = 2 * half_rows

    def span(first, size):
        return pl.ds(pl.multiple_of(first, piece), size)

    def chunk_span(index):
        return span(index * chunk_rows, chunk_rows)

    def send(src, dst, sems, slot, peer):
        return pltpu.make_async_remote_copy(
            src_ref=src,
            dst_ref=dst,
            send_sem=sems.at[(0, *slot)],
            recv_sem=sems.at[(1, *slot)],
            device_id=peer,
            device_id_type=MESH,
        )

    def load(index):
        rows = chunk_span(index)
        return pltpu.make_async_copy(
            big_hbm.at[core, :, rows], kept.at[:, rows], load_sem.at[index]
        )

    def core_copy(index):
        rows = chunk_span(index)
        return send(
            big_hbm.at[1 - core, :, rows], core_recv.at[:, rows], core_sem, (index,), core_peer
        )

    def y_copy(index):
        rows = chunk_span(index)
        return send(kept.at[1 - side, rows], y_recv.at[rows], y_sem, (index,), y_peer)

    def x_copy(index):
        other = span(index * chunk_rows + (1 - half) * half_rows, half_rows)
        return send(
            kept.at[side, other], x_recv.at[span(index * half_rows, half_rows)], x_sem, (index,), x_peer
        )

    def z_rows(index, which):
        return span(index * chunk_rows + half * half_rows + which * piece, piece)

    def z_copy(index, step):
        target = lax.rem(plane + step, planes)
        return send(
            kept.at[side, z_rows(index, target)],
            z_recv.at[step - 1, span(index * piece, piece)],
            z_sem,
            (index, step - 1),
            z_peer(step),
        )

    def gz_copy(index, step):
        rows = z_rows(index, plane)
        return send(fin.at[rows], fin.at[rows], gz_sem, (index, step - 1), z_peer(step))

    def gx_copy(index):
        rows = span(index * chunk_rows + half * half_rows, half_rows)
        return send(fin.at[rows], fin.at[rows], gx_sem, (index,), x_peer)

    barrier = pltpu.get_barrier_semaphore()
    peers = [core_peer, y_peer, x_peer] + [z_peer(step) for step in range(1, planes)]
    for peer in peers:
        pl.semaphore_signal(barrier, inc=1, device_id=peer, device_id_type=MESH)
    pl.semaphore_wait(barrier, len(peers))

    tiny_core = send(small_in.at[1 - core], small_c, tiny_sem, (0,), core_peer)
    tiny_core.start()

    def begin(index, carry):
        load(index).start()
        core_copy(index).start()
        return carry

    lax.fori_loop(0, chunks, begin, 0)

    tiny_core.wait()
    small_a[...] = small_in[core] + small_c[...]
    tiny_y = send(small_a.at[1 - side], small_y, tiny_sem, (1,), y_peer)
    tiny_y.start()

    def tick(step, carry):
        @pl.when(step < chunks)
        def _():
            load(step).wait()
            core_copy(step).wait()
            rows = chunk_span(step)
            for other in range(2):
                kept[other, rows, :] = add_low(kept[other, rows, :], core_recv[other, rows, :])
            y_copy(step).start()

        @pl.when((step >= 2) & (step < chunks + 2))
        def _():
            index = step - 2
            y_copy(index).wait()
            rows = chunk_span(index)
            kept[side, rows, :] = add_low(kept[side, rows, :], y_recv[rows, :])
            x_copy(index).start()

        @pl.when((step >= 4) & (step < chunks + 4))
        def _():
            index = step - 4
            x_copy(index).wait()
            rows = span(index * chunk_rows + half * half_rows, half_rows)
            kept[side, rows, :] = add_low(
                kept[side, rows, :], x_recv[span(index * half_rows, half_rows), :]
            )
            for step_z in range(1, planes):
                z_copy(index, step_z).start()

        @pl.when((step >= 6) & (step < chunks + 6))
        def _():
            index = step - 6
            total = kept[side, z_rows(index, plane), :].astype(jnp.float32)
            for step_z in range(1, planes):
                z_copy(index, step_z).wait()
                total = total + z_recv[step_z - 1, span(index * piece, piece), :].astype(jnp.float32)
            fin[z_rows(index, plane), :] = total.astype(jnp.bfloat16)
            for step_z in range(1, planes):
                gz_copy(index, step_z).start()

        @pl.when((step >= 8) & (step < chunks + 8))
        def _():
            index = step - 8
            for step_z in range(1, planes):
                gz_copy(index, step_z).wait()
            gx_copy(index).start()

        @pl.when(step >= 10)
        def _():
            gx_copy(step - 10).wait()

        return carry

    lax.fori_loop(0, chunks + 10, tick, 0)

    tiny_y.wait()
    small_out[...] = small_a[side] + small_y[...]
    tiny_x = send(small_out, small_x, tiny_sem, (2,), x_peer)
    tiny_x.start()
    tiny_x.wait()
    small_y[...] = small_out[...] + small_x[...]
    copies = []
    for step in range(1, planes):
        copy = send(small_y, small_z.at[step - 1], tiny_sem, (2 + step,), z_peer(step))
        copy.start()
        copies.append(copy)
    for copy in copies:
        copy.wait()
    total = small_y[...]
    for step in range(1, planes):
        total = total + small_z[step - 1]
    small_out[...] = total


def reduce_grads(big, small, rows_all):
    planes = rows_all // 2
    count, width = big.shape[2:]
    piece = 16
    chunk_rows = 2 * planes * piece
    chunks = count // chunk_rows
    tall = small.shape[2]
    tiny = (tall, width)
    return pl.pallas_call(
        functools.partial(reduce_kernel, planes, piece, chunks),
        out_shape=(
            jax.ShapeDtypeStruct((count, width), jnp.bfloat16),
            jax.ShapeDtypeStruct(tiny, jnp.float32),
        ),
        in_specs=[
            pl.BlockSpec(memory_space=pl.ANY),
            pl.BlockSpec(memory_space=pltpu.VMEM),
        ],
        out_specs=[pl.BlockSpec(memory_space=pltpu.VMEM)] * 2,
        scratch_shapes=[
            pltpu.VMEM((2, count, width), jnp.bfloat16),
            pltpu.VMEM((2, count, width), jnp.bfloat16),
            pltpu.VMEM((count, width), jnp.bfloat16),
            pltpu.VMEM((count // 2, width), jnp.bfloat16),
            pltpu.VMEM((planes - 1, chunks * piece, width), jnp.bfloat16),
            pltpu.VMEM((2, *tiny), jnp.float32),
            pltpu.VMEM((2, *tiny), jnp.float32),
            pltpu.VMEM(tiny, jnp.float32),
            pltpu.VMEM(tiny, jnp.float32),
            pltpu.VMEM((planes - 1, *tiny), jnp.float32),
            pltpu.SemaphoreType.DMA((chunks,)),
            pltpu.SemaphoreType.DMA((2, chunks)),
            pltpu.SemaphoreType.DMA((2, chunks)),
            pltpu.SemaphoreType.DMA((2, chunks)),
            pltpu.SemaphoreType.DMA((2, chunks, planes - 1)),
            pltpu.SemaphoreType.DMA((2, chunks, planes - 1)),
            pltpu.SemaphoreType.DMA((2, chunks)),
            pltpu.SemaphoreType.DMA((2, 2 + planes)),
        ],
        compiler_params=pltpu.CompilerParams(
            collective_id=0, has_side_effects=True, vmem_limit_bytes=56 * 2**20
        ),
        name="reduce_grads",
    )(big, small)


def by_place(grad):
    width = 768
    parts = grad.shape[0] // 4
    pieces = grad.reshape(2, 2, parts, grad.shape[1])
    pieces = jnp.transpose(pieces, (1, 0, 2, 3))
    if grad.shape[1] == width:
        return pieces
    blocks = grad.shape[1] // width
    pieces = pieces.reshape(2, 2, parts, blocks, width)
    return jnp.transpose(pieces, (0, 1, 3, 2, 4)).reshape(2, 2, parts * blocks, width)


def on_device(
    dec_states,
    enc_states,
    out_grad,
    dec_lengths,
    enc_lengths,
    self_query,
    self_key,
    self_value,
    self_output,
    cross_query,
    cross_key,
    cross_value,
    cross_output,
    ffn_in,
    ffn_out,
    gain_self,
    gain_cross,
    gain_ffn,
    position_bias,
):
    count = dec_states.shape[1]
    heads = position_bias.shape[1]
    total = count * lax.axis_size("seq")
    first_place = lax.axis_index("seq") * count
    own_places = first_place + jnp.arange(count, dtype=jnp.int32)
    all_places = jnp.arange(total, dtype=jnp.int32)
    dec_items = item_ids(dec_lengths[0], total)
    enc_items = item_ids(enc_lengths[0], total)
    own_items = lax.dynamic_slice_in_dim(dec_items, first_place, count)
    bucket_range = jnp.arange(position_bias.shape[0], dtype=jnp.int32)

    def self_allowed(start, span):
        same = own_items[:, None] == dec_items[start : start + span][None, :]
        return same & (all_places[start : start + span][None, :] <= own_places[:, None])

    def cross_allowed(start, span):
        return own_items[:, None] == enc_items[start : start + span][None, :]

    def position_terms(start, span):
        distance = jnp.maximum(own_places[:, None] - all_places[start : start + span][None, :], 0)
        return (bucket_of(distance)[:, :, None] == bucket_range[None, None, :]).astype(jnp.bfloat16)

    states = dec_states[0].astype(jnp.float32)
    encoded = enc_states[0]
    gain_one = gain_self.astype(jnp.float32)
    gain_two = gain_cross.astype(jnp.float32)
    gain_three = gain_ffn.astype(jnp.float32)
    normed_self = norm_rows(states, gain_one).astype(jnp.bfloat16)
    queries = matmul(normed_self, self_query).astype(jnp.bfloat16)
    keys_own = matmul(normed_self, self_key).astype(jnp.bfloat16)
    values_own = matmul(normed_self, self_value).astype(jnp.bfloat16)
    keys_all, values_all = (
        lax.all_gather(keys_own, "seq", axis=0, tiled=True),
        lax.all_gather(values_own, "seq", axis=0, tiled=True),
    )
    context, self_mass = attention_forward(
        queries, keys_all, values_all, self_allowed, position_terms, position_bias, heads
    )
    context_low = context.astype(jnp.bfloat16)
    first = states + matmul(context_low, self_output)
    normed_cross = norm_rows(first, gain_two).astype(jnp.bfloat16)
    cross_queries = matmul(normed_cross, cross_query).astype(jnp.bfloat16)
    cross_keys_own = matmul(encoded, cross_key).astype(jnp.bfloat16)
    cross_values_own = matmul(encoded, cross_value).astype(jnp.bfloat16)
    cross_keys_all, cross_values_all = (
        lax.all_gather(cross_keys_own, "seq", axis=0, tiled=True),
        lax.all_gather(cross_values_own, "seq", axis=0, tiled=True),
    )
    cross_context, cross_mass = attention_forward(
        cross_queries, cross_keys_all, cross_values_all, cross_allowed, None, None, heads
    )
    cross_low = cross_context.astype(jnp.bfloat16)
    second = first + matmul(cross_low, cross_output)
    normed_ffn = norm_rows(second, gain_three).astype(jnp.bfloat16)
    pre_act = matmul(normed_ffn, ffn_in)
    inner_low = jax.nn.gelu(pre_act, approximate=False).astype(jnp.bfloat16)
    layer_out = (second + matmul(inner_low, ffn_out)).astype(jnp.bfloat16)
    cotangent = out_grad[0].astype(jnp.float32)
    ffn_head_grad = cotangent.astype(jnp.bfloat16)
    grad_ffn_out = matmul_left_t(inner_low, ffn_head_grad)
    inner_grad = matmul_right_t(ffn_head_grad, ffn_out)
    _, gelu_back = jax.vjp(lambda values: jax.nn.gelu(values, approximate=False), pre_act)
    pre_grad = gelu_back(inner_grad)[0].astype(jnp.bfloat16)
    grad_ffn_in = matmul_left_t(normed_ffn, pre_grad)
    _, ffn_norm_back = jax.vjp(norm_rows, second, gain_three)
    second_part, gain_ffn_grad = ffn_norm_back(matmul_right_t(pre_grad, ffn_in))
    second_grad = cotangent + second_part
    cross_head_grad = second_grad.astype(jnp.bfloat16)
    grad_cross_output = matmul_left_t(cross_low, cross_head_grad)
    cross_context_grad = matmul_right_t(cross_head_grad, cross_output).astype(jnp.bfloat16)
    cross_query_grad, cross_key_part, cross_value_part, _ = attention_backward(
        cross_queries,
        cross_keys_all,
        cross_values_all,
        cross_allowed,
        None,
        None,
        heads,
        cross_context,
        cross_mass,
        cross_context_grad,
    )
    cross_key_own, cross_value_own = (
        lax.psum_scatter(
            cross_key_part.astype(jnp.bfloat16), "seq", scatter_dimension=0, tiled=True
        ).astype(jnp.float32),
        lax.psum_scatter(
            cross_value_part.astype(jnp.bfloat16), "seq", scatter_dimension=0, tiled=True
        ).astype(jnp.float32),
    )
    cross_query_low = cross_query_grad.astype(jnp.bfloat16)
    cross_key_low = cross_key_own.astype(jnp.bfloat16)
    cross_value_low = cross_value_own.astype(jnp.bfloat16)
    grad_cross_query = matmul_left_t(normed_cross, cross_query_low)
    grad_cross_key = matmul_left_t(encoded, cross_key_low)
    grad_cross_value = matmul_left_t(encoded, cross_value_low)
    enc_grad = matmul_right_t(cross_key_low, cross_key) + matmul_right_t(
        cross_value_low, cross_value
    )
    _, cross_norm_back = jax.vjp(norm_rows, first, gain_two)
    first_part, gain_cross_grad = cross_norm_back(matmul_right_t(cross_query_low, cross_query))
    first_grad = second_grad + first_part
    self_head_grad = first_grad.astype(jnp.bfloat16)
    grad_self_output = matmul_left_t(context_low, self_head_grad)
    context_grad = matmul_right_t(self_head_grad, self_output).astype(jnp.bfloat16)
    query_grad, key_part, value_part, bias_grad = attention_backward(
        queries,
        keys_all,
        values_all,
        self_allowed,
        position_terms,
        position_bias,
        heads,
        context,
        self_mass,
        context_grad,
    )
    key_own, value_own = (
        lax.psum_scatter(
            key_part.astype(jnp.bfloat16), "seq", scatter_dimension=0, tiled=True
        ).astype(jnp.float32),
        lax.psum_scatter(
            value_part.astype(jnp.bfloat16), "seq", scatter_dimension=0, tiled=True
        ).astype(jnp.float32),
    )
    query_low = query_grad.astype(jnp.bfloat16)
    key_low = key_own.astype(jnp.bfloat16)
    value_low = value_own.astype(jnp.bfloat16)
    grad_self_query = matmul_left_t(normed_self, query_low)
    grad_self_key = matmul_left_t(normed_self, key_low)
    grad_self_value = matmul_left_t(normed_self, value_low)
    normed_grad = (
        matmul_right_t(query_low, self_query)
        + matmul_right_t(key_low, self_key)
        + matmul_right_t(value_low, self_value)
    )
    _, self_norm_back = jax.vjp(norm_rows, states, gain_one)
    state_part, gain_self_grad = self_norm_back(normed_grad)
    dec_grad = first_grad + state_part
    width = dec_states.shape[2]
    fan = ffn_in.shape[1] // width
    own = width // 4
    big = jnp.concatenate(
        [
            by_place(grad.astype(jnp.bfloat16))
            for grad in (
                grad_ffn_out,
                grad_ffn_in,
                grad_cross_output,
                grad_cross_query,
                grad_cross_key,
                grad_cross_value,
                grad_self_output,
                grad_self_query,
                grad_self_key,
                grad_self_value,
            )
        ],
        axis=2,
    )
    gains = jnp.stack([gain_self_grad, gain_cross_grad, gain_ffn_grad]).reshape(3, 4, own)
    gains = jnp.transpose(gains, (1, 0, 2))
    gains = jnp.pad(gains, ((0, 0), (0, 0), (0, width - own)))
    near = bias_grad.reshape(4, 1, -1)
    near = jnp.pad(near, ((0, 0), (0, 4), (0, width - near.shape[2])))
    small = jnp.concatenate([gains, near], axis=1)
    small = jnp.transpose(small.reshape(2, 2, 8, width), (1, 0, 2, 3))
    summed, tiny = reduce_grads(big, small, lax.axis_size("dp"))

    def rows(first, count):
        return summed[first : first + count].astype(jnp.float32)

    tall = own * fan
    out_ffn_in = jnp.transpose(rows(tall, tall).reshape(fan, own, width), (1, 0, 2))
    base = 2 * tall
    heads_own = bias_grad.shape[0] // 4
    return (
        layer_out[None],
        dec_grad[None],
        enc_grad[None],
        rows(base + 5 * own, own),
        rows(base + 6 * own, own),
        rows(base + 7 * own, own),
        rows(base + 4 * own, own),
        rows(base + own, own),
        rows(base + 2 * own, own),
        rows(base + 3 * own, own),
        rows(base, own),
        out_ffn_in.reshape(own, fan * width),
        rows(0, tall),
        tiny[0, :own],
        tiny[1, :own],
        tiny[2, :own],
        tiny[3, : heads_own * heads].reshape(heads_own, heads),
    )


def solution(mesh):
    return jax.shard_map(
        on_device,
        mesh=mesh,
        in_specs=(
            P("dp", "seq", None),
            P("dp", "seq", None),
            P("dp", "seq", None),
            P("dp", None),
            P("dp", None),
            P(),
            P(),
            P(),
            P(),
            P(),
            P(),
            P(),
            P(),
            P(),
            P(),
            P(),
            P(),
            P(),
            P(),
        ),
        out_specs=(
            P("dp", "seq", None),
            P("dp", "seq", None),
            P("dp", "seq", None),
            P("seq", None),
            P("seq", None),
            P("seq", None),
            P("seq", None),
            P("seq", None),
            P("seq", None),
            P("seq", None),
            P("seq", None),
            P("seq", None),
            P("seq", None),
            P("seq"),
            P("seq"),
            P("seq"),
            P("seq", None),
        ),
        check_vma=False,
    )
```

```python
import functools
import math
from types import SimpleNamespace

import jax
import jax.numpy as jnp
from jax import lax
from jax.experimental import pallas as pl
from jax.experimental.pallas import tpu as pltpu
from jax.sharding import PartitionSpec as P

MESH = pl.DeviceIdType.MESH
EPS = 1e-06
NEG = -1000000000.0
NEAR = 128
F32 = jnp.float32
LOW = jnp.bfloat16


def dot(left, right):
    return jnp.dot(left, right, preferred_element_type=F32)


def dot_nt(left, right):
    return lax.dot_general(left, right, (((1,), (1,)), ((), ())), preferred_element_type=F32)


def add_low(left, right):
    return (left.astype(F32) + right.astype(F32)).astype(LOW)


def block(index, size):
    return pl.ds(pl.multiple_of(index * size, size), size)


def bucket_of(distance):
    farther = jnp.full(distance.shape, 16, jnp.int32)
    for level in range(1, 16):
        farther = farther + (distance >= math.ceil(16 * 8 ** (level / 16))).astype(jnp.int32)
    return jnp.where(distance < 16, distance, farther)


def bucket_terms(buckets):
    shape = (buckets, 2 * NEAR)
    lanes = lax.broadcasted_iota(jnp.int32, shape, 1)
    return (bucket_of(lanes) == lax.broadcasted_iota(jnp.int32, shape, 0)).astype(F32)


def scale_of(values):
    return lax.rsqrt(jnp.mean(values * values, axis=-1, keepdims=True) + EPS)


def norm_back(values, gain, grad):
    scale = scale_of(values)
    gain_grad = jnp.sum(grad * values * scale, axis=0, keepdims=True)
    inner = jnp.mean(values * gain * grad, axis=-1, keepdims=True)
    return scale * gain * grad - values * (scale * scale * scale) * inner, gain_grad


def head_blocks(pair):
    size = pair.shape[0] // 2
    zero = jnp.zeros((size, pair.shape[1]), pair.dtype)
    return jnp.concatenate(
        [
            jnp.concatenate([pair[:size], zero], axis=1),
            jnp.concatenate([zero, pair[size:]], axis=1),
        ],
        axis=0,
    )


def head_rows(both):
    size, count = both.shape[0] // 2, both.shape[1] // 2
    return jnp.concatenate([both[:size, :count], both[size:, count:]], axis=0)


def twice(values):
    return jnp.concatenate([values, values], axis=1)


def fold(values):
    return values.reshape(values.shape[0] // 8, 8, values.shape[1])


class Mesh2:
    def __init__(self):
        self.row = lax.axis_index("dp")
        self.place = lax.axis_index("seq")
        self.side, self.core = self.place // 2, lax.rem(self.place, 2)
        self.sibling = self.side * 2 + 1 - self.core
        self.across = (1 - self.side) * 2 + self.core
        self.diagonal = (1 - self.side) * 2 + 1 - self.core
        self.core_peer = (self.row, self.sibling)
        self.y_peer = (self.row, self.across)

    def greet(self, peers):
        barrier = pltpu.get_barrier_semaphore()
        for peer in peers:
            pl.semaphore_signal(barrier, inc=1, device_id=peer, device_id_type=MESH)
        pl.semaphore_wait(barrier, len(peers))


def send(src, dst, sems, slot, peer):
    return pltpu.make_async_remote_copy(
        src_ref=src,
        dst_ref=dst,
        send_sem=sems.at[(0, *slot)],
        recv_sem=sems.at[(1, *slot)],
        device_id=peer,
        device_id_type=MESH,
    )


def softmax_pair(pair, r, count, steps, keys, turned, terms, queries_t, masses, out_t, probs, place):
    lanes = block(pair, 2 * r.head_dim)
    queries = head_blocks(queries_t[lanes, :])
    near = place is not None
    if near:
        tiles = [
            pltpu.roll(
                jnp.broadcast_to(r.near_bias[pl.ds(pair * 2 + head, 1), :], (NEAR, 2 * NEAR)),
                0,
                1,
                stride=1,
                stride_axis=0,
            )
            for head in range(2)
        ]
        below = [tile[:, NEAR:] for tile in tiles]
        on = [tile[:, :NEAR] for tile in tiles]
        none = jnp.zeros((NEAR, NEAR), F32)
        before = jnp.concatenate([below[0], none, below[1], none], axis=1)
        first = jnp.concatenate([on[0], below[0], on[1], below[1]], axis=1)
        second = jnp.concatenate([none, on[0], none, on[1]], axis=1)

    def score(index, top):
        rows = block(index, count)
        raw = dot(keys[rows, lanes], queries) + twice(terms[rows, :])
        r.scores[rows, :] = raw
        return jnp.maximum(top, jnp.max(fold(raw), axis=0))

    top = jnp.full((8, 2 * count), -jnp.inf, F32)
    if near:
        def score_far(index, carry):
            rows = block(index, count)
            r.scores[rows, :] = dot(keys[rows, lanes], queries) + twice(terms[rows, :])
            return carry

        lax.fori_loop(0, place, score_far, 0)
        rows = block(place, count)
        raw = dot(keys[rows, lanes], queries) + twice(terms[rows, :])
        raw = raw + jnp.concatenate([first, second], axis=0)
        r.scores[rows, :] = raw
        top = jnp.maximum(top, jnp.max(fold(raw), axis=0))

        @pl.when(place > 0)
        def _():
            last = block(place * (count // NEAR) - 1, NEAR)
            r.scores[last, :] = r.scores[last, :] + before

        def raise_top(index, top):
            return jnp.maximum(top, jnp.max(fold(r.scores[block(index, count), :]), axis=0))

        top = lax.fori_loop(0, place, raise_top, top)
    else:
        for index in range(steps):
            top = score(index, top)
    top = jnp.max(top, axis=0, keepdims=True)

    def weigh(index, carry):
        mass, context = carry
        rows = block(index, count)
        weights = jnp.exp(r.scores[rows, :] - top)
        low = weights.astype(LOW)
        probs[rows, :] = low
        context = context + dot(turned[lanes, rows], low)
        return mass + jnp.sum(fold(weights), axis=0), context

    carry = (
        jnp.zeros((8, 2 * count), F32),
        jnp.zeros((2 * r.head_dim, 2 * count), F32),
    )
    if near:
        mass, context = lax.fori_loop(0, place + 1, weigh, carry)
    else:
        for index in range(steps):
            carry = weigh(index, carry)
        mass, context = carry
    inverse = 1.0 / jnp.sum(mass, axis=0, keepdims=True)
    masses[pair] = inverse
    out_t[lanes, :] = head_rows(context * inverse)


def forward_kernel(names, dims, *refs):
    r = SimpleNamespace(**dict(zip(names, refs)), head_dim=dims.head_dim)
    m = Mesh2()
    count, places, pairs, fan, width = dims.count, dims.places, dims.pairs, dims.fan, dims.width
    q_place = m.place

    def load(slot, src, dst):
        copy = pltpu.make_async_copy(src, dst, r.load_sem.at[slot])
        copy.start()
        return copy

    loads = SimpleNamespace(
        wk=load(0, r.wk_hbm, r.wk),
        wv=load(1, r.wv_hbm, r.wv),
        wq=load(2, r.wq_hbm, r.wq),
        wout=load(3, r.wout_hbm, r.wout),
        cwk=load(4, r.cwk_hbm, r.cwk),
        cwv=load(5, r.cwv_hbm, r.cwv),
        wo=load(6, r.wo_hbm, r.wo),
        cwq=load(7, r.cwq_hbm, r.cwq),
        cwo=load(8, r.cwo_hbm, r.cwo),
        win=load(9, r.win_hbm, r.win),
    )

    m.greet([m.core_peer, m.y_peer])
    x_y = send(r.x, r.xs.at[m.place], r.link_sem, (0,), m.y_peer)
    x_core = send(r.x, r.xs.at[m.place], r.link_sem, (1,), m.core_peer)
    x_on = send(r.xs.at[m.across], r.xs.at[m.across], r.link_sem, (2,), m.core_peer)
    e_y = send(r.e, r.es.at[m.place], r.link_sem, (3,), m.y_peer)
    e_core = send(r.e, r.es.at[m.place], r.link_sem, (4,), m.core_peer)
    e_on = send(r.es.at[m.across], r.es.at[m.across], r.link_sem, (5,), m.core_peer)
    x_y.start()
    x_core.start()
    e_core.start()
    r.xs[m.place] = r.x[...]
    r.es[m.place] = r.e[...]

    gain_self = r.gain_self[...].astype(F32)
    gain_cross = r.gain_cross[...].astype(F32)
    gain_ffn = r.gain_ffn[...].astype(F32)

    items = dims.items
    dec_starts, enc_starts = [0], [0]
    for index in range(items):
        dec_starts.append(dec_starts[-1] + r.dec_len[0, index])
        enc_starts.append(enc_starts[-1] + r.enc_len[0, index])
    query_at = q_place * count + lax.broadcasted_iota(jnp.int32, (1, count), 1)
    low_self = jnp.zeros((1, count), jnp.int32)
    low_cross = jnp.zeros((1, count), jnp.int32)
    high_cross = jnp.full((1, count), enc_starts[1], jnp.int32)
    for index in range(1, items):
        inside = query_at >= dec_starts[index]
        low_self = jnp.where(inside, dec_starts[index], low_self)
        low_cross = jnp.where(inside, enc_starts[index], low_cross)
        high_cross = jnp.where(inside, enc_starts[index + 1], high_cross)

    def masks(index, carry):
        rows = block(index, count)
        key_at = index * count + lax.broadcasted_iota(jnp.int32, (count, count), 0)
        r.self_terms[rows, :] = jnp.where((key_at >= low_self) & (key_at <= query_at), 0.0, NEG)
        r.cross_terms[rows, :] = jnp.where((key_at >= low_cross) & (key_at < high_cross), 0.0, NEG)
        return carry

    lax.fori_loop(0, places, masks, 0)

    buckets = r.table.shape[0]
    terms = bucket_terms(buckets)
    last = lax.broadcasted_iota(jnp.int32, terms.shape, 0) == buckets - 1
    terms = terms - last.astype(F32)
    r.near_bias[...] = lax.dot_general(
        r.table[...], terms.astype(LOW), (((0,), (0,)), ((), ())), preferred_element_type=F32
    )

    def self_block(place):
        rows = block(place, count)
        states = r.xs[place].astype(F32)
        normed = (states * scale_of(states) * gain_self).astype(LOW)
        r.a1[rows, :] = normed
        r.keys[rows, :] = dot(normed, r.wk[...]).astype(LOW)
        values = dot(normed, r.wv[...]).astype(LOW)
        r.values[rows, :] = values
        r.values_t[:, rows] = jnp.transpose(values)

    def cross_block(place):
        rows = block(place, count)
        encoded = r.es[place]
        r.ckeys[rows, :] = dot(encoded, r.cwk[...]).astype(LOW)
        values = dot(encoded, r.cwv[...]).astype(LOW)
        r.cvalues[rows, :] = values
        r.cvalues_t[:, rows] = jnp.transpose(values)

    loads.wk.wait()
    loads.wv.wait()
    self_block(m.place)
    loads.wq.wait()
    r.queries_t[...] = jnp.transpose(dot(r.a1[block(m.place, count), :], r.wq[...]).astype(LOW))
    x_core.wait()
    self_block(m.sibling)
    loads.wout.wait()
    cotangent = r.go[...]

    def inner_grad(index, carry):
        r.inner_grad[index] = dot_nt(cotangent, r.wout[block(index, width), :])
        return carry

    lax.fori_loop(0, fan, inner_grad, 0)
    loads.cwk.wait()
    loads.cwv.wait()
    cross_block(m.place)
    e_core.wait()
    cross_block(m.sibling)
    x_y.wait()
    x_on.start()
    e_y.start()
    self_block(m.across)
    x_on.wait()
    self_block(m.diagonal)

    def keep(src, dst, slot):
        copy = pltpu.make_async_copy(src, dst, r.keep_sem.at[slot])
        copy.start()
        return copy

    kept = [
        keep(r.keys, r.keys_out, 0),
        keep(r.values, r.values_out, 1),
        keep(r.a1, r.a1_out, 2),
    ]

    def probs_copy(slot, out, pair):
        return pltpu.make_async_copy(r.probs.at[slot], out.at[pair], r.probs_sem.at[slot])

    def attend(first, last, earlier, steps, keys, turned, terms, queries_t, masses, out_t, out, place):
        def one(pair, carry):
            slot = lax.rem(pair, 2)
            if earlier:
                probs_copy(slot, out, pair).wait()
            else:
                @pl.when(pair >= 2)
                def _():
                    probs_copy(slot, out, pair).wait()
            softmax_pair(
                pair, r, count, steps, keys, turned, terms, queries_t, masses, out_t,
                r.probs.at[slot], place,
            )
            probs_copy(slot, out, pair).start()
            return carry

        lax.fori_loop(first, last, one, 0)

    split = pairs - 2
    attend(
        0, split, False, places, r.keys, r.values_t, r.self_terms, r.queries_t,
        r.self_masses, r.context_t, r.self_probs, q_place,
    )
    e_y.wait()
    e_on.start()
    attend(
        split, pairs, split >= 2, places, r.keys, r.values_t, r.self_terms, r.queries_t,
        r.self_masses, r.context_t, r.self_probs, q_place,
    )
    loads.wo.wait()
    context = jnp.transpose(r.context_t[...]).astype(LOW)
    first = r.x[...].astype(F32) + dot(context, r.wo[...])
    r.first[...] = first
    normed_cross = (first * scale_of(first) * gain_cross).astype(LOW)
    r.a2[...] = normed_cross
    loads.cwq.wait()
    r.cqueries_t[...] = jnp.transpose(dot(normed_cross, r.cwq[...]).astype(LOW))
    cross_block(m.across)
    e_on.wait()
    cross_block(m.diagonal)
    kept += [
        keep(r.ckeys, r.ckeys_out, 3),
        keep(r.cvalues, r.cvalues_out, 4),
        keep(r.es, r.es_out, 5),
    ]
    attend(
        0, pairs, True, places, r.ckeys, r.cvalues_t, r.cross_terms, r.cqueries_t,
        r.cross_masses, r.ccontext_t, r.cross_probs, None,
    )
    loads.cwo.wait()
    context = jnp.transpose(r.ccontext_t[...]).astype(LOW)
    second = r.first[...] + dot(context, r.cwo[...])
    normed_ffn = (second * scale_of(second) * gain_ffn).astype(LOW)
    r.a3[...] = normed_ffn
    r.a3_t[...] = jnp.transpose(normed_ffn)
    r.total[...] = second
    r.back[...] = jnp.zeros_like(second)
    loads.win.wait()

    own = width // places

    def head_copy(slot, index):
        side, core = index // 2, lax.rem(index, 2)
        return pltpu.make_async_copy(
            r.head_stage.at[slot], r.big.at[core, side, pl.ds(0, width)], r.head_sem.at[slot]
        )

    def tail_copy(slot, index):
        rows = pl.ds(pl.multiple_of(width + index * own, own), own)
        return pltpu.make_async_copy(
            r.tail_stage.at[slot], r.big.at[:, :, rows], r.tail_sem.at[slot]
        )

    def feed(index, carry):
        slot = lax.rem(index, 2)
        cols = block(index, width)
        pre = dot(r.a3[...], r.win[:, cols])
        half = 0.5 + 0.5 * lax.erf(pre * (0.5**0.5))
        inner = (pre * half).astype(LOW)
        slope = half + pre * jnp.exp(-0.5 * pre * pre) * ((2.0 * math.pi) ** -0.5)
        pre_grad = (slope * r.inner_grad[index]).astype(LOW)
        r.total[...] += dot(inner, r.wout[block(index, width), :])
        r.back[...] += dot_nt(pre_grad, r.win[:, cols])

        @pl.when(index >= 2)
        def _():
            head_copy(slot, index).wait()
            tail_copy(slot, index).wait()

        r.head_stage[slot] = dot(jnp.transpose(inner), r.go[...]).astype(LOW)
        grad = dot(r.a3_t[...], pre_grad).astype(LOW)
        for place in range(places):
            r.tail_stage[slot, place % 2, place // 2] = grad[place * own : (place + 1) * own]
        head_copy(slot, index).start()
        tail_copy(slot, index).start()
        return carry

    lax.fori_loop(0, fan, feed, 0)
    r.layer_out[...] = r.total[...].astype(LOW)
    second_part, gain_grad = norm_back(second, gain_ffn, r.back[...])
    r.second_grad[...] = r.go[...].astype(F32) + second_part
    r.gain_ffn_grad[...] = gain_grad
    for slot in range(2):
        probs_copy(slot, r.cross_probs, pairs - 2 + slot).wait()
        head_copy(slot, fan - 2 + slot).wait()
        tail_copy(slot, fan - 2 + slot).wait()
    for copy in kept:
        copy.wait()


def call(kernel, name, collective, limit, inputs, outputs, scratch, aliases=None):
    names = (*inputs, *outputs, *scratch)
    results = pl.pallas_call(
        functools.partial(kernel, names),
        out_shape=tuple(jax.ShapeDtypeStruct(shape, kind) for shape, kind, _ in outputs.values()),
        in_specs=[pl.BlockSpec(memory_space=space) for _, space in inputs.values()],
        out_specs=tuple(pl.BlockSpec(memory_space=space) for _, _, space in outputs.values()),
        scratch_shapes=list(scratch.values()),
        input_output_aliases=aliases or {},
        compiler_params=pltpu.CompilerParams(
            collective_id=collective, has_side_effects=True, vmem_limit_bytes=limit * 2**20
        ),
        name=name,
    )(*(array for array, _ in inputs.values()))
    return SimpleNamespace(**dict(zip(outputs, results)))


def run_forward(dims, a):
    count, total, width = dims.count, dims.count * dims.places, dims.width
    near, far, scalars = pltpu.VMEM, pl.ANY, pltpu.SMEM
    pairs, fan = dims.pairs, dims.fan
    square = (width, width)
    own = (count, width)
    inputs = dict(
        x=(a.dec_states[0], near),
        e=(a.enc_states[0], near),
        go=(a.out_grad[0], near),
        dec_len=(a.dec_lengths, scalars),
        enc_len=(a.enc_lengths, scalars),
        table=(a.position_bias, near),
        gain_self=(a.gain_self[None], near),
        gain_cross=(a.gain_cross[None], near),
        gain_ffn=(a.gain_ffn[None], near),
        wk_hbm=(a.self_key, far),
        wv_hbm=(a.self_value, far),
        wq_hbm=(a.self_query, far),
        wout_hbm=(a.ffn_out, far),
        cwk_hbm=(a.cross_key, far),
        cwv_hbm=(a.cross_value, far),
        wo_hbm=(a.self_output, far),
        cwq_hbm=(a.cross_query, far),
        cwo_hbm=(a.cross_output, far),
        win_hbm=(a.ffn_in, far),
    )
    outputs = dict(
        layer_out=(own, LOW, near),
        first=(own, F32, near),
        second_grad=(own, F32, near),
        gain_ffn_grad=((1, width), F32, near),
        queries_t=((width, count), LOW, near),
        cqueries_t=((width, count), LOW, near),
        context_t=((width, count), F32, near),
        ccontext_t=((width, count), F32, near),
        self_masses=((pairs, 1, 2 * count), F32, near),
        cross_masses=((pairs, 1, 2 * count), F32, near),
        a2=(own, LOW, near),
        keys_out=((total, width), LOW, far),
        values_out=((total, width), LOW, far),
        a1_out=((total, width), LOW, far),
        ckeys_out=((total, width), LOW, far),
        cvalues_out=((total, width), LOW, far),
        es_out=((dims.places, *own), LOW, far),
        self_probs=((pairs, total, 2 * count), LOW, far),
        cross_probs=((pairs, total, 2 * count), LOW, far),
        big=((2, 2, 4 * width, width), LOW, far),
    )
    scratch = dict(
        xs=pltpu.VMEM((dims.places, *own), LOW),
        es=pltpu.VMEM((dims.places, *own), LOW),
        wk=pltpu.VMEM(square, LOW),
        wv=pltpu.VMEM(square, LOW),
        wq=pltpu.VMEM(square, LOW),
        wout=pltpu.VMEM((fan * width, width), LOW),
        cwk=pltpu.VMEM(square, LOW),
        cwv=pltpu.VMEM(square, LOW),
        wo=pltpu.VMEM(square, LOW),
        cwq=pltpu.VMEM(square, LOW),
        cwo=pltpu.VMEM(square, LOW),
        win=pltpu.VMEM((width, fan * width), LOW),
        a1=pltpu.VMEM((total, width), LOW),
        keys=pltpu.VMEM((total, width), LOW),
        values=pltpu.VMEM((total, width), LOW),
        values_t=pltpu.VMEM((width, total), LOW),
        ckeys=pltpu.VMEM((total, width), LOW),
        cvalues=pltpu.VMEM((total, width), LOW),
        cvalues_t=pltpu.VMEM((width, total), LOW),
        self_terms=pltpu.VMEM((total, count), F32),
        cross_terms=pltpu.VMEM((total, count), F32),
        near_bias=pltpu.VMEM((dims.heads, 2 * NEAR), F32),
        scores=pltpu.VMEM((total, 2 * count), F32),
        probs=pltpu.VMEM((2, total, 2 * count), LOW),
        inner_grad=pltpu.VMEM((fan, count, width), F32),
        a3=pltpu.VMEM(own, LOW),
        a3_t=pltpu.VMEM((width, count), LOW),
        total=pltpu.VMEM(own, F32),
        back=pltpu.VMEM(own, F32),
        head_stage=pltpu.VMEM((2, width, width), LOW),
        tail_stage=pltpu.VMEM((2, 2, 2, width // dims.places, width), LOW),
        load_sem=pltpu.SemaphoreType.DMA((10,)),
        link_sem=pltpu.SemaphoreType.DMA((2, 6)),
        keep_sem=pltpu.SemaphoreType.DMA((6,)),
        probs_sem=pltpu.SemaphoreType.DMA((2,)),
        head_sem=pltpu.SemaphoreType.DMA((2,)),
        tail_sem=pltpu.SemaphoreType.DMA((2,)),
    )
    return call(
        lambda names, *refs: forward_kernel(names, dims, *refs),
        "forward", 0, 60, inputs, outputs, scratch,
    )


class Reducer:
    LAG = 10

    def __init__(self, r, m, dims):
        self.r, self.m = r, m
        self.planes = dims.planes
        self.piece = dims.piece
        self.half_rows = self.piece * self.planes
        self.chunk_rows = 2 * self.half_rows
        self.chunks = dims.chunks
        self.ring = dims.ring
        self.plane, self.half = m.row // 2, lax.rem(m.row, 2)
        self.x_peer = (self.plane * 2 + 1 - self.half, m.place)
        self.published = 0
        self.done = 0

    def z_peer(self, step):
        return (lax.rem(self.plane + step, self.planes) * 2 + self.half, self.m.place)

    def peers(self):
        return [self.x_peer] + [self.z_peer(step) for step in range(1, self.planes)]

    def span(self, first, size):
        return pl.ds(pl.multiple_of(first, self.piece), size)

    def rows(self, index):
        return self.span(index * self.chunk_rows, self.chunk_rows)

    def kept_rows(self, index, first=0, size=None):
        slot = lax.rem(index, self.ring)
        return self.span(slot * self.chunk_rows + first, size or self.chunk_rows)

    def load(self, index):
        r = self.r
        return pltpu.make_async_copy(
            r.big.at[self.m.core, :, self.rows(index)],
            r.kept.at[:, self.kept_rows(index)],
            r.chunk_sem.at[index],
        )

    def core_copy(self, index):
        r, rows = self.r, self.rows(index)
        return send(
            r.big.at[1 - self.m.core, :, rows], r.core_recv.at[:, rows], r.core_sem, (index,),
            self.m.core_peer,
        )

    def y_copy(self, index):
        r = self.r
        return send(
            r.kept.at[1 - self.m.side, self.kept_rows(index)], r.fin.at[self.rows(index)],
            r.y_sem, (index,), self.m.y_peer,
        )

    def x_copy(self, index):
        r = self.r
        other = self.kept_rows(index, (1 - self.half) * self.half_rows, self.half_rows)
        return send(
            r.kept.at[self.m.side, other],
            r.x_recv.at[self.span(index * self.half_rows, self.half_rows)],
            r.x_sem, (index,), self.x_peer,
        )

    def z_first(self, which):
        return self.half * self.half_rows + which * self.piece

    def z_copy(self, index, step):
        r = self.r
        target = lax.rem(self.plane + step, self.planes)
        return send(
            r.kept.at[self.m.side, self.kept_rows(index, self.z_first(target), self.piece)],
            r.z_recv.at[step - 1, self.span(index * self.piece, self.piece)],
            r.z_sem, (index, step - 1), self.z_peer(step),
        )

    def own_rows(self, index):
        return self.span(index * self.chunk_rows + self.z_first(self.plane), self.piece)

    def gz_copy(self, index, step):
        r, rows = self.r, self.own_rows(index)
        return send(r.fin.at[rows], r.fin.at[rows], r.gz_sem, (index, step - 1), self.z_peer(step))

    def gx_copy(self, index):
        r = self.r
        rows = self.span(index * self.chunk_rows + self.half * self.half_rows, self.half_rows)
        return send(r.fin.at[rows], r.fin.at[rows], r.gx_sem, (index,), self.x_peer)

    def publish(self, rows):
        last = rows // self.chunk_rows

        def begin(index, carry):
            self.core_copy(index).start()
            return carry

        def fetch(index, carry):
            self.load(index).start()
            return carry

        lax.fori_loop(self.published, last, begin, 0)
        first_load = max(self.published, 0)
        last_load = min(last, max(self.ring, self.freed() + self.ring))
        lax.fori_loop(first_load, last_load, fetch, 0)
        self.published = last
        self.loaded = last_load

    def freed(self):
        return max(0, self.done - 6)

    def tick(self, step):
        r, m, chunks = self.r, self.m, self.chunks

        @pl.when(step < chunks)
        def _():
            self.load(step).wait()
            self.core_copy(step).wait()
            rows, kept = self.rows(step), self.kept_rows(step)
            for other in range(2):
                r.kept[other, kept, :] = add_low(r.kept[other, kept, :], r.core_recv[other, rows, :])
            self.y_copy(step).start()

        @pl.when((step >= 2) & (step < chunks + 2))
        def _():
            index = step - 2
            self.y_copy(index).wait()
            kept = self.kept_rows(index)
            r.kept[m.side, kept, :] = add_low(r.kept[m.side, kept, :], r.fin[self.rows(index), :])
            self.x_copy(index).start()

        @pl.when((step >= 4) & (step < chunks + 4))
        def _():
            index = step - 4
            self.x_copy(index).wait()
            kept = self.kept_rows(index, self.half * self.half_rows, self.half_rows)
            arrived = r.x_recv[self.span(index * self.half_rows, self.half_rows), :]
            r.kept[m.side, kept, :] = add_low(r.kept[m.side, kept, :], arrived)
            for plane in range(1, self.planes):
                self.z_copy(index, plane).start()

        @pl.when((step >= 6) & (step < chunks + 6))
        def _():
            index = step - 6
            kept = self.kept_rows(index, self.z_first(self.plane), self.piece)
            total = r.kept[m.side, kept, :].astype(F32)
            for plane in range(1, self.planes):
                self.z_copy(index, plane).wait()
                arrived = r.z_recv[plane - 1, self.span(index * self.piece, self.piece), :]
                total = total + arrived.astype(F32)
            r.fin[self.own_rows(index), :] = total.astype(LOW)
            for plane in range(1, self.planes):
                self.gz_copy(index, plane).start()

        @pl.when((step >= 8) & (step < chunks + 8))
        def _():
            index = step - 8
            for plane in range(1, self.planes):
                self.gz_copy(index, plane).wait()
            self.gx_copy(index).start()

        @pl.when(step >= 10)
        def _():
            self.gx_copy(step - 10).wait()

    def fetch_next(self, step, limit):
        index = step - 6 + self.ring

        @pl.when((step >= 6) & (index >= self.loaded) & (index < limit))
        def _():
            self.load(index).start()

    def run(self, ticks):
        first = self.done

        def one(step, carry):
            self.tick(step)
            self.fetch_next(step, self.published)
            return carry

        lax.fori_loop(first, first + ticks, one, 0)
        self.advance(ticks)

    def advance(self, ticks):
        self.done += ticks
        self.loaded = max(self.loaded, min(self.published, self.freed() + self.ring))

    def ready(self):
        if self.published == self.chunks:
            return self.chunks + self.LAG - self.done
        return self.published - self.done

    def beside(self, loops):
        first, ticks = self.done, min(loops, self.ready())

        def one(index):
            @pl.when(index < ticks)
            def _():
                self.tick(first + index)
                self.fetch_next(first + index, self.published)

        def after():
            self.advance(ticks)

        return one, after


def attend_back(pair, r, count, keys, keys_t, values, queries_t, masses, context_t, grad_t, probs, place, places):
    lanes = block(pair, 2 * r.head_dim)
    inverse = masses[pair]
    grads = grad_t[lanes, :].astype(F32)
    product = grads * context_t[lanes, :]
    sums = [
        jnp.sum(product[: r.head_dim], axis=0, keepdims=True),
        jnp.sum(product[r.head_dim :], axis=0, keepdims=True),
    ]
    inner = jnp.concatenate(sums, axis=1) * inverse
    grads = (head_blocks(grads) * inverse).astype(LOW)
    queries = head_blocks(queries_t[lanes, :])

    def one(index, total):
        rows = block(index, count)
        weights = probs[rows, :]
        score_grad = weights.astype(F32) * (dot(values[rows, lanes], grads) - inner)
        low = score_grad.astype(LOW)
        side, core = index // 2, lax.rem(index, 2)
        r.value_grad[side, core, :, lanes] = dot_nt(weights, grads).astype(LOW)
        r.key_grad[side, core, :, lanes] = dot_nt(low, queries).astype(LOW)
        return total + dot(keys_t[lanes, rows], low), score_grad

    total = jnp.zeros((2 * r.head_dim, 2 * count), F32)
    if place is None:
        for index in range(places):
            total, _ = one(index, total)
    else:
        r.before[...] = jnp.zeros_like(r.before)

        def far(index, carry):
            total, beyond = carry
            total, score_grad = one(index, total)
            split = count - NEAR
            beyond = beyond + jnp.sum(fold(score_grad[:split]), axis=0)
            rest = score_grad[split:]
            is_last = index == place - 1

            @pl.when(is_last)
            def _():
                r.before[...] = rest

            beyond = beyond + jnp.where(is_last, 0.0, jnp.sum(fold(rest), axis=0))
            return total, beyond

        carry = (total, jnp.zeros((8, 2 * count), F32))
        total, beyond = lax.fori_loop(0, place, far, carry)
        total, own = one(place, total)
        before = r.before[...]
        parts = []
        for head in range(2):
            at = head * count
            on = own[:NEAR, at : at + NEAR] + own[NEAR:, at + NEAR : at + 2 * NEAR]
            below = before[:, at : at + NEAR] + own[:NEAR, at + NEAR : at + 2 * NEAR]
            both = jnp.concatenate([on, below], axis=1)
            summed = both[:8]
            for group in range(1, NEAR // 8):
                summed = summed + pltpu.roll(
                    both[8 * group : 8 * group + 8], 2 * NEAR - 8 * group, 1
                )
            parts.append(summed)
        summed = jnp.concatenate(parts, axis=0)
        sublane = lax.broadcasted_iota(jnp.int32, summed.shape, 0)
        for bit in (1, 2, 4):
            summed = jnp.where(
                (sublane & bit) != 0, pltpu.roll(summed, 2 * NEAR - bit, 1), summed
            )
        lane = lax.broadcasted_iota(jnp.int32, (1, 2 * NEAR), 1)
        for head in range(2):
            at = head * count
            line = jnp.sum(summed[8 * head : 8 * head + 8], axis=0, keepdims=True)
            rest = jnp.sum(beyond[:, at : at + count]) + jnp.sum(before[:, at + NEAR : at + 2 * NEAR])
            line = line + jnp.where(lane == 2 * NEAR - 1, rest, 0.0)
            r.by_distance[pl.ds(pair * 2 + head, 1), :] = line
    r.query_grad_t[lanes, :] = head_rows(total).astype(LOW)


def backward_kernel(names, dims, *refs):
    r = SimpleNamespace(**dict(zip(names, refs)), head_dim=dims.head_dim)
    m = Mesh2()
    count, places, pairs, width = dims.count, dims.places, dims.pairs, dims.width
    own = width // places
    engine = Reducer(r, m, dims)

    loads = SimpleNamespace()
    slots = iter(range(r.load_sem.shape[0]))

    def load(src, dst):
        copy = pltpu.make_async_copy(src, dst, r.load_sem.at[next(slots)])
        copy.start()
        return copy

    def probs_copy(src, pair):
        slot = lax.rem(pair, 2)
        return pltpu.make_async_copy(src.at[pair], r.probs.at[slot], r.probs_sem.at[slot])

    loads.second = load(r.second_hbm, r.dec_grad)
    loads.cwo = load(r.cwo_hbm, r.wo)
    loads.ckeys = load(r.ckeys_hbm, r.keys)
    loads.cvalues = load(r.cvalues_hbm, r.values)
    probs_copy(r.cross_probs, 0).start()
    probs_copy(r.cross_probs, 1).start()
    loads.first = load(r.first_hbm, r.enc_grad)
    loads.cwq = load(r.cwq_hbm, r.wq)
    loads.cwk = load(r.cwk_hbm, r.wk)
    loads.cwv = load(r.cwv_hbm, r.wv)
    loads.es0 = load(r.es_hbm.at[m.core], r.group.at[0])
    loads.es1 = load(r.es_hbm.at[m.core + 2], r.group.at[1])

    m.greet([m.core_peer, m.y_peer] + engine.peers())
    engine.publish(2 * width)

    gain_self = r.gain_self[...].astype(F32)
    gain_cross = r.gain_cross[...].astype(F32)
    staged = {}

    def unit_copy(unit):
        rows = pl.ds(2 * width + unit * own, own)
        return pltpu.make_async_copy(
            r.stage.at[unit % 2], r.big.at[:, :, rows], r.stage_sem.at[unit % 2]
        )

    def give(unit, left_t, right):
        if unit - 2 in staged:
            staged.pop(unit - 2).wait()
        for place in range(places):
            grad = dot(left_t[place * own : (place + 1) * own, :], right)
            r.stage[unit % 2, place % 2, place // 2] = grad.astype(LOW)
        staged[unit] = unit_copy(unit)
        staged[unit].start()

    def settle(rows):
        for unit in sorted(staged):
            staged.pop(unit).wait()
        engine.publish(rows)

    def turn(src, dst):
        def one(index, carry):
            rows = block(index, count)
            dst[:, rows] = jnp.transpose(src[rows, :])
            return carry

        lax.fori_loop(0, places, one, 0)

    def attend(src, queries_t, masses, context_t, grad_t, place):
        tick, after = engine.beside(pairs)

        def one(pair, carry):
            probs_copy(src, pair).wait()
            attend_back(
                pair, r, count, r.keys, r.keys_t, r.values, queries_t, masses, context_t, grad_t,
                r.probs.at[lax.rem(pair, 2)], place, places,
            )

            @pl.when(pair + 2 < pairs)
            def _():
                probs_copy(src, pair + 2).start()

            tick(pair)
            return carry

        lax.fori_loop(0, pairs, one, 0)
        after()

    def exchange(slot, key_recv, value_recv):
        copies = [
            send(r.key_grad.at[:, 1 - m.core], key_recv, r.link_sem, (slot,), m.core_peer),
            send(r.value_grad.at[:, 1 - m.core], value_recv, r.link_sem, (slot + 1,), m.core_peer),
        ]
        for copy in copies:
            copy.start()
        return copies

    def chip_sum(grad, arrived):
        return add_low(grad[:, m.core], arrived[...]).reshape(2 * count, width)

    def partial(slot, side):
        key_grad = add_low(r.key_grad[side, m.core], r.key_recv[slot, side])
        value_grad = add_low(r.value_grad[side, m.core], r.value_recv[slot, side])
        return dot_nt(key_grad, r.wk[...]) + dot_nt(value_grad, r.wv[...])

    loads.second.wait()
    head_grad = r.dec_grad[...].astype(LOW)
    loads.cwo.wait()
    r.grad_t[...] = dot_nt(r.wo[...], head_grad).astype(LOW)
    loads.wo = load(r.wo_hbm, r.wo)
    give(0, r.ccontext_t[...].astype(LOW), head_grad)
    loads.ckeys.wait()
    turn(r.keys, r.keys_t)
    loads.cvalues.wait()
    attend(r.cross_probs, r.cqueries_t, r.cross_masses, r.ccontext_t, r.grad_t, None)
    copies = exchange(0, r.key_recv.at[0], r.value_recv.at[0])
    loads.keys = load(r.keys_hbm, r.keys)
    loads.values = load(r.values_hbm, r.values)
    probs_copy(r.self_probs, 0).start()
    probs_copy(r.self_probs, 1).start()
    query_grad = jnp.transpose(r.query_grad_t[...])
    loads.cwq.wait()
    normed_grad = dot_nt(query_grad, r.wq[...])
    loads.wq = load(r.wq_hbm, r.wq)
    loads.first.wait()
    first_part, gain_cross_grad = norm_back(r.enc_grad[...], gain_cross, normed_grad)
    r.dec_grad[...] += first_part
    give(1, jnp.transpose(r.a2[...]), query_grad)
    loads.es0.wait()
    loads.es1.wait()
    for side in range(2):
        r.group_t[:, side * count : (side + 1) * count] = jnp.transpose(r.group[side])
    loads.a10 = load(r.a1_hbm.at[block(m.core, count)], r.group.at[0])
    loads.a11 = load(r.a1_hbm.at[block(m.core + 2, count)], r.group.at[1])
    for copy in copies:
        copy.wait()
    key_grad = chip_sum(r.key_grad, r.key_recv.at[0])
    value_grad = chip_sum(r.value_grad, r.value_recv.at[0])
    loads.cwk.wait()
    loads.cwv.wait()
    r.partial_low[...] = partial(0, 1 - m.side).astype(LOW)
    enc_copy = send(r.partial_low, r.partial_recv.at[0], r.link_sem, (4,), m.y_peer)
    enc_copy.start()
    r.enc_grad[...] = partial(0, m.side)
    loads.wk = load(r.wk_hbm, r.wk)
    loads.wv = load(r.wv_hbm, r.wv)
    give(2, r.group_t[...], key_grad)
    give(3, r.group_t[...], value_grad)
    settle(3 * width)

    first_grad = r.dec_grad[...]
    head_grad = first_grad.astype(LOW)
    loads.wo.wait()
    r.grad_t[...] = dot_nt(r.wo[...], head_grad).astype(LOW)
    give(4, r.context_t[...].astype(LOW), head_grad)
    loads.keys.wait()
    turn(r.keys, r.keys_t)
    loads.values.wait()

    def clear(index, carry):
        side, core = index // 2, lax.rem(index, 2)
        r.key_grad[side, core] = jnp.zeros((count, width), LOW)
        r.value_grad[side, core] = jnp.zeros((count, width), LOW)
        return carry

    lax.fori_loop(m.place + 1, places, clear, 0)
    r.by_distance[...] = jnp.zeros_like(r.by_distance)
    attend(r.self_probs, r.queries_t, r.self_masses, r.context_t, r.grad_t, m.place)
    copies = exchange(2, r.key_recv.at[1], r.value_recv.at[1])
    query_grad = jnp.transpose(r.query_grad_t[...])
    loads.wq.wait()
    normed_grad = dot_nt(query_grad, r.wq[...])
    loads.a10.wait()
    loads.a11.wait()
    for side in range(2):
        r.group_t[:, side * count : (side + 1) * count] = jnp.transpose(r.group[side])
    give(5, jnp.transpose(r.group[m.side]), query_grad)
    for copy in copies:
        copy.wait()
    key_grad = chip_sum(r.key_grad, r.key_recv.at[1])
    value_grad = chip_sum(r.value_grad, r.value_recv.at[1])
    loads.wk.wait()
    loads.wv.wait()
    enc_copy.wait()
    r.enc_grad[...] += r.partial_recv[0].astype(F32)
    r.partial_low[...] = partial(1, 1 - m.side).astype(LOW)
    dec_copy = send(r.partial_low, r.partial_recv.at[1], r.link_sem, (5,), m.y_peer)
    dec_copy.start()
    normed_grad = normed_grad + partial(1, m.side)
    give(6, r.group_t[...], key_grad)
    give(7, r.group_t[...], value_grad)
    settle(4 * width)
    dec_copy.wait()
    normed_grad = normed_grad + r.partial_recv[1].astype(F32)
    state_part, gain_self_grad = norm_back(r.x[...].astype(F32), gain_self, normed_grad)
    r.dec_grad[...] += state_part

    buckets = dims.buckets
    table = lax.dot_general(
        bucket_terms(buckets), r.by_distance[...], (((1,), (1,)), ((), ())),
        precision=lax.Precision.HIGHEST, preferred_element_type=F32,
    )
    r.tiny[0] = jnp.zeros(r.tiny.shape[1:], F32)
    r.tiny[0, 0:1] = gain_self_grad
    r.tiny[0, 1:2] = gain_cross_grad
    r.tiny[0, 2:3] = r.gain_ffn_grad[...]
    part = buckets // places
    for place in range(places):
        r.tiny[0, 8 : 8 + part, 128 * place : 128 * (place + 1)] = table[
            place * part : (place + 1) * part
        ]
    for slot, peer in enumerate((m.core_peer, m.y_peer, engine.x_peer)):
        copy = send(r.tiny.at[slot], r.tiny_recv.at[slot], r.tiny_sem, (slot,), peer)
        copy.start()
        copy.wait()
        r.tiny[slot + 1] = r.tiny[slot] + r.tiny_recv[slot]
    copies = []
    for step in range(1, dims.planes):
        copy = send(
            r.tiny.at[3], r.tiny_recv.at[2 + step], r.tiny_sem, (2 + step,), engine.z_peer(step)
        )
        copy.start()
        copies.append(copy)
    for copy in copies:
        copy.wait()
    total = r.tiny[3]
    for step in range(1, dims.planes):
        total = total + r.tiny_recv[2 + step]
    r.small[...] = total
    engine.run(engine.ready())


def run_backward(dims, a, f):
    count, total, width = dims.count, dims.count * dims.places, dims.width
    near, far = pltpu.VMEM, pl.ANY
    pairs, planes, chunks, piece = dims.pairs, dims.planes, dims.chunks, dims.piece
    square = (width, width)
    own = (count, width)
    inputs = dict(
        x=(a.dec_states[0], near),
        gain_self=(a.gain_self[None], near),
        gain_cross=(a.gain_cross[None], near),
        first_hbm=(f.first, far),
        second_hbm=(f.second_grad, far),
        gain_ffn_grad=(f.gain_ffn_grad, near),
        queries_t=(f.queries_t, near),
        cqueries_t=(f.cqueries_t, near),
        context_t=(f.context_t, near),
        ccontext_t=(f.ccontext_t, near),
        self_masses=(f.self_masses, near),
        cross_masses=(f.cross_masses, near),
        a2=(f.a2, near),
        keys_hbm=(f.keys_out, far),
        values_hbm=(f.values_out, far),
        a1_hbm=(f.a1_out, far),
        ckeys_hbm=(f.ckeys_out, far),
        cvalues_hbm=(f.cvalues_out, far),
        es_hbm=(f.es_out, far),
        self_probs=(f.self_probs, far),
        cross_probs=(f.cross_probs, far),
        wo_hbm=(a.self_output, far),
        wq_hbm=(a.self_query, far),
        wk_hbm=(a.self_key, far),
        wv_hbm=(a.self_value, far),
        cwo_hbm=(a.cross_output, far),
        cwq_hbm=(a.cross_query, far),
        cwk_hbm=(a.cross_key, far),
        cwv_hbm=(a.cross_value, far),
        big_in=(f.big, far),
    )
    outputs = dict(
        big=(f.big.shape, LOW, far),
        fin=((4 * width, width), LOW, near),
        dec_grad=(own, F32, near),
        enc_grad=(own, F32, near),
        small=((16, width), F32, near),
    )
    dma = pltpu.SemaphoreType.DMA
    rows = 4 * width
    chunk_rows = 2 * planes * piece
    scratch = dict(
        wo=pltpu.VMEM(square, LOW),
        wq=pltpu.VMEM(square, LOW),
        wk=pltpu.VMEM(square, LOW),
        wv=pltpu.VMEM(square, LOW),
        keys=pltpu.VMEM((total, width), LOW),
        values=pltpu.VMEM((total, width), LOW),
        keys_t=pltpu.VMEM((width, total), LOW),
        probs=pltpu.VMEM((2, total, 2 * count), LOW),
        grad_t=pltpu.VMEM((width, count), LOW),
        query_grad_t=pltpu.VMEM((width, count), LOW),
        key_grad=pltpu.VMEM((2, 2, *own), LOW),
        value_grad=pltpu.VMEM((2, 2, *own), LOW),
        key_recv=pltpu.VMEM((2, 2, *own), LOW),
        value_recv=pltpu.VMEM((2, 2, *own), LOW),
        partial_low=pltpu.VMEM(own, LOW),
        partial_recv=pltpu.VMEM((2, *own), LOW),
        group=pltpu.VMEM((2, *own), LOW),
        group_t=pltpu.VMEM((width, 2 * count), LOW),
        before=pltpu.VMEM((NEAR, 2 * count), F32),
        by_distance=pltpu.VMEM((128, 2 * NEAR), F32),
        stage=pltpu.VMEM((2, 2, 2, width // dims.places, width), LOW),
        kept=pltpu.VMEM((2, dims.ring * chunk_rows, width), LOW),
        core_recv=pltpu.VMEM((2, rows, width), LOW),
        x_recv=pltpu.VMEM((rows // 2, width), LOW),
        z_recv=pltpu.VMEM((planes - 1, chunks * piece, width), LOW),
        tiny=pltpu.VMEM((4, 16, width), F32),
        tiny_recv=pltpu.VMEM((2 + planes, 16, width), F32),
        load_sem=dma((18,)),
        probs_sem=dma((2,)),
        stage_sem=dma((2,)),
        link_sem=dma((2, 6)),
        chunk_sem=dma((chunks,)),
        core_sem=dma((2, chunks)),
        y_sem=dma((2, chunks)),
        x_sem=dma((2, chunks)),
        z_sem=dma((2, chunks, planes - 1)),
        gz_sem=dma((2, chunks, planes - 1)),
        gx_sem=dma((2, chunks)),
        tiny_sem=dma((2, 2 + planes)),
    )
    return call(
        lambda names, *refs: backward_kernel(names, dims, *refs),
        "backward", 1, 63, inputs, outputs, scratch, {len(inputs) - 1: 0},
    )


def place_kernel(names, dims, *refs):
    r = SimpleNamespace(**dict(zip(names, refs)))
    width, fan = dims.width, dims.fan
    own = width // dims.places
    r.ffn_out_grad[...] = r.fin[:width].astype(F32)
    for index in range(fan):
        first = width + index * own
        r.ffn_in_grad[:, index * width : (index + 1) * width] = r.fin[first : first + own].astype(F32)
    units = (
        r.cross_output, r.cross_query, r.cross_key, r.cross_value,
        r.self_output, r.self_query, r.self_key, r.self_value,
    )
    for index, grad in enumerate(units):
        first = 2 * width + index * own
        grad[...] = r.fin[first : first + own].astype(F32)
    r.layer[...] = r.layer_in[...]
    r.dec[...] = r.dec_in[...]
    r.enc[...] = r.enc_in[...]
    at = lax.axis_index("seq")
    part = dims.buckets // dims.places
    for place in range(dims.places):
        @pl.when(at == place)
        def _():
            for index, grad in enumerate((r.gain_self, r.gain_cross, r.gain_ffn)):
                grad[...] = r.small[index : index + 1, place * own : (place + 1) * own]
            r.table_grad[...] = r.small[8 : 8 + part, 128 * place : 128 * place + dims.heads]


def run_place(dims, f, b):
    near = pltpu.VMEM
    width, own = dims.width, dims.width // dims.places
    square, gain = ((own, width), F32, near), ((1, own), F32, near)
    inputs = dict(
        fin=(b.fin, near),
        small=(b.small, near),
        layer_in=(f.layer_out, near),
        dec_in=(b.dec_grad, near),
        enc_in=(b.enc_grad, near),
    )
    outputs = dict(
        layer=(f.layer_out.shape, LOW, near),
        dec=(b.dec_grad.shape, F32, near),
        enc=(b.enc_grad.shape, F32, near),
        ffn_out_grad=((width, width), F32, near),
        ffn_in_grad=((own, dims.fan * width), F32, near),
        cross_output=square,
        cross_query=square,
        cross_key=square,
        cross_value=square,
        self_output=square,
        self_query=square,
        self_key=square,
        self_value=square,
        gain_self=gain,
        gain_cross=gain,
        gain_ffn=gain,
        table_grad=((dims.buckets // dims.places, dims.heads), F32, near),
    )
    names = (*inputs, *outputs)
    results = pl.pallas_call(
        lambda *refs: place_kernel(names, dims, *refs),
        out_shape=tuple(jax.ShapeDtypeStruct(shape, kind) for shape, kind, _ in outputs.values()),
        in_specs=[pl.BlockSpec(memory_space=space) for _, space in inputs.values()],
        out_specs=tuple(pl.BlockSpec(memory_space=space) for _, _, space in outputs.values()),
        compiler_params=pltpu.CompilerParams(vmem_limit_bytes=40 * 2**20),
        name="place",
    )(*(array for array, _ in inputs.values()))
    return SimpleNamespace(**dict(zip(outputs, results)))


def on_device(
    dec_states,
    enc_states,
    out_grad,
    dec_lengths,
    enc_lengths,
    self_query,
    self_key,
    self_value,
    self_output,
    cross_query,
    cross_key,
    cross_value,
    cross_output,
    ffn_in,
    ffn_out,
    gain_self,
    gain_cross,
    gain_ffn,
    position_bias,
):
    a = SimpleNamespace(
        dec_states=dec_states,
        enc_states=enc_states,
        out_grad=out_grad,
        dec_lengths=dec_lengths,
        enc_lengths=enc_lengths,
        self_query=self_query,
        self_key=self_key,
        self_value=self_value,
        self_output=self_output,
        cross_query=cross_query,
        cross_key=cross_key,
        cross_value=cross_value,
        cross_output=cross_output,
        ffn_in=ffn_in,
        ffn_out=ffn_out,
        gain_self=gain_self,
        gain_cross=gain_cross,
        gain_ffn=gain_ffn,
        position_bias=position_bias,
    )
    count, width = a.dec_states.shape[1:]
    buckets, heads = a.position_bias.shape
    planes, piece = lax.axis_size("dp") // 2, 16
    chunks = 4 * width // (2 * planes * piece)
    dims = SimpleNamespace(
        count=count,
        width=width,
        places=lax.axis_size("seq"),
        heads=heads,
        head_dim=width // heads,
        pairs=heads // 2,
        fan=a.ffn_in.shape[1] // width,
        items=a.dec_lengths.shape[1],
        buckets=buckets,
        planes=planes,
        piece=piece,
        chunks=chunks,
        ring=min(chunks, 12),
    )
    f = run_forward(dims, a)
    b = run_backward(dims, a, f)
    o = run_place(dims, f, b)
    return (
        o.layer[None],
        o.dec[None],
        o.enc[None],
        o.self_query,
        o.self_key,
        o.self_value,
        o.self_output,
        o.cross_query,
        o.cross_key,
        o.cross_value,
        o.cross_output,
        o.ffn_in_grad,
        o.ffn_out_grad,
        o.gain_self[0],
        o.gain_cross[0],
        o.gain_ffn[0],
        o.table_grad,
    )


def solution(mesh):
    split = P("dp", "seq", None)
    rows = P("seq", None)
    return jax.shard_map(
        on_device,
        mesh=mesh,
        in_specs=(split,) * 3 + (P("dp", None),) * 2 + (P(),) * 14,
        out_specs=(split,) * 3 + (rows,) * 10 + (P("seq"),) * 3 + (rows,),
        check_vma=False,
    )
```

```python
import functools
import math
from types import SimpleNamespace

import jax
import jax.numpy as jnp
from jax import lax
from jax.experimental import pallas as pl
from jax.experimental.pallas import tpu as pltpu
from jax.sharding import PartitionSpec as P

MESH = pl.DeviceIdType.MESH
EPS = 1e-06
NEG = -1000000000.0
NEAR = 128
F32 = jnp.float32
LOW = jnp.bfloat16


def dot(left, right):
    return jnp.dot(left, right, preferred_element_type=F32)


def dot_nt(left, right):
    return lax.dot_general(left, right, (((1,), (1,)), ((), ())), preferred_element_type=F32)


def add_low(left, right):
    return (left.astype(F32) + right.astype(F32)).astype(LOW)


def block(index, size):
    return pl.ds(pl.multiple_of(index * size, size), size)


def bucket_of(distance):
    farther = jnp.full(distance.shape, 16, jnp.int32)
    for level in range(1, 16):
        farther = farther + (distance >= math.ceil(16 * 8 ** (level / 16))).astype(jnp.int32)
    return jnp.where(distance < 16, distance, farther)


def bucket_terms(buckets):
    shape = (buckets, 2 * NEAR)
    lanes = lax.broadcasted_iota(jnp.int32, shape, 1)
    return (bucket_of(lanes) == lax.broadcasted_iota(jnp.int32, shape, 0)).astype(F32)


def scale_of(values):
    return lax.rsqrt(jnp.mean(values * values, axis=-1, keepdims=True) + EPS)


def norm_back(values, gain, grad):
    scale = scale_of(values)
    gain_grad = jnp.sum(grad * values * scale, axis=0, keepdims=True)
    inner = jnp.mean(values * gain * grad, axis=-1, keepdims=True)
    return scale * gain * grad - values * (scale * scale * scale) * inner, gain_grad


def head_blocks(pair):
    size = pair.shape[0] // 2
    zero = jnp.zeros((size, pair.shape[1]), pair.dtype)
    return jnp.concatenate(
        [
            jnp.concatenate([pair[:size], zero], axis=1),
            jnp.concatenate([zero, pair[size:]], axis=1),
        ],
        axis=0,
    )


def head_rows(both):
    size, count = both.shape[0] // 2, both.shape[1] // 2
    return jnp.concatenate([both[:size, :count], both[size:, count:]], axis=0)


def twice(values):
    return jnp.concatenate([values, values], axis=1)


def fold(values):
    return values.reshape(values.shape[0] // 8, 8, values.shape[1])


class Mesh2:
    def __init__(self):
        self.row = lax.axis_index("dp")
        self.place = lax.axis_index("seq")
        self.side, self.core = self.place // 2, lax.rem(self.place, 2)
        self.sibling = self.side * 2 + 1 - self.core
        self.across = (1 - self.side) * 2 + self.core
        self.diagonal = (1 - self.side) * 2 + 1 - self.core
        self.core_peer = (self.row, self.sibling)
        self.y_peer = (self.row, self.across)

    def greet(self, peers):
        barrier = pltpu.get_barrier_semaphore()
        for peer in peers:
            pl.semaphore_signal(barrier, inc=1, device_id=peer, device_id_type=MESH)
        pl.semaphore_wait(barrier, len(peers))


def send(src, dst, sems, slot, peer):
    return pltpu.make_async_remote_copy(
        src_ref=src,
        dst_ref=dst,
        send_sem=sems.at[(0, *slot)],
        recv_sem=sems.at[(1, *slot)],
        device_id=peer,
        device_id_type=MESH,
    )


def softmax_pair(pair, r, count, steps, keys, turned, terms, queries_t, masses, out_t, probs, place):
    lanes = block(pair, 2 * r.head_dim)
    queries = head_blocks(queries_t[lanes, :])
    near = place is not None
    if near:
        tiles = [
            pltpu.roll(
                jnp.broadcast_to(r.near_bias[pl.ds(pair * 2 + head, 1), :], (NEAR, 2 * NEAR)),
                0,
                1,
                stride=1,
                stride_axis=0,
            )
            for head in range(2)
        ]
        below = [tile[:, NEAR:] for tile in tiles]
        on = [tile[:, :NEAR] for tile in tiles]
        none = jnp.zeros((NEAR, NEAR), F32)
        before = jnp.concatenate([below[0], none, below[1], none], axis=1)
        first = jnp.concatenate([on[0], below[0], on[1], below[1]], axis=1)
        second = jnp.concatenate([none, on[0], none, on[1]], axis=1)

    def score(index, top):
        rows = block(index, count)
        raw = dot(keys[rows, lanes], queries) + twice(terms[rows, :])
        r.scores[rows, :] = raw
        return jnp.maximum(top, jnp.max(fold(raw), axis=0))

    top = jnp.full((8, 2 * count), -jnp.inf, F32)
    if near:
        def score_far(index, carry):
            rows = block(index, count)
            r.scores[rows, :] = dot(keys[rows, lanes], queries) + twice(terms[rows, :])
            return carry

        lax.fori_loop(0, place, score_far, 0)
        rows = block(place, count)
        raw = dot(keys[rows, lanes], queries) + twice(terms[rows, :])
        raw = raw + jnp.concatenate([first, second], axis=0)
        r.scores[rows, :] = raw
        top = jnp.maximum(top, jnp.max(fold(raw), axis=0))

        @pl.when(place > 0)
        def _():
            last = block(place * (count // NEAR) - 1, NEAR)
            r.scores[last, :] = r.scores[last, :] + before

        def raise_top(index, top):
            return jnp.maximum(top, jnp.max(fold(r.scores[block(index, count), :]), axis=0))

        top = lax.fori_loop(0, place, raise_top, top)
    else:
        for index in range(steps):
            top = score(index, top)
    top = jnp.max(top, axis=0, keepdims=True)

    def weigh(index, carry):
        mass, context = carry
        rows = block(index, count)
        weights = jnp.exp(r.scores[rows, :] - top)
        low = weights.astype(LOW)
        probs[rows, :] = low
        context = context + dot(turned[lanes, rows], low)
        return mass + jnp.sum(fold(weights), axis=0), context

    carry = (
        jnp.zeros((8, 2 * count), F32),
        jnp.zeros((2 * r.head_dim, 2 * count), F32),
    )
    if near:
        mass, context = lax.fori_loop(0, place + 1, weigh, carry)
    else:
        for index in range(steps):
            carry = weigh(index, carry)
        mass, context = carry
    inverse = 1.0 / jnp.sum(mass, axis=0, keepdims=True)
    masses[pair] = inverse
    out_t[lanes, :] = head_rows(context * inverse)


def forward_kernel(names, dims, *refs):
    r = SimpleNamespace(**dict(zip(names, refs)), head_dim=dims.head_dim)
    m = Mesh2()
    count, places, pairs, fan, width = dims.count, dims.places, dims.pairs, dims.fan, dims.width
    q_place = m.place

    def load(slot, src, dst):
        copy = pltpu.make_async_copy(src, dst, r.load_sem.at[slot])
        copy.start()
        return copy

    loads = SimpleNamespace(
        wk=load(0, r.wk_hbm, r.wk),
        wv=load(1, r.wv_hbm, r.wv),
        wq=load(2, r.wq_hbm, r.wq),
        wout=load(3, r.wout_hbm, r.wout),
        cwk=load(4, r.cwk_hbm, r.cwk),
        cwv=load(5, r.cwv_hbm, r.cwv),
        wo=load(6, r.wo_hbm, r.wo),
        cwq=load(7, r.cwq_hbm, r.cwq),
        cwo=load(8, r.cwo_hbm, r.cwo),
        win=load(9, r.win_hbm, r.win),
    )

    m.greet([m.core_peer, m.y_peer])
    x_y = send(r.x, r.xs.at[m.place], r.link_sem, (0,), m.y_peer)
    x_core = send(r.x, r.xs.at[m.place], r.link_sem, (1,), m.core_peer)
    x_on = send(r.xs.at[m.across], r.xs.at[m.across], r.link_sem, (2,), m.core_peer)
    e_y = send(r.e, r.es.at[m.place], r.link_sem, (3,), m.y_peer)
    e_core = send(r.e, r.es.at[m.place], r.link_sem, (4,), m.core_peer)
    e_on = send(r.es.at[m.across], r.es.at[m.across], r.link_sem, (5,), m.core_peer)
    x_y.start()
    x_core.start()
    e_core.start()
    r.xs[m.place] = r.x[...]
    r.es[m.place] = r.e[...]

    gain_self = r.gain_self[...].astype(F32).reshape(1, width)
    gain_cross = r.gain_cross[...].astype(F32).reshape(1, width)
    gain_ffn = r.gain_ffn[...].astype(F32).reshape(1, width)

    items = dims.items
    dec_starts, enc_starts = [0], [0]
    for index in range(items):
        dec_starts.append(dec_starts[-1] + r.dec_len[0, index])
        enc_starts.append(enc_starts[-1] + r.enc_len[0, index])
    query_at = q_place * count + lax.broadcasted_iota(jnp.int32, (1, count), 1)
    low_self = jnp.zeros((1, count), jnp.int32)
    low_cross = jnp.zeros((1, count), jnp.int32)
    high_cross = jnp.full((1, count), enc_starts[1], jnp.int32)
    for index in range(1, items):
        inside = query_at >= dec_starts[index]
        low_self = jnp.where(inside, dec_starts[index], low_self)
        low_cross = jnp.where(inside, enc_starts[index], low_cross)
        high_cross = jnp.where(inside, enc_starts[index + 1], high_cross)

    def masks(index, carry):
        rows = block(index, count)
        key_at = index * count + lax.broadcasted_iota(jnp.int32, (count, count), 0)
        r.self_terms[rows, :] = jnp.where((key_at >= low_self) & (key_at <= query_at), 0.0, NEG)
        r.cross_terms[rows, :] = jnp.where((key_at >= low_cross) & (key_at < high_cross), 0.0, NEG)
        return carry

    lax.fori_loop(0, places, masks, 0)

    buckets = r.table.shape[1]
    terms = bucket_terms(buckets)
    last = lax.broadcasted_iota(jnp.int32, terms.shape, 0) == buckets - 1
    terms = terms - last.astype(F32)
    r.near_bias[...] = dot(r.table[...], terms.astype(LOW))

    def self_block(place):
        rows = block(place, count)
        states = r.xs[place].astype(F32)
        normed = (states * scale_of(states) * gain_self).astype(LOW)
        r.a1[rows, :] = normed
        r.keys[rows, :] = dot(normed, r.wk[...]).astype(LOW)
        values = dot(normed, r.wv[...]).astype(LOW)
        r.values[rows, :] = values
        r.values_t[:, rows] = jnp.transpose(values)

    def cross_block(place):
        rows = block(place, count)
        encoded = r.es[place]
        r.ckeys[rows, :] = dot(encoded, r.cwk[...]).astype(LOW)
        values = dot(encoded, r.cwv[...]).astype(LOW)
        r.cvalues[rows, :] = values
        r.cvalues_t[:, rows] = jnp.transpose(values)

    loads.wk.wait()
    loads.wv.wait()
    self_block(m.place)
    loads.wq.wait()
    r.queries_t[...] = jnp.transpose(dot(r.a1[block(m.place, count), :], r.wq[...]).astype(LOW))
    x_core.wait()
    self_block(m.sibling)
    loads.wout.wait()
    cotangent = r.go[...]

    def inner_grad(index, carry):
        r.inner_grad[index] = dot_nt(cotangent, r.wout[block(index, width), :])
        return carry

    lax.fori_loop(0, fan, inner_grad, 0)
    loads.cwk.wait()
    loads.cwv.wait()
    cross_block(m.place)
    e_core.wait()
    cross_block(m.sibling)
    x_y.wait()
    x_on.start()
    e_y.start()
    self_block(m.across)
    x_on.wait()
    self_block(m.diagonal)

    def keep(src, dst, slot):
        copy = pltpu.make_async_copy(src, dst, r.keep_sem.at[slot])
        copy.start()
        return copy

    kept = [
        keep(r.keys, r.keys_out, 0),
        keep(r.values, r.values_out, 1),
        keep(r.a1, r.a1_out, 2),
    ]

    def probs_copy(slot, out, pair):
        return pltpu.make_async_copy(r.probs.at[slot], out.at[pair], r.probs_sem.at[slot])

    def attend(first, last, earlier, steps, keys, turned, terms, queries_t, masses, out_t, out, place):
        def one(pair, carry):
            slot = lax.rem(pair, 2)
            if earlier:
                probs_copy(slot, out, pair).wait()
            else:
                @pl.when(pair >= 2)
                def _():
                    probs_copy(slot, out, pair).wait()
            softmax_pair(
                pair, r, count, steps, keys, turned, terms, queries_t, masses, out_t,
                r.probs.at[slot], place,
            )
            probs_copy(slot, out, pair).start()
            return carry

        lax.fori_loop(first, last, one, 0)

    split = pairs - 2
    attend(
        0, split, False, places, r.keys, r.values_t, r.self_terms, r.queries_t,
        r.self_masses, r.context_t, r.self_probs, q_place,
    )
    e_y.wait()
    e_on.start()
    attend(
        split, pairs, split >= 2, places, r.keys, r.values_t, r.self_terms, r.queries_t,
        r.self_masses, r.context_t, r.self_probs, q_place,
    )
    loads.wo.wait()
    context = jnp.transpose(r.context_t[...]).astype(LOW)
    first = r.x[...].astype(F32) + dot(context, r.wo[...])
    r.first[...] = first
    normed_cross = (first * scale_of(first) * gain_cross).astype(LOW)
    r.a2[...] = normed_cross
    loads.cwq.wait()
    r.cqueries_t[...] = jnp.transpose(dot(normed_cross, r.cwq[...]).astype(LOW))
    cross_block(m.across)
    e_on.wait()
    cross_block(m.diagonal)
    kept += [
        keep(r.ckeys, r.ckeys_out, 3),
        keep(r.cvalues, r.cvalues_out, 4),
        keep(r.es, r.es_out, 5),
    ]
    attend(
        0, pairs, True, places, r.ckeys, r.cvalues_t, r.cross_terms, r.cqueries_t,
        r.cross_masses, r.ccontext_t, r.cross_probs, None,
    )
    loads.cwo.wait()
    context = jnp.transpose(r.ccontext_t[...]).astype(LOW)
    second = r.first[...] + dot(context, r.cwo[...])
    normed_ffn = (second * scale_of(second) * gain_ffn).astype(LOW)
    r.a3[...] = normed_ffn
    r.a3_t[...] = jnp.transpose(normed_ffn)
    r.total[...] = second
    r.back[...] = jnp.zeros_like(second)
    loads.win.wait()

    own = width // places

    def head_copy(slot, index):
        side, core = index // 2, lax.rem(index, 2)
        return pltpu.make_async_copy(
            r.head_stage.at[slot], r.big.at[core, side, pl.ds(0, width)], r.head_sem.at[slot]
        )

    def tail_copy(slot, index):
        rows = pl.ds(pl.multiple_of(width + index * own, own), own)
        return pltpu.make_async_copy(
            r.tail_stage.at[slot], r.big.at[:, :, rows], r.tail_sem.at[slot]
        )

    def feed(index, carry):
        slot = lax.rem(index, 2)
        cols = block(index, width)
        pre = dot(r.a3[...], r.win[:, cols])
        half = 0.5 + 0.5 * lax.erf(pre * (0.5**0.5))
        inner = (pre * half).astype(LOW)
        slope = half + pre * jnp.exp(-0.5 * pre * pre) * ((2.0 * math.pi) ** -0.5)
        pre_grad = (slope * r.inner_grad[index]).astype(LOW)
        r.total[...] += dot(inner, r.wout[block(index, width), :])
        r.back[...] += dot_nt(pre_grad, r.win[:, cols])

        @pl.when(index >= 2)
        def _():
            head_copy(slot, index).wait()
            tail_copy(slot, index).wait()

        r.head_stage[slot] = dot(jnp.transpose(inner), r.go[...]).astype(LOW)
        grad = dot(r.a3_t[...], pre_grad).astype(LOW)
        for place in range(places):
            r.tail_stage[slot, place % 2, place // 2] = grad[place * own : (place + 1) * own]
        head_copy(slot, index).start()
        tail_copy(slot, index).start()
        return carry

    lax.fori_loop(0, fan, feed, 0)
    r.layer_out[...] = r.total[...].astype(LOW)
    second_part, gain_grad = norm_back(second, gain_ffn, r.back[...])
    r.second_grad[...] = r.go[...].astype(F32) + second_part
    r.gain_ffn_grad[...] = gain_grad
    for slot in range(2):
        probs_copy(slot, r.cross_probs, pairs - 2 + slot).wait()
        head_copy(slot, fan - 2 + slot).wait()
        tail_copy(slot, fan - 2 + slot).wait()
    for copy in kept:
        copy.wait()


def call(kernel, name, collective, limit, inputs, outputs, scratch, aliases=None):
    names = (*inputs, *outputs, *scratch)
    results = pl.pallas_call(
        functools.partial(kernel, names),
        out_shape=tuple(jax.ShapeDtypeStruct(shape, kind) for shape, kind, _ in outputs.values()),
        in_specs=[pl.BlockSpec(memory_space=space) for _, space in inputs.values()],
        out_specs=tuple(pl.BlockSpec(memory_space=space) for _, _, space in outputs.values()),
        scratch_shapes=list(scratch.values()),
        input_output_aliases=aliases or {},
        compiler_params=pltpu.CompilerParams(
            collective_id=collective, has_side_effects=True, vmem_limit_bytes=limit * 2**20
        ),
        name=name,
    )(*(array for array, _ in inputs.values()))
    return SimpleNamespace(**dict(zip(outputs, results)))


def run_forward(dims, a):
    count, total, width = dims.count, dims.count * dims.places, dims.width
    near, far, scalars = pltpu.VMEM, pl.ANY, pltpu.SMEM
    pairs, fan = dims.pairs, dims.fan
    square = (width, width)
    own = (count, width)
    inputs = dict(
        x=(a.dec_states[0], near),
        e=(a.enc_states[0], near),
        go=(a.out_grad[0], near),
        dec_len=(a.dec_lengths, scalars),
        enc_len=(a.enc_lengths, scalars),
        table=(a.position_bias.T, near),
        gain_self=(a.gain_self, near),
        gain_cross=(a.gain_cross, near),
        gain_ffn=(a.gain_ffn, near),
        wk_hbm=(a.self_key, far),
        wv_hbm=(a.self_value, far),
        wq_hbm=(a.self_query, far),
        wout_hbm=(a.ffn_out, far),
        cwk_hbm=(a.cross_key, far),
        cwv_hbm=(a.cross_value, far),
        wo_hbm=(a.self_output, far),
        cwq_hbm=(a.cross_query, far),
        cwo_hbm=(a.cross_output, far),
        win_hbm=(a.ffn_in, far),
    )
    outputs = dict(
        layer_out=(own, LOW, near),
        first=(own, F32, near),
        second_grad=(own, F32, near),
        gain_ffn_grad=((1, width), F32, near),
        queries_t=((width, count), LOW, near),
        cqueries_t=((width, count), LOW, near),
        context_t=((width, count), F32, near),
        ccontext_t=((width, count), F32, near),
        self_masses=((pairs, 1, 2 * count), F32, near),
        cross_masses=((pairs, 1, 2 * count), F32, near),
        a2=(own, LOW, near),
        keys_out=((total, width), LOW, far),
        values_out=((total, width), LOW, far),
        a1_out=((total, width), LOW, far),
        ckeys_out=((total, width), LOW, far),
        cvalues_out=((total, width), LOW, far),
        es_out=((dims.places, *own), LOW, far),
        self_probs=((pairs, total, 2 * count), LOW, far),
        cross_probs=((pairs, total, 2 * count), LOW, far),
        big=((2, 2, 4 * width, width), LOW, far),
    )
    scratch = dict(
        xs=pltpu.VMEM((dims.places, *own), LOW),
        es=pltpu.VMEM((dims.places, *own), LOW),
        wk=pltpu.VMEM(square, LOW),
        wv=pltpu.VMEM(square, LOW),
        wq=pltpu.VMEM(square, LOW),
        wout=pltpu.VMEM((fan * width, width), LOW),
        cwk=pltpu.VMEM(square, LOW),
        cwv=pltpu.VMEM(square, LOW),
        wo=pltpu.VMEM(square, LOW),
        cwq=pltpu.VMEM(square, LOW),
        cwo=pltpu.VMEM(square, LOW),
        win=pltpu.VMEM((width, fan * width), LOW),
        a1=pltpu.VMEM((total, width), LOW),
        keys=pltpu.VMEM((total, width), LOW),
        values=pltpu.VMEM((total, width), LOW),
        values_t=pltpu.VMEM((width, total), LOW),
        ckeys=pltpu.VMEM((total, width), LOW),
        cvalues=pltpu.VMEM((total, width), LOW),
        cvalues_t=pltpu.VMEM((width, total), LOW),
        self_terms=pltpu.VMEM((total, count), F32),
        cross_terms=pltpu.VMEM((total, count), F32),
        near_bias=pltpu.VMEM((dims.heads, 2 * NEAR), F32),
        scores=pltpu.VMEM((total, 2 * count), F32),
        probs=pltpu.VMEM((2, total, 2 * count), LOW),
        inner_grad=pltpu.VMEM((fan, count, width), F32),
        a3=pltpu.VMEM(own, LOW),
        a3_t=pltpu.VMEM((width, count), LOW),
        total=pltpu.VMEM(own, F32),
        back=pltpu.VMEM(own, F32),
        head_stage=pltpu.VMEM((2, width, width), LOW),
        tail_stage=pltpu.VMEM((2, 2, 2, width // dims.places, width), LOW),
        load_sem=pltpu.SemaphoreType.DMA((10,)),
        link_sem=pltpu.SemaphoreType.DMA((2, 6)),
        keep_sem=pltpu.SemaphoreType.DMA((6,)),
        probs_sem=pltpu.SemaphoreType.DMA((2,)),
        head_sem=pltpu.SemaphoreType.DMA((2,)),
        tail_sem=pltpu.SemaphoreType.DMA((2,)),
    )
    return call(
        lambda names, *refs: forward_kernel(names, dims, *refs),
        "forward", 0, 60, inputs, outputs, scratch,
    )


class Reducer:
    LAGS = (0, 3, 5, 7, 9, 11)

    def __init__(self, r, m, dims):
        self.r, self.m = r, m
        self.planes = dims.planes
        self.line = dims.line
        self.piece = dims.piece
        self.chunk_rows = dims.chunk_rows
        self.half_rows = dims.chunk_rows // 2
        self.chunks = dims.chunks
        self.ring = dims.ring
        self.plane, self.half = m.row // 2, lax.rem(m.row, 2)
        self.x_peer = (self.plane * 2 + 1 - self.half, m.place)
        self.published = self.loaded = self.fed = self.moved = 0

    def z_peer(self, step):
        return (lax.rem(self.plane + step, self.planes) * 2 + self.half, self.m.place)

    def plane_peer(self, plane):
        return (plane * 2 + self.half, self.m.place)

    def peers(self):
        return [self.x_peer] + [self.z_peer(step) for step in range(1, self.planes)]

    def span(self, first, size):
        return pl.ds(pl.multiple_of(first, self.piece), size)

    def rows(self, index):
        return self.span(index * self.chunk_rows, self.chunk_rows)

    def by_planes(self, index):
        return lax.rem(index, 3) == 1

    def route(self, index, first, other):
        if not self.line:
            first(index)
            return
        special = self.by_planes(index)

        @pl.when(jnp.logical_not(special))
        def _():
            first(index)

        @pl.when(special)
        def _():
            other(index)

    def half_of(self, index, half):
        return self.span(index * self.chunk_rows + half * self.half_rows, self.half_rows)

    def packed(self, index):
        return self.span(index * self.half_rows, self.half_rows)

    def fresh_rows(self, index):
        return self.span(lax.rem(index, self.ring) * self.chunk_rows, self.chunk_rows)

    def load(self, index):
        r = self.r
        return pltpu.make_async_copy(
            r.big.at[self.m.core, :, self.rows(index)],
            r.fresh.at[:, self.fresh_rows(index)],
            r.chunk_sem.at[index],
        )

    def core_copy(self, index):
        r, rows = self.r, self.rows(index)
        return send(
            r.big.at[1 - self.m.core, :, rows], r.sums.at[:, rows], r.core_sem, (index,),
            self.m.core_peer,
        )

    def y_copy(self, index):
        r, rows = self.r, self.rows(index)
        return send(
            r.sums.at[1 - self.m.side, rows], r.fin.at[rows], r.y_sem, (index,), self.m.y_peer
        )

    def x_copy(self, index):
        r = self.r
        return send(
            r.sums.at[self.m.side, self.half_of(index, 1 - self.half)],
            r.x_recv.at[self.packed(index)],
            r.x_sem, (index,), self.x_peer,
        )

    def in_copy(self, index, inner):
        r = self.r
        return send(
            r.sums.at[self.m.side, self.half_of(index, self.half)],
            r.z_recv.at[0, self.packed(index)],
            r.z_sem, (index, 0), self.plane_peer(inner),
        )

    def mid_copy(self, index):
        r = self.r
        return send(
            r.sums.at[self.m.side, self.half_of(index, self.half)],
            r.z_recv.at[1, self.packed(index)],
            r.z_sem, (index, 1), self.plane_peer(3 - self.plane),
        )

    def out_copy(self, index, outer):
        r, rows = self.r, self.half_of(index, self.half)
        return send(r.fin.at[rows], r.fin.at[rows], r.gz_sem, (index, 0), self.plane_peer(outer))

    def z_part(self, index, which):
        first = index * self.chunk_rows + self.half * self.half_rows + which * self.piece
        return self.span(first, self.piece)

    def z_copy(self, index, step):
        r = self.r
        target = lax.rem(self.plane + step, self.planes)
        return send(
            r.sums.at[self.m.side, self.z_part(index, target)],
            r.z_recv.at[step - 1, self.span(index * self.piece, self.piece)],
            r.z_sem, (index, step - 1), self.z_peer(step),
        )

    def gz_copy(self, index, step):
        r, rows = self.r, self.z_part(index, self.plane)
        return send(r.fin.at[rows], r.fin.at[rows], r.gz_sem, (index, step - 1), self.z_peer(step))

    def gx_copy(self, index):
        r, rows = self.r, self.half_of(index, self.half)
        return send(r.fin.at[rows], r.fin.at[rows], r.gx_sem, (index,), self.x_peer)

    def publish(self, rows):
        last = rows // self.chunk_rows

        def begin(index, carry):
            self.core_copy(index).start()
            return carry

        def fetch(index, carry):
            self.load(index).start()
            return carry

        lax.fori_loop(self.published, last, begin, 0)
        ahead = min(last, self.fed + self.ring)
        lax.fori_loop(self.loaded, ahead, fetch, 0)
        self.published, self.loaded = last, max(self.loaded, ahead)

    def feed(self, index):
        r = self.r
        self.load(index).wait()
        self.core_copy(index).wait()
        rows, fresh = self.rows(index), self.fresh_rows(index)
        for side in range(2):
            r.sums[side, rows, :] = add_low(r.sums[side, rows, :], r.fresh[side, fresh, :])
        self.route(
            index, lambda at: self.y_copy(at).start(), lambda at: self.swap_copy(at).start()
        )

        @pl.when(index + self.ring < self.published)
        def _():
            self.load(index + self.ring).start()

    def move(self, step):
        stages = (
            (self.after_y, self.after_swap),
            (self.after_x, self.swapped_y),
            (self.inward, self.swapped_x),
            (self.middle, self.swapped_pair),
            (self.outward, self.swapped_back),
            (self.finish, self.swapped_finish),
        )
        for lag, stage in reversed(tuple(zip(self.LAGS, stages))):
            index = step - lag

            @pl.when((index >= 0) & (index < self.chunks))
            def _():
                self.route(index, *stage)


    def parity(self):
        return lax.rem(self.plane, 2)

    def neighbour(self):
        return self.plane_peer(self.plane + 1 - 2 * self.parity())

    def quarter_of(self, index, half):
        size = self.half_rows // 2
        first = index * self.chunk_rows + self.parity() * self.half_rows + half * size
        return self.span(first, size)

    def packed_quarter(self, index, which):
        size = self.half_rows // 2
        return self.span(index * self.half_rows + which * size, size)

    def swap_copy(self, index):
        r = self.r
        return send(
            r.sums.at[:, self.half_of(index, 1 - self.parity())],
            r.z_recv.at[:, self.packed(index)],
            r.z_sem, (index, 0), self.neighbour(),
        )

    def swapped_y_copy(self, index):
        r, rows = self.r, self.half_of(index, self.parity())
        return send(
            r.sums.at[1 - self.m.side, rows], r.fin.at[rows], r.y_sem, (index,), self.m.y_peer
        )

    def swapped_x_copy(self, index):
        r = self.r
        return send(
            r.sums.at[self.m.side, self.quarter_of(index, 1 - self.half)],
            r.x_recv.at[self.packed_quarter(index, 0)],
            r.x_sem, (index,), self.x_peer,
        )

    def pair_copy(self, index):
        r = self.r
        return send(
            r.sums.at[self.m.side, self.quarter_of(index, self.half)],
            r.x_recv.at[self.packed_quarter(index, 1)],
            r.z_sem, (index, 1), self.z_peer(2),
        )

    def swapped_gx_copy(self, index):
        r, rows = self.r, self.quarter_of(index, self.half)
        return send(r.fin.at[rows], r.fin.at[rows], r.gx_sem, (index,), self.x_peer)

    def swapped_gz_copy(self, index):
        r, rows = self.r, self.half_of(index, self.parity())
        return send(r.fin.at[rows], r.fin.at[rows], r.gz_sem, (index, 0), self.neighbour())

    def after_swap(self, index):
        r = self.r
        self.swap_copy(index).wait()
        rows, packed = self.half_of(index, self.parity()), self.packed(index)
        for side in range(2):
            r.sums[side, rows, :] = add_low(r.sums[side, rows, :], r.z_recv[side, packed, :])
        self.swapped_y_copy(index).start()

    def swapped_y(self, index):
        r, m = self.r, self.m
        self.swapped_y_copy(index).wait()
        rows = self.half_of(index, self.parity())
        r.sums[m.side, rows, :] = add_low(r.sums[m.side, rows, :], r.fin[rows, :])
        self.swapped_x_copy(index).start()

    def swapped_x(self, index):
        r, m = self.r, self.m
        self.swapped_x_copy(index).wait()
        rows = self.quarter_of(index, self.half)
        arrived = r.x_recv[self.packed_quarter(index, 0), :]
        r.sums[m.side, rows, :] = add_low(r.sums[m.side, rows, :], arrived)
        self.pair_copy(index).start()

    def swapped_pair(self, index):
        r, m = self.r, self.m
        self.pair_copy(index).wait()
        rows = self.quarter_of(index, self.half)
        arrived = r.x_recv[self.packed_quarter(index, 1), :]
        r.fin[rows, :] = add_low(r.sums[m.side, rows, :], arrived)
        self.swapped_gx_copy(index).start()

    def swapped_back(self, index):
        self.swapped_gx_copy(index).wait()
        self.swapped_gz_copy(index).start()

    def swapped_finish(self, index):
        self.swapped_gz_copy(index).wait()

    def after_y(self, index):
        r, m = self.r, self.m
        self.y_copy(index).wait()
        rows = self.rows(index)
        r.sums[m.side, rows, :] = add_low(r.sums[m.side, rows, :], r.fin[rows, :])
        self.x_copy(index).start()

    def after_x(self, index):
        r, m = self.r, self.m
        self.x_copy(index).wait()
        rows = self.half_of(index, self.half)
        r.sums[m.side, rows, :] = add_low(r.sums[m.side, rows, :], r.x_recv[self.packed(index), :])
        if not self.line:
            for step in range(1, self.planes):
                self.z_copy(index, step).start()
            return
        for outer, inner in ((0, 1), (3, 2)):
            @pl.when(self.plane == outer)
            def _():
                self.in_copy(index, inner).start()

    def inward(self, index):
        r, m = self.r, self.m
        if not self.line:
            return
        for outer, inner in ((0, 1), (3, 2)):
            @pl.when(self.plane == outer)
            def _():
                self.in_copy(index, inner).wait_send()

        @pl.when((self.plane == 1) | (self.plane == 2))
        def _():
            self.in_copy(index, self.plane).wait_recv()
            rows = self.half_of(index, self.half)
            arrived = r.z_recv[0, self.packed(index), :]
            r.sums[m.side, rows, :] = add_low(r.sums[m.side, rows, :], arrived)
            self.mid_copy(index).start()

    def middle(self, index):
        r, m = self.r, self.m
        if not self.line:
            part = self.z_part(index, self.plane)
            total = r.sums[m.side, part, :].astype(F32)
            for step in range(1, self.planes):
                self.z_copy(index, step).wait()
                arrived = r.z_recv[step - 1, self.span(index * self.piece, self.piece), :]
                total = total + arrived.astype(F32)
            r.fin[part, :] = total.astype(LOW)
            for step in range(1, self.planes):
                self.gz_copy(index, step).start()
            return

        @pl.when((self.plane == 1) | (self.plane == 2))
        def _():
            self.mid_copy(index).wait()
            rows = self.half_of(index, self.half)
            arrived = r.z_recv[1, self.packed(index), :]
            r.fin[rows, :] = add_low(r.sums[m.side, rows, :], arrived)
            for outer, inner in ((0, 1), (3, 2)):
                @pl.when(self.plane == inner)
                def _():
                    self.out_copy(index, outer).start()
            self.gx_copy(index).start()

    def outward(self, index):
        if not self.line:
            for step in range(1, self.planes):
                self.gz_copy(index, step).wait()
            self.gx_copy(index).start()
            return
        for outer, inner in ((0, 1), (3, 2)):
            @pl.when(self.plane == inner)
            def _():
                self.out_copy(index, outer).wait_send()

            @pl.when(self.plane == outer)
            def _():
                self.out_copy(index, inner).wait_recv()
                self.gx_copy(index).start()

    def finish(self, index):
        self.gx_copy(index).wait()

    def run(self, feeds, moves):
        loops = max(1, feeds, moves)
        one, after = self.beside(loops, feeds, moves)

        def body(index, carry):
            one(index)
            return carry

        lax.fori_loop(0, loops, body, 0)
        after()

    def beside(self, loops, feeds, moves):
        feeds = max(0, min(feeds, self.published - self.fed))
        fed = self.fed + feeds
        limit = self.chunks + self.LAGS[-1] if fed == self.chunks else fed
        moves = max(0, min(moves, limit - self.moved))
        first_feed, first_move = self.fed, self.moved

        each = -(-feeds // loops)

        def one(index):
            if feeds > 0:
                def feed(step, carry):
                    self.feed(first_feed + step)
                    return carry

                lax.fori_loop(
                    jnp.minimum(index * each, feeds), jnp.minimum((index + 1) * each, feeds), feed, 0
                )
            if moves > 0:
                def move(step, carry):
                    self.move(first_move + step)
                    return carry

                lax.fori_loop(index * moves // loops, (index + 1) * moves // loops, move, 0)

        def after():
            self.fed, self.moved = fed, first_move + moves
            self.loaded = max(self.loaded, min(self.published, self.fed + self.ring))

        return one, after

    def left(self):
        return self.chunks + self.LAGS[-1] - self.moved


def attend_back(pair, r, count, keys, keys_t, values, queries_t, masses, context_t, grad_t, probs, place, places):
    lanes = block(pair, 2 * r.head_dim)
    inverse = masses[pair]
    grads = grad_t[lanes, :].astype(F32)
    product = grads * context_t[lanes, :]
    sums = [
        jnp.sum(product[: r.head_dim], axis=0, keepdims=True),
        jnp.sum(product[r.head_dim :], axis=0, keepdims=True),
    ]
    inner = jnp.concatenate(sums, axis=1) * inverse
    grads = (head_blocks(grads) * inverse).astype(LOW)
    queries = head_blocks(queries_t[lanes, :])

    def one(index, total):
        rows = block(index, count)
        weights = probs[rows, :]
        score_grad = weights.astype(F32) * (dot(values[rows, lanes], grads) - inner)
        low = score_grad.astype(LOW)
        side, core = index // 2, lax.rem(index, 2)
        r.value_grad[side, core, :, lanes] = dot_nt(weights, grads).astype(LOW)
        r.key_grad[side, core, :, lanes] = dot_nt(low, queries).astype(LOW)
        return total + dot(keys_t[lanes, rows], low), score_grad

    total = jnp.zeros((2 * r.head_dim, 2 * count), F32)
    if place is None:
        for index in range(places):
            total, _ = one(index, total)
    else:
        r.before[...] = jnp.zeros_like(r.before)

        def far(index, carry):
            total, beyond = carry
            total, score_grad = one(index, total)
            split = count - NEAR
            beyond = beyond + jnp.sum(fold(score_grad[:split]), axis=0)
            rest = score_grad[split:]
            is_last = index == place - 1

            @pl.when(is_last)
            def _():
                r.before[...] = rest

            beyond = beyond + jnp.where(is_last, 0.0, jnp.sum(fold(rest), axis=0))
            return total, beyond

        carry = (total, jnp.zeros((8, 2 * count), F32))
        total, beyond = lax.fori_loop(0, place, far, carry)
        total, own = one(place, total)
        before = r.before[...]
        parts = []
        for head in range(2):
            at = head * count
            on = own[:NEAR, at : at + NEAR] + own[NEAR:, at + NEAR : at + 2 * NEAR]
            below = before[:, at : at + NEAR] + own[:NEAR, at + NEAR : at + 2 * NEAR]
            both = jnp.concatenate([on, below], axis=1)
            summed = both[:8]
            for group in range(1, NEAR // 8):
                summed = summed + pltpu.roll(
                    both[8 * group : 8 * group + 8], 2 * NEAR - 8 * group, 1
                )
            parts.append(summed)
        summed = jnp.concatenate(parts, axis=0)
        sublane = lax.broadcasted_iota(jnp.int32, summed.shape, 0)
        for bit in (1, 2, 4):
            summed = jnp.where(
                (sublane & bit) != 0, pltpu.roll(summed, 2 * NEAR - bit, 1), summed
            )
        lane = lax.broadcasted_iota(jnp.int32, (1, 2 * NEAR), 1)
        for head in range(2):
            at = head * count
            line = jnp.sum(summed[8 * head : 8 * head + 8], axis=0, keepdims=True)
            rest = jnp.sum(beyond[:, at : at + count]) + jnp.sum(before[:, at + NEAR : at + 2 * NEAR])
            line = line + jnp.where(lane == 2 * NEAR - 1, rest, 0.0)
            r.by_distance[pl.ds(pair * 2 + head, 1), :] = line
    r.query_grad_t[lanes, :] = head_rows(total).astype(LOW)


def backward_kernel(names, dims, *refs):
    r = SimpleNamespace(**dict(zip(names, refs)), head_dim=dims.head_dim)
    m = Mesh2()
    count, places, pairs, width = dims.count, dims.places, dims.pairs, dims.width
    own = width // places
    engine = Reducer(r, m, dims)

    loads = SimpleNamespace()
    slots = iter(range(r.load_sem.shape[0]))

    def load(src, dst):
        copy = pltpu.make_async_copy(src, dst, r.load_sem.at[next(slots)])
        copy.start()
        return copy

    def probs_copy(src, pair):
        slot = lax.rem(pair, 2)
        return pltpu.make_async_copy(src.at[pair], r.probs.at[slot], r.probs_sem.at[slot])

    loads.second = load(r.second_hbm, r.dec_grad)
    loads.cwo = load(r.cwo_hbm, r.wo)
    loads.ckeys = load(r.ckeys_hbm, r.keys)
    loads.cvalues = load(r.cvalues_hbm, r.values)
    probs_copy(r.cross_probs, 0).start()
    probs_copy(r.cross_probs, 1).start()
    loads.first = load(r.first_hbm, r.enc_grad)
    loads.cwq = load(r.cwq_hbm, r.wq)
    loads.cwk = load(r.cwk_hbm, r.wk)
    loads.cwv = load(r.cwv_hbm, r.wv)
    loads.es0 = load(r.es_hbm.at[m.core], r.group.at[0])
    loads.es1 = load(r.es_hbm.at[m.core + 2], r.group.at[1])

    m.greet([m.core_peer, m.y_peer] + engine.peers())
    engine.publish(2 * width)

    gain_self = r.gain_self[...].astype(F32).reshape(1, width)
    gain_cross = r.gain_cross[...].astype(F32).reshape(1, width)
    staged = {}

    def unit_copy(unit):
        rows = pl.ds(2 * width + unit * own, own)
        return pltpu.make_async_copy(
            r.stage.at[unit % 2], r.big.at[:, :, rows], r.stage_sem.at[unit % 2]
        )

    def give(unit, left_t, right):
        if unit - 2 in staged:
            staged.pop(unit - 2).wait()
        for place in range(places):
            grad = dot(left_t[place * own : (place + 1) * own, :], right)
            r.stage[unit % 2, place % 2, place // 2] = grad.astype(LOW)
        staged[unit] = unit_copy(unit)
        staged[unit].start()

    def settle(rows):
        for unit in sorted(staged):
            staged.pop(unit).wait()
        engine.publish(rows)

    def turn(src, dst):
        def one(index, carry):
            rows = block(index, count)
            dst[:, rows] = jnp.transpose(src[rows, :])
            return carry

        lax.fori_loop(0, places, one, 0)

    def attend(src, queries_t, masses, context_t, grad_t, place, feeds, moves):
        beside, after = engine.beside(pairs, feeds, moves)

        def one(pair, carry):
            probs_copy(src, pair).wait()
            attend_back(
                pair, r, count, r.keys, r.keys_t, r.values, queries_t, masses, context_t, grad_t,
                r.probs.at[lax.rem(pair, 2)], place, places,
            )

            @pl.when(pair + 2 < pairs)
            def _():
                probs_copy(src, pair + 2).start()

            beside(pair)
            return carry

        lax.fori_loop(0, pairs, one, 0)
        after()

    def exchange(slot, key_recv, value_recv):
        copies = [
            send(r.key_grad.at[:, 1 - m.core], key_recv, r.link_sem, (slot,), m.core_peer),
            send(r.value_grad.at[:, 1 - m.core], value_recv, r.link_sem, (slot + 1,), m.core_peer),
        ]
        for copy in copies:
            copy.start()
        return copies

    def chip_sum(grad, arrived):
        return add_low(grad[:, m.core], arrived[...]).reshape(2 * count, width)

    def partial(slot, side):
        key_grad = add_low(r.key_grad[side, m.core], r.key_recv[slot, side])
        value_grad = add_low(r.value_grad[side, m.core], r.value_recv[slot, side])
        return dot_nt(key_grad, r.wk[...]) + dot_nt(value_grad, r.wv[...])

    loads.second.wait()
    head_grad = r.dec_grad[...].astype(LOW)
    loads.cwo.wait()
    r.grad_t[...] = dot_nt(r.wo[...], head_grad).astype(LOW)
    loads.wo = load(r.wo_hbm, r.wo)
    engine.run(2, 0)
    give(0, r.ccontext_t[...].astype(LOW), head_grad)
    loads.ckeys.wait()
    turn(r.keys, r.keys_t)
    loads.cvalues.wait()
    attend(r.cross_probs, r.cqueries_t, r.cross_masses, r.ccontext_t, r.grad_t, None, 4, 3)
    copies = exchange(0, r.key_recv.at[0], r.value_recv.at[0])
    loads.keys = load(r.keys_hbm, r.keys)
    loads.values = load(r.values_hbm, r.values)
    probs_copy(r.self_probs, 0).start()
    probs_copy(r.self_probs, 1).start()
    query_grad = jnp.transpose(r.query_grad_t[...])
    engine.run(0, 1)
    loads.cwq.wait()
    normed_grad = dot_nt(query_grad, r.wq[...])
    loads.wq = load(r.wq_hbm, r.wq)
    loads.first.wait()
    first_part, gain_cross_grad = norm_back(r.enc_grad[...], gain_cross, normed_grad)
    r.dec_grad[...] += first_part
    give(1, jnp.transpose(r.a2[...]), query_grad)
    engine.run(0, 1)
    loads.es0.wait()
    loads.es1.wait()
    for side in range(2):
        r.group_t[:, side * count : (side + 1) * count] = jnp.transpose(r.group[side])
    loads.a10 = load(r.a1_hbm.at[block(m.core, count)], r.group.at[0])
    loads.a11 = load(r.a1_hbm.at[block(m.core + 2, count)], r.group.at[1])
    for copy in copies:
        copy.wait()
    key_grad = chip_sum(r.key_grad, r.key_recv.at[0])
    value_grad = chip_sum(r.value_grad, r.value_recv.at[0])
    loads.cwk.wait()
    loads.cwv.wait()
    r.partial_low[...] = partial(0, 1 - m.side).astype(LOW)
    enc_copy = send(r.partial_low, r.partial_recv.at[0], r.link_sem, (4,), m.y_peer)
    enc_copy.start()
    r.enc_grad[...] = partial(0, m.side)
    loads.wk = load(r.wk_hbm, r.wk)
    loads.wv = load(r.wv_hbm, r.wv)
    give(2, r.group_t[...], key_grad)
    give(3, r.group_t[...], value_grad)
    settle(3 * width)
    engine.run(3, 2)

    first_grad = r.dec_grad[...]
    head_grad = first_grad.astype(LOW)
    loads.wo.wait()
    r.grad_t[...] = dot_nt(r.wo[...], head_grad).astype(LOW)
    give(4, r.context_t[...].astype(LOW), head_grad)
    loads.keys.wait()
    turn(r.keys, r.keys_t)
    loads.values.wait()

    def clear(index, carry):
        side, core = index // 2, lax.rem(index, 2)
        r.key_grad[side, core] = jnp.zeros((count, width), LOW)
        r.value_grad[side, core] = jnp.zeros((count, width), LOW)
        return carry

    lax.fori_loop(m.place + 1, places, clear, 0)
    r.by_distance[...] = jnp.zeros_like(r.by_distance)
    attend(r.self_probs, r.queries_t, r.self_masses, r.context_t, r.grad_t, m.place, 6, 6)
    copies = exchange(2, r.key_recv.at[1], r.value_recv.at[1])
    query_grad = jnp.transpose(r.query_grad_t[...])
    engine.run(0, 1)
    loads.wq.wait()
    normed_grad = dot_nt(query_grad, r.wq[...])
    loads.a10.wait()
    loads.a11.wait()
    for side in range(2):
        r.group_t[:, side * count : (side + 1) * count] = jnp.transpose(r.group[side])
    give(5, jnp.transpose(r.group[m.side]), query_grad)
    engine.run(0, 1)
    for copy in copies:
        copy.wait()
    key_grad = chip_sum(r.key_grad, r.key_recv.at[1])
    value_grad = chip_sum(r.value_grad, r.value_recv.at[1])
    loads.wk.wait()
    loads.wv.wait()
    enc_copy.wait()
    r.enc_grad[...] += r.partial_recv[0].astype(F32)
    r.partial_low[...] = partial(1, 1 - m.side).astype(LOW)
    dec_copy = send(r.partial_low, r.partial_recv.at[1], r.link_sem, (5,), m.y_peer)
    dec_copy.start()
    normed_grad = normed_grad + partial(1, m.side)
    give(6, r.group_t[...], key_grad)
    give(7, r.group_t[...], value_grad)
    settle(4 * width)
    engine.run(4, 2)
    dec_copy.wait()
    normed_grad = normed_grad + r.partial_recv[1].astype(F32)
    state_part, gain_self_grad = norm_back(r.x[...].astype(F32), gain_self, normed_grad)
    r.dec_grad[...] += state_part

    buckets = dims.buckets
    table = lax.dot_general(
        bucket_terms(buckets), r.by_distance[...], (((1,), (1,)), ((), ())),
        precision=lax.Precision.HIGHEST, preferred_element_type=F32,
    )
    r.tiny[0] = jnp.zeros(r.tiny.shape[1:], F32)
    r.tiny[0, 0:1] = gain_self_grad
    r.tiny[0, 1:2] = gain_cross_grad
    r.tiny[0, 2:3] = r.gain_ffn_grad[...]
    part = buckets // places
    for place in range(places):
        r.tiny[0, 8 : 8 + part, 128 * place : 128 * (place + 1)] = table[
            place * part : (place + 1) * part
        ]
    for slot, peer in enumerate((m.core_peer, m.y_peer, engine.x_peer)):
        copy = send(r.tiny.at[slot], r.tiny_recv.at[slot], r.tiny_sem, (slot,), peer)
        copy.start()
        engine.run(1, 1)
        copy.wait()
        r.tiny[slot + 1] = r.tiny[slot] + r.tiny_recv[slot]
    copies = []
    for step in range(1, dims.planes):
        copy = send(
            r.tiny.at[3], r.tiny_recv.at[2 + step], r.tiny_sem, (2 + step,), engine.z_peer(step)
        )
        copy.start()
        copies.append(copy)
    engine.run(1, 1)
    for copy in copies:
        copy.wait()
    total = r.tiny[3]
    for step in range(1, dims.planes):
        total = total + r.tiny_recv[2 + step]
    r.small[...] = total
    engine.run(engine.chunks, engine.left())


def run_backward(dims, a, f):
    count, total, width = dims.count, dims.count * dims.places, dims.width
    near, far = pltpu.VMEM, pl.ANY
    pairs, planes, chunks, piece = dims.pairs, dims.planes, dims.chunks, dims.piece
    square = (width, width)
    own = (count, width)
    inputs = dict(
        x=(a.dec_states[0], near),
        gain_self=(a.gain_self, near),
        gain_cross=(a.gain_cross, near),
        first_hbm=(f.first, far),
        second_hbm=(f.second_grad, far),
        gain_ffn_grad=(f.gain_ffn_grad, near),
        queries_t=(f.queries_t, near),
        cqueries_t=(f.cqueries_t, near),
        context_t=(f.context_t, near),
        ccontext_t=(f.ccontext_t, near),
        self_masses=(f.self_masses, near),
        cross_masses=(f.cross_masses, near),
        a2=(f.a2, near),
        keys_hbm=(f.keys_out, far),
        values_hbm=(f.values_out, far),
        a1_hbm=(f.a1_out, far),
        ckeys_hbm=(f.ckeys_out, far),
        cvalues_hbm=(f.cvalues_out, far),
        es_hbm=(f.es_out, far),
        self_probs=(f.self_probs, far),
        cross_probs=(f.cross_probs, far),
        wo_hbm=(a.self_output, far),
        wq_hbm=(a.self_query, far),
        wk_hbm=(a.self_key, far),
        wv_hbm=(a.self_value, far),
        cwo_hbm=(a.cross_output, far),
        cwq_hbm=(a.cross_query, far),
        cwk_hbm=(a.cross_key, far),
        cwv_hbm=(a.cross_value, far),
        big_in=(f.big, far),
    )
    outputs = dict(
        big=(f.big.shape, LOW, far),
        fin=((4 * width, width), LOW, near),
        dec_grad=(own, F32, near),
        enc_grad=(own, F32, near),
        small=((16, width), F32, near),
    )
    dma = pltpu.SemaphoreType.DMA
    rows = 4 * width
    scratch = dict(
        wo=pltpu.VMEM(square, LOW),
        wq=pltpu.VMEM(square, LOW),
        wk=pltpu.VMEM(square, LOW),
        wv=pltpu.VMEM(square, LOW),
        keys=pltpu.VMEM((total, width), LOW),
        values=pltpu.VMEM((total, width), LOW),
        keys_t=pltpu.VMEM((width, total), LOW),
        probs=pltpu.VMEM((2, total, 2 * count), LOW),
        grad_t=pltpu.VMEM((width, count), LOW),
        query_grad_t=pltpu.VMEM((width, count), LOW),
        key_grad=pltpu.VMEM((2, 2, *own), LOW),
        value_grad=pltpu.VMEM((2, 2, *own), LOW),
        key_recv=pltpu.VMEM((2, 2, *own), LOW),
        value_recv=pltpu.VMEM((2, 2, *own), LOW),
        partial_low=pltpu.VMEM(own, LOW),
        partial_recv=pltpu.VMEM((2, *own), LOW),
        group=pltpu.VMEM((2, *own), LOW),
        group_t=pltpu.VMEM((width, 2 * count), LOW),
        before=pltpu.VMEM((NEAR, 2 * count), F32),
        by_distance=pltpu.VMEM((128, 2 * NEAR), F32),
        stage=pltpu.VMEM((2, 2, 2, width // dims.places, width), LOW),
        fresh=pltpu.VMEM((2, dims.ring * dims.chunk_rows, width), LOW),
        sums=pltpu.VMEM((2, rows, width), LOW),
        x_recv=pltpu.VMEM((rows // 2, width), LOW),
        z_recv=pltpu.VMEM(
            (2, rows // 2, width) if dims.line else (planes - 1, chunks * piece, width), LOW
        ),
        tiny=pltpu.VMEM((4, 16, width), F32),
        tiny_recv=pltpu.VMEM((2 + planes, 16, width), F32),
        load_sem=dma((18,)),
        probs_sem=dma((2,)),
        stage_sem=dma((2,)),
        link_sem=dma((2, 6)),
        chunk_sem=dma((chunks,)),
        core_sem=dma((2, chunks)),
        y_sem=dma((2, chunks)),
        x_sem=dma((2, chunks)),
        z_sem=dma((2, chunks, planes - 1)),
        gz_sem=dma((2, chunks, planes - 1)),
        gx_sem=dma((2, chunks)),
        tiny_sem=dma((2, 2 + planes)),
    )
    return call(
        lambda names, *refs: backward_kernel(names, dims, *refs),
        "backward", 1, 63, inputs, outputs, scratch, {len(inputs) - 1: 0},
    )


def place_kernel(names, dims, *refs):
    r = SimpleNamespace(**dict(zip(names, refs)))
    width, fan = dims.width, dims.fan
    own = width // dims.places
    passed = (
        (r.layer_in, r.layer_held, r.layer),
        (r.dec_in, r.dec_held, r.dec),
        (r.enc_in, r.enc_held, r.enc),
    )
    inward = [
        pltpu.make_async_copy(src, held, r.pass_sem.at[0, slot])
        for slot, (src, held, _) in enumerate(passed)
    ]
    copies = [
        pltpu.make_async_copy(held, dst, r.pass_sem.at[1, slot])
        for slot, (_, held, dst) in enumerate(passed)
    ]
    groups = 4 * width // own
    loads, stores = [], []
    for index in range(4):
        rows = pl.ds(index * width, width)
        loads.append(pltpu.make_async_copy(r.fin.at[rows], r.low.at[rows], r.load_sem.at[index]))
        loads[-1].start()
    for copy in inward:
        copy.start()
    units = (
        r.cross_output, r.cross_query, r.cross_key, r.cross_value,
        r.self_output, r.self_query, r.self_key, r.self_value,
    )
    for index in range(groups):
        if index % (groups // 4) == 0:
            loads[index // (groups // 4)].wait()
        rows = pl.ds(index * own, own)
        r.wide[rows, :] = r.low[rows, :].astype(F32)
        if index < fan:
            dst = r.ffn_out.at[rows]
        elif index < 2 * fan:
            dst = r.ffn_in.at[:, pl.ds((index - fan) * width, width)]
        else:
            dst = units[index - 2 * fan]
        copy = pltpu.make_async_copy(r.wide.at[rows], dst, r.store_sem.at[index])
        copy.start()
        stores.append(copy)
    for arrival, copy in zip(inward, copies):
        arrival.wait()
        copy.start()
    at = lax.axis_index("seq")
    part = dims.buckets // dims.places
    for place in range(dims.places):
        @pl.when(at == place)
        def _():
            for index, grad in enumerate((r.gain_self, r.gain_cross, r.gain_ffn)):
                grad[...] = r.small[index : index + 1, place * own : (place + 1) * own]
            r.table_grad[...] = r.small[8 : 8 + part, 128 * place : 128 * place + dims.heads]
    for copy in stores + copies:
        copy.wait()


def run_place(dims, f, b):
    near, far = pltpu.VMEM, pl.ANY
    width, own = dims.width, dims.width // dims.places
    square, gain = ((own, width), F32, far), ((1, own), F32, near)
    rows = 4 * width
    inputs = dict(
        fin=(b.fin, far),
        small=(b.small, near),
        layer_in=(f.layer_out, far),
        dec_in=(b.dec_grad, far),
        enc_in=(b.enc_grad, far),
    )
    outputs = dict(
        layer=(f.layer_out.shape, LOW, far),
        dec=(b.dec_grad.shape, F32, far),
        enc=(b.enc_grad.shape, F32, far),
        ffn_out=((width, width), F32, far),
        ffn_in=((own, dims.fan * width), F32, far),
        cross_output=square,
        cross_query=square,
        cross_key=square,
        cross_value=square,
        self_output=square,
        self_query=square,
        self_key=square,
        self_value=square,
        gain_self=gain,
        gain_cross=gain,
        gain_ffn=gain,
        table_grad=((dims.buckets // dims.places, dims.heads), F32, near),
    )
    scratch = dict(
        low=pltpu.VMEM((rows, width), LOW),
        wide=pltpu.VMEM((rows, width), F32),
        layer_held=pltpu.VMEM(f.layer_out.shape, LOW),
        dec_held=pltpu.VMEM(b.dec_grad.shape, F32),
        enc_held=pltpu.VMEM(b.enc_grad.shape, F32),
        pass_sem=pltpu.SemaphoreType.DMA((2, 3)),
        load_sem=pltpu.SemaphoreType.DMA((4,)),
        store_sem=pltpu.SemaphoreType.DMA((rows // own,)),
    )
    names = (*inputs, *outputs, *scratch)
    results = pl.pallas_call(
        lambda *refs: place_kernel(names, dims, *refs),
        out_shape=tuple(jax.ShapeDtypeStruct(shape, kind) for shape, kind, _ in outputs.values()),
        in_specs=[pl.BlockSpec(memory_space=space) for _, space in inputs.values()],
        out_specs=tuple(pl.BlockSpec(memory_space=space) for _, _, space in outputs.values()),
        scratch_shapes=list(scratch.values()),
        compiler_params=pltpu.CompilerParams(vmem_limit_bytes=60 * 2**20),
        name="place",
    )(*(array for array, _ in inputs.values()))
    return SimpleNamespace(**dict(zip(outputs, results)))


def on_device(
    dec_states,
    enc_states,
    out_grad,
    dec_lengths,
    enc_lengths,
    self_query,
    self_key,
    self_value,
    self_output,
    cross_query,
    cross_key,
    cross_value,
    cross_output,
    ffn_in,
    ffn_out,
    gain_self,
    gain_cross,
    gain_ffn,
    position_bias,
):
    a = SimpleNamespace(
        dec_states=dec_states,
        enc_states=enc_states,
        out_grad=out_grad,
        dec_lengths=dec_lengths,
        enc_lengths=enc_lengths,
        self_query=self_query,
        self_key=self_key,
        self_value=self_value,
        self_output=self_output,
        cross_query=cross_query,
        cross_key=cross_key,
        cross_value=cross_value,
        cross_output=cross_output,
        ffn_in=ffn_in,
        ffn_out=ffn_out,
        gain_self=gain_self,
        gain_cross=gain_cross,
        gain_ffn=gain_ffn,
        position_bias=position_bias,
    )
    count, width = a.dec_states.shape[1:]
    buckets, heads = a.position_bias.shape
    planes, piece = lax.axis_size("dp") // 2, 16
    line = planes == 4
    chunk_rows = 128 if line else 2 * planes * piece
    chunks = 4 * width // chunk_rows
    dims = SimpleNamespace(
        count=count,
        width=width,
        places=lax.axis_size("seq"),
        heads=heads,
        head_dim=width // heads,
        pairs=heads // 2,
        fan=a.ffn_in.shape[1] // width,
        items=a.dec_lengths.shape[1],
        buckets=buckets,
        planes=planes,
        piece=piece,
        chunks=chunks,
        ring=4 if line else 1,
        line=line,
        chunk_rows=chunk_rows,
    )
    f = run_forward(dims, a)
    b = run_backward(dims, a, f)
    o = run_place(dims, f, b)
    return (
        o.layer[None],
        o.dec[None],
        o.enc[None],
        o.self_query,
        o.self_key,
        o.self_value,
        o.self_output,
        o.cross_query,
        o.cross_key,
        o.cross_value,
        o.cross_output,
        o.ffn_in,
        o.ffn_out,
        o.gain_self[0],
        o.gain_cross[0],
        o.gain_ffn[0],
        o.table_grad,
    )


def solution(mesh):
    split = P("dp", "seq", None)
    rows = P("seq", None)
    return jax.shard_map(
        on_device,
        mesh=mesh,
        in_specs=(split,) * 3 + (P("dp", None),) * 2 + (P(),) * 14,
        out_specs=(split,) * 3 + (rows,) * 10 + (P("seq"),) * 3 + (rows,),
        check_vma=False,
    )
```

```python
import functools
import math
from types import SimpleNamespace

import jax
import jax.numpy as jnp
from jax import lax
from jax.experimental import pallas as pl
from jax.experimental.pallas import tpu as pltpu
from jax.sharding import PartitionSpec as P

MESH = pl.DeviceIdType.MESH
EPS = 1e-06
NEG = -1000000000.0
NEAR = 128
F32 = jnp.float32
LOW = jnp.bfloat16


def dot(left, right):
    return jnp.dot(left, right, preferred_element_type=F32)


def dot_nt(left, right):
    return lax.dot_general(left, right, (((1,), (1,)), ((), ())), preferred_element_type=F32)


def add_low(left, right):
    return (left.astype(F32) + right.astype(F32)).astype(LOW)


def block(index, size):
    return pl.ds(pl.multiple_of(index * size, size), size)


def bucket_of(distance):
    farther = jnp.full(distance.shape, 16, jnp.int32)
    for level in range(1, 16):
        farther = farther + (distance >= math.ceil(16 * 8 ** (level / 16))).astype(jnp.int32)
    return jnp.where(distance < 16, distance, farther)


def bucket_terms(buckets):
    shape = (buckets, 2 * NEAR)
    lanes = lax.broadcasted_iota(jnp.int32, shape, 1)
    return (bucket_of(lanes) == lax.broadcasted_iota(jnp.int32, shape, 0)).astype(F32)


def scale_of(values):
    return lax.rsqrt(jnp.mean(values * values, axis=-1, keepdims=True) + EPS)


def norm_back(values, gain, grad):
    scale = scale_of(values)
    gain_grad = jnp.sum(grad * values * scale, axis=0, keepdims=True)
    inner = jnp.mean(values * gain * grad, axis=-1, keepdims=True)
    return scale * gain * grad - values * (scale * scale * scale) * inner, gain_grad


def head_blocks(pair):
    size = pair.shape[0] // 2
    zero = jnp.zeros((size, pair.shape[1]), pair.dtype)
    return jnp.concatenate(
        [
            jnp.concatenate([pair[:size], zero], axis=1),
            jnp.concatenate([zero, pair[size:]], axis=1),
        ],
        axis=0,
    )


def head_rows(both):
    size, count = both.shape[0] // 2, both.shape[1] // 2
    return jnp.concatenate([both[:size, :count], both[size:, count:]], axis=0)


def twice(values):
    return jnp.concatenate([values, values], axis=1)


def fold(values):
    return values.reshape(values.shape[0] // 8, 8, values.shape[1])


class Mesh2:
    def __init__(self):
        self.row = lax.axis_index("dp")
        self.place = lax.axis_index("seq")
        self.side, self.core = self.place // 2, lax.rem(self.place, 2)
        self.sibling = self.side * 2 + 1 - self.core
        self.across = (1 - self.side) * 2 + self.core
        self.diagonal = (1 - self.side) * 2 + 1 - self.core
        self.core_peer = (self.row, self.sibling)
        self.y_peer = (self.row, self.across)

    def greet(self, peers):
        barrier = pltpu.get_barrier_semaphore()
        for peer in peers:
            pl.semaphore_signal(barrier, inc=1, device_id=peer, device_id_type=MESH)
        pl.semaphore_wait(barrier, len(peers))


def send(src, dst, sems, slot, peer):
    return pltpu.make_async_remote_copy(
        src_ref=src,
        dst_ref=dst,
        send_sem=sems.at[(0, *slot)],
        recv_sem=sems.at[(1, *slot)],
        device_id=peer,
        device_id_type=MESH,
    )


def softmax_pair(pair, r, count, steps, keys, turned, terms, queries_t, masses, out_t, probs, place):
    lanes = block(pair, 2 * r.head_dim)
    queries = head_blocks(queries_t[lanes, :])
    near = place is not None
    if near:
        tiles = [
            pltpu.roll(
                jnp.broadcast_to(r.near_bias[pl.ds(pair * 2 + head, 1), :], (NEAR, 2 * NEAR)),
                0,
                1,
                stride=1,
                stride_axis=0,
            )
            for head in range(2)
        ]
        below = [tile[:, NEAR:] for tile in tiles]
        on = [tile[:, :NEAR] for tile in tiles]
        none = jnp.zeros((NEAR, NEAR), F32)
        before = jnp.concatenate([below[0], none, below[1], none], axis=1)
        first = jnp.concatenate([on[0], below[0], on[1], below[1]], axis=1)
        second = jnp.concatenate([none, on[0], none, on[1]], axis=1)

    top = jnp.full((8, 2 * count), -jnp.inf, F32)
    for index in range(steps):
        rows = block(index, count)
        raw = dot(keys[index, :, lanes], queries) + twice(terms[rows, :])
        r.scores[rows, :] = raw
        if not near:
            top = jnp.maximum(top, jnp.max(fold(raw), axis=0))
    if near:
        rows = block(place, count)
        r.scores[rows, :] = r.scores[rows, :] + jnp.concatenate([first, second], axis=0)

        @pl.when(place > 0)
        def _():
            last = block(place * (count // NEAR) - 1, NEAR)
            r.scores[last, :] = r.scores[last, :] + before

        for index in range(steps):
            top = jnp.maximum(top, jnp.max(fold(r.scores[block(index, count), :]), axis=0))
    top = jnp.max(top, axis=0, keepdims=True)
    mass = jnp.zeros((8, 2 * count), F32)
    context = jnp.zeros((2 * r.head_dim, 2 * count), F32)
    for index in range(steps):
        rows = block(index, count)
        weights = jnp.exp(r.scores[rows, :] - top)
        low = weights.astype(LOW)
        probs[rows, :] = low
        context = context + dot(turned[lanes, rows], low)
        mass = mass + jnp.sum(fold(weights), axis=0)
    inverse = 1.0 / jnp.sum(mass, axis=0, keepdims=True)
    masses[pair] = inverse
    out_t[lanes, :] = head_rows(context * inverse)


def forward_kernel(names, dims, *refs):
    r = SimpleNamespace(**dict(zip(names, refs)), head_dim=dims.head_dim)
    m = Mesh2()
    count, places, pairs, fan, width = dims.count, dims.places, dims.pairs, dims.fan, dims.width
    q_place = m.place

    def load(slot, src, dst):
        copy = pltpu.make_async_copy(src, dst, r.load_sem.at[slot])
        copy.start()
        return copy

    loads = SimpleNamespace(
        wk=load(0, r.wk_hbm, r.wk),
        wv=load(1, r.wv_hbm, r.wv),
        wq=load(2, r.wq_hbm, r.wq),
        wout=load(3, r.wout_hbm, r.wout),
        cwk=load(4, r.cwk_hbm, r.cwk),
        cwv=load(5, r.cwv_hbm, r.cwv),
        wo=load(6, r.wo_hbm, r.wo),
        cwq=load(7, r.cwq_hbm, r.cwq),
        cwo=load(8, r.cwo_hbm, r.cwo),
    )

    m.greet([m.core_peer, m.y_peer])
    x_y = send(r.x, r.xs.at[m.place], r.link_sem, (0,), m.y_peer)
    x_core = send(r.x, r.xs.at[m.place], r.link_sem, (1,), m.core_peer)
    x_on = send(r.xs.at[m.across], r.xs.at[m.across], r.link_sem, (2,), m.core_peer)
    e_y = send(r.e, r.es.at[m.place], r.link_sem, (3,), m.y_peer)
    e_core = send(r.e, r.es.at[m.place], r.link_sem, (4,), m.core_peer)
    e_on = send(r.es.at[m.across], r.es.at[m.across], r.link_sem, (5,), m.core_peer)
    x_y.start()
    x_core.start()
    e_core.start()
    r.xs[m.place] = r.x[...]
    r.es[m.place] = r.e[...]

    gain_self = r.gain_self[...].astype(F32).reshape(1, width)
    gain_cross = r.gain_cross[...].astype(F32).reshape(1, width)

    items = dims.items
    dec_starts, enc_starts = [0], [0]
    for index in range(items):
        dec_starts.append(dec_starts[-1] + r.dec_len[0, index])
        enc_starts.append(enc_starts[-1] + r.enc_len[0, index])
    query_at = q_place * count + lax.broadcasted_iota(jnp.int32, (1, count), 1)
    low_self = jnp.zeros((1, count), jnp.int32)
    low_cross = jnp.zeros((1, count), jnp.int32)
    high_cross = jnp.full((1, count), enc_starts[1], jnp.int32)
    for index in range(1, items):
        inside = query_at >= dec_starts[index]
        low_self = jnp.where(inside, dec_starts[index], low_self)
        low_cross = jnp.where(inside, enc_starts[index], low_cross)
        high_cross = jnp.where(inside, enc_starts[index + 1], high_cross)

    def masks(index, carry):
        rows = block(index, count)
        key_at = index * count + lax.broadcasted_iota(jnp.int32, (count, count), 0)
        r.self_terms[rows, :] = jnp.where((key_at >= low_self) & (key_at <= query_at), 0.0, NEG)
        r.cross_terms[rows, :] = jnp.where((key_at >= low_cross) & (key_at < high_cross), 0.0, NEG)
        return carry

    lax.fori_loop(0, places, masks, 0)

    buckets = r.table.shape[1]
    terms = bucket_terms(buckets)
    last = lax.broadcasted_iota(jnp.int32, terms.shape, 0) == buckets - 1
    terms = terms - last.astype(F32)
    r.near_bias[...] = dot(r.table[...], terms.astype(LOW))

    def self_block(place):
        rows = block(place, count)
        states = r.xs[place].astype(F32)
        normed = (states * scale_of(states) * gain_self).astype(LOW)
        r.a1[place] = normed
        r.keys[place] = dot(normed, r.wk[...]).astype(LOW)
        values = dot(normed, r.wv[...]).astype(LOW)
        r.values[place] = values
        r.values_t[:, rows] = jnp.transpose(values)

    def cross_block(place):
        rows = block(place, count)
        encoded = r.es[place]
        r.ckeys[place] = dot(encoded, r.cwk[...]).astype(LOW)
        values = dot(encoded, r.cwv[...]).astype(LOW)
        r.cvalues[place] = values
        r.cvalues_t[:, rows] = jnp.transpose(values)

    loads.wk.wait()
    loads.wv.wait()
    self_block(m.place)
    loads.wq.wait()
    r.queries_t[...] = jnp.transpose(dot(r.a1[m.place], r.wq[...]).astype(LOW))
    x_core.wait()
    self_block(m.sibling)
    loads.wout.wait()
    cotangent = r.go[...]

    def inner_grad(index, carry):
        r.inner_grad[index] = dot_nt(cotangent, r.wout[block(index, width), :]).astype(LOW)
        return carry

    lax.fori_loop(0, fan, inner_grad, 0)
    loads.cwk.wait()
    loads.cwv.wait()
    cross_block(m.place)
    e_core.wait()
    cross_block(m.sibling)
    x_y.wait()
    x_on.start()
    e_y.start()
    self_block(m.across)
    x_on.wait()
    self_block(m.diagonal)

    def keep(src, dst, slot):
        copy = pltpu.make_async_copy(src, dst, r.keep_sem.at[slot])
        copy.start()
        return copy

    kept = [
        keep(r.keys, r.keys_out, 0),
        keep(r.values, r.values_out, 1),
        keep(r.a1, r.a1_out, 2),
        keep(r.inner_grad, r.inner_out, 6),
    ]

    def probs_copy(slot, out, pair):
        return pltpu.make_async_copy(r.probs.at[slot], out.at[pair], r.probs_sem.at[slot])

    def attend(first, last, earlier, steps, keys, turned, terms, queries_t, masses, out_t, out, place):
        def one(pair, carry):
            slot = lax.rem(pair, 2)
            if earlier:
                probs_copy(slot, out, pair).wait()
            else:
                @pl.when(pair >= 2)
                def _():
                    probs_copy(slot, out, pair).wait()
            softmax_pair(
                pair, r, count, steps, keys, turned, terms, queries_t, masses, out_t,
                r.probs.at[slot], place,
            )
            probs_copy(slot, out, pair).start()
            return carry

        lax.fori_loop(first, last, one, 0)

    split = pairs - 2
    attend(
        0, split, False, places, r.keys, r.values_t, r.self_terms, r.queries_t,
        r.self_masses, r.context_t, r.self_probs, q_place,
    )
    e_y.wait()
    e_on.start()
    attend(
        split, pairs, split >= 2, places, r.keys, r.values_t, r.self_terms, r.queries_t,
        r.self_masses, r.context_t, r.self_probs, q_place,
    )
    loads.wo.wait()
    context = jnp.transpose(r.context_t[...]).astype(LOW)
    first = r.x[...].astype(F32) + dot(context, r.wo[...])
    r.first[...] = first
    normed_cross = (first * scale_of(first) * gain_cross).astype(LOW)
    r.a2[...] = normed_cross
    loads.cwq.wait()
    r.cqueries_t[...] = jnp.transpose(dot(normed_cross, r.cwq[...]).astype(LOW))
    cross_block(m.across)
    e_on.wait()
    cross_block(m.diagonal)
    kept += [
        keep(r.ckeys, r.ckeys_out, 3),
        keep(r.cvalues, r.cvalues_out, 4),
        keep(r.es, r.es_out, 5),
    ]
    attend(
        0, pairs, True, places, r.ckeys, r.cvalues_t, r.cross_terms, r.cqueries_t,
        r.cross_masses, r.ccontext_t, r.cross_probs, None,
    )
    loads.cwo.wait()
    context = jnp.transpose(r.ccontext_t[...]).astype(LOW)
    r.second[...] = r.first[...] + dot(context, r.cwo[...])
    for slot in range(2):
        probs_copy(slot, r.cross_probs, pairs - 2 + slot).wait()
    for copy in kept:
        copy.wait()


def call(kernel, name, collective, limit, inputs, outputs, scratch, aliases=None):
    names = (*inputs, *outputs, *scratch)
    results = pl.pallas_call(
        functools.partial(kernel, names),
        out_shape=tuple(jax.ShapeDtypeStruct(shape, kind) for shape, kind, _ in outputs.values()),
        in_specs=[pl.BlockSpec(memory_space=space) for _, space in inputs.values()],
        out_specs=tuple(pl.BlockSpec(memory_space=space) for _, _, space in outputs.values()),
        scratch_shapes=list(scratch.values()),
        input_output_aliases=aliases or {},
        compiler_params=pltpu.CompilerParams(
            collective_id=collective, has_side_effects=True, vmem_limit_bytes=limit * 2**20
        ),
        name=name,
    )(*(array for array, _ in inputs.values()))
    return SimpleNamespace(**dict(zip(outputs, results)))


def run_forward(dims, a):
    count, total, width = dims.count, dims.count * dims.places, dims.width
    near, far, scalars = pltpu.VMEM, pl.ANY, pltpu.SMEM
    pairs, fan = dims.pairs, dims.fan
    square = (width, width)
    own = (count, width)
    inputs = dict(
        x=(a.dec_states[0], near),
        e=(a.enc_states[0], near),
        go=(a.out_grad[0], near),
        dec_len=(a.dec_lengths, scalars),
        enc_len=(a.enc_lengths, scalars),
        table=(a.position_bias.T, near),
        gain_self=(a.gain_self, near),
        gain_cross=(a.gain_cross, near),
        wk_hbm=(a.self_key, far),
        wv_hbm=(a.self_value, far),
        wq_hbm=(a.self_query, far),
        wout_hbm=(a.ffn_out, far),
        cwk_hbm=(a.cross_key, far),
        cwv_hbm=(a.cross_value, far),
        wo_hbm=(a.self_output, far),
        cwq_hbm=(a.cross_query, far),
        cwo_hbm=(a.cross_output, far),
    )
    outputs = dict(
        first=(own, F32, near),
        second=(own, F32, near),
        inner_out=((fan, *own), LOW, far),
        queries_t=((width, count), LOW, near),
        cqueries_t=((width, count), LOW, near),
        context_t=((width, count), F32, near),
        ccontext_t=((width, count), F32, near),
        self_masses=((pairs, 1, 2 * count), F32, near),
        cross_masses=((pairs, 1, 2 * count), F32, near),
        a2=(own, LOW, near),
        keys_out=((dims.places, *own), LOW, far),
        values_out=((dims.places, *own), LOW, far),
        a1_out=((dims.places, *own), LOW, far),
        ckeys_out=((dims.places, *own), LOW, far),
        cvalues_out=((dims.places, *own), LOW, far),
        es_out=((dims.places, *own), LOW, far),
        self_probs=((pairs, total, 2 * count), LOW, far),
        cross_probs=((pairs, total, 2 * count), LOW, far),
    )
    scratch = dict(
        xs=pltpu.VMEM((dims.places, *own), LOW),
        es=pltpu.VMEM((dims.places, *own), LOW),
        wk=pltpu.VMEM(square, LOW),
        wv=pltpu.VMEM(square, LOW),
        wq=pltpu.VMEM(square, LOW),
        wout=pltpu.VMEM((fan * width, width), LOW),
        cwk=pltpu.VMEM(square, LOW),
        cwv=pltpu.VMEM(square, LOW),
        wo=pltpu.VMEM(square, LOW),
        cwq=pltpu.VMEM(square, LOW),
        cwo=pltpu.VMEM(square, LOW),
        a1=pltpu.VMEM((dims.places, *own), LOW),
        keys=pltpu.VMEM((dims.places, *own), LOW),
        values=pltpu.VMEM((dims.places, *own), LOW),
        values_t=pltpu.VMEM((width, total), LOW),
        ckeys=pltpu.VMEM((dims.places, *own), LOW),
        cvalues=pltpu.VMEM((dims.places, *own), LOW),
        cvalues_t=pltpu.VMEM((width, total), LOW),
        self_terms=pltpu.VMEM((total, count), F32),
        cross_terms=pltpu.VMEM((total, count), F32),
        near_bias=pltpu.VMEM((dims.heads, 2 * NEAR), F32),
        scores=pltpu.VMEM((total, 2 * count), F32),
        probs=pltpu.VMEM((2, total, 2 * count), LOW),
        inner_grad=pltpu.VMEM((fan, *own), LOW),
        load_sem=pltpu.SemaphoreType.DMA((10,)),
        link_sem=pltpu.SemaphoreType.DMA((2, 6)),
        keep_sem=pltpu.SemaphoreType.DMA((7,)),
        probs_sem=pltpu.SemaphoreType.DMA((2,)),
    )
    return call(
        lambda names, *refs: forward_kernel(names, dims, *refs),
        "forward", 0, 56, inputs, outputs, scratch,
    )


SWAPPED = (1, 5, 8, 10, 11, 13, 16, 19)


class Reducer:
    LAGS = (0, 2, 4, 6, 9, 16)

    def __init__(self, r, m, dims):
        self.r, self.m = r, m
        self.planes = dims.planes
        self.line = dims.line
        self.piece = dims.piece
        self.chunk_rows = dims.chunk_rows
        self.half_rows = dims.chunk_rows // 2
        self.chunks = dims.chunks
        self.ring = dims.ring
        self.plane, self.half = m.row // 2, lax.rem(m.row, 2)
        self.x_peer = (self.plane * 2 + 1 - self.half, m.place)
        self.published = self.loaded = self.fed = self.moved = 0

    def z_peer(self, step):
        return (lax.rem(self.plane + step, self.planes) * 2 + self.half, self.m.place)

    def plane_peer(self, plane):
        return (plane * 2 + self.half, self.m.place)

    def peers(self):
        return [self.x_peer] + [self.z_peer(step) for step in range(1, self.planes)]

    def span(self, first, size):
        return pl.ds(pl.multiple_of(first, self.piece), size)

    def rows(self, index):
        return self.span(index * self.chunk_rows, self.chunk_rows)

    def by_planes(self, index):
        found = index == SWAPPED[0]
        for other in SWAPPED[1:]:
            found = found | (index == other)
        return found

    def route(self, index, first, other):
        if not self.line:
            first(index)
            return
        special = self.by_planes(index)

        @pl.when(jnp.logical_not(special))
        def _():
            first(index)

        @pl.when(special)
        def _():
            other(index)

    def half_of(self, index, half):
        return self.span(index * self.chunk_rows + half * self.half_rows, self.half_rows)

    def packed(self, index):
        return self.span(index * self.half_rows, self.half_rows)

    def fresh_rows(self, index):
        return self.span(lax.rem(index, self.ring) * self.chunk_rows, self.chunk_rows)

    def load(self, index):
        r = self.r
        return pltpu.make_async_copy(
            r.big.at[self.m.core, :, self.rows(index)],
            r.fresh.at[:, self.fresh_rows(index)],
            r.chunk_sem.at[index],
        )

    def core_copy(self, index):
        r, rows = self.r, self.rows(index)
        return send(
            r.big.at[1 - self.m.core, :, rows], r.sums.at[:, rows], r.core_sem, (index,),
            self.m.core_peer,
        )

    def y_copy(self, index):
        r, rows = self.r, self.rows(index)
        return send(
            r.sums.at[1 - self.m.side, rows], r.fin.at[rows], r.y_sem, (index,), self.m.y_peer
        )

    def x_copy(self, index):
        r = self.r
        return send(
            r.sums.at[self.m.side, self.half_of(index, 1 - self.half)],
            r.x_recv.at[self.packed(index)],
            r.x_sem, (index,), self.x_peer,
        )

    def in_copy(self, index, inner):
        r = self.r
        return send(
            r.sums.at[self.m.side, self.half_of(index, self.half)],
            r.z_recv.at[0, self.packed(index)],
            r.z_sem, (index, 0), self.plane_peer(inner),
        )

    def mid_copy(self, index):
        r = self.r
        return send(
            r.sums.at[self.m.side, self.half_of(index, self.half)],
            r.z_recv.at[1, self.packed(index)],
            r.z_sem, (index, 1), self.plane_peer(3 - self.plane),
        )

    def out_copy(self, index, outer):
        r, rows = self.r, self.half_of(index, self.half)
        return send(r.fin.at[rows], r.fin.at[rows], r.gz_sem, (index, 0), self.plane_peer(outer))

    def z_part(self, index, which):
        first = index * self.chunk_rows + self.half * self.half_rows + which * self.piece
        return self.span(first, self.piece)

    def z_copy(self, index, step):
        r = self.r
        target = lax.rem(self.plane + step, self.planes)
        return send(
            r.sums.at[self.m.side, self.z_part(index, target)],
            r.z_recv.at[step - 1, self.span(index * self.piece, self.piece)],
            r.z_sem, (index, step - 1), self.z_peer(step),
        )

    def gz_copy(self, index, step):
        r, rows = self.r, self.z_part(index, self.plane)
        return send(r.fin.at[rows], r.fin.at[rows], r.gz_sem, (index, step - 1), self.z_peer(step))

    def gx_copy(self, index):
        r, rows = self.r, self.half_of(index, self.half)
        return send(r.fin.at[rows], r.fin.at[rows], r.gx_sem, (index,), self.x_peer)

    def publish(self, rows):
        last = rows // self.chunk_rows

        def begin(index, carry):
            self.core_copy(index).start()
            return carry

        def fetch(index, carry):
            self.load(index).start()
            return carry

        lax.fori_loop(self.published, last, begin, 0)
        ahead = min(last, self.fed + self.ring)
        lax.fori_loop(self.loaded, ahead, fetch, 0)
        self.published, self.loaded = last, max(self.loaded, ahead)

    def feed(self, index):
        r = self.r
        self.load(index).wait()
        self.core_copy(index).wait()
        rows, fresh = self.rows(index), self.fresh_rows(index)
        for side in range(2):
            r.sums[side, rows, :] = add_low(r.sums[side, rows, :], r.fresh[side, fresh, :])
        self.route(
            index, lambda at: self.y_copy(at).start(), lambda at: self.swap_copy(at).start()
        )

        @pl.when(index + self.ring < self.published)
        def _():
            self.load(index + self.ring).start()

    def move(self, step):
        stages = (
            (self.after_y, self.after_swap),
            (self.after_x, self.swapped_y),
            (self.inward, self.swapped_x),
            (self.middle, self.swapped_pair),
            (self.outward, self.swapped_back),
            (self.finish, self.swapped_finish),
        )
        for lag, stage in reversed(tuple(zip(self.LAGS, stages))):
            index = step - lag

            @pl.when((index >= 0) & (index < self.chunks))
            def _():
                self.route(index, *stage)


    def parity(self):
        return lax.rem(self.plane, 2)

    def neighbour(self):
        return self.plane_peer(self.plane + 1 - 2 * self.parity())

    def quarter_of(self, index, half):
        size = self.half_rows // 2
        first = index * self.chunk_rows + self.parity() * self.half_rows + half * size
        return self.span(first, size)

    def packed_quarter(self, index, which):
        size = self.half_rows // 2
        return self.span(index * self.half_rows + which * size, size)

    def swap_copy(self, index):
        r = self.r
        return send(
            r.sums.at[:, self.half_of(index, 1 - self.parity())],
            r.z_recv.at[:, self.packed(index)],
            r.z_sem, (index, 0), self.neighbour(),
        )

    def swapped_y_copy(self, index):
        r, rows = self.r, self.half_of(index, self.parity())
        return send(
            r.sums.at[1 - self.m.side, rows], r.fin.at[rows], r.y_sem, (index,), self.m.y_peer
        )

    def swapped_x_copy(self, index):
        r = self.r
        return send(
            r.sums.at[self.m.side, self.quarter_of(index, 1 - self.half)],
            r.x_recv.at[self.packed_quarter(index, 0)],
            r.x_sem, (index,), self.x_peer,
        )

    def pair_copy(self, index):
        r = self.r
        return send(
            r.sums.at[self.m.side, self.quarter_of(index, self.half)],
            r.x_recv.at[self.packed_quarter(index, 1)],
            r.z_sem, (index, 1), self.z_peer(2),
        )

    def swapped_gx_copy(self, index):
        r, rows = self.r, self.quarter_of(index, self.half)
        return send(r.fin.at[rows], r.fin.at[rows], r.gx_sem, (index,), self.x_peer)

    def swapped_gz_copy(self, index):
        r, rows = self.r, self.half_of(index, self.parity())
        return send(r.fin.at[rows], r.fin.at[rows], r.gz_sem, (index, 0), self.neighbour())

    def after_swap(self, index):
        r = self.r
        self.swap_copy(index).wait()
        rows, packed = self.half_of(index, self.parity()), self.packed(index)
        for side in range(2):
            r.sums[side, rows, :] = add_low(r.sums[side, rows, :], r.z_recv[side, packed, :])
        self.swapped_y_copy(index).start()

    def swapped_y(self, index):
        r, m = self.r, self.m
        self.swapped_y_copy(index).wait()
        rows = self.half_of(index, self.parity())
        r.sums[m.side, rows, :] = add_low(r.sums[m.side, rows, :], r.fin[rows, :])
        self.swapped_x_copy(index).start()

    def swapped_x(self, index):
        r, m = self.r, self.m
        self.swapped_x_copy(index).wait()
        rows = self.quarter_of(index, self.half)
        arrived = r.x_recv[self.packed_quarter(index, 0), :]
        r.sums[m.side, rows, :] = add_low(r.sums[m.side, rows, :], arrived)
        self.pair_copy(index).start()

    def swapped_pair(self, index):
        r, m = self.r, self.m
        self.pair_copy(index).wait()
        rows = self.quarter_of(index, self.half)
        arrived = r.x_recv[self.packed_quarter(index, 1), :]
        r.fin[rows, :] = add_low(r.sums[m.side, rows, :], arrived)
        self.swapped_gx_copy(index).start()

    def swapped_back(self, index):
        self.swapped_gx_copy(index).wait()
        self.swapped_gz_copy(index).start()

    def swapped_finish(self, index):
        self.swapped_gz_copy(index).wait()

    def after_y(self, index):
        r, m = self.r, self.m
        self.y_copy(index).wait()
        rows = self.rows(index)
        r.sums[m.side, rows, :] = add_low(r.sums[m.side, rows, :], r.fin[rows, :])
        self.x_copy(index).start()

    def after_x(self, index):
        r, m = self.r, self.m
        self.x_copy(index).wait()
        rows = self.half_of(index, self.half)
        r.sums[m.side, rows, :] = add_low(r.sums[m.side, rows, :], r.x_recv[self.packed(index), :])
        if not self.line:
            for step in range(1, self.planes):
                self.z_copy(index, step).start()
            return
        for outer, inner in ((0, 1), (3, 2)):
            @pl.when(self.plane == outer)
            def _():
                self.in_copy(index, inner).start()

    def inward(self, index):
        r, m = self.r, self.m
        if not self.line:
            return
        for outer, inner in ((0, 1), (3, 2)):
            @pl.when(self.plane == outer)
            def _():
                self.in_copy(index, inner).wait_send()

        @pl.when((self.plane == 1) | (self.plane == 2))
        def _():
            self.in_copy(index, self.plane).wait_recv()
            rows = self.half_of(index, self.half)
            arrived = r.z_recv[0, self.packed(index), :]
            r.sums[m.side, rows, :] = add_low(r.sums[m.side, rows, :], arrived)
            self.mid_copy(index).start()

    def middle(self, index):
        r, m = self.r, self.m
        if not self.line:
            part = self.z_part(index, self.plane)
            total = r.sums[m.side, part, :].astype(F32)
            for step in range(1, self.planes):
                self.z_copy(index, step).wait()
                arrived = r.z_recv[step - 1, self.span(index * self.piece, self.piece), :]
                total = total + arrived.astype(F32)
            r.fin[part, :] = total.astype(LOW)
            for step in range(1, self.planes):
                self.gz_copy(index, step).start()
            return

        @pl.when((self.plane == 1) | (self.plane == 2))
        def _():
            self.mid_copy(index).wait()
            rows = self.half_of(index, self.half)
            arrived = r.z_recv[1, self.packed(index), :]
            r.fin[rows, :] = add_low(r.sums[m.side, rows, :], arrived)
            for outer, inner in ((0, 1), (3, 2)):
                @pl.when(self.plane == inner)
                def _():
                    self.out_copy(index, outer).start()
            self.gx_copy(index).start()

    def outward(self, index):
        if not self.line:
            for step in range(1, self.planes):
                self.gz_copy(index, step).wait()
            self.gx_copy(index).start()
            return
        for outer, inner in ((0, 1), (3, 2)):
            @pl.when(self.plane == inner)
            def _():
                self.out_copy(index, outer).wait_send()

            @pl.when(self.plane == outer)
            def _():
                self.out_copy(index, inner).wait_recv()
                self.gx_copy(index).start()

    def finish(self, index):
        self.gx_copy(index).wait()

    def run(self, feeds, moves):
        loops = max(1, feeds, moves)
        one, after = self.beside(loops, feeds, moves)

        def body(index, carry):
            one(index)
            return carry

        lax.fori_loop(0, loops, body, 0)
        after()

    def beside(self, loops, feeds, moves):
        feeds = max(0, min(feeds, self.published - self.fed))
        fed = self.fed + feeds
        limit = self.chunks + self.LAGS[-1] if fed == self.chunks else fed
        moves = max(0, min(moves, limit - self.moved))
        first_feed, first_move = self.fed, self.moved

        each = -(-feeds // loops)

        def one(index):
            if feeds > 0:
                def feed(step, carry):
                    self.feed(first_feed + step)
                    return carry

                lax.fori_loop(
                    jnp.minimum(index * each, feeds), jnp.minimum((index + 1) * each, feeds), feed, 0
                )
            if moves > 0:
                def move(step, carry):
                    self.move(first_move + step)
                    return carry

                lax.fori_loop(index * moves // loops, (index + 1) * moves // loops, move, 0)

        def after():
            self.fed, self.moved = fed, first_move + moves
            self.loaded = max(self.loaded, min(self.published, self.fed + self.ring))

        return one, after

    def left(self):
        return self.chunks + self.LAGS[-1] - self.moved


def attend_back(pair, r, count, keys, keys_t, values, queries_t, masses, context_t, grad_t, probs, place, places):
    lanes = block(pair, 2 * r.head_dim)
    inverse = masses[pair]
    grads = grad_t[lanes, :].astype(F32)
    product = grads * context_t[lanes, :]
    sums = [
        jnp.sum(product[: r.head_dim], axis=0, keepdims=True),
        jnp.sum(product[r.head_dim :], axis=0, keepdims=True),
    ]
    inner = jnp.concatenate(sums, axis=1) * inverse
    grads = (head_blocks(grads) * inverse).astype(LOW)
    queries = head_blocks(queries_t[lanes, :])

    total = jnp.zeros((2 * r.head_dim, 2 * count), F32)
    beyond = jnp.zeros((8, 2 * count), F32)
    split = count - NEAR
    if place is not None:
        r.before[...] = jnp.zeros_like(r.before)
    for index in range(places):
        rows = block(index, count)
        weights = probs[rows, :]
        score_grad = weights.astype(F32) * (dot(values[index, :, lanes], grads) - inner)
        low = score_grad.astype(LOW)
        r.value_grad[index, :, lanes] = dot_nt(weights, grads).astype(LOW)
        r.key_grad[index, :, lanes] = dot_nt(low, queries).astype(LOW)
        total = total + dot(keys_t[lanes, rows], low)
        if place is not None:
            early = jnp.sum(fold(score_grad[:split]), axis=0)
            late = jnp.sum(fold(score_grad[split:]), axis=0)
            beyond = beyond + jnp.where(index < place, early, 0.0)
            beyond = beyond + jnp.where(index < place - 1, late, 0.0)

            @pl.when(index == place - 1)
            def _():
                r.before[...] = score_grad[split:]

            @pl.when(index == place)
            def _():
                r.own[...] = score_grad

    if place is not None:
        own, before = r.own[...], r.before[...]
        parts = []
        for head in range(2):
            at = head * count
            on = own[:NEAR, at : at + NEAR] + own[NEAR:, at + NEAR : at + 2 * NEAR]
            below = before[:, at : at + NEAR] + own[:NEAR, at + NEAR : at + 2 * NEAR]
            both = jnp.concatenate([on, below], axis=1)
            summed = both[:8]
            for group in range(1, NEAR // 8):
                summed = summed + pltpu.roll(
                    both[8 * group : 8 * group + 8], 2 * NEAR - 8 * group, 1
                )
            parts.append(summed)
        summed = jnp.concatenate(parts, axis=0)
        sublane = lax.broadcasted_iota(jnp.int32, summed.shape, 0)
        for bit in (1, 2, 4):
            summed = jnp.where(
                (sublane & bit) != 0, pltpu.roll(summed, 2 * NEAR - bit, 1), summed
            )
        lane = lax.broadcasted_iota(jnp.int32, (1, 2 * NEAR), 1)
        for head in range(2):
            at = head * count
            line = jnp.sum(summed[8 * head : 8 * head + 8], axis=0, keepdims=True)
            rest = jnp.sum(beyond[:, at : at + count]) + jnp.sum(before[:, at + NEAR : at + 2 * NEAR])
            line = line + jnp.where(lane == 2 * NEAR - 1, rest, 0.0)
            r.by_distance[pl.ds(pair * 2 + head, 1), :] = line
    r.query_grad_t[lanes, :] = head_rows(total).astype(LOW)


PLAN = ((10, 0), (0, 0), (0, 0), (2, 0), (0, 0), (0, 1), (4, 2), (1, 0), (0, 2), (1, 1), (2, 1), (1, 2), (17, 6), (1, 0), (9, 1), (3, 4), (18, 1), (15, 1), (10, 6), (18, 2), (15, 11))


def backward_kernel(names, dims, *refs):
    r = SimpleNamespace(**dict(zip(names, refs)), head_dim=dims.head_dim)
    m = Mesh2()
    count, places, pairs, fan, width = dims.count, dims.places, dims.pairs, dims.fan, dims.width
    own = width // places
    engine = Reducer(r, m, dims)
    plan = iter(PLAN)
    r.wo, r.wq, r.wk, r.wv = (r.squares.at[index] for index in range(4))
    r.keys, r.values, r.key_grad, r.value_grad = (r.tall.at[pl.ds(4 * k, 4)] for k in range(4))

    loads = SimpleNamespace()
    slots = iter(range(r.load_sem.shape[0]))

    def load(src, dst):
        copy = pltpu.make_async_copy(src, dst, r.load_sem.at[next(slots)])
        copy.start()
        return copy

    def probs_copy(src, pair):
        slot = lax.rem(pair, 2)
        return pltpu.make_async_copy(src.at[pair], r.probs.at[slot], r.probs_sem.at[slot])

    third = width // count
    loads.second = load(r.second_hbm, r.second)
    win, wout = [], []
    for index in range(fan):
        win.append(load(r.win_hbm.at[:, pl.ds(index * width, width)], r.squares.at[index]))
        if index == 0:
            loads.inner = load(r.inner_hbm, r.value_grad)
        wout.append(
            load(r.wout_hbm.at[pl.ds(index * third, third)], r.tall.at[pl.ds(index * third, third)])
        )
    probs_copy(r.cross_probs, 0).start()
    probs_copy(r.cross_probs, 1).start()
    loads.es0 = load(r.es_hbm.at[m.core], r.group.at[0])
    loads.es1 = load(r.es_hbm.at[m.core + 2], r.group.at[1])
    loads.cqueries = load(r.cqueries_hbm, r.cqueries_t)
    loads.ccontext = load(r.ccontext_hbm, r.ccontext_t)
    loads.queries = load(r.queries_hbm, r.queries_t)
    loads.context = load(r.context_hbm, r.context_t)
    loads.a2 = load(r.a2_hbm, r.a2)

    m.greet([m.core_peer, m.y_peer] + engine.peers())

    gain_self = r.gain_self[...].astype(F32).reshape(1, width)
    gain_cross = r.gain_cross[...].astype(F32).reshape(1, width)
    staged = {}

    def unit_copy(unit):
        rows = pl.ds(2 * width + unit * own, own)
        return pltpu.make_async_copy(
            r.stage.at[unit % 2], r.big.at[:, :, rows], r.stage_sem.at[unit % 2]
        )

    def give(unit, left_t, right):
        if unit - 2 in staged:
            staged.pop(unit - 2).wait()
        for place in range(places):
            grad = dot(left_t[place * own : (place + 1) * own, :], right)
            r.stage[unit % 2, place % 2, place // 2] = grad.astype(LOW)
        staged[unit] = unit_copy(unit)
        staged[unit].start()

    def settle(rows):
        for unit in sorted(staged):
            staged.pop(unit).wait()
        engine.publish(rows)

    def turn(src, dst):
        def one(index, carry):
            rows = block(index, count)
            dst[:, rows] = jnp.transpose(src[index])
            return carry

        lax.fori_loop(0, places, one, 0)

    def attend(src, queries_t, masses, context_t, grad_t, place):
        beside, after = engine.beside(pairs, *next(plan))

        def one(pair, carry):
            probs_copy(src, pair).wait()
            attend_back(
                pair, r, count, r.keys, r.keys_t, r.values, queries_t, masses, context_t, grad_t,
                r.probs.at[lax.rem(pair, 2)], place, places,
            )

            @pl.when(pair + 2 < pairs)
            def _():
                probs_copy(src, pair + 2).start()

            beside(pair)
            return carry

        lax.fori_loop(0, pairs, one, 0)
        after()

    def exchange(slot):
        copies = []
        for side in range(2):
            theirs = side * 2 + 1 - m.core
            for part, (src, dst) in enumerate(
                ((r.key_grad, r.key_recv), (r.value_grad, r.value_recv))
            ):
                copies.append(
                    send(
                        src.at[theirs], dst.at[slot, side], r.swap_sem, (slot, side, part),
                        m.core_peer,
                    )
                )
                copies[-1].start()
        return copies

    def chip_sum(grad, arrived):
        parts = [add_low(grad[side * 2 + m.core], arrived[side]) for side in range(2)]
        return jnp.concatenate(parts, axis=0)

    def partial(slot, side):
        key_grad = add_low(r.key_grad[side * 2 + m.core], r.key_recv[slot, side])
        value_grad = add_low(r.value_grad[side * 2 + m.core], r.value_recv[slot, side])
        return dot_nt(key_grad, r.wk[...]) + dot_nt(value_grad, r.wv[...])

    gain_ffn = r.gain_ffn[...].astype(F32).reshape(1, width)
    loads.second.wait()
    second = r.second[...]
    normed_ffn = (second * scale_of(second) * gain_ffn).astype(LOW)
    r.grad_t[...] = jnp.transpose(normed_ffn)
    r.a3[...] = normed_ffn
    head = None
    for index in range(fan):
        win[index].wait()
        pre = dot(r.a3[...], r.squares[index])
        half = 0.5 + 0.5 * lax.erf(pre * (0.5**0.5))
        inner = (pre * half).astype(LOW)
        slope = half + pre * jnp.exp(-0.5 * pre * pre) * ((2.0 * math.pi) ** -0.5)
        if index == 0:
            loads.inner.wait()
        pre_grad = (slope * r.value_grad[index].astype(F32)).astype(LOW)
        for place in range(places):
            grad = dot(r.grad_t[place * own : (place + 1) * own, :], pre_grad)
            r.stage[index % 2, place % 2, place // 2] = grad.astype(LOW)
        tail = pltpu.make_async_copy(
            r.stage.at[index % 2], r.big.at[:, :, pl.ds(index * own, own)], r.stage_sem.at[index % 2]
        )
        tail.start()
        wout[index].wait()
        rows = r.tall[index * third : (index + 1) * third].reshape(width, width)
        total = dot(inner, rows)
        back = dot_nt(pre_grad, r.squares[index])
        r.dec_grad[...] = total if index == 0 else r.dec_grad[...] + total
        r.enc_grad[...] = back if index == 0 else r.enc_grad[...] + back
        if head is not None:
            head.wait()
        r.keys_t[:, :width] = dot(jnp.transpose(inner), r.go[...]).astype(LOW)
        head = pltpu.make_async_copy(
            r.keys_t.at[:, pl.ds(0, width)],
            r.big.at[index % 2, index // 2, pl.ds(width, width)],
            r.head_sem,
        )
        head.start()
        if index == 0:
            loads.cwo = load(r.cwo_hbm, r.wo)
        if index == 1:
            loads.cwq = load(r.cwq_hbm, r.wq)
            loads.ckeys = load(r.ckeys_hbm, r.keys)
        if index == 2:
            loads.cwk = load(r.cwk_hbm, r.wk)
            loads.cvalues = load(r.cvalues_hbm, r.values)
        if index == 3:
            loads.cwv = load(r.cwv_hbm, r.wv)
        tail.wait()
        engine.publish((index + 1) * own)
        engine.run(*next(plan))
    r.layer_out[...] = (second + r.dec_grad[...]).astype(LOW)
    second_part, gain_ffn_grad = norm_back(second, gain_ffn, r.enc_grad[...])
    loads.first = load(r.first_hbm, r.enc_grad)
    r.dec_grad[...] = r.go[...].astype(F32) + second_part
    r.tiny[0] = jnp.zeros(r.tiny.shape[1:], F32)
    r.tiny[0, 2:3] = gain_ffn_grad
    head.wait()
    engine.publish(2 * width)
    engine.run(*next(plan))

    head_grad = r.dec_grad[...].astype(LOW)
    loads.cwo.wait()
    r.grad_t[...] = dot_nt(r.wo[...], head_grad).astype(LOW)
    loads.wo = load(r.wo_hbm, r.wo)
    engine.run(*next(plan))
    loads.ccontext.wait()
    give(0, r.ccontext_t[...].astype(LOW), head_grad)
    loads.ckeys.wait()
    turn(r.keys, r.keys_t)
    loads.cvalues.wait()
    loads.cqueries.wait()
    attend(r.cross_probs, r.cqueries_t, r.cross_masses, r.ccontext_t, r.grad_t, None)
    copies = exchange(0)
    loads.keys = load(r.keys_hbm, r.keys)
    loads.values = load(r.values_hbm, r.values)
    probs_copy(r.self_probs, 0).start()
    probs_copy(r.self_probs, 1).start()
    query_grad = jnp.transpose(r.query_grad_t[...])
    engine.run(*next(plan))
    loads.cwq.wait()
    normed_grad = dot_nt(query_grad, r.wq[...])
    loads.wq = load(r.wq_hbm, r.wq)
    loads.first.wait()
    first_part, gain_cross_grad = norm_back(r.enc_grad[...], gain_cross, normed_grad)
    r.dec_grad[...] += first_part
    r.tiny[0, 1:2] = gain_cross_grad
    loads.a2.wait()
    give(1, jnp.transpose(r.a2[...]), query_grad)
    engine.run(*next(plan))
    loads.es0.wait()
    loads.es1.wait()
    for side in range(2):
        r.group_t[:, side * count : (side + 1) * count] = jnp.transpose(r.group[side])
    loads.a10 = load(r.a1_hbm.at[m.core], r.group.at[0])
    loads.a11 = load(r.a1_hbm.at[m.core + 2], r.group.at[1])
    for copy in copies:
        copy.wait()
    key_grad = chip_sum(r.key_grad, r.key_recv.at[0])
    value_grad = chip_sum(r.value_grad, r.value_recv.at[0])
    loads.cwk.wait()
    loads.cwv.wait()
    r.partial_low[...] = partial(0, 1 - m.side).astype(LOW)
    enc_copy = send(r.partial_low, r.partial_recv.at[0], r.link_sem, (0,), m.y_peer)
    enc_copy.start()
    r.enc_grad[...] = partial(0, m.side)
    loads.wk = load(r.wk_hbm, r.wk)
    loads.wv = load(r.wv_hbm, r.wv)
    engine.run(*next(plan))
    give(2, r.group_t[...], key_grad)
    give(3, r.group_t[...], value_grad)
    settle(3 * width)
    engine.run(*next(plan))

    first_grad = r.dec_grad[...]
    head_grad = first_grad.astype(LOW)
    loads.wo.wait()
    r.grad_t[...] = dot_nt(r.wo[...], head_grad).astype(LOW)
    loads.context.wait()
    engine.run(*next(plan))
    give(4, r.context_t[...].astype(LOW), head_grad)
    loads.keys.wait()
    turn(r.keys, r.keys_t)
    loads.values.wait()
    loads.queries.wait()

    r.by_distance[...] = jnp.zeros_like(r.by_distance)
    attend(r.self_probs, r.queries_t, r.self_masses, r.context_t, r.grad_t, m.place)
    copies = exchange(1)
    query_grad = jnp.transpose(r.query_grad_t[...])
    engine.run(*next(plan))
    loads.wq.wait()
    normed_grad = dot_nt(query_grad, r.wq[...])
    loads.a10.wait()
    loads.a11.wait()
    for side in range(2):
        r.group_t[:, side * count : (side + 1) * count] = jnp.transpose(r.group[side])
    give(5, jnp.transpose(r.group[m.side]), query_grad)
    engine.run(*next(plan))
    for copy in copies:
        copy.wait()
    key_grad = chip_sum(r.key_grad, r.key_recv.at[1])
    value_grad = chip_sum(r.value_grad, r.value_recv.at[1])
    loads.wk.wait()
    loads.wv.wait()
    enc_copy.wait()
    r.enc_grad[...] += r.partial_recv[0].astype(F32)
    r.partial_low[...] = partial(1, 1 - m.side).astype(LOW)
    dec_copy = send(r.partial_low, r.partial_recv.at[1], r.link_sem, (1,), m.y_peer)
    dec_copy.start()
    normed_grad = normed_grad + partial(1, m.side)
    give(6, r.group_t[...], key_grad)
    give(7, r.group_t[...], value_grad)
    settle(4 * width)
    engine.run(*next(plan))
    engine.run(*next(plan))
    dec_copy.wait()
    normed_grad = normed_grad + r.partial_recv[1].astype(F32)
    state_part, gain_self_grad = norm_back(r.x[...].astype(F32), gain_self, normed_grad)
    r.dec_grad[...] += state_part

    buckets = dims.buckets
    table = lax.dot_general(
        bucket_terms(buckets), r.by_distance[...], (((1,), (1,)), ((), ())),
        precision=lax.Precision.HIGHEST, preferred_element_type=F32,
    )
    r.tiny[0, 0:1] = gain_self_grad
    part = buckets // places
    for place in range(places):
        r.tiny[0, 8 : 8 + part, 128 * place : 128 * (place + 1)] = table[
            place * part : (place + 1) * part
        ]
    for slot, peer in enumerate((m.core_peer, m.y_peer, engine.x_peer)):
        copy = send(r.tiny.at[slot], r.tiny_recv.at[slot], r.tiny_sem, (slot,), peer)
        copy.start()
        engine.run(*next(plan))
        copy.wait()
        r.tiny[slot + 1] = r.tiny[slot] + r.tiny_recv[slot]
    copies = []
    for step in range(1, dims.planes):
        copy = send(
            r.tiny.at[3], r.tiny_recv.at[2 + step], r.tiny_sem, (2 + step,), engine.z_peer(step)
        )
        copy.start()
        copies.append(copy)
    engine.run(*next(plan))
    for copy in copies:
        copy.wait()
    total = r.tiny[3]
    for step in range(1, dims.planes):
        total = total + r.tiny_recv[2 + step]
    r.small[...] = total
    engine.run(engine.chunks, engine.left())


def run_backward(dims, a, f):
    count, total, width = dims.count, dims.count * dims.places, dims.width
    near, far = pltpu.VMEM, pl.ANY
    pairs, planes, chunks, piece = dims.pairs, dims.planes, dims.chunks, dims.piece
    square = (width, width)
    own = (count, width)
    inputs = dict(
        x=(a.dec_states[0], near),
        go=(a.out_grad[0], near),
        gain_self=(a.gain_self, near),
        gain_cross=(a.gain_cross, near),
        gain_ffn=(a.gain_ffn, near),
        self_masses=(f.self_masses, near),
        cross_masses=(f.cross_masses, near),
        first_hbm=(f.first, far),
        second_hbm=(f.second, far),
        inner_hbm=(f.inner_out, far),
        win_hbm=(a.ffn_in, far),
        wout_hbm=(a.ffn_out.reshape(-1, *own), far),
        queries_hbm=(f.queries_t, far),
        cqueries_hbm=(f.cqueries_t, far),
        context_hbm=(f.context_t, far),
        ccontext_hbm=(f.ccontext_t, far),
        a2_hbm=(f.a2, far),
        keys_hbm=(f.keys_out, far),
        values_hbm=(f.values_out, far),
        a1_hbm=(f.a1_out, far),
        ckeys_hbm=(f.ckeys_out, far),
        cvalues_hbm=(f.cvalues_out, far),
        es_hbm=(f.es_out, far),
        self_probs=(f.self_probs, far),
        cross_probs=(f.cross_probs, far),
        wo_hbm=(a.self_output, far),
        wq_hbm=(a.self_query, far),
        wk_hbm=(a.self_key, far),
        wv_hbm=(a.self_value, far),
        cwo_hbm=(a.cross_output, far),
        cwq_hbm=(a.cross_query, far),
        cwk_hbm=(a.cross_key, far),
        cwv_hbm=(a.cross_value, far),
    )
    outputs = dict(
        big=((2, 2, 4 * width, width), LOW, far),
        layer_out=(own, LOW, near),
        fin=((4 * width, width), LOW, near),
        dec_grad=(own, F32, near),
        enc_grad=(own, F32, near),
        small=((16, width), F32, near),
    )
    dma = pltpu.SemaphoreType.DMA
    rows = 4 * width
    scratch = dict(
        squares=pltpu.VMEM((4, *square), LOW),
        tall=pltpu.VMEM((16, *own), LOW),
        second=pltpu.VMEM(own, F32),
        keys_t=pltpu.VMEM((width, total), LOW),
        probs=pltpu.VMEM((2, total, 2 * count), LOW),
        grad_t=pltpu.VMEM((width, count), LOW),
        a3=pltpu.VMEM(own, LOW),
        a2=pltpu.VMEM(own, LOW),
        queries_t=pltpu.VMEM((width, count), LOW),
        cqueries_t=pltpu.VMEM((width, count), LOW),
        context_t=pltpu.VMEM((width, count), F32),
        ccontext_t=pltpu.VMEM((width, count), F32),
        query_grad_t=pltpu.VMEM((width, count), LOW),
        key_recv=pltpu.VMEM((2, 2, *own), LOW),
        value_recv=pltpu.VMEM((2, 2, *own), LOW),
        partial_low=pltpu.VMEM(own, LOW),
        partial_recv=pltpu.VMEM((2, *own), LOW),
        group=pltpu.VMEM((2, *own), LOW),
        group_t=pltpu.VMEM((width, 2 * count), LOW),
        before=pltpu.VMEM((NEAR, 2 * count), F32),
        own=pltpu.VMEM((count, 2 * count), F32),
        by_distance=pltpu.VMEM((128, 2 * NEAR), F32),
        stage=pltpu.VMEM((2, 2, 2, width // dims.places, width), LOW),
        fresh=pltpu.VMEM((2, dims.ring * dims.chunk_rows, width), LOW),
        sums=pltpu.VMEM((2, rows, width), LOW),
        x_recv=pltpu.VMEM((rows // 2, width), LOW),
        z_recv=pltpu.VMEM(
            (2, rows // 2, width) if dims.line else (planes - 1, chunks * piece, width), LOW
        ),
        tiny=pltpu.VMEM((4, 16, width), F32),
        tiny_recv=pltpu.VMEM((2 + planes, 16, width), F32),
        load_sem=dma((40,)),
        head_sem=dma,
        probs_sem=dma((2,)),
        stage_sem=dma((2,)),
        link_sem=dma((2, 2)),
        swap_sem=dma((2, 2, 2, 2)),
        chunk_sem=dma((chunks,)),
        core_sem=dma((2, chunks)),
        y_sem=dma((2, chunks)),
        x_sem=dma((2, chunks)),
        z_sem=dma((2, chunks, planes - 1)),
        gz_sem=dma((2, chunks, planes - 1)),
        gx_sem=dma((2, chunks)),
        tiny_sem=dma((2, 2 + planes)),
    )
    return call(
        lambda names, *refs: backward_kernel(names, dims, *refs),
        "backward", 1, 63, inputs, outputs, scratch,
    )


def place_kernel(names, dims, *refs):
    r = SimpleNamespace(**dict(zip(names, refs)))
    width, fan = dims.width, dims.fan
    own = width // dims.places
    passed = (
        (r.layer_in, r.layer_held, r.layer),
        (r.dec_in, r.dec_held, r.dec),
        (r.enc_in, r.enc_held, r.enc),
    )
    inward = [
        pltpu.make_async_copy(src, held, r.pass_sem.at[0, slot])
        for slot, (src, held, _) in enumerate(passed)
    ]
    copies = [
        pltpu.make_async_copy(held, dst, r.pass_sem.at[1, slot])
        for slot, (_, held, dst) in enumerate(passed)
    ]
    groups = 4 * width // own
    loads, stores = [], []
    for index in range(4):
        rows = pl.ds(index * width, width)
        loads.append(pltpu.make_async_copy(r.fin.at[rows], r.low.at[rows], r.load_sem.at[index]))
        loads[-1].start()
    for copy in inward:
        copy.start()
    units = (
        r.cross_output, r.cross_query, r.cross_key, r.cross_value,
        r.self_output, r.self_query, r.self_key, r.self_value,
    )
    for index in range(groups):
        if index % (groups // 4) == 0:
            loads[index // (groups // 4)].wait()
        rows = pl.ds(index * own, own)
        r.wide[rows, :] = r.low[rows, :].astype(F32)
        if index < fan:
            dst = r.ffn_in.at[:, pl.ds(index * width, width)]
        elif index < 2 * fan:
            dst = r.ffn_out.at[pl.ds((index - fan) * own, own)]
        else:
            dst = units[index - 2 * fan]
        copy = pltpu.make_async_copy(r.wide.at[rows], dst, r.store_sem.at[index])
        copy.start()
        stores.append(copy)
    for arrival, copy in zip(inward, copies):
        arrival.wait()
        copy.start()
    at = lax.axis_index("seq")
    part = dims.buckets // dims.places
    for place in range(dims.places):
        @pl.when(at == place)
        def _():
            for index, grad in enumerate((r.gain_self, r.gain_cross, r.gain_ffn)):
                grad[...] = r.small[index : index + 1, place * own : (place + 1) * own]
            r.table_grad[...] = r.small[8 : 8 + part, 128 * place : 128 * place + dims.heads]
    for copy in stores + copies:
        copy.wait()


def run_place(dims, f, b):
    near, far = pltpu.VMEM, pl.ANY
    width, own = dims.width, dims.width // dims.places
    square, gain = ((own, width), F32, far), ((1, own), F32, near)
    rows = 4 * width
    inputs = dict(
        fin=(b.fin, far),
        small=(b.small, near),
        layer_in=(b.layer_out, far),
        dec_in=(b.dec_grad, far),
        enc_in=(b.enc_grad, far),
    )
    outputs = dict(
        layer=(b.layer_out.shape, LOW, far),
        dec=(b.dec_grad.shape, F32, far),
        enc=(b.enc_grad.shape, F32, far),
        ffn_out=((width, width), F32, far),
        ffn_in=((own, dims.fan * width), F32, far),
        cross_output=square,
        cross_query=square,
        cross_key=square,
        cross_value=square,
        self_output=square,
        self_query=square,
        self_key=square,
        self_value=square,
        gain_self=gain,
        gain_cross=gain,
        gain_ffn=gain,
        table_grad=((dims.buckets // dims.places, dims.heads), F32, near),
    )
    scratch = dict(
        low=pltpu.VMEM((rows, width), LOW),
        wide=pltpu.VMEM((rows, width), F32),
        layer_held=pltpu.VMEM(b.layer_out.shape, LOW),
        dec_held=pltpu.VMEM(b.dec_grad.shape, F32),
        enc_held=pltpu.VMEM(b.enc_grad.shape, F32),
        pass_sem=pltpu.SemaphoreType.DMA((2, 3)),
        load_sem=pltpu.SemaphoreType.DMA((4,)),
        store_sem=pltpu.SemaphoreType.DMA((rows // own,)),
    )
    names = (*inputs, *outputs, *scratch)
    results = pl.pallas_call(
        lambda *refs: place_kernel(names, dims, *refs),
        out_shape=tuple(jax.ShapeDtypeStruct(shape, kind) for shape, kind, _ in outputs.values()),
        in_specs=[pl.BlockSpec(memory_space=space) for _, space in inputs.values()],
        out_specs=tuple(pl.BlockSpec(memory_space=space) for _, _, space in outputs.values()),
        scratch_shapes=list(scratch.values()),
        compiler_params=pltpu.CompilerParams(vmem_limit_bytes=60 * 2**20),
        name="place",
    )(*(array for array, _ in inputs.values()))
    return SimpleNamespace(**dict(zip(outputs, results)))


def on_device(
    dec_states,
    enc_states,
    out_grad,
    dec_lengths,
    enc_lengths,
    self_query,
    self_key,
    self_value,
    self_output,
    cross_query,
    cross_key,
    cross_value,
    cross_output,
    ffn_in,
    ffn_out,
    gain_self,
    gain_cross,
    gain_ffn,
    position_bias,
):
    a = SimpleNamespace(
        dec_states=dec_states,
        enc_states=enc_states,
        out_grad=out_grad,
        dec_lengths=dec_lengths,
        enc_lengths=enc_lengths,
        self_query=self_query,
        self_key=self_key,
        self_value=self_value,
        self_output=self_output,
        cross_query=cross_query,
        cross_key=cross_key,
        cross_value=cross_value,
        cross_output=cross_output,
        ffn_in=ffn_in,
        ffn_out=ffn_out,
        gain_self=gain_self,
        gain_cross=gain_cross,
        gain_ffn=gain_ffn,
        position_bias=position_bias,
    )
    count, width = a.dec_states.shape[1:]
    buckets, heads = a.position_bias.shape
    planes, piece = lax.axis_size("dp") // 2, 16
    line = planes == 4
    chunk_rows = 128 if line else 2 * planes * piece
    chunks = 4 * width // chunk_rows
    dims = SimpleNamespace(
        count=count,
        width=width,
        places=lax.axis_size("seq"),
        heads=heads,
        head_dim=width // heads,
        pairs=heads // 2,
        fan=a.ffn_in.shape[1] // width,
        items=a.dec_lengths.shape[1],
        buckets=buckets,
        planes=planes,
        piece=piece,
        chunks=chunks,
        ring=4 if line else 1,
        line=line,
        chunk_rows=chunk_rows,
    )
    f = run_forward(dims, a)
    b = run_backward(dims, a, f)
    o = run_place(dims, f, b)
    return (
        o.layer[None],
        o.dec[None],
        o.enc[None],
        o.self_query,
        o.self_key,
        o.self_value,
        o.self_output,
        o.cross_query,
        o.cross_key,
        o.cross_value,
        o.cross_output,
        o.ffn_in,
        o.ffn_out,
        o.gain_self[0],
        o.gain_cross[0],
        o.gain_ffn[0],
        o.table_grad,
    )


def solution(mesh):
    split = P("dp", "seq", None)
    rows = P("seq", None)
    return jax.shard_map(
        on_device,
        mesh=mesh,
        in_specs=(split,) * 3 + (P("dp", None),) * 2 + (P(),) * 14,
        out_specs=(split,) * 3 + (rows,) * 10 + (P("seq"),) * 3 + (rows,),
        check_vma=False,
    )
```

```python
import functools
import math
from types import SimpleNamespace

import jax
import jax.numpy as jnp
from jax import lax
from jax.experimental import pallas as pl
from jax.experimental.pallas import tpu as pltpu
from jax.sharding import PartitionSpec as P

MESH = pl.DeviceIdType.MESH
EPS = 1e-06
NEG = -1000000000.0
NEAR = 128
F32 = jnp.float32
LOW = jnp.bfloat16


def dot(left, right):
    return jnp.dot(left, right, preferred_element_type=F32)


def dot_nt(left, right):
    return lax.dot_general(left, right, (((1,), (1,)), ((), ())), preferred_element_type=F32)


def add_low(left, right):
    return (left.astype(F32) + right.astype(F32)).astype(LOW)


def block(index, size):
    return pl.ds(pl.multiple_of(index * size, size), size)


def bucket_of(distance):
    farther = jnp.full(distance.shape, 16, jnp.int32)
    for level in range(1, 16):
        farther = farther + (distance >= math.ceil(16 * 8 ** (level / 16))).astype(jnp.int32)
    return jnp.where(distance < 16, distance, farther)


def bucket_terms(buckets):
    shape = (buckets, 2 * NEAR)
    lanes = lax.broadcasted_iota(jnp.int32, shape, 1)
    return (bucket_of(lanes) == lax.broadcasted_iota(jnp.int32, shape, 0)).astype(F32)


def scale_of(values):
    return lax.rsqrt(jnp.mean(values * values, axis=-1, keepdims=True) + EPS)


def norm_back(values, gain, grad):
    scale = scale_of(values)
    gain_grad = jnp.sum(grad * values * scale, axis=0, keepdims=True)
    inner = jnp.mean(values * gain * grad, axis=-1, keepdims=True)
    return scale * gain * grad - values * (scale * scale * scale) * inner, gain_grad


def head_blocks(pair):
    size = pair.shape[0] // 2
    zero = jnp.zeros((size, pair.shape[1]), pair.dtype)
    return jnp.concatenate(
        [
            jnp.concatenate([pair[:size], zero], axis=1),
            jnp.concatenate([zero, pair[size:]], axis=1),
        ],
        axis=0,
    )


def head_rows(both):
    size, count = both.shape[0] // 2, both.shape[1] // 2
    return jnp.concatenate([both[:size, :count], both[size:, count:]], axis=0)


def twice(values):
    return jnp.concatenate([values, values], axis=1)


def fold(values):
    return values.reshape(values.shape[0] // 8, 8, values.shape[1])


class Mesh2:
    def __init__(self):
        self.row = lax.axis_index("dp")
        self.place = lax.axis_index("seq")
        self.side, self.core = self.place // 2, lax.rem(self.place, 2)
        self.sibling = self.side * 2 + 1 - self.core
        self.across = (1 - self.side) * 2 + self.core
        self.diagonal = (1 - self.side) * 2 + 1 - self.core
        self.core_peer = (self.row, self.sibling)
        self.y_peer = (self.row, self.across)

    def greet(self, peers):
        barrier = pltpu.get_barrier_semaphore()
        for peer in peers:
            pl.semaphore_signal(barrier, inc=1, device_id=peer, device_id_type=MESH)
        pl.semaphore_wait(barrier, len(peers))


def send(src, dst, sems, slot, peer):
    return pltpu.make_async_remote_copy(
        src_ref=src,
        dst_ref=dst,
        send_sem=sems.at[(0, *slot)],
        recv_sem=sems.at[(1, *slot)],
        device_id=peer,
        device_id_type=MESH,
    )


def softmax_pair(pair, r, count, steps, keys, turned, terms, queries_t, masses, out_t, probs, place):
    lanes = block(pair, 2 * r.head_dim)
    queries = head_blocks(queries_t[lanes, :])
    near = place is not None
    if near:
        tiles = [
            pltpu.roll(
                jnp.broadcast_to(r.near_bias[pl.ds(pair * 2 + head, 1), :], (NEAR, 2 * NEAR)),
                0,
                1,
                stride=1,
                stride_axis=0,
            )
            for head in range(2)
        ]
        below = [tile[:, NEAR:] for tile in tiles]
        on = [tile[:, :NEAR] for tile in tiles]
        none = jnp.zeros((NEAR, NEAR), F32)
        before = jnp.concatenate([below[0], none, below[1], none], axis=1)
        first = jnp.concatenate([on[0], below[0], on[1], below[1]], axis=1)
        second = jnp.concatenate([none, on[0], none, on[1]], axis=1)

    top = jnp.full((8, 2 * count), -jnp.inf, F32)
    for index in range(steps):
        rows = block(index, count)
        raw = dot(keys[index, :, lanes], queries) + twice(terms[rows, :])
        r.scores[rows, :] = raw
        if not near:
            top = jnp.maximum(top, jnp.max(fold(raw), axis=0))
    if near:
        rows = block(place, count)
        r.scores[rows, :] = r.scores[rows, :] + jnp.concatenate([first, second], axis=0)

        @pl.when(place > 0)
        def _():
            last = block(place * (count // NEAR) - 1, NEAR)
            r.scores[last, :] = r.scores[last, :] + before

        for index in range(steps):
            top = jnp.maximum(top, jnp.max(fold(r.scores[block(index, count), :]), axis=0))
    top = jnp.max(top, axis=0, keepdims=True)
    mass = jnp.zeros((8, 2 * count), F32)
    context = jnp.zeros((2 * r.head_dim, 2 * count), F32)
    for index in range(steps):
        rows = block(index, count)
        weights = jnp.exp(r.scores[rows, :] - top)
        low = weights.astype(LOW)
        probs[rows, :] = low
        context = context + dot(turned[lanes, rows], low)
        mass = mass + jnp.sum(fold(weights), axis=0)
    inverse = 1.0 / jnp.sum(mass, axis=0, keepdims=True)
    masses[pair] = inverse
    out_t[lanes, :] = head_rows(context * inverse)


def forward_kernel(names, dims, *refs):
    r = SimpleNamespace(**dict(zip(names, refs)), head_dim=dims.head_dim)
    m = Mesh2()
    count, places, pairs, fan, width = dims.count, dims.places, dims.pairs, dims.fan, dims.width
    q_place = m.place

    def load(slot, src, dst):
        copy = pltpu.make_async_copy(src, dst, r.load_sem.at[slot])
        copy.start()
        return copy

    loads = SimpleNamespace(
        wk=load(0, r.wk_hbm, r.wk),
        wv=load(1, r.wv_hbm, r.wv),
        wq=load(2, r.wq_hbm, r.wq),
        wout=load(3, r.wout_hbm, r.wout),
        cwk=load(4, r.cwk_hbm, r.cwk),
        cwv=load(5, r.cwv_hbm, r.cwv),
        wo=load(6, r.wo_hbm, r.wo),
        cwq=load(7, r.cwq_hbm, r.cwq),
        cwo=load(8, r.cwo_hbm, r.cwo),
    )

    m.greet([m.core_peer, m.y_peer])
    x_y = send(r.x, r.xs.at[m.place], r.link_sem, (0,), m.y_peer)
    x_core = send(r.x, r.xs.at[m.place], r.link_sem, (1,), m.core_peer)
    x_on = send(r.xs.at[m.across], r.xs.at[m.across], r.link_sem, (2,), m.core_peer)
    e_y = send(r.e, r.es.at[m.place], r.link_sem, (3,), m.y_peer)
    e_core = send(r.e, r.es.at[m.place], r.link_sem, (4,), m.core_peer)
    e_on = send(r.es.at[m.across], r.es.at[m.across], r.link_sem, (5,), m.core_peer)
    x_y.start()
    x_core.start()
    e_core.start()
    r.xs[m.place] = r.x[...]
    r.es[m.place] = r.e[...]

    gain_self = r.gain_self[...].astype(F32).reshape(1, width)
    gain_cross = r.gain_cross[...].astype(F32).reshape(1, width)

    items = dims.items
    dec_starts, enc_starts = [0], [0]
    for index in range(items):
        dec_starts.append(dec_starts[-1] + r.dec_len[0, index])
        enc_starts.append(enc_starts[-1] + r.enc_len[0, index])
    query_at = q_place * count + lax.broadcasted_iota(jnp.int32, (1, count), 1)
    low_self = jnp.zeros((1, count), jnp.int32)
    low_cross = jnp.zeros((1, count), jnp.int32)
    high_cross = jnp.full((1, count), enc_starts[1], jnp.int32)
    for index in range(1, items):
        inside = query_at >= dec_starts[index]
        low_self = jnp.where(inside, dec_starts[index], low_self)
        low_cross = jnp.where(inside, enc_starts[index], low_cross)
        high_cross = jnp.where(inside, enc_starts[index + 1], high_cross)

    def masks(index, carry):
        rows = block(index, count)
        key_at = index * count + lax.broadcasted_iota(jnp.int32, (count, count), 0)
        r.self_terms[rows, :] = jnp.where((key_at >= low_self) & (key_at <= query_at), 0.0, NEG)
        r.cross_terms[rows, :] = jnp.where((key_at >= low_cross) & (key_at < high_cross), 0.0, NEG)
        return carry

    lax.fori_loop(0, places, masks, 0)

    buckets = r.table.shape[1]
    terms = bucket_terms(buckets)
    last = lax.broadcasted_iota(jnp.int32, terms.shape, 0) == buckets - 1
    terms = terms - last.astype(F32)
    r.near_bias[...] = dot(r.table[...], terms.astype(LOW))

    def self_block(place):
        rows = block(place, count)
        states = r.xs[place].astype(F32)
        normed = (states * scale_of(states) * gain_self).astype(LOW)
        r.a1[place] = normed
        r.keys[place] = dot(normed, r.wk[...]).astype(LOW)
        values = dot(normed, r.wv[...]).astype(LOW)
        r.values[place] = values
        r.values_t[:, rows] = jnp.transpose(values)

    def cross_block(place):
        rows = block(place, count)
        encoded = r.es[place]
        r.ckeys[place] = dot(encoded, r.cwk[...]).astype(LOW)
        values = dot(encoded, r.cwv[...]).astype(LOW)
        r.cvalues[place] = values
        r.cvalues_t[:, rows] = jnp.transpose(values)

    def nth_place(k):
        return lax.rem(m.side + k // 2, 2) * 2 + lax.rem(m.core + lax.rem(k, 2), 2)

    def cross_blocks(k, carry):
        @pl.when(k == 1)
        def _():
            e_core.wait()

        @pl.when(k == 3)
        def _():
            e_on.wait()

        cross_block(nth_place(k))
        return carry

    def inner_grad(index, carry):
        r.inner_grad[index] = dot_nt(r.go[...], r.wout[block(index, width), :]).astype(LOW)
        return carry

    def self_blocks(k, carry):
        @pl.when(k == 1)
        def _():
            x_core.wait()

        @pl.when(k == 2)
        def _():
            loads.wout.wait()
            lax.fori_loop(0, fan, inner_grad, 0)
            loads.cwk.wait()
            loads.cwv.wait()
            lax.fori_loop(0, 2, cross_blocks, 0)
            x_y.wait()
            x_on.start()
            e_y.start()

        @pl.when(k == 3)
        def _():
            x_on.wait()

        self_block(nth_place(k))

        @pl.when(k == 0)
        def _():
            loads.wq.wait()
            r.queries_t[...] = jnp.transpose(dot(r.a1[m.place], r.wq[...]).astype(LOW))

        return carry

    loads.wk.wait()
    loads.wv.wait()
    lax.fori_loop(0, 4, self_blocks, 0)

    def keep(src, dst, slot):
        copy = pltpu.make_async_copy(src, dst, r.keep_sem.at[slot])
        copy.start()
        return copy

    kept = [
        keep(r.keys, r.keys_out, 0),
        keep(r.values, r.values_out, 1),
        keep(r.a1, r.a1_out, 2),
        keep(r.inner_grad, r.inner_out, 6),
    ]

    def probs_copy(slot, out, pair):
        return pltpu.make_async_copy(r.probs.at[slot], out.at[pair], r.probs_sem.at[slot])

    def attend(earlier, keys, turned, terms, queries_t, masses, out_t, out, place):
        def one(pair, carry):
            slot = lax.rem(pair, 2)
            if earlier:
                probs_copy(slot, out, pair).wait()
            else:
                @pl.when(pair >= 2)
                def _():
                    probs_copy(slot, out, pair).wait()

                @pl.when(pair == pairs - 2)
                def _():
                    e_y.wait()
                    e_on.start()
            softmax_pair(
                pair, r, count, places, keys, turned, terms, queries_t, masses, out_t,
                r.probs.at[slot], place,
            )
            probs_copy(slot, out, pair).start()
            return carry

        lax.fori_loop(0, pairs, one, 0)

    attend(
        False, r.keys, r.values_t, r.self_terms, r.queries_t, r.self_masses, r.context_t,
        r.self_probs, q_place,
    )
    loads.wo.wait()
    context = jnp.transpose(r.context_t[...]).astype(LOW)
    first = r.x[...].astype(F32) + dot(context, r.wo[...])
    r.first[...] = first
    normed_cross = (first * scale_of(first) * gain_cross).astype(LOW)
    r.a2[...] = normed_cross
    loads.cwq.wait()
    r.cqueries_t[...] = jnp.transpose(dot(normed_cross, r.cwq[...]).astype(LOW))
    lax.fori_loop(2, 4, cross_blocks, 0)
    kept += [
        keep(r.ckeys, r.ckeys_out, 3),
        keep(r.cvalues, r.cvalues_out, 4),
        keep(r.es, r.es_out, 5),
    ]
    attend(
        True, r.ckeys, r.cvalues_t, r.cross_terms, r.cqueries_t, r.cross_masses, r.ccontext_t,
        r.cross_probs, None,
    )
    loads.cwo.wait()
    context = jnp.transpose(r.ccontext_t[...]).astype(LOW)
    r.second[...] = r.first[...] + dot(context, r.cwo[...])
    for slot in range(2):
        probs_copy(slot, r.cross_probs, pairs - 2 + slot).wait()
    for copy in kept:
        copy.wait()


def call(kernel, name, collective, limit, inputs, outputs, scratch, aliases=None):
    names = (*inputs, *outputs, *scratch)
    results = pl.pallas_call(
        functools.partial(kernel, names),
        out_shape=tuple(jax.ShapeDtypeStruct(shape, kind) for shape, kind, _ in outputs.values()),
        in_specs=[pl.BlockSpec(memory_space=space) for _, space in inputs.values()],
        out_specs=tuple(pl.BlockSpec(memory_space=space) for _, _, space in outputs.values()),
        scratch_shapes=list(scratch.values()),
        input_output_aliases=aliases or {},
        compiler_params=pltpu.CompilerParams(
            collective_id=collective, has_side_effects=True, vmem_limit_bytes=limit * 2**20
        ),
        name=name,
    )(*(array for array, _ in inputs.values()))
    return SimpleNamespace(**dict(zip(outputs, results)))


def run_forward(dims, a):
    count, total, width = dims.count, dims.count * dims.places, dims.width
    near, far, scalars = pltpu.VMEM, pl.ANY, pltpu.SMEM
    pairs, fan = dims.pairs, dims.fan
    square = (width, width)
    own = (count, width)
    inputs = dict(
        x=(a.dec_states[0], near),
        e=(a.enc_states[0], near),
        go=(a.out_grad[0], near),
        dec_len=(a.dec_lengths, scalars),
        enc_len=(a.enc_lengths, scalars),
        table=(a.position_bias.T, near),
        gain_self=(a.gain_self, near),
        gain_cross=(a.gain_cross, near),
        wk_hbm=(a.self_key, far),
        wv_hbm=(a.self_value, far),
        wq_hbm=(a.self_query, far),
        wout_hbm=(a.ffn_out, far),
        cwk_hbm=(a.cross_key, far),
        cwv_hbm=(a.cross_value, far),
        wo_hbm=(a.self_output, far),
        cwq_hbm=(a.cross_query, far),
        cwo_hbm=(a.cross_output, far),
    )
    outputs = dict(
        first=(own, F32, near),
        second=(own, F32, near),
        inner_out=((fan, *own), LOW, far),
        queries_t=((width, count), LOW, near),
        cqueries_t=((width, count), LOW, near),
        context_t=((width, count), F32, near),
        ccontext_t=((width, count), F32, near),
        self_masses=((pairs, 1, 2 * count), F32, near),
        cross_masses=((pairs, 1, 2 * count), F32, near),
        a2=(own, LOW, near),
        keys_out=((dims.places, *own), LOW, far),
        values_out=((dims.places, *own), LOW, far),
        a1_out=((dims.places, *own), LOW, far),
        ckeys_out=((dims.places, *own), LOW, far),
        cvalues_out=((dims.places, *own), LOW, far),
        es_out=((dims.places, *own), LOW, far),
        self_probs=((pairs, total, 2 * count), LOW, far),
        cross_probs=((pairs, total, 2 * count), LOW, far),
    )
    scratch = dict(
        xs=pltpu.VMEM((dims.places, *own), LOW),
        es=pltpu.VMEM((dims.places, *own), LOW),
        wk=pltpu.VMEM(square, LOW),
        wv=pltpu.VMEM(square, LOW),
        wq=pltpu.VMEM(square, LOW),
        wout=pltpu.VMEM((fan * width, width), LOW),
        cwk=pltpu.VMEM(square, LOW),
        cwv=pltpu.VMEM(square, LOW),
        wo=pltpu.VMEM(square, LOW),
        cwq=pltpu.VMEM(square, LOW),
        cwo=pltpu.VMEM(square, LOW),
        a1=pltpu.VMEM((dims.places, *own), LOW),
        keys=pltpu.VMEM((dims.places, *own), LOW),
        values=pltpu.VMEM((dims.places, *own), LOW),
        values_t=pltpu.VMEM((width, total), LOW),
        ckeys=pltpu.VMEM((dims.places, *own), LOW),
        cvalues=pltpu.VMEM((dims.places, *own), LOW),
        cvalues_t=pltpu.VMEM((width, total), LOW),
        self_terms=pltpu.VMEM((total, count), F32),
        cross_terms=pltpu.VMEM((total, count), F32),
        near_bias=pltpu.VMEM((dims.heads, 2 * NEAR), F32),
        scores=pltpu.VMEM((total, 2 * count), F32),
        probs=pltpu.VMEM((2, total, 2 * count), LOW),
        inner_grad=pltpu.VMEM((fan, *own), LOW),
        load_sem=pltpu.SemaphoreType.DMA((10,)),
        link_sem=pltpu.SemaphoreType.DMA((2, 6)),
        keep_sem=pltpu.SemaphoreType.DMA((7,)),
        probs_sem=pltpu.SemaphoreType.DMA((2,)),
    )
    return call(
        lambda names, *refs: forward_kernel(names, dims, *refs),
        "forward", 0, 56, inputs, outputs, scratch,
    )


SWAPPED = (1, 4, 6, 8, 10, 13, 16, 19, 22)


class Reducer:
    LAGS = (0, 3, 5, 7, 10, 14)

    def __init__(self, r, m, dims):
        self.r, self.m = r, m
        self.planes = dims.planes
        self.line = dims.line
        self.piece = dims.piece
        self.chunk_rows = dims.chunk_rows
        self.half_rows = dims.chunk_rows // 2
        self.chunks = dims.chunks
        self.ring = dims.ring
        self.plane, self.half = m.row // 2, lax.rem(m.row, 2)
        self.x_peer = (self.plane * 2 + 1 - self.half, m.place)
        self.published = self.loaded = self.fed = self.moved = 0

    def z_peer(self, step):
        return (lax.rem(self.plane + step, self.planes) * 2 + self.half, self.m.place)

    def plane_peer(self, plane):
        return (plane * 2 + self.half, self.m.place)

    def peers(self):
        return [self.x_peer] + [self.z_peer(step) for step in range(1, self.planes)]

    def span(self, first, size):
        return pl.ds(pl.multiple_of(first, self.piece), size)

    def rows(self, index):
        return self.span(index * self.chunk_rows, self.chunk_rows)

    def by_planes(self, index):
        found = index == SWAPPED[0]
        for other in SWAPPED[1:]:
            found = found | (index == other)
        return found

    def route(self, index, first, other):
        if not self.line:
            first(index)
            return
        special = self.by_planes(index)

        @pl.when(jnp.logical_not(special))
        def _():
            first(index)

        @pl.when(special)
        def _():
            other(index)

    def half_of(self, index, half):
        return self.span(index * self.chunk_rows + half * self.half_rows, self.half_rows)

    def packed(self, index):
        return self.span(index * self.half_rows, self.half_rows)

    def fresh_rows(self, index):
        return self.span(lax.rem(index, self.ring) * self.chunk_rows, self.chunk_rows)

    def load(self, index):
        r = self.r
        return pltpu.make_async_copy(
            r.big.at[self.m.core, :, self.rows(index)],
            r.fresh.at[:, self.fresh_rows(index)],
            r.chunk_sem.at[index],
        )

    def core_copy(self, index):
        r, rows = self.r, self.rows(index)
        return send(
            r.big.at[1 - self.m.core, :, rows], r.sums.at[:, rows], r.core_sem, (index,),
            self.m.core_peer,
        )

    def y_copy(self, index):
        r, rows = self.r, self.rows(index)
        return send(
            r.sums.at[1 - self.m.side, rows], r.fin.at[rows], r.y_sem, (index,), self.m.y_peer
        )

    def x_copy(self, index):
        r = self.r
        return send(
            r.sums.at[self.m.side, self.half_of(index, 1 - self.half)],
            r.x_recv.at[self.packed(index)],
            r.x_sem, (index,), self.x_peer,
        )

    def in_copy(self, index, inner):
        r = self.r
        return send(
            r.sums.at[self.m.side, self.half_of(index, self.half)],
            r.z_recv.at[0, self.packed(index)],
            r.z_sem, (index, 0), self.plane_peer(inner),
        )

    def mid_copy(self, index):
        r = self.r
        return send(
            r.sums.at[self.m.side, self.half_of(index, self.half)],
            r.z_recv.at[1, self.packed(index)],
            r.z_sem, (index, 1), self.plane_peer(3 - self.plane),
        )

    def out_copy(self, index, outer):
        r, rows = self.r, self.half_of(index, self.half)
        return send(r.fin.at[rows], r.fin.at[rows], r.gz_sem, (index, 0), self.plane_peer(outer))

    def z_part(self, index, which):
        first = index * self.chunk_rows + self.half * self.half_rows + which * self.piece
        return self.span(first, self.piece)

    def z_copy(self, index, step):
        r = self.r
        target = lax.rem(self.plane + step, self.planes)
        return send(
            r.sums.at[self.m.side, self.z_part(index, target)],
            r.z_recv.at[step - 1, self.span(index * self.piece, self.piece)],
            r.z_sem, (index, step - 1), self.z_peer(step),
        )

    def gz_copy(self, index, step):
        r, rows = self.r, self.z_part(index, self.plane)
        return send(r.fin.at[rows], r.fin.at[rows], r.gz_sem, (index, step - 1), self.z_peer(step))

    def gx_copy(self, index):
        r, rows = self.r, self.half_of(index, self.half)
        return send(r.fin.at[rows], r.fin.at[rows], r.gx_sem, (index,), self.x_peer)

    def publish(self, rows):
        last = rows // self.chunk_rows

        def begin(index, carry):
            self.core_copy(index).start()
            return carry

        def fetch(index, carry):
            self.load(index).start()
            return carry

        lax.fori_loop(self.published, last, begin, 0)
        ahead = min(last, self.fed + self.ring)
        lax.fori_loop(self.loaded, ahead, fetch, 0)
        self.published, self.loaded = last, max(self.loaded, ahead)

    def publish_part(self, first, last):
        def begin(index, carry):
            self.core_copy(index).start()

            @pl.when(index < self.ring)
            def _():
                self.load(index).start()

            return carry

        lax.fori_loop(first, last, begin, 0)

    def parts_done(self, last, fed):
        self.published, self.fed = last, fed
        self.loaded = min(last, self.ring)

    def feed(self, index, prefetch=True):
        r = self.r
        self.load(index).wait()
        self.core_copy(index).wait()
        rows, fresh = self.rows(index), self.fresh_rows(index)
        for side in range(2):
            r.sums[side, rows, :] = add_low(r.sums[side, rows, :], r.fresh[side, fresh, :])
        self.route(
            index, lambda at: self.y_copy(at).start(), lambda at: self.swap_copy(at).start()
        )

        if not prefetch:
            return

        @pl.when(index + self.ring < self.published)
        def _():
            self.load(index + self.ring).start()

    def move(self, step):
        stages = (
            (self.after_y, self.after_swap),
            (self.after_x, self.swapped_y),
            (self.inward, self.swapped_x),
            (self.middle, self.swapped_pair),
            (self.outward, self.swapped_back),
            (self.finish, self.swapped_finish),
        )
        for lag, stage in reversed(tuple(zip(self.LAGS, stages))):
            index = step - lag

            @pl.when((index >= 0) & (index < self.chunks))
            def _():
                self.route(index, *stage)


    def parity(self):
        return lax.rem(self.plane, 2)

    def neighbour(self):
        return self.plane_peer(self.plane + 1 - 2 * self.parity())

    def quarter_of(self, index, half):
        size = self.half_rows // 2
        first = index * self.chunk_rows + self.parity() * self.half_rows + half * size
        return self.span(first, size)

    def packed_quarter(self, index, which):
        size = self.half_rows // 2
        return self.span(index * self.half_rows + which * size, size)

    def swap_copy(self, index):
        r = self.r
        return send(
            r.sums.at[:, self.half_of(index, 1 - self.parity())],
            r.z_recv.at[:, self.packed(index)],
            r.z_sem, (index, 0), self.neighbour(),
        )

    def swapped_y_copy(self, index):
        r, rows = self.r, self.half_of(index, self.parity())
        return send(
            r.sums.at[1 - self.m.side, rows], r.fin.at[rows], r.y_sem, (index,), self.m.y_peer
        )

    def swapped_x_copy(self, index):
        r = self.r
        return send(
            r.sums.at[self.m.side, self.quarter_of(index, 1 - self.half)],
            r.x_recv.at[self.packed_quarter(index, 0)],
            r.x_sem, (index,), self.x_peer,
        )

    def pair_copy(self, index):
        r = self.r
        return send(
            r.sums.at[self.m.side, self.quarter_of(index, self.half)],
            r.x_recv.at[self.packed_quarter(index, 1)],
            r.z_sem, (index, 1), self.z_peer(2),
        )

    def swapped_gx_copy(self, index):
        r, rows = self.r, self.quarter_of(index, self.half)
        return send(r.fin.at[rows], r.fin.at[rows], r.gx_sem, (index,), self.x_peer)

    def swapped_gz_copy(self, index):
        r, rows = self.r, self.half_of(index, self.parity())
        return send(r.fin.at[rows], r.fin.at[rows], r.gz_sem, (index, 0), self.neighbour())

    def after_swap(self, index):
        r = self.r
        self.swap_copy(index).wait()
        rows, packed = self.half_of(index, self.parity()), self.packed(index)
        for side in range(2):
            r.sums[side, rows, :] = add_low(r.sums[side, rows, :], r.z_recv[side, packed, :])
        self.swapped_y_copy(index).start()

    def swapped_y(self, index):
        r, m = self.r, self.m
        self.swapped_y_copy(index).wait()
        rows = self.half_of(index, self.parity())
        r.sums[m.side, rows, :] = add_low(r.sums[m.side, rows, :], r.fin[rows, :])
        self.swapped_x_copy(index).start()

    def swapped_x(self, index):
        r, m = self.r, self.m
        self.swapped_x_copy(index).wait()
        rows = self.quarter_of(index, self.half)
        arrived = r.x_recv[self.packed_quarter(index, 0), :]
        r.sums[m.side, rows, :] = add_low(r.sums[m.side, rows, :], arrived)
        self.pair_copy(index).start()

    def swapped_pair(self, index):
        r, m = self.r, self.m
        self.pair_copy(index).wait()
        rows = self.quarter_of(index, self.half)
        arrived = r.x_recv[self.packed_quarter(index, 1), :]
        r.fin[rows, :] = add_low(r.sums[m.side, rows, :], arrived)
        self.swapped_gx_copy(index).start()

    def swapped_back(self, index):
        self.swapped_gx_copy(index).wait()
        self.swapped_gz_copy(index).start()

    def swapped_finish(self, index):
        self.swapped_gz_copy(index).wait()

    def after_y(self, index):
        r, m = self.r, self.m
        self.y_copy(index).wait()
        rows = self.rows(index)
        r.sums[m.side, rows, :] = add_low(r.sums[m.side, rows, :], r.fin[rows, :])
        self.x_copy(index).start()

    def after_x(self, index):
        r, m = self.r, self.m
        self.x_copy(index).wait()
        rows = self.half_of(index, self.half)
        r.sums[m.side, rows, :] = add_low(r.sums[m.side, rows, :], r.x_recv[self.packed(index), :])
        if not self.line:
            for step in range(1, self.planes):
                self.z_copy(index, step).start()
            return
        for outer, inner in ((0, 1), (3, 2)):
            @pl.when(self.plane == outer)
            def _():
                self.in_copy(index, inner).start()

    def inward(self, index):
        r, m = self.r, self.m
        if not self.line:
            return
        for outer, inner in ((0, 1), (3, 2)):
            @pl.when(self.plane == outer)
            def _():
                self.in_copy(index, inner).wait_send()

        @pl.when((self.plane == 1) | (self.plane == 2))
        def _():
            self.in_copy(index, self.plane).wait_recv()
            rows = self.half_of(index, self.half)
            arrived = r.z_recv[0, self.packed(index), :]
            r.sums[m.side, rows, :] = add_low(r.sums[m.side, rows, :], arrived)
            self.mid_copy(index).start()

    def middle(self, index):
        r, m = self.r, self.m
        if not self.line:
            part = self.z_part(index, self.plane)
            total = r.sums[m.side, part, :].astype(F32)
            for step in range(1, self.planes):
                self.z_copy(index, step).wait()
                arrived = r.z_recv[step - 1, self.span(index * self.piece, self.piece), :]
                total = total + arrived.astype(F32)
            r.fin[part, :] = total.astype(LOW)
            for step in range(1, self.planes):
                self.gz_copy(index, step).start()
            return

        @pl.when((self.plane == 1) | (self.plane == 2))
        def _():
            self.mid_copy(index).wait()
            rows = self.half_of(index, self.half)
            arrived = r.z_recv[1, self.packed(index), :]
            r.fin[rows, :] = add_low(r.sums[m.side, rows, :], arrived)
            for outer, inner in ((0, 1), (3, 2)):
                @pl.when(self.plane == inner)
                def _():
                    self.out_copy(index, outer).start()
            self.gx_copy(index).start()

    def outward(self, index):
        if not self.line:
            for step in range(1, self.planes):
                self.gz_copy(index, step).wait()
            self.gx_copy(index).start()
            return
        for outer, inner in ((0, 1), (3, 2)):
            @pl.when(self.plane == inner)
            def _():
                self.out_copy(index, outer).wait_send()

            @pl.when(self.plane == outer)
            def _():
                self.out_copy(index, inner).wait_recv()
                self.gx_copy(index).start()

    def finish(self, index):
        self.gx_copy(index).wait()

    def run(self, feeds, moves):
        loops = max(1, feeds, moves)
        one, after = self.beside(loops, feeds, moves)

        def body(index, carry):
            one(index)
            return carry

        lax.fori_loop(0, loops, body, 0)
        after()

    def beside(self, loops, feeds, moves):
        feeds = max(0, min(feeds, self.published - self.fed))
        fed = self.fed + feeds
        limit = self.chunks + self.LAGS[-1] if fed == self.chunks else fed
        moves = max(0, min(moves, limit - self.moved))
        first_feed, first_move = self.fed, self.moved

        each = -(-feeds // loops)

        def one(index):
            if feeds > 0:
                def feed(step, carry):
                    self.feed(first_feed + step)
                    return carry

                lax.fori_loop(
                    jnp.minimum(index * each, feeds), jnp.minimum((index + 1) * each, feeds), feed, 0
                )
            if moves > 0:
                def move(step, carry):
                    self.move(first_move + step)
                    return carry

                lax.fori_loop(index * moves // loops, (index + 1) * moves // loops, move, 0)

        def after():
            self.fed, self.moved = fed, first_move + moves
            self.loaded = max(self.loaded, min(self.published, self.fed + self.ring))

        return one, after

    def finish_all(self, each, events):
        feeds, moves = self.chunks - self.fed, self.left()
        first_feed, first_move = self.fed, self.moved
        events = [(min(step, moves - 1), event) for step, event in events]

        def body(step, carry):
            for at, event in events:
                @pl.when(step == at)
                def _():
                    event()

            def feed(index, carry):
                self.feed(first_feed + index)
                return carry

            lax.fori_loop(
                jnp.minimum(step * each, feeds), jnp.minimum((step + 1) * each, feeds), feed, 0
            )
            self.move(first_move + step)
            return carry

        lax.fori_loop(0, moves, body, 0)

    def left(self):
        return self.chunks + self.LAGS[-1] - self.moved


def attend_back(pair, r, count, keys, keys_t, values, queries_t, masses, context_t, grad_t, probs, place, places):
    lanes = block(pair, 2 * r.head_dim)
    inverse = masses[pair]
    grads = grad_t[lanes, :].astype(F32)
    product = grads * context_t[lanes, :]
    sums = [
        jnp.sum(product[: r.head_dim], axis=0, keepdims=True),
        jnp.sum(product[r.head_dim :], axis=0, keepdims=True),
    ]
    inner = jnp.concatenate(sums, axis=1) * inverse
    grads = (head_blocks(grads) * inverse).astype(LOW)
    queries = head_blocks(queries_t[lanes, :])

    total = jnp.zeros((2 * r.head_dim, 2 * count), F32)
    beyond = jnp.zeros((8, 2 * count), F32)
    split = count - NEAR
    if place is not None:
        r.before[...] = jnp.zeros_like(r.before)
    for index in range(places):
        rows = block(index, count)
        weights = probs[rows, :]
        score_grad = weights.astype(F32) * (dot(values[index, :, lanes], grads) - inner)
        low = score_grad.astype(LOW)
        r.value_grad[index, :, lanes] = dot_nt(weights, grads).astype(LOW)
        r.key_grad[index, :, lanes] = dot_nt(low, queries).astype(LOW)
        total = total + dot(keys_t[lanes, rows], low)
        if place is not None:
            early = jnp.sum(fold(score_grad[:split]), axis=0)
            late = jnp.sum(fold(score_grad[split:]), axis=0)
            beyond = beyond + jnp.where(index < place, early, 0.0)
            beyond = beyond + jnp.where(index < place - 1, late, 0.0)

            @pl.when(index == place - 1)
            def _():
                r.before[...] = score_grad[split:]

            @pl.when(index == place)
            def _():
                r.own[...] = score_grad

    if place is not None:
        own, before = r.own[...], r.before[...]
        parts = []
        for head in range(2):
            at = head * count
            on = own[:NEAR, at : at + NEAR] + own[NEAR:, at + NEAR : at + 2 * NEAR]
            below = before[:, at : at + NEAR] + own[:NEAR, at + NEAR : at + 2 * NEAR]
            both = jnp.concatenate([on, below], axis=1)
            summed = both[:8]
            for group in range(1, NEAR // 8):
                summed = summed + pltpu.roll(
                    both[8 * group : 8 * group + 8], 2 * NEAR - 8 * group, 1
                )
            parts.append(summed)
        summed = jnp.concatenate(parts, axis=0)
        sublane = lax.broadcasted_iota(jnp.int32, summed.shape, 0)
        for bit in (1, 2, 4):
            summed = jnp.where(
                (sublane & bit) != 0, pltpu.roll(summed, 2 * NEAR - bit, 1), summed
            )
        lane = lax.broadcasted_iota(jnp.int32, (1, 2 * NEAR), 1)
        for head in range(2):
            at = head * count
            line = jnp.sum(summed[8 * head : 8 * head + 8], axis=0, keepdims=True)
            rest = jnp.sum(beyond[:, at : at + count]) + jnp.sum(before[:, at + NEAR : at + 2 * NEAR])
            line = line + jnp.where(lane == 2 * NEAR - 1, rest, 0.0)
            r.by_distance[pl.ds(pair * 2 + head, 1), :] = line
    r.query_grad_t[lanes, :] = head_rows(total).astype(LOW)


FFN_FEEDS = 3
PLAN = (
    (0, 0), (0, 0), (3, 1), (2, 1), (0, 2), (1, 0),
    (0, 3), (3, 2), (27, 6), (3, 0), (19, 1),
)
TAIL_FEEDS = 1
TAIL = (3, 6, 15, 19, 31)


def backward_kernel(names, dims, *refs):
    r = SimpleNamespace(**dict(zip(names, refs)), head_dim=dims.head_dim)
    m = Mesh2()
    count, places, pairs, fan, width = dims.count, dims.places, dims.pairs, dims.fan, dims.width
    own = width // places
    engine = Reducer(r, m, dims)
    plan = iter(PLAN)
    r.wo, r.wq, r.wk, r.wv = (r.squares.at[index] for index in range(4))
    r.keys, r.values, r.key_grad, r.value_grad = (r.tall.at[pl.ds(4 * k, 4)] for k in range(4))

    loads = SimpleNamespace()
    slots = iter(range(r.load_sem.shape[0]))

    def later(src, dst):
        return pltpu.make_async_copy(src, dst, r.load_sem.at[next(slots)])

    def load(src, dst):
        copy = later(src, dst)
        copy.start()
        return copy

    def probs_copy(src, pair):
        slot = lax.rem(pair, 2)
        return pltpu.make_async_copy(src.at[pair], r.probs.at[slot], r.probs_sem.at[slot])

    third = width // count
    loads.second = load(r.second_hbm, r.second)

    def ffn_copies(index):
        rows = pl.ds(index * third, third)
        win = r.win_hbm.at[:, block(index, width)]
        return (
            pltpu.make_async_copy(win, r.squares.at[index], r.win_sem.at[index]),
            pltpu.make_async_copy(r.wout_hbm.at[rows], r.tall.at[rows], r.wout_sem.at[index]),
        )

    for index in range(fan):
        win, wout = ffn_copies(index)
        win.start()
        if index == 0:
            loads.inner = load(r.inner_hbm, r.value_grad)
        wout.start()
    probs_copy(r.cross_probs, 0).start()
    probs_copy(r.cross_probs, 1).start()
    loads.es0 = load(r.es_hbm.at[m.core], r.group.at[0])
    loads.es1 = load(r.es_hbm.at[m.core + 2], r.group.at[1])
    loads.cqueries = load(r.cqueries_hbm, r.cqueries_t)
    loads.ccontext = load(r.ccontext_hbm, r.ccontext_t)
    loads.queries = load(r.queries_hbm, r.queries_t)
    loads.context = load(r.context_hbm, r.context_t)
    loads.a2 = load(r.a2_hbm, r.a2)

    m.greet([m.core_peer, m.y_peer] + engine.peers())

    gain_self = r.gain_self[...].astype(F32).reshape(1, width)
    gain_cross = r.gain_cross[...].astype(F32).reshape(1, width)
    staged = {}

    def unit_copy(unit):
        rows = pl.ds(2 * width + unit * own, own)
        return pltpu.make_async_copy(
            r.stage.at[unit % 2], r.big.at[:, :, rows], r.stage_sem.at[unit % 2]
        )

    def give(unit, left_t, right):
        if unit - 2 in staged:
            staged.pop(unit - 2).wait()

        for place in range(places):
            grad = dot(left_t[place * own : (place + 1) * own, :], right)
            r.stage[unit % 2, place % 2, place // 2] = grad.astype(LOW)
        staged[unit] = unit_copy(unit)
        staged[unit].start()

    def settle(rows):
        for unit in sorted(staged):
            staged.pop(unit).wait()
        engine.publish(rows)

    def turn(src, dst):
        def one(index, carry):
            rows = block(index, count)
            dst[:, rows] = jnp.transpose(src[index])
            return carry

        lax.fori_loop(0, places, one, 0)

    def attend(src, queries_t, masses, context_t, grad_t, place):
        beside, after = engine.beside(pairs, *next(plan))

        def one(pair, carry):
            probs_copy(src, pair).wait()
            attend_back(
                pair, r, count, r.keys, r.keys_t, r.values, queries_t, masses, context_t, grad_t,
                r.probs.at[lax.rem(pair, 2)], place, places,
            )

            @pl.when(pair + 2 < pairs)
            def _():
                probs_copy(src, pair + 2).start()

            beside(pair)
            return carry

        lax.fori_loop(0, pairs, one, 0)
        after()

    def exchange(slot):
        copies = []
        for side in range(2):
            theirs = side * 2 + 1 - m.core
            for part, (src, dst) in enumerate(
                ((r.key_grad, r.key_recv), (r.value_grad, r.value_recv))
            ):
                copies.append(
                    send(
                        src.at[theirs], dst.at[slot, side], r.swap_sem, (slot, side, part),
                        m.core_peer,
                    )
                )
                copies[-1].start()
        return copies

    def chip_sum(grad, arrived):
        parts = [add_low(grad[side * 2 + m.core], arrived[side]) for side in range(2)]
        return jnp.concatenate(parts, axis=0)

    def partial(slot, side):
        key_grad = add_low(r.key_grad[side * 2 + m.core], r.key_recv[slot, side])
        value_grad = add_low(r.value_grad[side * 2 + m.core], r.value_recv[slot, side])
        return dot_nt(key_grad, r.wk[...]) + dot_nt(value_grad, r.wv[...])

    gain_ffn = r.gain_ffn[...].astype(F32).reshape(1, width)
    loads.second.wait()
    second = r.second[...]
    normed_ffn = (second * scale_of(second) * gain_ffn).astype(LOW)
    r.grad_t[...] = jnp.transpose(normed_ffn)
    r.a3[...] = normed_ffn
    r.dec_grad[...] = jnp.zeros_like(second)
    r.enc_grad[...] = jnp.zeros_like(second)
    loads.cwo, loads.cwq = later(r.cwo_hbm, r.wo), later(r.cwq_hbm, r.wq)
    loads.cwk, loads.cwv = later(r.cwk_hbm, r.wk), later(r.cwv_hbm, r.wv)
    loads.ckeys, loads.cvalues = later(r.ckeys_hbm, r.keys), later(r.cvalues_hbm, r.values)
    freed = ((loads.cwo,), (loads.cwq, loads.ckeys), (loads.cwk, loads.cvalues), (loads.cwv,))
    loads.inner.wait()

    def head_copy(index):
        return pltpu.make_async_copy(
            r.keys_t.at[:, pl.ds(0, width)],
            r.big.at[lax.rem(index, 2), index // 2, pl.ds(width, width)],
            r.head_sem,
        )

    def feed_forward(index, carry):
        slot = lax.rem(index, 2)
        win, wout = ffn_copies(index)
        win.wait()
        pre = dot(r.a3[...], r.squares[index])
        half = 0.5 + 0.5 * lax.erf(pre * (0.5**0.5))
        inner = (pre * half).astype(LOW)
        slope = half + pre * jnp.exp(-0.5 * pre * pre) * ((2.0 * math.pi) ** -0.5)
        pre_grad = (slope * r.value_grad[index].astype(F32)).astype(LOW)

        def rows_of(place, carry):
            grad = dot(r.grad_t[block(place, own), :], pre_grad)
            r.stage[slot, lax.rem(place, 2), place // 2] = grad.astype(LOW)
            return carry

        lax.fori_loop(0, places, rows_of, 0)
        tail = pltpu.make_async_copy(
            r.stage.at[slot], r.big.at[:, :, block(index, own)], r.stage_sem.at[slot]
        )
        tail.start()
        wout.wait()
        rows = r.tall[pl.ds(index * third, third)].reshape(width, width)
        r.dec_grad[...] += dot(inner, rows)
        r.enc_grad[...] += dot_nt(pre_grad, r.squares[index])

        @pl.when(index > 0)
        def _():
            head_copy(index - 1).wait()

        r.keys_t[:, :width] = dot(jnp.transpose(inner), r.go[...]).astype(LOW)
        head_copy(index).start()
        for step, copies in enumerate(freed):
            @pl.when(index == step)
            def _():
                for copy in copies:
                    copy.start()
        tail.wait()
        chunk_rows = engine.chunk_rows
        engine.publish_part(index * own // chunk_rows, (index + 1) * own // chunk_rows)

        def feed(step, carry):
            engine.feed(step, prefetch=False)
            return carry

        lax.fori_loop(index * ffn_feeds // fan, (index + 1) * ffn_feeds // fan, feed, 0)
        return carry

    ffn_feeds = min(FFN_FEEDS, fan * own // engine.chunk_rows)
    lax.fori_loop(0, fan, feed_forward, 0)
    engine.parts_done(fan * own // engine.chunk_rows, ffn_feeds)
    r.layer_out[...] = (second + r.dec_grad[...]).astype(LOW)
    second_part, gain_ffn_grad = norm_back(second, gain_ffn, r.enc_grad[...])
    loads.first = load(r.first_hbm, r.enc_grad)
    r.dec_grad[...] = r.go[...].astype(F32) + second_part
    r.tiny[0] = jnp.zeros(r.tiny.shape[1:], F32)
    r.tiny[0, 2:3] = gain_ffn_grad
    head_copy(fan - 1).wait()
    engine.publish(2 * width)
    engine.run(*next(plan))

    head_grad = r.dec_grad[...].astype(LOW)
    loads.cwo.wait()
    r.grad_t[...] = dot_nt(r.wo[...], head_grad).astype(LOW)
    loads.wo = load(r.wo_hbm, r.wo)
    engine.run(*next(plan))
    loads.ccontext.wait()
    r.query_grad_t[...] = r.ccontext_t[...].astype(LOW)
    give(0, r.query_grad_t, head_grad)
    loads.ckeys.wait()
    turn(r.keys, r.keys_t)
    loads.cvalues.wait()
    loads.cqueries.wait()
    attend(r.cross_probs, r.cqueries_t, r.cross_masses, r.ccontext_t, r.grad_t, None)
    copies = exchange(0)
    loads.keys = load(r.keys_hbm, r.keys)
    loads.values = load(r.values_hbm, r.values)
    probs_copy(r.self_probs, 0).start()
    probs_copy(r.self_probs, 1).start()
    query_grad = jnp.transpose(r.query_grad_t[...])
    engine.run(*next(plan))
    loads.cwq.wait()
    normed_grad = dot_nt(query_grad, r.wq[...])
    loads.wq = load(r.wq_hbm, r.wq)
    loads.first.wait()
    first_part, gain_cross_grad = norm_back(r.enc_grad[...], gain_cross, normed_grad)
    r.dec_grad[...] += first_part
    r.tiny[0, 1:2] = gain_cross_grad
    loads.a2.wait()
    r.query_grad_t[...] = jnp.transpose(r.a2[...])
    give(1, r.query_grad_t, query_grad)
    engine.run(*next(plan))
    loads.es0.wait()
    loads.es1.wait()
    for side in range(2):
        r.group_t[:, side * count : (side + 1) * count] = jnp.transpose(r.group[side])
    loads.a10 = load(r.a1_hbm.at[m.core], r.group.at[0])
    loads.a11 = load(r.a1_hbm.at[m.core + 2], r.group.at[1])
    for copy in copies:
        copy.wait()
    key_grad = chip_sum(r.key_grad, r.key_recv.at[0])
    value_grad = chip_sum(r.value_grad, r.value_recv.at[0])
    loads.cwk.wait()
    loads.cwv.wait()
    r.partial_low[...] = partial(0, 1 - m.side).astype(LOW)
    enc_copy = send(r.partial_low, r.partial_recv.at[0], r.link_sem, (0,), m.y_peer)
    enc_copy.start()
    r.enc_grad[...] = partial(0, m.side)
    loads.wk = load(r.wk_hbm, r.wk)
    loads.wv = load(r.wv_hbm, r.wv)
    engine.run(*next(plan))
    give(2, r.group_t, key_grad)
    give(3, r.group_t, value_grad)
    settle(3 * width)
    engine.run(*next(plan))

    first_grad = r.dec_grad[...]
    head_grad = first_grad.astype(LOW)
    loads.wo.wait()
    r.grad_t[...] = dot_nt(r.wo[...], head_grad).astype(LOW)
    loads.context.wait()
    engine.run(*next(plan))
    r.query_grad_t[...] = r.context_t[...].astype(LOW)
    give(4, r.query_grad_t, head_grad)
    loads.keys.wait()
    turn(r.keys, r.keys_t)
    loads.values.wait()
    loads.queries.wait()

    r.by_distance[...] = jnp.zeros_like(r.by_distance)
    attend(r.self_probs, r.queries_t, r.self_masses, r.context_t, r.grad_t, m.place)
    copies = exchange(1)
    query_grad = jnp.transpose(r.query_grad_t[...])
    engine.run(*next(plan))
    loads.wq.wait()
    normed_grad = dot_nt(query_grad, r.wq[...])
    loads.a10.wait()
    loads.a11.wait()
    for side in range(2):
        r.group_t[:, side * count : (side + 1) * count] = jnp.transpose(r.group[side])
    give(5, r.group_t.at[:, block(m.side, count)], query_grad)
    engine.run(*next(plan))
    for copy in copies:
        copy.wait()
    key_grad = chip_sum(r.key_grad, r.key_recv.at[1])
    value_grad = chip_sum(r.value_grad, r.value_recv.at[1])
    loads.wk.wait()
    loads.wv.wait()
    enc_copy.wait()
    r.enc_grad[...] += r.partial_recv[0].astype(F32)
    r.partial_low[...] = partial(1, 1 - m.side).astype(LOW)
    dec_copy = send(r.partial_low, r.partial_recv.at[1], r.link_sem, (1,), m.y_peer)
    dec_copy.start()
    normed_grad = normed_grad + partial(1, m.side)
    give(6, r.group_t, key_grad)
    give(7, r.group_t, value_grad)
    settle(4 * width)
    r.second[...] = normed_grad

    def hop(slot):
        peer = (m.core_peer, m.y_peer, engine.x_peer)[slot]
        return send(r.tiny.at[slot], r.tiny_recv.at[slot], r.tiny_sem, (slot,), peer)

    def spread(step):
        return send(
            r.tiny.at[3], r.tiny_recv.at[2 + step], r.tiny_sem, (2 + step,), engine.z_peer(step)
        )

    def arrive(slot):
        hop(slot).wait()
        r.tiny[slot + 1] = r.tiny[slot] + r.tiny_recv[slot]
        if slot < 2:
            hop(slot + 1).start()
            return
        for step in range(1, dims.planes):
            spread(step).start()

    def states():
        dec_copy.wait()
        normed_grad = r.second[...] + r.partial_recv[1].astype(F32)
        state_part, gain_self_grad = norm_back(r.x[...].astype(F32), gain_self, normed_grad)
        r.dec_grad[...] += state_part
        buckets = dims.buckets
        table = lax.dot_general(
            bucket_terms(buckets), r.by_distance[...], (((1,), (1,)), ((), ())),
            precision=lax.Precision.HIGHEST, preferred_element_type=F32,
        )
        r.tiny[0, 0:1] = gain_self_grad
        part = buckets // places
        for place in range(places):
            r.tiny[0, 8 : 8 + part, 128 * place : 128 * (place + 1)] = table[
                place * part : (place + 1) * part
            ]
        hop(0).start()

    def totals():
        total = r.tiny[3]
        for step in range(1, dims.planes):
            spread(step).wait()
            total = total + r.tiny_recv[2 + step]
        r.small[...] = total

    steps = (states, lambda: arrive(0), lambda: arrive(1), lambda: arrive(2), totals)
    engine.finish_all(TAIL_FEEDS, tuple(zip(TAIL, steps)))


def run_backward(dims, a, f):
    count, total, width = dims.count, dims.count * dims.places, dims.width
    near, far = pltpu.VMEM, pl.ANY
    pairs, planes, chunks, piece = dims.pairs, dims.planes, dims.chunks, dims.piece
    square = (width, width)
    own = (count, width)
    inputs = dict(
        x=(a.dec_states[0], near),
        go=(a.out_grad[0], near),
        gain_self=(a.gain_self, near),
        gain_cross=(a.gain_cross, near),
        gain_ffn=(a.gain_ffn, near),
        self_masses=(f.self_masses, near),
        cross_masses=(f.cross_masses, near),
        first_hbm=(f.first, far),
        second_hbm=(f.second, far),
        inner_hbm=(f.inner_out, far),
        win_hbm=(a.ffn_in, far),
        wout_hbm=(a.ffn_out.reshape(-1, *own), far),
        queries_hbm=(f.queries_t, far),
        cqueries_hbm=(f.cqueries_t, far),
        context_hbm=(f.context_t, far),
        ccontext_hbm=(f.ccontext_t, far),
        a2_hbm=(f.a2, far),
        keys_hbm=(f.keys_out, far),
        values_hbm=(f.values_out, far),
        a1_hbm=(f.a1_out, far),
        ckeys_hbm=(f.ckeys_out, far),
        cvalues_hbm=(f.cvalues_out, far),
        es_hbm=(f.es_out, far),
        self_probs=(f.self_probs, far),
        cross_probs=(f.cross_probs, far),
        wo_hbm=(a.self_output, far),
        wq_hbm=(a.self_query, far),
        wk_hbm=(a.self_key, far),
        wv_hbm=(a.self_value, far),
        cwo_hbm=(a.cross_output, far),
        cwq_hbm=(a.cross_query, far),
        cwk_hbm=(a.cross_key, far),
        cwv_hbm=(a.cross_value, far),
    )
    outputs = dict(
        big=((2, 2, 4 * width, width), LOW, far),
        layer_out=(own, LOW, near),
        fin=((4 * width, width), LOW, near),
        dec_grad=(own, F32, near),
        enc_grad=(own, F32, near),
        small=((16, width), F32, near),
    )
    dma = pltpu.SemaphoreType.DMA
    rows = 4 * width
    scratch = dict(
        squares=pltpu.VMEM((4, *square), LOW),
        tall=pltpu.VMEM((16, *own), LOW),
        second=pltpu.VMEM(own, F32),
        keys_t=pltpu.VMEM((width, total), LOW),
        probs=pltpu.VMEM((2, total, 2 * count), LOW),
        grad_t=pltpu.VMEM((width, count), LOW),
        a3=pltpu.VMEM(own, LOW),
        a2=pltpu.VMEM(own, LOW),
        queries_t=pltpu.VMEM((width, count), LOW),
        cqueries_t=pltpu.VMEM((width, count), LOW),
        context_t=pltpu.VMEM((width, count), F32),
        ccontext_t=pltpu.VMEM((width, count), F32),
        query_grad_t=pltpu.VMEM((width, count), LOW),
        key_recv=pltpu.VMEM((2, 2, *own), LOW),
        value_recv=pltpu.VMEM((2, 2, *own), LOW),
        partial_low=pltpu.VMEM(own, LOW),
        partial_recv=pltpu.VMEM((2, *own), LOW),
        group=pltpu.VMEM((2, *own), LOW),
        group_t=pltpu.VMEM((width, 2 * count), LOW),
        before=pltpu.VMEM((NEAR, 2 * count), F32),
        own=pltpu.VMEM((count, 2 * count), F32),
        by_distance=pltpu.VMEM((128, 2 * NEAR), F32),
        stage=pltpu.VMEM((2, 2, 2, width // dims.places, width), LOW),
        fresh=pltpu.VMEM((2, dims.ring * dims.chunk_rows, width), LOW),
        sums=pltpu.VMEM((2, rows, width), LOW),
        x_recv=pltpu.VMEM((rows // 2, width), LOW),
        z_recv=pltpu.VMEM(
            (2, rows // 2, width) if dims.line else (planes - 1, chunks * piece, width), LOW
        ),
        tiny=pltpu.VMEM((4, 16, width), F32),
        tiny_recv=pltpu.VMEM((2 + planes, 16, width), F32),
        load_sem=dma((40,)),
        win_sem=dma((4,)),
        wout_sem=dma((4,)),
        head_sem=dma,
        probs_sem=dma((2,)),
        stage_sem=dma((2,)),
        link_sem=dma((2, 2)),
        swap_sem=dma((2, 2, 2, 2)),
        chunk_sem=dma((chunks,)),
        core_sem=dma((2, chunks)),
        y_sem=dma((2, chunks)),
        x_sem=dma((2, chunks)),
        z_sem=dma((2, chunks, planes - 1)),
        gz_sem=dma((2, chunks, planes - 1)),
        gx_sem=dma((2, chunks)),
        tiny_sem=dma((2, 2 + planes)),
    )
    return call(
        lambda names, *refs: backward_kernel(names, dims, *refs),
        "backward", 1, 63, inputs, outputs, scratch,
    )


def place_kernel(names, dims, *refs):
    r = SimpleNamespace(**dict(zip(names, refs)))
    width, fan = dims.width, dims.fan
    own = width // dims.places
    passed = (
        (r.layer_in, r.layer_held, r.layer),
        (r.dec_in, r.dec_held, r.dec),
        (r.enc_in, r.enc_held, r.enc),
    )
    inward = [
        pltpu.make_async_copy(src, held, r.pass_sem.at[0, slot])
        for slot, (src, held, _) in enumerate(passed)
    ]
    copies = [
        pltpu.make_async_copy(held, dst, r.pass_sem.at[1, slot])
        for slot, (_, held, dst) in enumerate(passed)
    ]
    groups = 4 * width // own
    loads, stores = [], []
    for index in range(4):
        rows = pl.ds(index * width, width)
        loads.append(pltpu.make_async_copy(r.fin.at[rows], r.low.at[rows], r.load_sem.at[index]))
        loads[-1].start()
    for copy in inward:
        copy.start()
    units = (
        r.cross_output, r.cross_query, r.cross_key, r.cross_value,
        r.self_output, r.self_query, r.self_key, r.self_value,
    )
    for index in range(groups):
        if index % (groups // 4) == 0:
            loads[index // (groups // 4)].wait()
        rows = pl.ds(index * own, own)
        r.wide[rows, :] = r.low[rows, :].astype(F32)
        if index < fan:
            dst = r.ffn_in.at[:, pl.ds(index * width, width)]
        elif index < 2 * fan:
            dst = r.ffn_out.at[pl.ds((index - fan) * own, own)]
        else:
            dst = units[index - 2 * fan]
        copy = pltpu.make_async_copy(r.wide.at[rows], dst, r.store_sem.at[index])
        copy.start()
        stores.append(copy)
    for arrival, copy in zip(inward, copies):
        arrival.wait()
        copy.start()
    at = lax.axis_index("seq")
    part = dims.buckets // dims.places
    for place in range(dims.places):
        @pl.when(at == place)
        def _():
            for index, grad in enumerate((r.gain_self, r.gain_cross, r.gain_ffn)):
                grad[...] = r.small[index : index + 1, place * own : (place + 1) * own]
            r.table_grad[...] = r.small[8 : 8 + part, 128 * place : 128 * place + dims.heads]
    for copy in stores + copies:
        copy.wait()


def run_place(dims, f, b):
    near, far = pltpu.VMEM, pl.ANY
    width, own = dims.width, dims.width // dims.places
    square, gain = ((own, width), F32, far), ((1, own), F32, near)
    rows = 4 * width
    inputs = dict(
        fin=(b.fin, far),
        small=(b.small, near),
        layer_in=(b.layer_out, far),
        dec_in=(b.dec_grad, far),
        enc_in=(b.enc_grad, far),
    )
    outputs = dict(
        layer=(b.layer_out.shape, LOW, far),
        dec=(b.dec_grad.shape, F32, far),
        enc=(b.enc_grad.shape, F32, far),
        ffn_out=((width, width), F32, far),
        ffn_in=((own, dims.fan * width), F32, far),
        cross_output=square,
        cross_query=square,
        cross_key=square,
        cross_value=square,
        self_output=square,
        self_query=square,
        self_key=square,
        self_value=square,
        gain_self=gain,
        gain_cross=gain,
        gain_ffn=gain,
        table_grad=((dims.buckets // dims.places, dims.heads), F32, near),
    )
    scratch = dict(
        low=pltpu.VMEM((rows, width), LOW),
        wide=pltpu.VMEM((rows, width), F32),
        layer_held=pltpu.VMEM(b.layer_out.shape, LOW),
        dec_held=pltpu.VMEM(b.dec_grad.shape, F32),
        enc_held=pltpu.VMEM(b.enc_grad.shape, F32),
        pass_sem=pltpu.SemaphoreType.DMA((2, 3)),
        load_sem=pltpu.SemaphoreType.DMA((4,)),
        store_sem=pltpu.SemaphoreType.DMA((rows // own,)),
    )
    names = (*inputs, *outputs, *scratch)
    results = pl.pallas_call(
        lambda *refs: place_kernel(names, dims, *refs),
        out_shape=tuple(jax.ShapeDtypeStruct(shape, kind) for shape, kind, _ in outputs.values()),
        in_specs=[pl.BlockSpec(memory_space=space) for _, space in inputs.values()],
        out_specs=tuple(pl.BlockSpec(memory_space=space) for _, _, space in outputs.values()),
        scratch_shapes=list(scratch.values()),
        compiler_params=pltpu.CompilerParams(vmem_limit_bytes=60 * 2**20),
        name="place",
    )(*(array for array, _ in inputs.values()))
    return SimpleNamespace(**dict(zip(outputs, results)))


def on_device(
    dec_states,
    enc_states,
    out_grad,
    dec_lengths,
    enc_lengths,
    self_query,
    self_key,
    self_value,
    self_output,
    cross_query,
    cross_key,
    cross_value,
    cross_output,
    ffn_in,
    ffn_out,
    gain_self,
    gain_cross,
    gain_ffn,
    position_bias,
):
    a = SimpleNamespace(
        dec_states=dec_states,
        enc_states=enc_states,
        out_grad=out_grad,
        dec_lengths=dec_lengths,
        enc_lengths=enc_lengths,
        self_query=self_query,
        self_key=self_key,
        self_value=self_value,
        self_output=self_output,
        cross_query=cross_query,
        cross_key=cross_key,
        cross_value=cross_value,
        cross_output=cross_output,
        ffn_in=ffn_in,
        ffn_out=ffn_out,
        gain_self=gain_self,
        gain_cross=gain_cross,
        gain_ffn=gain_ffn,
        position_bias=position_bias,
    )
    count, width = a.dec_states.shape[1:]
    buckets, heads = a.position_bias.shape
    planes, piece = lax.axis_size("dp") // 2, 16
    line = planes == 4
    chunk_rows = 128 if line else 2 * planes * piece
    chunks = 4 * width // chunk_rows
    dims = SimpleNamespace(
        count=count,
        width=width,
        places=lax.axis_size("seq"),
        heads=heads,
        head_dim=width // heads,
        pairs=heads // 2,
        fan=a.ffn_in.shape[1] // width,
        items=a.dec_lengths.shape[1],
        buckets=buckets,
        planes=planes,
        piece=piece,
        chunks=chunks,
        ring=4 if line else 1,
        line=line,
        chunk_rows=chunk_rows,
    )
    f = run_forward(dims, a)
    b = run_backward(dims, a, f)
    o = run_place(dims, f, b)
    return (
        o.layer[None],
        o.dec[None],
        o.enc[None],
        o.self_query,
        o.self_key,
        o.self_value,
        o.self_output,
        o.cross_query,
        o.cross_key,
        o.cross_value,
        o.cross_output,
        o.ffn_in,
        o.ffn_out,
        o.gain_self[0],
        o.gain_cross[0],
        o.gain_ffn[0],
        o.table_grad,
    )


def solution(mesh):
    split = P("dp", "seq", None)
    rows = P("seq", None)
    return jax.shard_map(
        on_device,
        mesh=mesh,
        in_specs=(split,) * 3 + (P("dp", None),) * 2 + (P(),) * 14,
        out_specs=(split,) * 3 + (rows,) * 10 + (P("seq"),) * 3 + (rows,),
        check_vma=False,
    )
```

```python
import functools
import math
from types import SimpleNamespace

import jax
import jax.numpy as jnp
from jax import lax
from jax.experimental import pallas as pl
from jax.experimental.pallas import tpu as pltpu
from jax.sharding import PartitionSpec as P

MESH = pl.DeviceIdType.MESH
EPS = 1e-06
NEG = -1000000000.0
NEAR = 128
F32 = jnp.float32
LOW = jnp.bfloat16


def dot(left, right):
    return jnp.dot(left, right, preferred_element_type=F32)


def dot_nt(left, right):
    return lax.dot_general(left, right, (((1,), (1,)), ((), ())), preferred_element_type=F32)


def add_low(left, right):
    return (left.astype(F32) + right.astype(F32)).astype(LOW)


def block(index, size):
    return pl.ds(pl.multiple_of(index * size, size), size)


def bucket_of(distance):
    farther = jnp.full(distance.shape, 16, jnp.int32)
    for level in range(1, 16):
        farther = farther + (distance >= math.ceil(16 * 8 ** (level / 16))).astype(jnp.int32)
    return jnp.where(distance < 16, distance, farther)


def bucket_terms(buckets):
    shape = (buckets, 2 * NEAR)
    lanes = lax.broadcasted_iota(jnp.int32, shape, 1)
    return (bucket_of(lanes) == lax.broadcasted_iota(jnp.int32, shape, 0)).astype(F32)


def scale_of(values):
    return lax.rsqrt(jnp.mean(values * values, axis=-1, keepdims=True) + EPS)


def norm_back(values, gain, grad):
    scale = scale_of(values)
    gain_grad = jnp.sum(grad * values * scale, axis=0, keepdims=True)
    inner = jnp.mean(values * gain * grad, axis=-1, keepdims=True)
    return scale * gain * grad - values * (scale * scale * scale) * inner, gain_grad


def head_blocks(pair):
    size = pair.shape[0] // 2
    zero = jnp.zeros((size, pair.shape[1]), pair.dtype)
    return jnp.concatenate(
        [
            jnp.concatenate([pair[:size], zero], axis=1),
            jnp.concatenate([zero, pair[size:]], axis=1),
        ],
        axis=0,
    )


def head_rows(both):
    size, count = both.shape[0] // 2, both.shape[1] // 2
    return jnp.concatenate([both[:size, :count], both[size:, count:]], axis=0)


def twice(values):
    return jnp.concatenate([values, values], axis=1)


def fold(values):
    return values.reshape(values.shape[0] // 8, 8, values.shape[1])


class Mesh2:
    def __init__(self):
        self.row = lax.axis_index("dp")
        self.place = lax.axis_index("seq")
        self.side, self.core = self.place // 2, lax.rem(self.place, 2)
        self.sibling = self.side * 2 + 1 - self.core
        self.across = (1 - self.side) * 2 + self.core
        self.diagonal = (1 - self.side) * 2 + 1 - self.core
        self.core_peer = (self.row, self.sibling)
        self.y_peer = (self.row, self.across)

    def greet(self, peers):
        barrier = pltpu.get_barrier_semaphore()
        for peer in peers:
            pl.semaphore_signal(barrier, inc=1, device_id=peer, device_id_type=MESH)
        pl.semaphore_wait(barrier, len(peers))


def send(src, dst, sems, slot, peer):
    return pltpu.make_async_remote_copy(
        src_ref=src,
        dst_ref=dst,
        send_sem=sems.at[(0, *slot)],
        recv_sem=sems.at[(1, *slot)],
        device_id=peer,
        device_id_type=MESH,
    )


def softmax_pair(pair, r, count, steps, keys, turned, terms, queries_t, masses, out_t, probs, place):
    lanes = block(pair, 2 * r.head_dim)
    queries = head_blocks(queries_t[lanes, :])
    near = place is not None
    if near:
        tiles = [
            pltpu.roll(
                jnp.broadcast_to(r.near_bias[pl.ds(pair * 2 + head, 1), :], (NEAR, 2 * NEAR)),
                0,
                1,
                stride=1,
                stride_axis=0,
            )
            for head in range(2)
        ]
        below = [tile[:, NEAR:] for tile in tiles]
        on = [tile[:, :NEAR] for tile in tiles]
        none = jnp.zeros((NEAR, NEAR), F32)
        before = jnp.concatenate([below[0], none, below[1], none], axis=1)
        first = jnp.concatenate([on[0], below[0], on[1], below[1]], axis=1)
        second = jnp.concatenate([none, on[0], none, on[1]], axis=1)

    top = jnp.full((8, 2 * count), -jnp.inf, F32)
    for index in range(steps):
        rows = block(index, count)
        raw = dot(keys[index, :, lanes], queries) + twice(terms[rows, :])
        r.scores[rows, :] = raw
        if not near:
            top = jnp.maximum(top, jnp.max(fold(raw), axis=0))
    if near:
        rows = block(place, count)
        r.scores[rows, :] = r.scores[rows, :] + jnp.concatenate([first, second], axis=0)

        @pl.when(place > 0)
        def _():
            last = block(place * (count // NEAR) - 1, NEAR)
            r.scores[last, :] = r.scores[last, :] + before

        for index in range(steps):
            top = jnp.maximum(top, jnp.max(fold(r.scores[block(index, count), :]), axis=0))
    top = jnp.max(top, axis=0, keepdims=True)
    mass = jnp.zeros((8, 2 * count), F32)
    context = jnp.zeros((2 * r.head_dim, 2 * count), F32)
    for index in range(steps):
        rows = block(index, count)
        weights = jnp.exp(r.scores[rows, :] - top)
        low = weights.astype(LOW)
        probs[rows, :] = low
        context = context + dot(turned[lanes, rows], low)
        mass = mass + jnp.sum(fold(weights), axis=0)
    inverse = 1.0 / jnp.sum(mass, axis=0, keepdims=True)
    masses[pair] = inverse
    out_t[lanes, :] = head_rows(context * inverse)


def forward_kernel(names, dims, *refs):
    r = SimpleNamespace(**dict(zip(names, refs)), head_dim=dims.head_dim)
    m = Mesh2()
    count, places, pairs, fan, width = dims.count, dims.places, dims.pairs, dims.fan, dims.width
    q_place = m.place

    def load(slot, src, dst):
        copy = pltpu.make_async_copy(src, dst, r.load_sem.at[slot])
        copy.start()
        return copy

    loads = SimpleNamespace(
        x=load(9, r.x_hbm, r.xs.at[m.place]),
        e=load(10, r.e_hbm, r.es.at[m.place]),
        go=load(11, r.go_hbm, r.go),
        wk=load(0, r.wk_hbm, r.wk),
        wv=load(1, r.wv_hbm, r.wv),
        wq=load(2, r.wq_hbm, r.wq),
        wout=load(3, r.wout_hbm, r.wout),
        cwk=load(4, r.cwk_hbm, r.cwk),
        cwv=load(5, r.cwv_hbm, r.cwv),
        wo=load(6, r.wo_hbm, r.wo),
        cwq=load(7, r.cwq_hbm, r.cwq),
        cwo=load(8, r.cwo_hbm, r.cwo),
    )

    m.greet([m.core_peer, m.y_peer])
    x_y = send(r.x_hbm, r.xs.at[m.place], r.link_sem, (0,), m.y_peer)
    x_core = send(r.x_hbm, r.xs.at[m.place], r.link_sem, (1,), m.core_peer)
    x_on = send(r.xs.at[m.across], r.xs.at[m.across], r.link_sem, (2,), m.core_peer)
    e_y = send(r.e_hbm, r.es.at[m.place], r.link_sem, (3,), m.y_peer)
    e_core = send(r.e_hbm, r.es.at[m.place], r.link_sem, (4,), m.core_peer)
    e_on = send(r.es.at[m.across], r.es.at[m.across], r.link_sem, (5,), m.core_peer)
    x_y.start()
    x_core.start()
    e_core.start()

    gain_self = r.gain_self[...].astype(F32).reshape(1, width)
    gain_cross = r.gain_cross[...].astype(F32).reshape(1, width)

    items = dims.items
    dec_starts, enc_starts = [0], [0]
    for index in range(items):
        dec_starts.append(dec_starts[-1] + r.dec_len[0, index])
        enc_starts.append(enc_starts[-1] + r.enc_len[0, index])
    query_at = q_place * count + lax.broadcasted_iota(jnp.int32, (1, count), 1)
    low_self = jnp.zeros((1, count), jnp.int32)
    low_cross = jnp.zeros((1, count), jnp.int32)
    high_cross = jnp.full((1, count), enc_starts[1], jnp.int32)
    for index in range(1, items):
        inside = query_at >= dec_starts[index]
        low_self = jnp.where(inside, dec_starts[index], low_self)
        low_cross = jnp.where(inside, enc_starts[index], low_cross)
        high_cross = jnp.where(inside, enc_starts[index + 1], high_cross)

    def masks(index, carry):
        rows = block(index, count)
        key_at = index * count + lax.broadcasted_iota(jnp.int32, (count, count), 0)
        r.self_terms[rows, :] = jnp.where((key_at >= low_self) & (key_at <= query_at), 0.0, NEG)
        r.cross_terms[rows, :] = jnp.where((key_at >= low_cross) & (key_at < high_cross), 0.0, NEG)
        return carry

    lax.fori_loop(0, places, masks, 0)

    buckets = r.table.shape[1]
    terms = bucket_terms(buckets)
    last = lax.broadcasted_iota(jnp.int32, terms.shape, 0) == buckets - 1
    terms = terms - last.astype(F32)
    r.near_bias[...] = dot(r.table[...], terms.astype(LOW))

    def self_block(place):
        rows = block(place, count)
        states = r.xs[place].astype(F32)
        normed = (states * scale_of(states) * gain_self).astype(LOW)
        r.a1[place] = normed
        r.keys[place] = dot(normed, r.wk[...]).astype(LOW)
        values = dot(normed, r.wv[...]).astype(LOW)
        r.values[place] = values
        r.values_t[:, rows] = jnp.transpose(values)

    def cross_block(place):
        rows = block(place, count)
        encoded = r.es[place]
        r.ckeys[place] = dot(encoded, r.cwk[...]).astype(LOW)
        values = dot(encoded, r.cwv[...]).astype(LOW)
        r.cvalues[place] = values
        r.cvalues_t[:, rows] = jnp.transpose(values)

    def nth_place(k):
        return lax.rem(m.side + k // 2, 2) * 2 + lax.rem(m.core + lax.rem(k, 2), 2)

    def cross_blocks(k, carry):
        @pl.when(k == 1)
        def _():
            e_core.wait()

        @pl.when(k == 3)
        def _():
            e_on.wait()

        cross_block(nth_place(k))
        return carry

    def inner_grad(index, carry):
        r.inner_grad[index] = dot_nt(r.go[...], r.wout[block(index, width), :]).astype(LOW)
        return carry

    def self_blocks(k, carry):
        @pl.when(k == 1)
        def _():
            x_core.wait()

        @pl.when(k == 2)
        def _():
            loads.wout.wait()
            loads.go.wait()
            loads.e.wait()
            lax.fori_loop(0, fan, inner_grad, 0)
            loads.cwk.wait()
            loads.cwv.wait()
            lax.fori_loop(0, 2, cross_blocks, 0)
            x_y.wait()
            x_on.start()
            e_y.start()

        @pl.when(k == 3)
        def _():
            x_on.wait()

        self_block(nth_place(k))

        @pl.when(k == 0)
        def _():
            loads.wq.wait()
            r.queries_t[...] = jnp.transpose(dot(r.a1[m.place], r.wq[...]).astype(LOW))

        return carry

    loads.x.wait()
    loads.wk.wait()
    loads.wv.wait()
    lax.fori_loop(0, 4, self_blocks, 0)

    def keep(src, dst, slot):
        copy = pltpu.make_async_copy(src, dst, r.keep_sem.at[slot])
        copy.start()
        return copy

    kept = [
        keep(r.keys, r.keys_out, 0),
        keep(r.values, r.values_out, 1),
        keep(r.a1, r.a1_out, 2),
        keep(r.inner_grad, r.inner_out, 6),
        keep(r.queries_t, r.queries_t_out, 7),
        keep(r.xs.at[m.across], r.across_out, 14),
    ]

    def probs_copy(slot, out, pair):
        return pltpu.make_async_copy(r.probs.at[slot], out.at[pair], r.probs_sem.at[slot])

    def attend(earlier, keys, turned, terms, queries_t, masses, out_t, out, place):
        def one(pair, carry):
            slot = lax.rem(pair, 2)
            if earlier:
                probs_copy(slot, out, pair).wait()
            else:
                @pl.when(pair >= 2)
                def _():
                    probs_copy(slot, out, pair).wait()

                @pl.when(pair == pairs - 2)
                def _():
                    e_y.wait()
                    e_on.start()
            softmax_pair(
                pair, r, count, places, keys, turned, terms, queries_t, masses, out_t,
                r.probs.at[slot], place,
            )
            probs_copy(slot, out, pair).start()
            return carry

        lax.fori_loop(0, pairs, one, 0)

    attend(
        False, r.keys, r.values_t, r.self_terms, r.queries_t, r.self_masses, r.context_t,
        r.self_probs, q_place,
    )
    loads.wo.wait()
    context = jnp.transpose(r.context_t[...]).astype(LOW)
    first = r.xs[m.place].astype(F32) + dot(context, r.wo[...])
    r.first[...] = first
    normed_cross = (first * scale_of(first) * gain_cross).astype(LOW)
    r.a2[...] = normed_cross
    loads.cwq.wait()
    r.cqueries_t[...] = jnp.transpose(dot(normed_cross, r.cwq[...]).astype(LOW))
    lax.fori_loop(2, 4, cross_blocks, 0)
    kept += [
        keep(r.ckeys, r.ckeys_out, 3),
        keep(r.cvalues, r.cvalues_out, 4),
        keep(r.es, r.es_out, 5),
        keep(r.context_t, r.context_t_out, 8),
        keep(r.first, r.first_out, 9),
        keep(r.a2, r.a2_out, 10),
        keep(r.cqueries_t, r.cqueries_t_out, 11),
    ]
    attend(
        True, r.ckeys, r.cvalues_t, r.cross_terms, r.cqueries_t, r.cross_masses, r.ccontext_t,
        r.cross_probs, None,
    )
    loads.cwo.wait()
    context = jnp.transpose(r.ccontext_t[...]).astype(LOW)
    kept.append(keep(r.ccontext_t, r.ccontext_t_out, 12))
    r.second[...] = r.first[...] + dot(context, r.cwo[...])
    kept.append(keep(r.second, r.second_out, 13))
    for slot in range(2):
        probs_copy(slot, r.cross_probs, pairs - 2 + slot).wait()
    for copy in kept:
        copy.wait()


def call(kernel, name, collective, limit, inputs, outputs, scratch, aliases=None):
    names = (*inputs, *outputs, *scratch)
    results = pl.pallas_call(
        functools.partial(kernel, names),
        out_shape=tuple(jax.ShapeDtypeStruct(shape, kind) for shape, kind, _ in outputs.values()),
        in_specs=[pl.BlockSpec(memory_space=space) for _, space in inputs.values()],
        out_specs=tuple(pl.BlockSpec(memory_space=space) for _, _, space in outputs.values()),
        scratch_shapes=list(scratch.values()),
        input_output_aliases=aliases or {},
        compiler_params=pltpu.CompilerParams(
            collective_id=collective, has_side_effects=True, vmem_limit_bytes=limit * 2**20
        ),
        name=name,
    )(*(array for array, _ in inputs.values()))
    return SimpleNamespace(**dict(zip(outputs, results)))


def run_forward(dims, a):
    count, total, width = dims.count, dims.count * dims.places, dims.width
    near, far, scalars = pltpu.VMEM, pl.ANY, pltpu.SMEM
    pairs, fan = dims.pairs, dims.fan
    square = (width, width)
    own = (count, width)
    inputs = dict(
        x_hbm=(a.dec_states[0], far),
        e_hbm=(a.enc_states[0], far),
        go_hbm=(a.out_grad[0], far),
        dec_len=(a.dec_lengths, scalars),
        enc_len=(a.enc_lengths, scalars),
        table=(a.position_bias.T, near),
        gain_self=(a.gain_self, near),
        gain_cross=(a.gain_cross, near),
        wk_hbm=(a.self_key, far),
        wv_hbm=(a.self_value, far),
        wq_hbm=(a.self_query, far),
        wout_hbm=(a.ffn_out, far),
        cwk_hbm=(a.cross_key, far),
        cwv_hbm=(a.cross_value, far),
        wo_hbm=(a.self_output, far),
        cwq_hbm=(a.cross_query, far),
        cwo_hbm=(a.cross_output, far),
    )
    outputs = dict(
        first_out=(own, F32, far),
        second_out=(own, F32, far),
        inner_out=((fan, *own), LOW, far),
        across_out=(own, LOW, far),
        queries_t_out=((width, count), LOW, far),
        cqueries_t_out=((width, count), LOW, far),
        context_t_out=((width, count), F32, far),
        ccontext_t_out=((width, count), F32, far),
        self_masses=((pairs, 1, 2 * count), F32, near),
        cross_masses=((pairs, 1, 2 * count), F32, near),
        a2_out=(own, LOW, far),
        keys_out=((dims.places, *own), LOW, far),
        values_out=((dims.places, *own), LOW, far),
        a1_out=((dims.places, *own), LOW, far),
        ckeys_out=((dims.places, *own), LOW, far),
        cvalues_out=((dims.places, *own), LOW, far),
        es_out=((dims.places, *own), LOW, far),
        self_probs=((pairs, total, 2 * count), LOW, far),
        cross_probs=((pairs, total, 2 * count), LOW, far),
    )
    scratch = dict(
        xs=pltpu.VMEM((dims.places, *own), LOW),
        go=pltpu.VMEM(own, LOW),
        first=pltpu.VMEM(own, F32),
        second=pltpu.VMEM(own, F32),
        queries_t=pltpu.VMEM((width, count), LOW),
        cqueries_t=pltpu.VMEM((width, count), LOW),
        context_t=pltpu.VMEM((width, count), F32),
        ccontext_t=pltpu.VMEM((width, count), F32),
        a2=pltpu.VMEM(own, LOW),
        es=pltpu.VMEM((dims.places, *own), LOW),
        wk=pltpu.VMEM(square, LOW),
        wv=pltpu.VMEM(square, LOW),
        wq=pltpu.VMEM(square, LOW),
        wout=pltpu.VMEM((fan * width, width), LOW),
        cwk=pltpu.VMEM(square, LOW),
        cwv=pltpu.VMEM(square, LOW),
        wo=pltpu.VMEM(square, LOW),
        cwq=pltpu.VMEM(square, LOW),
        cwo=pltpu.VMEM(square, LOW),
        a1=pltpu.VMEM((dims.places, *own), LOW),
        keys=pltpu.VMEM((dims.places, *own), LOW),
        values=pltpu.VMEM((dims.places, *own), LOW),
        values_t=pltpu.VMEM((width, total), LOW),
        ckeys=pltpu.VMEM((dims.places, *own), LOW),
        cvalues=pltpu.VMEM((dims.places, *own), LOW),
        cvalues_t=pltpu.VMEM((width, total), LOW),
        self_terms=pltpu.VMEM((total, count), F32),
        cross_terms=pltpu.VMEM((total, count), F32),
        near_bias=pltpu.VMEM((dims.heads, 2 * NEAR), F32),
        scores=pltpu.VMEM((total, 2 * count), F32),
        probs=pltpu.VMEM((2, total, 2 * count), LOW),
        inner_grad=pltpu.VMEM((fan, *own), LOW),
        load_sem=pltpu.SemaphoreType.DMA((12,)),
        link_sem=pltpu.SemaphoreType.DMA((2, 6)),
        keep_sem=pltpu.SemaphoreType.DMA((15,)),
        probs_sem=pltpu.SemaphoreType.DMA((2,)),
    )
    return call(
        lambda names, *refs: forward_kernel(names, dims, *refs),
        "forward", 0, 56, inputs, outputs, scratch,
    )


SWAPPED = (1, 4, 7, 10, 12, 13, 16, 19)


class Reducer:
    LAGS = (0, 3, 6, 8, 11, 15)

    def __init__(self, r, m, dims):
        self.r, self.m = r, m
        self.planes = dims.planes
        self.line = dims.line
        self.piece = dims.piece
        self.chunk_rows = dims.chunk_rows
        self.half_rows = dims.chunk_rows // 2
        self.chunks = dims.chunks
        self.ring = dims.ring
        self.plane, self.half = m.row // 2, lax.rem(m.row, 2)
        self.x_peer = (self.plane * 2 + 1 - self.half, m.place)
        self.published = self.loaded = self.fed = self.moved = 0

    def z_peer(self, step):
        return (lax.rem(self.plane + step, self.planes) * 2 + self.half, self.m.place)

    def plane_peer(self, plane):
        return (plane * 2 + self.half, self.m.place)

    def peers(self):
        return [self.x_peer] + [self.z_peer(step) for step in range(1, self.planes)]

    def span(self, first, size):
        return pl.ds(pl.multiple_of(first, self.piece), size)

    def rows(self, index):
        return self.span(index * self.chunk_rows, self.chunk_rows)

    def by_planes(self, index):
        found = index == SWAPPED[0]
        for other in SWAPPED[1:]:
            found = found | (index == other)
        return found

    def by_halves(self, index):
        return lax.rem(index, 6) == 3

    def route(self, index, first, other, third=None):
        if not self.line:
            first(index)
            return
        special = self.by_planes(index)
        usual = jnp.logical_not(special)
        if third is not None:
            early = self.by_halves(index)
            usual = usual & jnp.logical_not(early)

            @pl.when(early)
            def _():
                third(index)

        @pl.when(usual)
        def _():
            first(index)

        @pl.when(special)
        def _():
            other(index)

    def half_of(self, index, half):
        return self.span(index * self.chunk_rows + half * self.half_rows, self.half_rows)

    def packed(self, index):
        return self.span(index * self.half_rows, self.half_rows)

    def fresh_rows(self, index):
        return self.span(lax.rem(index, self.ring) * self.chunk_rows, self.chunk_rows)

    def load(self, index):
        r = self.r
        return pltpu.make_async_copy(
            r.big.at[self.m.core, :, self.rows(index)],
            r.fresh.at[:, self.fresh_rows(index)],
            r.chunk_sem.at[index],
        )

    def core_copy(self, index):
        r, rows = self.r, self.rows(index)
        return send(
            r.big.at[1 - self.m.core, :, rows], r.sums.at[:, rows], r.core_sem, (index,),
            self.m.core_peer,
        )

    def y_copy(self, index):
        r, rows = self.r, self.rows(index)
        return send(
            r.sums.at[1 - self.m.side, rows], r.fin.at[rows], r.y_sem, (index,), self.m.y_peer
        )

    def x_copy(self, index):
        r = self.r
        return send(
            r.sums.at[self.m.side, self.half_of(index, 1 - self.half)],
            r.x_recv.at[self.packed(index)],
            r.x_sem, (index,), self.x_peer,
        )

    def in_copy(self, index, inner):
        r = self.r
        return send(
            r.sums.at[self.m.side, self.half_of(index, self.half)],
            r.z_recv.at[0, self.packed(index)],
            r.z_sem, (index, 0), self.plane_peer(inner),
        )

    def mid_copy(self, index):
        r = self.r
        return send(
            r.sums.at[self.m.side, self.half_of(index, self.half)],
            r.z_recv.at[1, self.packed(index)],
            r.z_sem, (index, 1), self.plane_peer(3 - self.plane),
        )

    def out_copy(self, index, outer):
        r, rows = self.r, self.half_of(index, self.half)
        return send(r.fin.at[rows], r.fin.at[rows], r.gz_sem, (index, 0), self.plane_peer(outer))

    def z_part(self, index, which):
        first = index * self.chunk_rows + self.half * self.half_rows + which * self.piece
        return self.span(first, self.piece)

    def z_copy(self, index, step):
        r = self.r
        target = lax.rem(self.plane + step, self.planes)
        return send(
            r.sums.at[self.m.side, self.z_part(index, target)],
            r.z_recv.at[step - 1, self.span(index * self.piece, self.piece)],
            r.z_sem, (index, step - 1), self.z_peer(step),
        )

    def gz_copy(self, index, step):
        r, rows = self.r, self.z_part(index, self.plane)
        return send(r.fin.at[rows], r.fin.at[rows], r.gz_sem, (index, step - 1), self.z_peer(step))

    def gx_copy(self, index):
        r, rows = self.r, self.half_of(index, self.half)
        return send(r.fin.at[rows], r.fin.at[rows], r.gx_sem, (index,), self.x_peer)

    def publish(self, rows):
        last = rows // self.chunk_rows

        def begin(index, carry):
            self.core_copy(index).start()
            return carry

        def fetch(index, carry):
            self.load(index).start()
            return carry

        lax.fori_loop(self.published, last, begin, 0)
        ahead = min(last, self.fed + self.ring)
        lax.fori_loop(self.loaded, ahead, fetch, 0)
        self.published, self.loaded = last, max(self.loaded, ahead)

    def publish_part(self, first, last):
        def begin(index, carry):
            self.core_copy(index).start()

            @pl.when(index < self.ring)
            def _():
                self.load(index).start()

            return carry

        lax.fori_loop(first, last, begin, 0)

    def parts_done(self, last, fed):
        self.published, self.fed = last, fed
        self.loaded = min(last, self.ring)

    def feed(self, index, prefetch=True):
        r = self.r
        self.load(index).wait()
        self.core_copy(index).wait()
        rows, fresh = self.rows(index), self.fresh_rows(index)
        for side in range(2):
            r.sums[side, rows, :] = add_low(r.sums[side, rows, :], r.fresh[side, fresh, :])
        self.route(
            index,
            lambda at: self.y_copy(at).start(),
            lambda at: self.swap_copy(at).start(),
            lambda at: self.early_copy(at).start(),
        )

        if not prefetch:
            return

        @pl.when(index + self.ring < self.published)
        def _():
            self.load(index + self.ring).start()

    def move(self, step):
        stages = (
            (self.after_y, self.after_swap, self.after_early),
            (self.after_x, self.swapped_y, self.early_y),
            (self.inward, self.swapped_x),
            (self.middle, self.swapped_pair),
            (self.outward, self.swapped_back),
            (self.finish, self.swapped_finish),
        )
        for lag, stage in reversed(tuple(zip(self.LAGS, stages))):
            index = step - lag

            @pl.when((index >= 0) & (index < self.chunks))
            def _():
                self.route(index, *stage)


    def early_rows(self, index):
        return self.span(index // 6 * self.half_rows, self.half_rows)

    def early_copy(self, index):
        r = self.r
        return send(
            r.sums.at[:, self.half_of(index, 1 - self.half)],
            r.early_recv.at[:, self.early_rows(index)],
            r.x_sem, (index,), self.x_peer,
        )

    def early_y_copy(self, index):
        r, rows = self.r, self.half_of(index, self.half)
        return send(
            r.sums.at[1 - self.m.side, rows], r.fin.at[rows], r.y_sem, (index,), self.m.y_peer
        )

    def after_early(self, index):
        r = self.r
        self.early_copy(index).wait()
        rows, packed = self.half_of(index, self.half), self.early_rows(index)
        for side in range(2):
            r.sums[side, rows, :] = add_low(r.sums[side, rows, :], r.early_recv[side, packed, :])
        self.early_y_copy(index).start()

    def early_y(self, index):
        r, m = self.r, self.m
        self.early_y_copy(index).wait()
        rows = self.half_of(index, self.half)
        r.sums[m.side, rows, :] = add_low(r.sums[m.side, rows, :], r.fin[rows, :])
        self.give_in(index)


    def parity(self):
        return lax.rem(self.plane, 2)

    def neighbour(self):
        return self.plane_peer(self.plane + 1 - 2 * self.parity())

    def quarter_of(self, index, half):
        size = self.half_rows // 2
        first = index * self.chunk_rows + self.parity() * self.half_rows + half * size
        return self.span(first, size)

    def packed_quarter(self, index, which):
        size = self.half_rows // 2
        return self.span(index * self.half_rows + which * size, size)

    def swap_copy(self, index):
        r = self.r
        return send(
            r.sums.at[:, self.half_of(index, 1 - self.parity())],
            r.z_recv.at[:, self.packed(index)],
            r.z_sem, (index, 0), self.neighbour(),
        )

    def swapped_y_copy(self, index):
        r, rows = self.r, self.half_of(index, self.parity())
        return send(
            r.sums.at[1 - self.m.side, rows], r.fin.at[rows], r.y_sem, (index,), self.m.y_peer
        )

    def swapped_x_copy(self, index):
        r = self.r
        return send(
            r.sums.at[self.m.side, self.quarter_of(index, 1 - self.half)],
            r.x_recv.at[self.packed_quarter(index, 0)],
            r.x_sem, (index,), self.x_peer,
        )

    def pair_copy(self, index):
        r = self.r
        return send(
            r.sums.at[self.m.side, self.quarter_of(index, self.half)],
            r.x_recv.at[self.packed_quarter(index, 1)],
            r.z_sem, (index, 1), self.z_peer(2),
        )

    def swapped_gx_copy(self, index):
        r, rows = self.r, self.quarter_of(index, self.half)
        return send(r.fin.at[rows], r.fin.at[rows], r.gx_sem, (index,), self.x_peer)

    def swapped_gz_copy(self, index):
        r, rows = self.r, self.half_of(index, self.parity())
        return send(r.fin.at[rows], r.fin.at[rows], r.gz_sem, (index, 0), self.neighbour())

    def after_swap(self, index):
        r = self.r
        self.swap_copy(index).wait()
        rows, packed = self.half_of(index, self.parity()), self.packed(index)
        for side in range(2):
            r.sums[side, rows, :] = add_low(r.sums[side, rows, :], r.z_recv[side, packed, :])
        self.swapped_y_copy(index).start()

    def swapped_y(self, index):
        r, m = self.r, self.m
        self.swapped_y_copy(index).wait()
        rows = self.half_of(index, self.parity())
        r.sums[m.side, rows, :] = add_low(r.sums[m.side, rows, :], r.fin[rows, :])
        self.swapped_x_copy(index).start()

    def swapped_x(self, index):
        r, m = self.r, self.m
        self.swapped_x_copy(index).wait()
        rows = self.quarter_of(index, self.half)
        arrived = r.x_recv[self.packed_quarter(index, 0), :]
        r.sums[m.side, rows, :] = add_low(r.sums[m.side, rows, :], arrived)
        self.pair_copy(index).start()

    def swapped_pair(self, index):
        r, m = self.r, self.m
        self.pair_copy(index).wait()
        rows = self.quarter_of(index, self.half)
        arrived = r.x_recv[self.packed_quarter(index, 1), :]
        r.fin[rows, :] = add_low(r.sums[m.side, rows, :], arrived)
        self.swapped_gx_copy(index).start()

    def swapped_back(self, index):
        self.swapped_gx_copy(index).wait()
        self.swapped_gz_copy(index).start()

    def swapped_finish(self, index):
        self.swapped_gz_copy(index).wait()

    def after_y(self, index):
        r, m = self.r, self.m
        self.y_copy(index).wait()
        rows = self.rows(index)
        r.sums[m.side, rows, :] = add_low(r.sums[m.side, rows, :], r.fin[rows, :])
        self.x_copy(index).start()

    def after_x(self, index):
        r, m = self.r, self.m
        self.x_copy(index).wait()
        rows = self.half_of(index, self.half)
        r.sums[m.side, rows, :] = add_low(r.sums[m.side, rows, :], r.x_recv[self.packed(index), :])
        if not self.line:
            for step in range(1, self.planes):
                self.z_copy(index, step).start()
            return
        self.give_in(index)

    def give_in(self, index):
        for outer, inner in ((0, 1), (3, 2)):
            @pl.when(self.plane == outer)
            def _():
                self.in_copy(index, inner).start()

    def inward(self, index):
        r, m = self.r, self.m
        if not self.line:
            return
        for outer, inner in ((0, 1), (3, 2)):
            @pl.when(self.plane == outer)
            def _():
                self.in_copy(index, inner).wait_send()

        @pl.when((self.plane == 1) | (self.plane == 2))
        def _():
            self.in_copy(index, self.plane).wait_recv()
            rows = self.half_of(index, self.half)
            arrived = r.z_recv[0, self.packed(index), :]
            r.sums[m.side, rows, :] = add_low(r.sums[m.side, rows, :], arrived)
            self.mid_copy(index).start()

    def middle(self, index):
        r, m = self.r, self.m
        if not self.line:
            part = self.z_part(index, self.plane)
            total = r.sums[m.side, part, :].astype(F32)
            for step in range(1, self.planes):
                self.z_copy(index, step).wait()
                arrived = r.z_recv[step - 1, self.span(index * self.piece, self.piece), :]
                total = total + arrived.astype(F32)
            r.fin[part, :] = total.astype(LOW)
            for step in range(1, self.planes):
                self.gz_copy(index, step).start()
            return

        @pl.when((self.plane == 1) | (self.plane == 2))
        def _():
            self.mid_copy(index).wait()
            rows = self.half_of(index, self.half)
            arrived = r.z_recv[1, self.packed(index), :]
            r.fin[rows, :] = add_low(r.sums[m.side, rows, :], arrived)
            for outer, inner in ((0, 1), (3, 2)):
                @pl.when(self.plane == inner)
                def _():
                    self.out_copy(index, outer).start()
            self.gx_copy(index).start()

    def outward(self, index):
        if not self.line:
            for step in range(1, self.planes):
                self.gz_copy(index, step).wait()
            self.gx_copy(index).start()
            return
        for outer, inner in ((0, 1), (3, 2)):
            @pl.when(self.plane == inner)
            def _():
                self.out_copy(index, outer).wait_send()

            @pl.when(self.plane == outer)
            def _():
                self.out_copy(index, inner).wait_recv()
                self.gx_copy(index).start()

    def finish(self, index):
        self.gx_copy(index).wait()

    def run(self, feeds, moves):
        loops = max(1, feeds, moves)
        one, after = self.beside(loops, feeds, moves)

        def body(index, carry):
            one(index)
            return carry

        lax.fori_loop(0, loops, body, 0)
        after()

    def beside(self, loops, feeds, moves):
        feeds = max(0, min(feeds, self.published - self.fed))
        fed = self.fed + feeds
        limit = self.chunks + self.LAGS[-1] if fed == self.chunks else fed
        moves = max(0, min(moves, limit - self.moved))
        first_feed, first_move = self.fed, self.moved

        each = -(-feeds // loops)

        def one(index):
            if feeds > 0:
                def feed(step, carry):
                    self.feed(first_feed + step)
                    return carry

                lax.fori_loop(
                    jnp.minimum(index * each, feeds), jnp.minimum((index + 1) * each, feeds), feed, 0
                )
            if moves > 0:
                def move(step, carry):
                    self.move(first_move + step)
                    return carry

                lax.fori_loop(index * moves // loops, (index + 1) * moves // loops, move, 0)

        def after():
            self.fed, self.moved = fed, first_move + moves
            self.loaded = max(self.loaded, min(self.published, self.fed + self.ring))

        return one, after

    def finish_all(self, each, events):
        feeds, moves = self.chunks - self.fed, self.left()
        first_feed, first_move = self.fed, self.moved
        events = [(min(step, moves - 1), event) for step, event in events]

        def body(step, carry):
            for at, event in events:
                @pl.when(step == at)
                def _():
                    event()

            def feed(index, carry):
                self.feed(first_feed + index)
                return carry

            lax.fori_loop(
                jnp.minimum(step * each, feeds), jnp.minimum((step + 1) * each, feeds), feed, 0
            )
            self.move(first_move + step)
            return carry

        lax.fori_loop(0, moves, body, 0)

    def left(self):
        return self.chunks + self.LAGS[-1] - self.moved


def attend_back(pair, r, count, keys, keys_t, values, queries_t, masses, context_t, grad_t, probs, place, places):
    lanes = block(pair, 2 * r.head_dim)
    inverse = masses[pair]
    grads = grad_t[lanes, :].astype(F32)
    product = grads * context_t[lanes, :]
    sums = [
        jnp.sum(product[: r.head_dim], axis=0, keepdims=True),
        jnp.sum(product[r.head_dim :], axis=0, keepdims=True),
    ]
    inner = jnp.concatenate(sums, axis=1) * inverse
    grads = (head_blocks(grads) * inverse).astype(LOW)
    queries = head_blocks(queries_t[lanes, :])

    total = jnp.zeros((2 * r.head_dim, 2 * count), F32)
    beyond = jnp.zeros((8, 2 * count), F32)
    split = count - NEAR
    if place is not None:
        r.before[...] = jnp.zeros_like(r.before)
    for index in range(places):
        rows = block(index, count)
        weights = probs[rows, :]
        score_grad = weights.astype(F32) * (dot(values[index, :, lanes], grads) - inner)
        low = score_grad.astype(LOW)
        r.value_grad[index, :, lanes] = dot_nt(weights, grads).astype(LOW)
        r.key_grad[index, :, lanes] = dot_nt(low, queries).astype(LOW)
        total = total + dot(keys_t[lanes, rows], low)
        if place is not None:
            early = jnp.sum(fold(score_grad[:split]), axis=0)
            late = jnp.sum(fold(score_grad[split:]), axis=0)
            beyond = beyond + jnp.where(index < place, early, 0.0)
            beyond = beyond + jnp.where(index < place - 1, late, 0.0)

            @pl.when(index == place - 1)
            def _():
                r.before[...] = score_grad[split:]

            @pl.when(index == place)
            def _():
                r.own[...] = score_grad

    if place is not None:
        own, before = r.own[...], r.before[...]
        parts = []
        for head in range(2):
            at = head * count
            on = own[:NEAR, at : at + NEAR] + own[NEAR:, at + NEAR : at + 2 * NEAR]
            below = before[:, at : at + NEAR] + own[:NEAR, at + NEAR : at + 2 * NEAR]
            both = jnp.concatenate([on, below], axis=1)
            summed = both[:8]
            for group in range(1, NEAR // 8):
                summed = summed + pltpu.roll(
                    both[8 * group : 8 * group + 8], 2 * NEAR - 8 * group, 1
                )
            parts.append(summed)
        summed = jnp.concatenate(parts, axis=0)
        sublane = lax.broadcasted_iota(jnp.int32, summed.shape, 0)
        for bit in (1, 2, 4):
            summed = jnp.where(
                (sublane & bit) != 0, pltpu.roll(summed, 2 * NEAR - bit, 1), summed
            )
        lane = lax.broadcasted_iota(jnp.int32, (1, 2 * NEAR), 1)
        for head in range(2):
            at = head * count
            line = jnp.sum(summed[8 * head : 8 * head + 8], axis=0, keepdims=True)
            rest = jnp.sum(beyond[:, at : at + count]) + jnp.sum(before[:, at + NEAR : at + 2 * NEAR])
            line = line + jnp.where(lane == 2 * NEAR - 1, rest, 0.0)
            r.by_distance[pl.ds(pair * 2 + head, 1), :] = line
    r.query_grad_t[lanes, :] = head_rows(total).astype(LOW)


FFN_FEEDS = 3
PLAN = (
    (0, 0), (4, 0), (0, 2), (10, 0), (4, 3), (7, 0),
    (0, 1), (2, 0), (21, 6), (19, 0), (32, 5),
)
TAIL_FEEDS = 2
TAIL = (2, 9, 13, 15, 24, 7, 38)


def backward_kernel(names, dims, *refs):
    r = SimpleNamespace(**dict(zip(names, refs)), head_dim=dims.head_dim)
    m = Mesh2()
    count, places, pairs, fan, width = dims.count, dims.places, dims.pairs, dims.fan, dims.width
    own = width // places
    engine = Reducer(r, m, dims)
    plan = iter(PLAN)
    r.wo, r.wq, r.wk, r.wv = (r.squares.at[index] for index in range(4))
    r.keys, r.values, r.key_grad, r.value_grad = (r.tall.at[pl.ds(4 * k, 4)] for k in range(4))

    loads = SimpleNamespace()
    slots = iter(range(r.load_sem.shape[0]))

    def later(src, dst):
        return pltpu.make_async_copy(src, dst, r.load_sem.at[next(slots)])

    def load(src, dst):
        copy = later(src, dst)
        copy.start()
        return copy

    def probs_copy(src, pair):
        slot = lax.rem(pair, 2)
        return pltpu.make_async_copy(src.at[pair], r.probs.at[slot], r.probs_sem.at[slot])

    third = width // count
    loads.second = load(r.second_hbm, r.second)
    loads.go = load(r.go_hbm, r.go)

    def ffn_copies(index):
        rows = pl.ds(index * third, third)
        win = r.win_hbm.at[:, block(index, width)]
        return (
            pltpu.make_async_copy(win, r.squares.at[index], r.win_sem.at[index]),
            pltpu.make_async_copy(r.wout_hbm.at[rows], r.tall.at[rows], r.wout_sem.at[index]),
        )

    for index in range(fan):
        win, wout = ffn_copies(index)
        win.start()
        if index == 0:
            loads.inner = load(r.inner_hbm, r.value_grad)
        wout.start()
    probs_copy(r.cross_probs, 0).start()
    probs_copy(r.cross_probs, 1).start()
    loads.es0 = load(r.es_hbm.at[m.core], r.group.at[0])
    loads.es1 = load(r.es_hbm.at[m.core + 2], r.group.at[1])
    loads.cqueries = load(r.cqueries_hbm, r.cqueries_t)
    loads.ccontext = load(r.ccontext_hbm, r.ccontext_t)
    loads.queries = load(r.queries_hbm, r.queries_t)
    loads.context = load(r.context_hbm, r.context_t)
    loads.a2 = load(r.a2_hbm, r.a2)
    loads.x = load(r.x_hbm, r.x)

    m.greet([m.core_peer, m.y_peer] + engine.peers())

    gain_self = r.gain_self[...].astype(F32).reshape(1, width)
    gain_cross = r.gain_cross[...].astype(F32).reshape(1, width)
    staged = {}

    def unit_copy(unit):
        rows = pl.ds(2 * width + unit * own, own)
        return pltpu.make_async_copy(
            r.stage.at[unit % 2], r.big.at[:, :, rows], r.stage_sem.at[unit % 2]
        )

    def give(unit, left_t, right):
        if unit - 2 in staged:
            staged.pop(unit - 2).wait()

        for place in range(places):
            grad = dot(left_t[place * own : (place + 1) * own, :], right)
            r.stage[unit % 2, place % 2, place // 2] = grad.astype(LOW)
        staged[unit] = unit_copy(unit)
        staged[unit].start()

    def settle(rows):
        for unit in sorted(staged):
            staged.pop(unit).wait()
        engine.publish(rows)

    def turn(src, dst):
        def one(index, carry):
            rows = block(index, count)
            dst[:, rows] = jnp.transpose(src[index])
            return carry

        lax.fori_loop(0, places, one, 0)

    def attend(src, queries_t, masses, context_t, grad_t, place):
        beside, after = engine.beside(pairs, *next(plan))

        def one(pair, carry):
            probs_copy(src, pair).wait()
            attend_back(
                pair, r, count, r.keys, r.keys_t, r.values, queries_t, masses, context_t, grad_t,
                r.probs.at[lax.rem(pair, 2)], place, places,
            )

            @pl.when(pair + 2 < pairs)
            def _():
                probs_copy(src, pair + 2).start()

            beside(pair)
            return carry

        lax.fori_loop(0, pairs, one, 0)
        after()

    def exchange(slot):
        copies = []
        for side in range(2):
            theirs = side * 2 + 1 - m.core
            for part, (src, dst) in enumerate(
                ((r.key_grad, r.key_recv), (r.value_grad, r.value_recv))
            ):
                copies.append(
                    send(
                        src.at[theirs], dst.at[slot, side], r.swap_sem, (slot, side, part),
                        m.core_peer,
                    )
                )
                copies[-1].start()
        return copies

    def chip_sum(grad, arrived):
        parts = [add_low(grad[side * 2 + m.core], arrived[side]) for side in range(2)]
        return jnp.concatenate(parts, axis=0)

    def partial(slot, side):
        key_grad = add_low(r.key_grad[side * 2 + m.core], r.key_recv[slot, side])
        value_grad = add_low(r.value_grad[side * 2 + m.core], r.value_recv[slot, side])
        return dot_nt(key_grad, r.wk[...]) + dot_nt(value_grad, r.wv[...])

    gain_ffn = r.gain_ffn[...].astype(F32).reshape(1, width)
    loads.second.wait()
    second = r.second[...]
    normed_ffn = (second * scale_of(second) * gain_ffn).astype(LOW)
    r.grad_t[...] = jnp.transpose(normed_ffn)
    r.a3[...] = normed_ffn
    r.dec_grad[...] = jnp.zeros_like(second)
    r.enc_grad[...] = jnp.zeros_like(second)
    loads.cwo, loads.cwq = later(r.cwo_hbm, r.wo), later(r.cwq_hbm, r.wq)
    loads.cwk, loads.cwv = later(r.cwk_hbm, r.wk), later(r.cwv_hbm, r.wv)
    loads.ckeys, loads.cvalues = later(r.ckeys_hbm, r.keys), later(r.cvalues_hbm, r.values)
    freed = ((loads.cwo,), (loads.cwq, loads.ckeys), (loads.cwk, loads.cvalues), (loads.cwv,))
    loads.inner.wait()
    loads.go.wait()

    def head_copy(index):
        return pltpu.make_async_copy(
            r.keys_t.at[:, pl.ds(0, width)],
            r.big.at[lax.rem(index, 2), index // 2, pl.ds(width, width)],
            r.head_sem,
        )

    def feed_forward(index, carry):
        slot = lax.rem(index, 2)
        win, wout = ffn_copies(index)
        win.wait()
        pre = dot(r.a3[...], r.squares[index])
        half = 0.5 + 0.5 * lax.erf(pre * (0.5**0.5))
        inner = (pre * half).astype(LOW)
        slope = half + pre * jnp.exp(-0.5 * pre * pre) * ((2.0 * math.pi) ** -0.5)
        pre_grad = (slope * r.value_grad[index].astype(F32)).astype(LOW)

        def rows_of(place, carry):
            grad = dot(r.grad_t[block(place, own), :], pre_grad)
            r.stage[slot, lax.rem(place, 2), place // 2] = grad.astype(LOW)
            return carry

        lax.fori_loop(0, places, rows_of, 0)
        tail = pltpu.make_async_copy(
            r.stage.at[slot], r.big.at[:, :, block(index, own)], r.stage_sem.at[slot]
        )
        tail.start()
        wout.wait()
        rows = r.tall[pl.ds(index * third, third)].reshape(width, width)
        r.dec_grad[...] += dot(inner, rows)
        r.enc_grad[...] += dot_nt(pre_grad, r.squares[index])

        @pl.when(index > 0)
        def _():
            head_copy(index - 1).wait()

        r.keys_t[:, :width] = dot(jnp.transpose(inner), r.go[...]).astype(LOW)
        head_copy(index).start()
        for step, copies in enumerate(freed):
            @pl.when(index == step)
            def _():
                for copy in copies:
                    copy.start()
        tail.wait()
        chunk_rows = engine.chunk_rows
        engine.publish_part(index * own // chunk_rows, (index + 1) * own // chunk_rows)

        def feed(step, carry):
            engine.feed(step, prefetch=False)
            return carry

        lax.fori_loop(index * ffn_feeds // fan, (index + 1) * ffn_feeds // fan, feed, 0)
        return carry

    ffn_feeds = min(FFN_FEEDS, fan * own // engine.chunk_rows)
    lax.fori_loop(0, fan, feed_forward, 0)
    engine.parts_done(fan * own // engine.chunk_rows, ffn_feeds)
    r.layer_out[...] = (second + r.dec_grad[...]).astype(LOW)
    second_part, gain_ffn_grad = norm_back(second, gain_ffn, r.enc_grad[...])
    loads.first = load(r.first_hbm, r.enc_grad)
    r.dec_grad[...] = r.go[...].astype(F32) + second_part
    r.tiny[0] = jnp.zeros(r.tiny.shape[1:], F32)
    r.tiny[0, 2:3] = gain_ffn_grad
    head_copy(fan - 1).wait()
    engine.publish(2 * width)
    engine.run(*next(plan))

    head_grad = r.dec_grad[...].astype(LOW)
    loads.cwo.wait()
    r.grad_t[...] = dot_nt(r.wo[...], head_grad).astype(LOW)
    loads.wo = load(r.wo_hbm, r.wo)
    engine.run(*next(plan))
    loads.ccontext.wait()
    r.query_grad_t[...] = r.ccontext_t[...].astype(LOW)
    give(0, r.query_grad_t, head_grad)
    loads.ckeys.wait()
    turn(r.keys, r.keys_t)
    loads.cvalues.wait()
    loads.cqueries.wait()
    attend(r.cross_probs, r.cqueries_t, r.cross_masses, r.ccontext_t, r.grad_t, None)
    copies = exchange(0)
    loads.keys = load(r.keys_hbm, r.keys)
    loads.values = load(r.values_hbm, r.values)
    probs_copy(r.self_probs, 0).start()
    probs_copy(r.self_probs, 1).start()
    query_grad = jnp.transpose(r.query_grad_t[...])
    engine.run(*next(plan))
    loads.cwq.wait()
    normed_grad = dot_nt(query_grad, r.wq[...])
    loads.wq = load(r.wq_hbm, r.wq)
    loads.first.wait()
    first_part, gain_cross_grad = norm_back(r.enc_grad[...], gain_cross, normed_grad)
    r.dec_grad[...] += first_part
    r.tiny[0, 1:2] = gain_cross_grad
    loads.a2.wait()
    r.query_grad_t[...] = jnp.transpose(r.a2[...])
    loads.across = load(r.across_hbm, r.a2)
    give(1, r.query_grad_t, query_grad)
    engine.run(*next(plan))
    loads.es0.wait()
    loads.es1.wait()
    for side in range(2):
        r.group_t[:, side * count : (side + 1) * count] = jnp.transpose(r.group[side])
    loads.a10 = load(r.a1_hbm.at[m.core], r.group.at[0])
    loads.a11 = load(r.a1_hbm.at[m.core + 2], r.group.at[1])
    for copy in copies:
        copy.wait()
    key_grad = chip_sum(r.key_grad, r.key_recv.at[0])
    value_grad = chip_sum(r.value_grad, r.value_recv.at[0])
    loads.cwk.wait()
    loads.cwv.wait()
    r.partial_low[...] = partial(0, 1 - m.side).astype(LOW)
    enc_copy = send(r.partial_low, r.partial_recv.at[0], r.link_sem, (0,), m.y_peer)
    enc_copy.start()
    r.enc_grad[...] = partial(0, m.side)
    loads.wk = load(r.wk_hbm, r.wk)
    loads.wv = load(r.wv_hbm, r.wv)
    engine.run(*next(plan))
    give(2, r.group_t, key_grad)
    give(3, r.group_t, value_grad)
    settle(3 * width)
    engine.run(*next(plan))

    first_grad = r.dec_grad[...]
    head_grad = first_grad.astype(LOW)
    loads.wo.wait()
    r.grad_t[...] = dot_nt(r.wo[...], head_grad).astype(LOW)
    loads.context.wait()
    engine.run(*next(plan))
    r.query_grad_t[...] = r.context_t[...].astype(LOW)
    give(4, r.query_grad_t, head_grad)
    loads.keys.wait()
    turn(r.keys, r.keys_t)
    loads.values.wait()
    loads.queries.wait()
    loads.x.wait()

    r.by_distance[...] = jnp.zeros_like(r.by_distance)
    attend(r.self_probs, r.queries_t, r.self_masses, r.context_t, r.grad_t, m.place)
    copies = exchange(1)
    query_grad = jnp.transpose(r.query_grad_t[...])
    engine.run(*next(plan))
    loads.wq.wait()
    normed_grad = dot_nt(query_grad, r.wq[...])
    loads.a10.wait()
    loads.a11.wait()
    for side in range(2):
        r.group_t[:, side * count : (side + 1) * count] = jnp.transpose(r.group[side])
    give(5, r.group_t.at[:, block(m.side, count)], query_grad)
    engine.run(*next(plan))
    for copy in copies:
        copy.wait()
    key_grad = chip_sum(r.key_grad, r.key_recv.at[1])
    value_grad = chip_sum(r.value_grad, r.value_recv.at[1])
    loads.wk.wait()
    loads.wv.wait()
    enc_copy.wait()
    r.enc_grad[...] += r.partial_recv[0].astype(F32)
    def gain_part(states, grad):
        return jnp.sum(grad * states * scale_of(states), axis=0, keepdims=True)

    loads.across.wait()
    theirs = partial(1, 1 - m.side)
    r.partial_low[...] = theirs.astype(LOW)
    dec_copy = send(r.partial_low, r.partial_recv.at[1], r.link_sem, (1,), m.y_peer)
    gain_self_grad = gain_part(r.a2[...].astype(F32), theirs)
    normed_grad = normed_grad + partial(1, m.side)
    gain_self_grad = gain_self_grad + gain_part(r.x[...].astype(F32), normed_grad)
    r.tiny[0, 0:1] = gain_self_grad
    give(6, r.group_t, key_grad)
    give(7, r.group_t, value_grad)
    settle(4 * width)
    r.second[...] = normed_grad

    def hop(slot):
        peer = (m.core_peer, m.y_peer, engine.x_peer)[slot]
        return send(r.tiny.at[slot], r.tiny_recv.at[slot], r.tiny_sem, (slot,), peer)

    def spread(step):
        return send(
            r.tiny.at[3], r.tiny_recv.at[2 + step], r.tiny_sem, (2 + step,), engine.z_peer(step)
        )

    def arrive(slot):
        hop(slot).wait()
        r.tiny[slot + 1] = r.tiny[slot] + r.tiny_recv[slot]
        if slot < 2:
            hop(slot + 1).start()
            return
        for step in range(1, dims.planes):
            spread(step).start()

    def states():
        dec_copy.wait()
        normed_grad = r.second[...] + r.partial_recv[1].astype(F32)
        state_part, _ = norm_back(r.x[...].astype(F32), gain_self, normed_grad)
        r.dec_grad[...] += state_part

    def smalls():
        buckets = dims.buckets
        table = lax.dot_general(
            bucket_terms(buckets), r.by_distance[...], (((1,), (1,)), ((), ())),
            precision=lax.Precision.HIGHEST, preferred_element_type=F32,
        )
        part = buckets // places
        for place in range(places):
            r.tiny[0, 8 : 8 + part, 128 * place : 128 * (place + 1)] = table[
                place * part : (place + 1) * part
            ]
        hop(0).start()

    def totals():
        total = r.tiny[3]
        for step in range(1, dims.planes):
            spread(step).wait()
            total = total + r.tiny_recv[2 + step]
        r.small[...] = total

    steps = (
        smalls, lambda: arrive(0), lambda: arrive(1), lambda: arrive(2), totals, dec_copy.start, states,
    )
    engine.finish_all(TAIL_FEEDS, tuple(zip(TAIL, steps)))


def run_backward(dims, a, f):
    count, total, width = dims.count, dims.count * dims.places, dims.width
    near, far = pltpu.VMEM, pl.ANY
    pairs, planes, chunks, piece = dims.pairs, dims.planes, dims.chunks, dims.piece
    square = (width, width)
    own = (count, width)
    inputs = dict(
        x_hbm=(a.dec_states[0], far),
        go_hbm=(a.out_grad[0], far),
        gain_self=(a.gain_self, near),
        gain_cross=(a.gain_cross, near),
        gain_ffn=(a.gain_ffn, near),
        self_masses=(f.self_masses, near),
        cross_masses=(f.cross_masses, near),
        first_hbm=(f.first_out, far),
        second_hbm=(f.second_out, far),
        inner_hbm=(f.inner_out, far),
        win_hbm=(a.ffn_in, far),
        wout_hbm=(a.ffn_out.reshape(-1, *own), far),
        queries_hbm=(f.queries_t_out, far),
        cqueries_hbm=(f.cqueries_t_out, far),
        context_hbm=(f.context_t_out, far),
        ccontext_hbm=(f.ccontext_t_out, far),
        a2_hbm=(f.a2_out, far),
        across_hbm=(f.across_out, far),
        keys_hbm=(f.keys_out, far),
        values_hbm=(f.values_out, far),
        a1_hbm=(f.a1_out, far),
        ckeys_hbm=(f.ckeys_out, far),
        cvalues_hbm=(f.cvalues_out, far),
        es_hbm=(f.es_out, far),
        self_probs=(f.self_probs, far),
        cross_probs=(f.cross_probs, far),
        wo_hbm=(a.self_output, far),
        wq_hbm=(a.self_query, far),
        wk_hbm=(a.self_key, far),
        wv_hbm=(a.self_value, far),
        cwo_hbm=(a.cross_output, far),
        cwq_hbm=(a.cross_query, far),
        cwk_hbm=(a.cross_key, far),
        cwv_hbm=(a.cross_value, far),
    )
    outputs = dict(
        big=((2, 2, 4 * width, width), LOW, far),
        layer_out=(own, LOW, near),
        fin=((4 * width, width), LOW, near),
        dec_grad=(own, F32, near),
        enc_grad=(own, F32, near),
        small=((16, width), F32, near),
    )
    dma = pltpu.SemaphoreType.DMA
    rows = 4 * width
    scratch = dict(
        squares=pltpu.VMEM((4, *square), LOW),
        tall=pltpu.VMEM((16, *own), LOW),
        second=pltpu.VMEM(own, F32),
        keys_t=pltpu.VMEM((width, total), LOW),
        probs=pltpu.VMEM((2, total, 2 * count), LOW),
        grad_t=pltpu.VMEM((width, count), LOW),
        a3=pltpu.VMEM(own, LOW),
        x=pltpu.VMEM(own, LOW),
        go=pltpu.VMEM(own, LOW),
        a2=pltpu.VMEM(own, LOW),
        queries_t=pltpu.VMEM((width, count), LOW),
        cqueries_t=pltpu.VMEM((width, count), LOW),
        context_t=pltpu.VMEM((width, count), F32),
        ccontext_t=pltpu.VMEM((width, count), F32),
        query_grad_t=pltpu.VMEM((width, count), LOW),
        key_recv=pltpu.VMEM((2, 2, *own), LOW),
        value_recv=pltpu.VMEM((2, 2, *own), LOW),
        partial_low=pltpu.VMEM(own, LOW),
        partial_recv=pltpu.VMEM((2, *own), LOW),
        group=pltpu.VMEM((2, *own), LOW),
        group_t=pltpu.VMEM((width, 2 * count), LOW),
        before=pltpu.VMEM((NEAR, 2 * count), F32),
        own=pltpu.VMEM((count, 2 * count), F32),
        by_distance=pltpu.VMEM((128, 2 * NEAR), F32),
        stage=pltpu.VMEM((2, 2, 2, width // dims.places, width), LOW),
        fresh=pltpu.VMEM((2, dims.ring * dims.chunk_rows, width), LOW),
        sums=pltpu.VMEM((2, rows, width), LOW),
        x_recv=pltpu.VMEM((rows // 2, width), LOW),
        early_recv=pltpu.VMEM(
            (2, -(-dims.chunks // 6) * dims.chunk_rows // 2 if dims.line else dims.piece, width), LOW
        ),
        z_recv=pltpu.VMEM(
            (2, rows // 2, width) if dims.line else (planes - 1, chunks * piece, width), LOW
        ),
        tiny=pltpu.VMEM((4, 16, width), F32),
        tiny_recv=pltpu.VMEM((2 + planes, 16, width), F32),
        load_sem=dma((40,)),
        win_sem=dma((4,)),
        wout_sem=dma((4,)),
        head_sem=dma,
        probs_sem=dma((2,)),
        stage_sem=dma((2,)),
        link_sem=dma((2, 2)),
        swap_sem=dma((2, 2, 2, 2)),
        chunk_sem=dma((chunks,)),
        core_sem=dma((2, chunks)),
        y_sem=dma((2, chunks)),
        x_sem=dma((2, chunks)),
        z_sem=dma((2, chunks, planes - 1)),
        gz_sem=dma((2, chunks, planes - 1)),
        gx_sem=dma((2, chunks)),
        tiny_sem=dma((2, 2 + planes)),
    )
    return call(
        lambda names, *refs: backward_kernel(names, dims, *refs),
        "backward", 1, 63, inputs, outputs, scratch,
    )


def place_kernel(names, dims, *refs):
    r = SimpleNamespace(**dict(zip(names, refs)))
    width, fan = dims.width, dims.fan
    own = width // dims.places
    passed = (
        (r.layer_in, r.layer_held, r.layer),
        (r.dec_in, r.dec_held, r.dec),
        (r.enc_in, r.enc_held, r.enc),
    )
    inward = [
        pltpu.make_async_copy(src, held, r.pass_sem.at[0, slot])
        for slot, (src, held, _) in enumerate(passed)
    ]
    copies = [
        pltpu.make_async_copy(held, dst, r.pass_sem.at[1, slot])
        for slot, (_, held, dst) in enumerate(passed)
    ]
    groups = 4 * width // own
    loads, stores = [], []
    for index in range(4):
        rows = pl.ds(index * width, width)
        loads.append(pltpu.make_async_copy(r.fin.at[rows], r.low.at[rows], r.load_sem.at[index]))
        loads[-1].start()
    for copy in inward:
        copy.start()
    units = (
        r.cross_output, r.cross_query, r.cross_key, r.cross_value,
        r.self_output, r.self_query, r.self_key, r.self_value,
    )
    for index in range(groups):
        if index % (groups // 4) == 0:
            loads[index // (groups // 4)].wait()
        rows = pl.ds(index * own, own)
        r.wide[rows, :] = r.low[rows, :].astype(F32)
        if index < fan:
            dst = r.ffn_in.at[:, pl.ds(index * width, width)]
        elif index < 2 * fan:
            dst = r.ffn_out.at[pl.ds((index - fan) * own, own)]
        else:
            dst = units[index - 2 * fan]
        copy = pltpu.make_async_copy(r.wide.at[rows], dst, r.store_sem.at[index])
        copy.start()
        stores.append(copy)
    for arrival, copy in zip(inward, copies):
        arrival.wait()
        copy.start()
    at = lax.axis_index("seq")
    part = dims.buckets // dims.places
    for place in range(dims.places):
        @pl.when(at == place)
        def _():
            for index, grad in enumerate((r.gain_self, r.gain_cross, r.gain_ffn)):
                grad[...] = r.small[index : index + 1, place * own : (place + 1) * own]
            r.table_grad[...] = r.small[8 : 8 + part, 128 * place : 128 * place + dims.heads]
    for copy in stores + copies:
        copy.wait()


def run_place(dims, f, b):
    near, far = pltpu.VMEM, pl.ANY
    width, own = dims.width, dims.width // dims.places
    square, gain = ((own, width), F32, far), ((1, own), F32, near)
    rows = 4 * width
    inputs = dict(
        fin=(b.fin, far),
        small=(b.small, near),
        layer_in=(b.layer_out, far),
        dec_in=(b.dec_grad, far),
        enc_in=(b.enc_grad, far),
    )
    outputs = dict(
        layer=(b.layer_out.shape, LOW, far),
        dec=(b.dec_grad.shape, F32, far),
        enc=(b.enc_grad.shape, F32, far),
        ffn_out=((width, width), F32, far),
        ffn_in=((own, dims.fan * width), F32, far),
        cross_output=square,
        cross_query=square,
        cross_key=square,
        cross_value=square,
        self_output=square,
        self_query=square,
        self_key=square,
        self_value=square,
        gain_self=gain,
        gain_cross=gain,
        gain_ffn=gain,
        table_grad=((dims.buckets // dims.places, dims.heads), F32, near),
    )
    scratch = dict(
        low=pltpu.VMEM((rows, width), LOW),
        wide=pltpu.VMEM((rows, width), F32),
        layer_held=pltpu.VMEM(b.layer_out.shape, LOW),
        dec_held=pltpu.VMEM(b.dec_grad.shape, F32),
        enc_held=pltpu.VMEM(b.enc_grad.shape, F32),
        pass_sem=pltpu.SemaphoreType.DMA((2, 3)),
        load_sem=pltpu.SemaphoreType.DMA((4,)),
        store_sem=pltpu.SemaphoreType.DMA((rows // own,)),
    )
    names = (*inputs, *outputs, *scratch)
    results = pl.pallas_call(
        lambda *refs: place_kernel(names, dims, *refs),
        out_shape=tuple(jax.ShapeDtypeStruct(shape, kind) for shape, kind, _ in outputs.values()),
        in_specs=[pl.BlockSpec(memory_space=space) for _, space in inputs.values()],
        out_specs=tuple(pl.BlockSpec(memory_space=space) for _, _, space in outputs.values()),
        scratch_shapes=list(scratch.values()),
        compiler_params=pltpu.CompilerParams(vmem_limit_bytes=60 * 2**20),
        name="place",
    )(*(array for array, _ in inputs.values()))
    return SimpleNamespace(**dict(zip(outputs, results)))


def on_device(
    dec_states,
    enc_states,
    out_grad,
    dec_lengths,
    enc_lengths,
    self_query,
    self_key,
    self_value,
    self_output,
    cross_query,
    cross_key,
    cross_value,
    cross_output,
    ffn_in,
    ffn_out,
    gain_self,
    gain_cross,
    gain_ffn,
    position_bias,
):
    a = SimpleNamespace(
        dec_states=dec_states,
        enc_states=enc_states,
        out_grad=out_grad,
        dec_lengths=dec_lengths,
        enc_lengths=enc_lengths,
        self_query=self_query,
        self_key=self_key,
        self_value=self_value,
        self_output=self_output,
        cross_query=cross_query,
        cross_key=cross_key,
        cross_value=cross_value,
        cross_output=cross_output,
        ffn_in=ffn_in,
        ffn_out=ffn_out,
        gain_self=gain_self,
        gain_cross=gain_cross,
        gain_ffn=gain_ffn,
        position_bias=position_bias,
    )
    count, width = a.dec_states.shape[1:]
    buckets, heads = a.position_bias.shape
    planes, piece = lax.axis_size("dp") // 2, 16
    line = planes == 4
    chunk_rows = 128 if line else 2 * planes * piece
    chunks = 4 * width // chunk_rows
    dims = SimpleNamespace(
        count=count,
        width=width,
        places=lax.axis_size("seq"),
        heads=heads,
        head_dim=width // heads,
        pairs=heads // 2,
        fan=a.ffn_in.shape[1] // width,
        items=a.dec_lengths.shape[1],
        buckets=buckets,
        planes=planes,
        piece=piece,
        chunks=chunks,
        ring=4 if line else 1,
        line=line,
        chunk_rows=chunk_rows,
    )
    f = run_forward(dims, a)
    b = run_backward(dims, a, f)
    o = run_place(dims, f, b)
    return (
        o.layer[None],
        o.dec[None],
        o.enc[None],
        o.self_query,
        o.self_key,
        o.self_value,
        o.self_output,
        o.cross_query,
        o.cross_key,
        o.cross_value,
        o.cross_output,
        o.ffn_in,
        o.ffn_out,
        o.gain_self[0],
        o.gain_cross[0],
        o.gain_ffn[0],
        o.table_grad,
    )


def solution(mesh):
    split = P("dp", "seq", None)
    rows = P("seq", None)
    return jax.shard_map(
        on_device,
        mesh=mesh,
        in_specs=(split,) * 3 + (P("dp", None),) * 2 + (P(),) * 14,
        out_specs=(split,) * 3 + (rows,) * 10 + (P("seq"),) * 3 + (rows,),
        check_vma=False,
    )
```

```python
import functools
import math
from types import SimpleNamespace

import jax
import jax.numpy as jnp
from jax import lax
from jax.experimental import pallas as pl
from jax.experimental.pallas import tpu as pltpu
from jax.sharding import PartitionSpec as P

MESH = pl.DeviceIdType.MESH
EPS = 1e-06
NEG = -1000000000.0
NEAR = 128
F32 = jnp.float32
LOW = jnp.bfloat16


def dot(left, right):
    return jnp.dot(left, right, preferred_element_type=F32)


def dot_nt(left, right):
    return lax.dot_general(left, right, (((1,), (1,)), ((), ())), preferred_element_type=F32)


def add_low(left, right):
    return (left.astype(F32) + right.astype(F32)).astype(LOW)


def block(index, size):
    return pl.ds(pl.multiple_of(index * size, size), size)


def bucket_of(distance):
    farther = jnp.full(distance.shape, 16, jnp.int32)
    for level in range(1, 16):
        farther = farther + (distance >= math.ceil(16 * 8 ** (level / 16))).astype(jnp.int32)
    return jnp.where(distance < 16, distance, farther)


def bucket_terms(buckets):
    shape = (buckets, 2 * NEAR)
    lanes = lax.broadcasted_iota(jnp.int32, shape, 1)
    return (bucket_of(lanes) == lax.broadcasted_iota(jnp.int32, shape, 0)).astype(F32)


def scale_of(values):
    return lax.rsqrt(jnp.mean(values * values, axis=-1, keepdims=True) + EPS)


def norm_back(values, gain, grad):
    scale = scale_of(values)
    gain_grad = jnp.sum(grad * values * scale, axis=0, keepdims=True)
    inner = jnp.mean(values * gain * grad, axis=-1, keepdims=True)
    return scale * gain * grad - values * (scale * scale * scale) * inner, gain_grad


def head_blocks(pair):
    size = pair.shape[0] // 2
    zero = jnp.zeros((size, pair.shape[1]), pair.dtype)
    return jnp.concatenate(
        [
            jnp.concatenate([pair[:size], zero], axis=1),
            jnp.concatenate([zero, pair[size:]], axis=1),
        ],
        axis=0,
    )


def head_rows(both):
    size, count = both.shape[0] // 2, both.shape[1] // 2
    return jnp.concatenate([both[:size, :count], both[size:, count:]], axis=0)


def twice(values):
    return jnp.concatenate([values, values], axis=1)


def fold(values):
    return values.reshape(values.shape[0] // 8, 8, values.shape[1])


class Mesh2:
    def __init__(self):
        self.row = lax.axis_index("dp")
        self.place = lax.axis_index("seq")
        self.side, self.core = self.place // 2, lax.rem(self.place, 2)
        self.sibling = self.side * 2 + 1 - self.core
        self.across = (1 - self.side) * 2 + self.core
        self.diagonal = (1 - self.side) * 2 + 1 - self.core
        self.core_peer = (self.row, self.sibling)
        self.y_peer = (self.row, self.across)

    def greet(self, peers):
        barrier = pltpu.get_barrier_semaphore()
        for peer in peers:
            pl.semaphore_signal(barrier, inc=1, device_id=peer, device_id_type=MESH)
        pl.semaphore_wait(barrier, len(peers))


def send(src, dst, sems, slot, peer):
    return pltpu.make_async_remote_copy(
        src_ref=src,
        dst_ref=dst,
        send_sem=sems.at[(0, *slot)],
        recv_sem=sems.at[(1, *slot)],
        device_id=peer,
        device_id_type=MESH,
    )


def softmax_pair(pair, r, count, steps, keys, turned, terms, queries_t, masses, out_t, probs, place):
    lanes = block(pair, 2 * r.head_dim)
    queries = head_blocks(queries_t[lanes, :])
    near = place is not None
    if near:
        tiles = [
            pltpu.roll(
                jnp.broadcast_to(r.near_bias[pl.ds(pair * 2 + head, 1), :], (NEAR, 2 * NEAR)),
                0,
                1,
                stride=1,
                stride_axis=0,
            )
            for head in range(2)
        ]
        below = [tile[:, NEAR:] for tile in tiles]
        on = [tile[:, :NEAR] for tile in tiles]
        none = jnp.zeros((NEAR, NEAR), F32)
        before = jnp.concatenate([below[0], none, below[1], none], axis=1)
        first = jnp.concatenate([on[0], below[0], on[1], below[1]], axis=1)
        second = jnp.concatenate([none, on[0], none, on[1]], axis=1)

    top = jnp.full((8, 2 * count), -jnp.inf, F32)
    for index in range(steps):
        rows = block(index, count)
        raw = dot(keys[index, :, lanes], queries) + twice(terms[rows, :])
        r.scores[rows, :] = raw
        if not near:
            top = jnp.maximum(top, jnp.max(fold(raw), axis=0))
    if near:
        rows = block(place, count)
        r.scores[rows, :] = r.scores[rows, :] + jnp.concatenate([first, second], axis=0)

        @pl.when(place > 0)
        def _():
            last = block(place * (count // NEAR) - 1, NEAR)
            r.scores[last, :] = r.scores[last, :] + before

        for index in range(steps):
            top = jnp.maximum(top, jnp.max(fold(r.scores[block(index, count), :]), axis=0))
    top = jnp.max(top, axis=0, keepdims=True)
    mass = jnp.zeros((8, 2 * count), F32)
    context = jnp.zeros((2 * r.head_dim, 2 * count), F32)
    for index in range(steps):
        rows = block(index, count)
        weights = jnp.exp(r.scores[rows, :] - top)
        low = weights.astype(LOW)
        probs[rows, :] = low
        context = context + dot(turned[lanes, rows], low)
        mass = mass + jnp.sum(fold(weights), axis=0)
    inverse = 1.0 / jnp.sum(mass, axis=0, keepdims=True)
    masses[pair] = inverse
    out_t[lanes, :] = head_rows(context * inverse)


def forward_kernel(names, dims, *refs):
    r = SimpleNamespace(**dict(zip(names, refs)), head_dim=dims.head_dim)
    m = Mesh2()
    count, places, pairs, fan, width = dims.count, dims.places, dims.pairs, dims.fan, dims.width
    q_place = m.place

    def load(slot, src, dst):
        copy = pltpu.make_async_copy(src, dst, r.load_sem.at[slot])
        copy.start()
        return copy

    loads = SimpleNamespace(
        x=load(9, r.x_hbm, r.xs.at[m.place]),
        e=load(10, r.e_hbm, r.es.at[m.place]),
        go=load(11, r.go_hbm, r.go),
        wk=load(0, r.wk_hbm, r.wk),
        wv=load(1, r.wv_hbm, r.wv),
        wq=load(2, r.wq_hbm, r.wq),
        wout=load(3, r.wout_hbm, r.wout),
        cwk=load(4, r.cwk_hbm, r.cwk),
        cwv=load(5, r.cwv_hbm, r.cwv),
        wo=load(6, r.wo_hbm, r.wo),
        cwq=load(7, r.cwq_hbm, r.cwq),
        cwo=load(8, r.cwo_hbm, r.cwo),
    )

    m.greet([m.core_peer, m.y_peer])
    x_y = send(r.x_hbm, r.xs.at[m.place], r.link_sem, (0,), m.y_peer)
    x_core = send(r.x_hbm, r.xs.at[m.place], r.link_sem, (1,), m.core_peer)
    x_on = send(r.xs.at[m.across], r.xs.at[m.across], r.link_sem, (2,), m.core_peer)
    e_y = send(r.e_hbm, r.es.at[m.place], r.link_sem, (3,), m.y_peer)
    e_core = send(r.e_hbm, r.es.at[m.place], r.link_sem, (4,), m.core_peer)
    e_on = send(r.es.at[m.across], r.es.at[m.across], r.link_sem, (5,), m.core_peer)
    x_y.start()
    x_core.start()
    e_core.start()

    gain_self = r.gain_self[...].astype(F32).reshape(1, width)
    gain_cross = r.gain_cross[...].astype(F32).reshape(1, width)

    items = dims.items
    dec_starts, enc_starts = [0], [0]
    for index in range(items):
        dec_starts.append(dec_starts[-1] + r.dec_len[0, index])
        enc_starts.append(enc_starts[-1] + r.enc_len[0, index])
    query_at = q_place * count + lax.broadcasted_iota(jnp.int32, (1, count), 1)
    low_self = jnp.zeros((1, count), jnp.int32)
    low_cross = jnp.zeros((1, count), jnp.int32)
    high_cross = jnp.full((1, count), enc_starts[1], jnp.int32)
    for index in range(1, items):
        inside = query_at >= dec_starts[index]
        low_self = jnp.where(inside, dec_starts[index], low_self)
        low_cross = jnp.where(inside, enc_starts[index], low_cross)
        high_cross = jnp.where(inside, enc_starts[index + 1], high_cross)

    def masks(index, carry):
        rows = block(index, count)
        key_at = index * count + lax.broadcasted_iota(jnp.int32, (count, count), 0)
        r.self_terms[rows, :] = jnp.where((key_at >= low_self) & (key_at <= query_at), 0.0, NEG)
        r.cross_terms[rows, :] = jnp.where((key_at >= low_cross) & (key_at < high_cross), 0.0, NEG)
        return carry

    lax.fori_loop(0, places, masks, 0)

    buckets = r.table.shape[1]
    terms = bucket_terms(buckets)
    last = lax.broadcasted_iota(jnp.int32, terms.shape, 0) == buckets - 1
    terms = terms - last.astype(F32)
    r.near_bias[...] = dot(r.table[...], terms.astype(LOW))

    def self_block(place):
        rows = block(place, count)
        states = r.xs[place].astype(F32)
        normed = (states * scale_of(states) * gain_self).astype(LOW)
        r.a1[place] = normed
        r.keys[place] = dot(normed, r.wk[...]).astype(LOW)
        values = dot(normed, r.wv[...]).astype(LOW)
        r.values[place] = values
        r.values_t[:, rows] = jnp.transpose(values)

    def cross_block(place):
        rows = block(place, count)
        encoded = r.es[place]
        r.ckeys[place] = dot(encoded, r.cwk[...]).astype(LOW)
        values = dot(encoded, r.cwv[...]).astype(LOW)
        r.cvalues[place] = values
        r.cvalues_t[:, rows] = jnp.transpose(values)

    def nth_place(k):
        return lax.rem(m.side + k // 2, 2) * 2 + lax.rem(m.core + lax.rem(k, 2), 2)

    def cross_blocks(k, carry):
        @pl.when(k == 1)
        def _():
            e_core.wait()

        @pl.when(k == 3)
        def _():
            e_on.wait()

        cross_block(nth_place(k))
        return carry

    def inner_grad(index, carry):
        r.inner_grad[index] = dot_nt(r.go[...], r.wout[block(index, width), :]).astype(LOW)
        return carry

    def self_blocks(k, carry):
        @pl.when(k == 1)
        def _():
            x_core.wait()

        @pl.when(k == 2)
        def _():
            loads.wout.wait()
            loads.go.wait()
            loads.e.wait()
            lax.fori_loop(0, fan, inner_grad, 0)
            loads.cwk.wait()
            loads.cwv.wait()
            lax.fori_loop(0, 2, cross_blocks, 0)
            x_y.wait()
            x_on.start()
            e_y.start()

        @pl.when(k == 3)
        def _():
            x_on.wait()

        self_block(nth_place(k))

        @pl.when(k == 0)
        def _():
            loads.wq.wait()
            r.queries_t[...] = jnp.transpose(dot(r.a1[m.place], r.wq[...]).astype(LOW))

        return carry

    loads.x.wait()
    loads.wk.wait()
    loads.wv.wait()
    lax.fori_loop(0, 4, self_blocks, 0)

    def keep(src, dst, slot):
        copy = pltpu.make_async_copy(src, dst, r.keep_sem.at[slot])
        copy.start()
        return copy

    kept = [
        keep(r.keys, r.keys_out, 0),
        keep(r.values, r.values_out, 1),
        keep(r.a1, r.a1_out, 2),
        keep(r.inner_grad, r.inner_out, 6),
        keep(r.queries_t, r.queries_t_out, 7),
        keep(r.xs.at[m.across], r.across_out, 14),
    ]

    def probs_copy(slot, out, pair):
        return pltpu.make_async_copy(r.probs.at[slot], out.at[pair], r.probs_sem.at[slot])

    def attend(earlier, keys, turned, terms, queries_t, masses, out_t, out, place):
        def one(pair, carry):
            slot = lax.rem(pair, 2)
            if earlier:
                probs_copy(slot, out, pair).wait()
            else:
                @pl.when(pair >= 2)
                def _():
                    probs_copy(slot, out, pair).wait()

                @pl.when(pair == pairs - 2)
                def _():
                    e_y.wait()
                    e_on.start()
            softmax_pair(
                pair, r, count, places, keys, turned, terms, queries_t, masses, out_t,
                r.probs.at[slot], place,
            )
            probs_copy(slot, out, pair).start()
            return carry

        lax.fori_loop(0, pairs, one, 0)

    attend(
        False, r.keys, r.values_t, r.self_terms, r.queries_t, r.self_masses, r.context_t,
        r.self_probs, q_place,
    )
    loads.wo.wait()
    context = jnp.transpose(r.context_t[...]).astype(LOW)
    first = r.xs[m.place].astype(F32) + dot(context, r.wo[...])
    r.first[...] = first
    normed_cross = (first * scale_of(first) * gain_cross).astype(LOW)
    r.a2[...] = normed_cross
    loads.cwq.wait()
    r.cqueries_t[...] = jnp.transpose(dot(normed_cross, r.cwq[...]).astype(LOW))
    lax.fori_loop(2, 4, cross_blocks, 0)
    kept += [
        keep(r.ckeys, r.ckeys_out, 3),
        keep(r.cvalues, r.cvalues_out, 4),
        keep(r.es, r.es_out, 5),
        keep(r.context_t, r.context_t_out, 8),
        keep(r.first, r.first_out, 9),
        keep(r.a2, r.a2_out, 10),
        keep(r.cqueries_t, r.cqueries_t_out, 11),
    ]
    attend(
        True, r.ckeys, r.cvalues_t, r.cross_terms, r.cqueries_t, r.cross_masses, r.ccontext_t,
        r.cross_probs, None,
    )
    loads.cwo.wait()
    context = jnp.transpose(r.ccontext_t[...]).astype(LOW)
    kept.append(keep(r.ccontext_t, r.ccontext_t_out, 12))
    r.second[...] = r.first[...] + dot(context, r.cwo[...])
    kept.append(keep(r.second, r.second_out, 13))
    for slot in range(2):
        probs_copy(slot, r.cross_probs, pairs - 2 + slot).wait()
    for copy in kept:
        copy.wait()


def call(kernel, name, collective, limit, inputs, outputs, scratch, aliases=None):
    names = (*inputs, *outputs, *scratch)
    results = pl.pallas_call(
        functools.partial(kernel, names),
        out_shape=tuple(jax.ShapeDtypeStruct(shape, kind) for shape, kind, _ in outputs.values()),
        in_specs=[pl.BlockSpec(memory_space=space) for _, space in inputs.values()],
        out_specs=tuple(pl.BlockSpec(memory_space=space) for _, _, space in outputs.values()),
        scratch_shapes=list(scratch.values()),
        input_output_aliases=aliases or {},
        compiler_params=pltpu.CompilerParams(
            collective_id=collective, has_side_effects=True, vmem_limit_bytes=limit * 2**20
        ),
        name=name,
    )(*(array for array, _ in inputs.values()))
    return SimpleNamespace(**dict(zip(outputs, results)))


def run_forward(dims, a):
    count, total, width = dims.count, dims.count * dims.places, dims.width
    near, far, scalars = pltpu.VMEM, pl.ANY, pltpu.SMEM
    pairs, fan = dims.pairs, dims.fan
    square = (width, width)
    own = (count, width)
    inputs = dict(
        x_hbm=(a.dec_states[0], far),
        e_hbm=(a.enc_states[0], far),
        go_hbm=(a.out_grad[0], far),
        dec_len=(a.dec_lengths, scalars),
        enc_len=(a.enc_lengths, scalars),
        table=(a.position_bias.T, near),
        gain_self=(a.gain_self, near),
        gain_cross=(a.gain_cross, near),
        wk_hbm=(a.self_key, far),
        wv_hbm=(a.self_value, far),
        wq_hbm=(a.self_query, far),
        wout_hbm=(a.ffn_out, far),
        cwk_hbm=(a.cross_key, far),
        cwv_hbm=(a.cross_value, far),
        wo_hbm=(a.self_output, far),
        cwq_hbm=(a.cross_query, far),
        cwo_hbm=(a.cross_output, far),
    )
    outputs = dict(
        first_out=(own, F32, far),
        second_out=(own, F32, far),
        inner_out=((fan, *own), LOW, far),
        across_out=(own, LOW, far),
        queries_t_out=((width, count), LOW, far),
        cqueries_t_out=((width, count), LOW, far),
        context_t_out=((width, count), F32, far),
        ccontext_t_out=((width, count), F32, far),
        self_masses=((pairs, 1, 2 * count), F32, near),
        cross_masses=((pairs, 1, 2 * count), F32, near),
        a2_out=(own, LOW, far),
        keys_out=((dims.places, *own), LOW, far),
        values_out=((dims.places, *own), LOW, far),
        a1_out=((dims.places, *own), LOW, far),
        ckeys_out=((dims.places, *own), LOW, far),
        cvalues_out=((dims.places, *own), LOW, far),
        es_out=((dims.places, *own), LOW, far),
        self_probs=((pairs, total, 2 * count), LOW, far),
        cross_probs=((pairs, total, 2 * count), LOW, far),
    )
    scratch = dict(
        xs=pltpu.VMEM((dims.places, *own), LOW),
        go=pltpu.VMEM(own, LOW),
        first=pltpu.VMEM(own, F32),
        second=pltpu.VMEM(own, F32),
        queries_t=pltpu.VMEM((width, count), LOW),
        cqueries_t=pltpu.VMEM((width, count), LOW),
        context_t=pltpu.VMEM((width, count), F32),
        ccontext_t=pltpu.VMEM((width, count), F32),
        a2=pltpu.VMEM(own, LOW),
        es=pltpu.VMEM((dims.places, *own), LOW),
        wk=pltpu.VMEM(square, LOW),
        wv=pltpu.VMEM(square, LOW),
        wq=pltpu.VMEM(square, LOW),
        wout=pltpu.VMEM((fan * width, width), LOW),
        cwk=pltpu.VMEM(square, LOW),
        cwv=pltpu.VMEM(square, LOW),
        wo=pltpu.VMEM(square, LOW),
        cwq=pltpu.VMEM(square, LOW),
        cwo=pltpu.VMEM(square, LOW),
        a1=pltpu.VMEM((dims.places, *own), LOW),
        keys=pltpu.VMEM((dims.places, *own), LOW),
        values=pltpu.VMEM((dims.places, *own), LOW),
        values_t=pltpu.VMEM((width, total), LOW),
        ckeys=pltpu.VMEM((dims.places, *own), LOW),
        cvalues=pltpu.VMEM((dims.places, *own), LOW),
        cvalues_t=pltpu.VMEM((width, total), LOW),
        self_terms=pltpu.VMEM((total, count), F32),
        cross_terms=pltpu.VMEM((total, count), F32),
        near_bias=pltpu.VMEM((dims.heads, 2 * NEAR), F32),
        scores=pltpu.VMEM((total, 2 * count), F32),
        probs=pltpu.VMEM((2, total, 2 * count), LOW),
        inner_grad=pltpu.VMEM((fan, *own), LOW),
        load_sem=pltpu.SemaphoreType.DMA((12,)),
        link_sem=pltpu.SemaphoreType.DMA((2, 6)),
        keep_sem=pltpu.SemaphoreType.DMA((15,)),
        probs_sem=pltpu.SemaphoreType.DMA((2,)),
    )
    return call(
        lambda names, *refs: forward_kernel(names, dims, *refs),
        "forward", 0, 56, inputs, outputs, scratch,
    )


SWAPPED = (1, 4, 5, 7, 10, 11, 13, 16, 19)


class Reducer:
    LAGS = (0, 4, 7, 9, 12, 19)

    def __init__(self, r, m, dims):
        self.r, self.m = r, m
        self.planes = dims.planes
        self.line = dims.line
        self.piece = dims.piece
        self.chunk_rows = dims.chunk_rows
        self.half_rows = dims.chunk_rows // 2
        self.chunks = dims.chunks
        self.ring = dims.ring
        self.plane, self.half = m.row // 2, lax.rem(m.row, 2)
        self.x_peer = (self.plane * 2 + 1 - self.half, m.place)
        self.published = self.loaded = self.fed = self.moved = 0

    def z_peer(self, step):
        return (lax.rem(self.plane + step, self.planes) * 2 + self.half, self.m.place)

    def plane_peer(self, plane):
        return (plane * 2 + self.half, self.m.place)

    def peers(self):
        return [self.x_peer] + [self.z_peer(step) for step in range(1, self.planes)]

    def span(self, first, size):
        return pl.ds(pl.multiple_of(first, self.piece), size)

    def rows(self, index):
        return self.span(index * self.chunk_rows, self.chunk_rows)

    def by_planes(self, index):
        found = index == SWAPPED[0]
        for other in SWAPPED[1:]:
            found = found | (index == other)
        return found

    def by_halves(self, index):
        return lax.rem(index, 6) == 3

    def route(self, index, first, other, third=None):
        if not self.line:
            first(index)
            return
        special = self.by_planes(index)
        usual = jnp.logical_not(special)
        if third is not None:
            early = self.by_halves(index)
            usual = usual & jnp.logical_not(early)

            @pl.when(early)
            def _():
                third(index)

        @pl.when(usual)
        def _():
            first(index)

        @pl.when(special)
        def _():
            other(index)

    def half_of(self, index, half):
        return self.span(index * self.chunk_rows + half * self.half_rows, self.half_rows)

    def packed(self, index):
        return self.span(index * self.half_rows, self.half_rows)

    def fresh_rows(self, index):
        return self.span(lax.rem(index, self.ring) * self.chunk_rows, self.chunk_rows)

    def load(self, index):
        r = self.r
        return pltpu.make_async_copy(
            r.big.at[self.m.core, :, self.rows(index)],
            r.fresh.at[:, self.fresh_rows(index)],
            r.chunk_sem.at[index],
        )

    def core_copy(self, index):
        r, rows = self.r, self.rows(index)
        return send(
            r.big.at[1 - self.m.core, :, rows], r.sums.at[:, rows], r.core_sem, (index,),
            self.m.core_peer,
        )

    def y_copy(self, index):
        r, rows = self.r, self.rows(index)
        return send(
            r.sums.at[1 - self.m.side, rows], r.fin.at[rows], r.y_sem, (index,), self.m.y_peer
        )

    def x_copy(self, index):
        r = self.r
        return send(
            r.sums.at[self.m.side, self.half_of(index, 1 - self.half)],
            r.x_recv.at[self.packed(index)],
            r.x_sem, (index,), self.x_peer,
        )

    def in_copy(self, index, inner):
        r = self.r
        return send(
            r.sums.at[self.m.side, self.half_of(index, self.half)],
            r.z_recv.at[0, self.packed(index)],
            r.z_sem, (index, 0), self.plane_peer(inner),
        )

    def mid_copy(self, index):
        r = self.r
        return send(
            r.sums.at[self.m.side, self.half_of(index, self.half)],
            r.z_recv.at[1, self.packed(index)],
            r.z_sem, (index, 1), self.plane_peer(3 - self.plane),
        )

    def out_copy(self, index, outer):
        r, rows = self.r, self.half_of(index, self.half)
        return send(r.fin.at[rows], r.fin.at[rows], r.gz_sem, (index, 0), self.plane_peer(outer))

    def z_part(self, index, which):
        first = index * self.chunk_rows + self.half * self.half_rows + which * self.piece
        return self.span(first, self.piece)

    def z_copy(self, index, step):
        r = self.r
        target = lax.rem(self.plane + step, self.planes)
        return send(
            r.sums.at[self.m.side, self.z_part(index, target)],
            r.z_recv.at[step - 1, self.span(index * self.piece, self.piece)],
            r.z_sem, (index, step - 1), self.z_peer(step),
        )

    def gz_copy(self, index, step):
        r, rows = self.r, self.z_part(index, self.plane)
        return send(r.fin.at[rows], r.fin.at[rows], r.gz_sem, (index, step - 1), self.z_peer(step))

    def gx_copy(self, index):
        r, rows = self.r, self.half_of(index, self.half)
        return send(r.fin.at[rows], r.fin.at[rows], r.gx_sem, (index,), self.x_peer)

    def publish(self, rows):
        last = rows // self.chunk_rows

        def begin(index, carry):
            self.core_copy(index).start()
            return carry

        def fetch(index, carry):
            self.load(index).start()
            return carry

        lax.fori_loop(self.published, last, begin, 0)
        ahead = min(last, self.fed + self.ring)
        lax.fori_loop(self.loaded, ahead, fetch, 0)
        self.published, self.loaded = last, max(self.loaded, ahead)

    def publish_part(self, first, last):
        def begin(index, carry):
            self.core_copy(index).start()

            @pl.when(index < self.ring)
            def _():
                self.load(index).start()

            return carry

        lax.fori_loop(first, last, begin, 0)

    def parts_done(self, last, fed):
        self.published, self.fed = last, fed
        self.loaded = min(last, self.ring)

    def feed(self, index, prefetch=True):
        r = self.r
        self.load(index).wait()
        self.core_copy(index).wait()
        rows, fresh = self.rows(index), self.fresh_rows(index)
        for side in range(2):
            r.sums[side, rows, :] = add_low(r.sums[side, rows, :], r.fresh[side, fresh, :])
        self.route(
            index,
            lambda at: self.y_copy(at).start(),
            lambda at: self.swap_copy(at).start(),
            lambda at: self.early_copy(at).start(),
        )

        if not prefetch:
            return

        @pl.when(index + self.ring < self.published)
        def _():
            self.load(index + self.ring).start()

    def move(self, step):
        stages = (
            (self.after_y, self.after_swap, self.after_early),
            (self.after_x, self.swapped_y, self.early_y),
            (self.inward, self.swapped_x),
            (self.middle, self.swapped_pair),
            (self.outward, self.swapped_back),
            (self.finish, self.swapped_finish),
        )
        for lag, stage in reversed(tuple(zip(self.LAGS, stages))):
            index = step - lag

            @pl.when((index >= 0) & (index < self.chunks))
            def _():
                self.route(index, *stage)


    def early_rows(self, index):
        return self.span(index // 6 * self.half_rows, self.half_rows)

    def early_copy(self, index):
        r = self.r
        return send(
            r.sums.at[:, self.half_of(index, 1 - self.half)],
            r.early_recv.at[:, self.early_rows(index)],
            r.x_sem, (index,), self.x_peer,
        )

    def early_y_copy(self, index):
        r, rows = self.r, self.half_of(index, self.half)
        return send(
            r.sums.at[1 - self.m.side, rows], r.fin.at[rows], r.y_sem, (index,), self.m.y_peer
        )

    def after_early(self, index):
        r = self.r
        self.early_copy(index).wait()
        rows, packed = self.half_of(index, self.half), self.early_rows(index)
        for side in range(2):
            r.sums[side, rows, :] = add_low(r.sums[side, rows, :], r.early_recv[side, packed, :])
        self.early_y_copy(index).start()

    def early_y(self, index):
        r, m = self.r, self.m
        self.early_y_copy(index).wait()
        rows = self.half_of(index, self.half)
        r.sums[m.side, rows, :] = add_low(r.sums[m.side, rows, :], r.fin[rows, :])
        self.give_in(index)


    def parity(self):
        return lax.rem(self.plane, 2)

    def neighbour(self):
        return self.plane_peer(self.plane + 1 - 2 * self.parity())

    def quarter_of(self, index, half):
        size = self.half_rows // 2
        first = index * self.chunk_rows + self.parity() * self.half_rows + half * size
        return self.span(first, size)

    def packed_quarter(self, index, which):
        size = self.half_rows // 2
        return self.span(index * self.half_rows + which * size, size)

    def swap_copy(self, index):
        r = self.r
        return send(
            r.sums.at[:, self.half_of(index, 1 - self.parity())],
            r.z_recv.at[:, self.packed(index)],
            r.z_sem, (index, 0), self.neighbour(),
        )

    def swapped_y_copy(self, index):
        r, rows = self.r, self.half_of(index, self.parity())
        return send(
            r.sums.at[1 - self.m.side, rows], r.fin.at[rows], r.y_sem, (index,), self.m.y_peer
        )

    def swapped_x_copy(self, index):
        r = self.r
        return send(
            r.sums.at[self.m.side, self.quarter_of(index, 1 - self.half)],
            r.x_recv.at[self.packed_quarter(index, 0)],
            r.x_sem, (index,), self.x_peer,
        )

    def pair_copy(self, index):
        r = self.r
        return send(
            r.sums.at[self.m.side, self.quarter_of(index, self.half)],
            r.x_recv.at[self.packed_quarter(index, 1)],
            r.z_sem, (index, 1), self.z_peer(2),
        )

    def swapped_gx_copy(self, index):
        r, rows = self.r, self.quarter_of(index, self.half)
        return send(r.fin.at[rows], r.fin.at[rows], r.gx_sem, (index,), self.x_peer)

    def swapped_gz_copy(self, index):
        r, rows = self.r, self.half_of(index, self.parity())
        return send(r.fin.at[rows], r.fin.at[rows], r.gz_sem, (index, 0), self.neighbour())

    def after_swap(self, index):
        r = self.r
        self.swap_copy(index).wait()
        rows, packed = self.half_of(index, self.parity()), self.packed(index)
        for side in range(2):
            r.sums[side, rows, :] = add_low(r.sums[side, rows, :], r.z_recv[side, packed, :])
        self.swapped_y_copy(index).start()

    def swapped_y(self, index):
        r, m = self.r, self.m
        self.swapped_y_copy(index).wait()
        rows = self.half_of(index, self.parity())
        r.sums[m.side, rows, :] = add_low(r.sums[m.side, rows, :], r.fin[rows, :])
        self.swapped_x_copy(index).start()

    def swapped_x(self, index):
        r, m = self.r, self.m
        self.swapped_x_copy(index).wait()
        rows = self.quarter_of(index, self.half)
        arrived = r.x_recv[self.packed_quarter(index, 0), :]
        r.sums[m.side, rows, :] = add_low(r.sums[m.side, rows, :], arrived)
        self.pair_copy(index).start()

    def swapped_pair(self, index):
        r, m = self.r, self.m
        self.pair_copy(index).wait()
        rows = self.quarter_of(index, self.half)
        arrived = r.x_recv[self.packed_quarter(index, 1), :]
        r.fin[rows, :] = add_low(r.sums[m.side, rows, :], arrived)
        self.swapped_gx_copy(index).start()

    def swapped_back(self, index):
        self.swapped_gx_copy(index).wait()
        self.swapped_gz_copy(index).start()

    def swapped_finish(self, index):
        self.swapped_gz_copy(index).wait()

    def after_y(self, index):
        r, m = self.r, self.m
        self.y_copy(index).wait()
        rows = self.rows(index)
        r.sums[m.side, rows, :] = add_low(r.sums[m.side, rows, :], r.fin[rows, :])
        self.x_copy(index).start()

    def after_x(self, index):
        r, m = self.r, self.m
        self.x_copy(index).wait()
        rows = self.half_of(index, self.half)
        r.sums[m.side, rows, :] = add_low(r.sums[m.side, rows, :], r.x_recv[self.packed(index), :])
        if not self.line:
            for step in range(1, self.planes):
                self.z_copy(index, step).start()
            return
        self.give_in(index)

    def give_in(self, index):
        for outer, inner in ((0, 1), (3, 2)):
            @pl.when(self.plane == outer)
            def _():
                self.in_copy(index, inner).start()

    def inward(self, index):
        r, m = self.r, self.m
        if not self.line:
            return
        for outer, inner in ((0, 1), (3, 2)):
            @pl.when(self.plane == outer)
            def _():
                self.in_copy(index, inner).wait_send()

        @pl.when((self.plane == 1) | (self.plane == 2))
        def _():
            self.in_copy(index, self.plane).wait_recv()
            rows = self.half_of(index, self.half)
            arrived = r.z_recv[0, self.packed(index), :]
            r.sums[m.side, rows, :] = add_low(r.sums[m.side, rows, :], arrived)
            self.mid_copy(index).start()

    def middle(self, index):
        r, m = self.r, self.m
        if not self.line:
            part = self.z_part(index, self.plane)
            total = r.sums[m.side, part, :].astype(F32)
            for step in range(1, self.planes):
                self.z_copy(index, step).wait()
                arrived = r.z_recv[step - 1, self.span(index * self.piece, self.piece), :]
                total = total + arrived.astype(F32)
            r.fin[part, :] = total.astype(LOW)
            for step in range(1, self.planes):
                self.gz_copy(index, step).start()
            return

        @pl.when((self.plane == 1) | (self.plane == 2))
        def _():
            self.mid_copy(index).wait()
            rows = self.half_of(index, self.half)
            arrived = r.z_recv[1, self.packed(index), :]
            r.fin[rows, :] = add_low(r.sums[m.side, rows, :], arrived)
            for outer, inner in ((0, 1), (3, 2)):
                @pl.when(self.plane == inner)
                def _():
                    self.out_copy(index, outer).start()
            self.gx_copy(index).start()

    def outward(self, index):
        if not self.line:
            for step in range(1, self.planes):
                self.gz_copy(index, step).wait()
            self.gx_copy(index).start()
            return
        for outer, inner in ((0, 1), (3, 2)):
            @pl.when(self.plane == inner)
            def _():
                self.out_copy(index, outer).wait_send()

            @pl.when(self.plane == outer)
            def _():
                self.out_copy(index, inner).wait_recv()
                self.gx_copy(index).start()

    def finish(self, index):
        self.gx_copy(index).wait()

    def run(self, feeds, moves):
        loops = max(1, feeds, moves)
        one, after = self.beside(loops, feeds, moves)

        def body(index, carry):
            one(index)
            return carry

        lax.fori_loop(0, loops, body, 0)
        after()

    def beside(self, loops, feeds, moves):
        feeds = max(0, min(feeds, self.published - self.fed))
        fed = self.fed + feeds
        limit = self.chunks + self.LAGS[-1] if fed == self.chunks else fed
        moves = max(0, min(moves, limit - self.moved))
        first_feed, first_move = self.fed, self.moved

        each = -(-feeds // loops)

        def one(index):
            if feeds > 0:
                def feed(step, carry):
                    self.feed(first_feed + step)
                    return carry

                lax.fori_loop(
                    jnp.minimum(index * each, feeds), jnp.minimum((index + 1) * each, feeds), feed, 0
                )
            if moves > 0:
                def move(step, carry):
                    self.move(first_move + step)
                    return carry

                lax.fori_loop(index * moves // loops, (index + 1) * moves // loops, move, 0)

        def after():
            self.fed, self.moved = fed, first_move + moves
            self.loaded = max(self.loaded, min(self.published, self.fed + self.ring))

        return one, after

    def finish_all(self, each, events):
        feeds, moves = self.chunks - self.fed, self.left()
        first_feed, first_move = self.fed, self.moved
        events = [(min(step, moves - 1), event) for step, event in events]

        def body(step, carry):
            for at, event in events:
                @pl.when(step == at)
                def _():
                    event()

            def feed(index, carry):
                self.feed(first_feed + index)
                return carry

            lax.fori_loop(
                jnp.minimum(step * each, feeds), jnp.minimum((step + 1) * each, feeds), feed, 0
            )
            self.move(first_move + step)
            return carry

        lax.fori_loop(0, moves, body, 0)

    def left(self):
        return self.chunks + self.LAGS[-1] - self.moved


def attend_back(pair, r, count, keys, keys_t, values, queries_t, masses, context_t, grad_t, probs, place, places):
    lanes = block(pair, 2 * r.head_dim)
    inverse = masses[pair]
    grads = grad_t[lanes, :].astype(F32)
    product = grads * context_t[lanes, :]
    sums = [
        jnp.sum(product[: r.head_dim], axis=0, keepdims=True),
        jnp.sum(product[r.head_dim :], axis=0, keepdims=True),
    ]
    inner = jnp.concatenate(sums, axis=1) * inverse
    grads = (head_blocks(grads) * inverse).astype(LOW)
    queries = head_blocks(queries_t[lanes, :])

    total = jnp.zeros((2 * r.head_dim, 2 * count), F32)
    beyond = jnp.zeros((8, 2 * count), F32)
    split = count - NEAR
    if place is not None:
        r.before[...] = jnp.zeros_like(r.before)
    for index in range(places):
        rows = block(index, count)
        weights = probs[rows, :]
        score_grad = weights.astype(F32) * (dot(values[index, :, lanes], grads) - inner)
        low = score_grad.astype(LOW)
        r.value_grad[index, :, lanes] = dot_nt(weights, grads).astype(LOW)
        r.key_grad[index, :, lanes] = dot_nt(low, queries).astype(LOW)
        total = total + dot(keys_t[lanes, rows], low)
        if place is not None:
            early = jnp.sum(fold(score_grad[:split]), axis=0)
            late = jnp.sum(fold(score_grad[split:]), axis=0)
            beyond = beyond + jnp.where(index < place, early, 0.0)
            beyond = beyond + jnp.where(index < place - 1, late, 0.0)

            @pl.when(index == place - 1)
            def _():
                r.before[...] = score_grad[split:]

            @pl.when(index == place)
            def _():
                r.own[...] = score_grad

    if place is not None:
        own, before = r.own[...], r.before[...]
        parts = []
        for head in range(2):
            at = head * count
            on = own[:NEAR, at : at + NEAR] + own[NEAR:, at + NEAR : at + 2 * NEAR]
            below = before[:, at : at + NEAR] + own[:NEAR, at + NEAR : at + 2 * NEAR]
            both = jnp.concatenate([on, below], axis=1)
            summed = both[:8]
            for group in range(1, NEAR // 8):
                summed = summed + pltpu.roll(
                    both[8 * group : 8 * group + 8], 2 * NEAR - 8 * group, 1
                )
            parts.append(summed)
        summed = jnp.concatenate(parts, axis=0)
        sublane = lax.broadcasted_iota(jnp.int32, summed.shape, 0)
        for bit in (1, 2, 4):
            summed = jnp.where(
                (sublane & bit) != 0, pltpu.roll(summed, 2 * NEAR - bit, 1), summed
            )
        lane = lax.broadcasted_iota(jnp.int32, (1, 2 * NEAR), 1)
        for head in range(2):
            at = head * count
            line = jnp.sum(summed[8 * head : 8 * head + 8], axis=0, keepdims=True)
            rest = jnp.sum(beyond[:, at : at + count]) + jnp.sum(before[:, at + NEAR : at + 2 * NEAR])
            line = line + jnp.where(lane == 2 * NEAR - 1, rest, 0.0)
            r.by_distance[pl.ds(pair * 2 + head, 1), :] = line
    r.query_grad_t[lanes, :] = head_rows(total).astype(LOW)


FFN_FEEDS = 3
PLAN = (
    (0, 0), (6, 0), (2, 5), (14, 0), (19, 0), (17, 3),
    (0, 1), (1, 0), (36, 6), (21, 1), (44, 23),
)
TAIL_FEEDS = 4
TAIL = (3, 8, 13, 16, 21, 9, 27)


def backward_kernel(names, dims, *refs):
    r = SimpleNamespace(**dict(zip(names, refs)), head_dim=dims.head_dim)
    m = Mesh2()
    count, places, pairs, fan, width = dims.count, dims.places, dims.pairs, dims.fan, dims.width
    own = width // places
    engine = Reducer(r, m, dims)
    plan = iter(PLAN)
    r.wo, r.wq, r.wk, r.wv = (r.squares.at[index] for index in range(4))
    r.keys, r.values, r.key_grad, r.value_grad = (r.tall.at[pl.ds(4 * k, 4)] for k in range(4))

    loads = SimpleNamespace()
    slots = iter(range(r.load_sem.shape[0]))

    def later(src, dst):
        return pltpu.make_async_copy(src, dst, r.load_sem.at[next(slots)])

    def load(src, dst):
        copy = later(src, dst)
        copy.start()
        return copy

    def probs_copy(src, pair):
        slot = lax.rem(pair, 2)
        return pltpu.make_async_copy(src.at[pair], r.probs.at[slot], r.probs_sem.at[slot])

    third = width // count
    loads.second = load(r.second_hbm, r.second)
    loads.go = load(r.go_hbm, r.go)

    def ffn_copies(index):
        rows = pl.ds(index * third, third)
        win = r.win_hbm.at[:, block(index, width)]
        return (
            pltpu.make_async_copy(win, r.squares.at[index], r.win_sem.at[index]),
            pltpu.make_async_copy(r.wout_hbm.at[rows], r.tall.at[rows], r.wout_sem.at[index]),
        )

    for index in range(fan):
        win, wout = ffn_copies(index)
        win.start()
        if index == 0:
            loads.inner = load(r.inner_hbm, r.value_grad)
        wout.start()
    probs_copy(r.cross_probs, 0).start()
    probs_copy(r.cross_probs, 1).start()
    loads.es0 = load(r.es_hbm.at[m.core], r.group.at[0])
    loads.es1 = load(r.es_hbm.at[m.core + 2], r.group.at[1])
    loads.cqueries = load(r.cqueries_hbm, r.cqueries_t)
    loads.ccontext = load(r.ccontext_hbm, r.ccontext_t)
    loads.queries = load(r.queries_hbm, r.queries_t)
    loads.context = load(r.context_hbm, r.context_t)
    loads.a2 = load(r.a2_hbm, r.a2)
    loads.x = load(r.x_hbm, r.x)

    m.greet([m.core_peer, m.y_peer] + engine.peers())

    gain_self = r.gain_self[...].astype(F32).reshape(1, width)
    gain_cross = r.gain_cross[...].astype(F32).reshape(1, width)
    staged = {}

    def unit_copy(unit):
        rows = pl.ds(2 * width + unit * own, own)
        return pltpu.make_async_copy(
            r.stage.at[unit % 2], r.big.at[:, :, rows], r.stage_sem.at[unit % 2]
        )

    def give(unit, left_t, right):
        if unit - 2 in staged:
            staged.pop(unit - 2).wait()

        for place in range(places):
            grad = dot(left_t[place * own : (place + 1) * own, :], right)
            r.stage[unit % 2, place % 2, place // 2] = grad.astype(LOW)
        staged[unit] = unit_copy(unit)
        staged[unit].start()

    def settle(rows):
        for unit in sorted(staged):
            staged.pop(unit).wait()
        engine.publish(rows)

    def turn(src, dst):
        def one(index, carry):
            rows = block(index, count)
            dst[:, rows] = jnp.transpose(src[index])
            return carry

        lax.fori_loop(0, places, one, 0)

    def attend(src, queries_t, masses, context_t, grad_t, place):
        beside, after = engine.beside(pairs, *next(plan))

        def one(pair, carry):
            probs_copy(src, pair).wait()
            attend_back(
                pair, r, count, r.keys, r.keys_t, r.values, queries_t, masses, context_t, grad_t,
                r.probs.at[lax.rem(pair, 2)], place, places,
            )

            @pl.when(pair + 2 < pairs)
            def _():
                probs_copy(src, pair + 2).start()

            beside(pair)
            return carry

        lax.fori_loop(0, pairs, one, 0)
        after()

    def exchange(slot):
        copies = []
        for side in range(2):
            theirs = side * 2 + 1 - m.core
            for part, (src, dst) in enumerate(
                ((r.key_grad, r.key_recv), (r.value_grad, r.value_recv))
            ):
                copies.append(
                    send(
                        src.at[theirs], dst.at[slot, side], r.swap_sem, (slot, side, part),
                        m.core_peer,
                    )
                )
                copies[-1].start()
        return copies

    def chip_sum(grad, arrived):
        parts = [add_low(grad[side * 2 + m.core], arrived[side]) for side in range(2)]
        return jnp.concatenate(parts, axis=0)

    def partial(slot, side):
        key_grad = add_low(r.key_grad[side * 2 + m.core], r.key_recv[slot, side])
        value_grad = add_low(r.value_grad[side * 2 + m.core], r.value_recv[slot, side])
        return dot_nt(key_grad, r.wk[...]) + dot_nt(value_grad, r.wv[...])

    gain_ffn = r.gain_ffn[...].astype(F32).reshape(1, width)
    loads.second.wait()
    second = r.second[...]
    normed_ffn = (second * scale_of(second) * gain_ffn).astype(LOW)
    r.grad_t[...] = jnp.transpose(normed_ffn)
    r.a3[...] = normed_ffn
    r.dec_grad[...] = jnp.zeros_like(second)
    r.enc_grad[...] = jnp.zeros_like(second)
    loads.cwo, loads.cwq = later(r.cwo_hbm, r.wo), later(r.cwq_hbm, r.wq)
    loads.cwk, loads.cwv = later(r.cwk_hbm, r.wk), later(r.cwv_hbm, r.wv)
    loads.ckeys, loads.cvalues = later(r.ckeys_hbm, r.keys), later(r.cvalues_hbm, r.values)
    freed = ((loads.cwo,), (loads.cwq, loads.ckeys), (loads.cwk, loads.cvalues), (loads.cwv,))
    loads.inner.wait()
    loads.go.wait()

    def head_copy(index):
        return pltpu.make_async_copy(
            r.keys_t.at[:, pl.ds(0, width)],
            r.big.at[lax.rem(index, 2), index // 2, pl.ds(width, width)],
            r.head_sem,
        )

    def feed_forward(index, carry):
        slot = lax.rem(index, 2)
        win, wout = ffn_copies(index)
        win.wait()
        pre = dot(r.a3[...], r.squares[index])
        half = 0.5 + 0.5 * lax.erf(pre * (0.5**0.5))
        inner = (pre * half).astype(LOW)
        slope = half + pre * jnp.exp(-0.5 * pre * pre) * ((2.0 * math.pi) ** -0.5)
        pre_grad = (slope * r.value_grad[index].astype(F32)).astype(LOW)

        def rows_of(place, carry):
            grad = dot(r.grad_t[block(place, own), :], pre_grad)
            r.stage[slot, lax.rem(place, 2), place // 2] = grad.astype(LOW)
            return carry

        lax.fori_loop(0, places, rows_of, 0)
        tail = pltpu.make_async_copy(
            r.stage.at[slot], r.big.at[:, :, block(index, own)], r.stage_sem.at[slot]
        )
        tail.start()
        wout.wait()
        rows = r.tall[pl.ds(index * third, third)].reshape(width, width)
        r.dec_grad[...] += dot(inner, rows)
        r.enc_grad[...] += dot_nt(pre_grad, r.squares[index])

        @pl.when(index > 0)
        def _():
            head_copy(index - 1).wait()

        r.keys_t[:, :width] = dot(jnp.transpose(inner), r.go[...]).astype(LOW)
        head_copy(index).start()
        for step, copies in enumerate(freed):
            @pl.when(index == step)
            def _():
                for copy in copies:
                    copy.start()
        tail.wait()
        chunk_rows = engine.chunk_rows
        engine.publish_part(index * own // chunk_rows, (index + 1) * own // chunk_rows)

        def feed(step, carry):
            engine.feed(step, prefetch=False)
            return carry

        lax.fori_loop(index * ffn_feeds // fan, (index + 1) * ffn_feeds // fan, feed, 0)
        return carry

    ffn_feeds = min(FFN_FEEDS, fan * own // engine.chunk_rows)
    lax.fori_loop(0, fan, feed_forward, 0)
    engine.parts_done(fan * own // engine.chunk_rows, ffn_feeds)
    r.layer_out[...] = (second + r.dec_grad[...]).astype(LOW)
    second_part, gain_ffn_grad = norm_back(second, gain_ffn, r.enc_grad[...])
    loads.first = load(r.first_hbm, r.enc_grad)
    r.dec_grad[...] = r.go[...].astype(F32) + second_part
    r.tiny[0] = jnp.zeros(r.tiny.shape[1:], F32)
    r.tiny[0, 2:3] = gain_ffn_grad
    head_copy(fan - 1).wait()
    engine.publish(2 * width)
    engine.run(*next(plan))

    head_grad = r.dec_grad[...].astype(LOW)
    loads.cwo.wait()
    r.grad_t[...] = dot_nt(r.wo[...], head_grad).astype(LOW)
    loads.wo = load(r.wo_hbm, r.wo)
    engine.run(*next(plan))
    loads.ccontext.wait()
    r.query_grad_t[...] = r.ccontext_t[...].astype(LOW)
    give(0, r.query_grad_t, head_grad)
    loads.ckeys.wait()
    turn(r.keys, r.keys_t)
    loads.cvalues.wait()
    loads.cqueries.wait()
    attend(r.cross_probs, r.cqueries_t, r.cross_masses, r.ccontext_t, r.grad_t, None)
    copies = exchange(0)
    loads.keys = load(r.keys_hbm, r.keys)
    loads.values = load(r.values_hbm, r.values)
    probs_copy(r.self_probs, 0).start()
    probs_copy(r.self_probs, 1).start()
    query_grad = jnp.transpose(r.query_grad_t[...])
    engine.run(*next(plan))
    loads.cwq.wait()
    normed_grad = dot_nt(query_grad, r.wq[...])
    loads.wq = load(r.wq_hbm, r.wq)
    loads.first.wait()
    first_part, gain_cross_grad = norm_back(r.enc_grad[...], gain_cross, normed_grad)
    r.dec_grad[...] += first_part
    r.tiny[0, 1:2] = gain_cross_grad
    loads.a2.wait()
    r.query_grad_t[...] = jnp.transpose(r.a2[...])
    loads.across = load(r.across_hbm, r.a2)
    give(1, r.query_grad_t, query_grad)
    engine.run(*next(plan))
    loads.es0.wait()
    loads.es1.wait()
    for side in range(2):
        r.group_t[:, side * count : (side + 1) * count] = jnp.transpose(r.group[side])
    loads.a10 = load(r.a1_hbm.at[m.core], r.group.at[0])
    loads.a11 = load(r.a1_hbm.at[m.core + 2], r.group.at[1])
    for copy in copies:
        copy.wait()
    key_grad = chip_sum(r.key_grad, r.key_recv.at[0])
    value_grad = chip_sum(r.value_grad, r.value_recv.at[0])
    loads.cwk.wait()
    loads.cwv.wait()
    r.partial_low[...] = partial(0, 1 - m.side).astype(LOW)
    enc_copy = send(r.partial_low, r.partial_recv.at[0], r.link_sem, (0,), m.y_peer)
    enc_copy.start()
    r.enc_grad[...] = partial(0, m.side)
    loads.wk = load(r.wk_hbm, r.wk)
    loads.wv = load(r.wv_hbm, r.wv)
    engine.run(*next(plan))
    give(2, r.group_t, key_grad)
    give(3, r.group_t, value_grad)
    settle(3 * width)
    engine.run(*next(plan))

    first_grad = r.dec_grad[...]
    head_grad = first_grad.astype(LOW)
    loads.wo.wait()
    r.grad_t[...] = dot_nt(r.wo[...], head_grad).astype(LOW)
    loads.context.wait()
    engine.run(*next(plan))
    r.query_grad_t[...] = r.context_t[...].astype(LOW)
    give(4, r.query_grad_t, head_grad)
    loads.keys.wait()
    turn(r.keys, r.keys_t)
    loads.values.wait()
    loads.queries.wait()
    loads.x.wait()

    r.by_distance[...] = jnp.zeros_like(r.by_distance)
    attend(r.self_probs, r.queries_t, r.self_masses, r.context_t, r.grad_t, m.place)
    copies = exchange(1)
    query_grad = jnp.transpose(r.query_grad_t[...])
    engine.run(*next(plan))
    loads.wq.wait()
    normed_grad = dot_nt(query_grad, r.wq[...])
    loads.a10.wait()
    loads.a11.wait()
    for side in range(2):
        r.group_t[:, side * count : (side + 1) * count] = jnp.transpose(r.group[side])
    give(5, r.group_t.at[:, block(m.side, count)], query_grad)
    engine.run(*next(plan))
    for copy in copies:
        copy.wait()
    key_grad = chip_sum(r.key_grad, r.key_recv.at[1])
    value_grad = chip_sum(r.value_grad, r.value_recv.at[1])
    loads.wk.wait()
    loads.wv.wait()
    enc_copy.wait()
    r.enc_grad[...] += r.partial_recv[0].astype(F32)
    def gain_part(states, grad):
        return jnp.sum(grad * states * scale_of(states), axis=0, keepdims=True)

    loads.across.wait()
    theirs = partial(1, 1 - m.side)
    r.partial_low[...] = theirs.astype(LOW)
    dec_copy = send(r.partial_low, r.partial_recv.at[1], r.link_sem, (1,), m.y_peer)
    gain_self_grad = gain_part(r.a2[...].astype(F32), theirs)
    normed_grad = normed_grad + partial(1, m.side)
    gain_self_grad = gain_self_grad + gain_part(r.x[...].astype(F32), normed_grad)
    r.tiny[0, 0:1] = gain_self_grad
    give(6, r.group_t, key_grad)
    give(7, r.group_t, value_grad)
    settle(4 * width)
    r.second[...] = normed_grad

    def hop(slot):
        peer = (m.core_peer, m.y_peer, engine.x_peer)[slot]
        return send(r.tiny.at[slot], r.tiny_recv.at[slot], r.tiny_sem, (slot,), peer)

    def spread(step):
        return send(
            r.tiny.at[3], r.tiny_recv.at[2 + step], r.tiny_sem, (2 + step,), engine.z_peer(step)
        )

    def arrive(slot):
        hop(slot).wait()
        r.tiny[slot + 1] = r.tiny[slot] + r.tiny_recv[slot]
        if slot < 2:
            hop(slot + 1).start()
            return
        for step in range(1, dims.planes):
            spread(step).start()

    def states():
        dec_copy.wait()
        normed_grad = r.second[...] + r.partial_recv[1].astype(F32)
        state_part, _ = norm_back(r.x[...].astype(F32), gain_self, normed_grad)
        r.dec_grad[...] += state_part

    def smalls():
        buckets = dims.buckets
        table = lax.dot_general(
            bucket_terms(buckets), r.by_distance[...], (((1,), (1,)), ((), ())),
            precision=lax.Precision.HIGHEST, preferred_element_type=F32,
        )
        part = buckets // places
        for place in range(places):
            r.tiny[0, 8 : 8 + part, 128 * place : 128 * (place + 1)] = table[
                place * part : (place + 1) * part
            ]
        hop(0).start()

    def totals():
        total = r.tiny[3]
        for step in range(1, dims.planes):
            spread(step).wait()
            total = total + r.tiny_recv[2 + step]
        r.small[...] = total

    steps = (
        smalls, lambda: arrive(0), lambda: arrive(1), lambda: arrive(2), totals, dec_copy.start, states,
    )
    engine.finish_all(TAIL_FEEDS, tuple(zip(TAIL, steps)))


def run_backward(dims, a, f):
    count, total, width = dims.count, dims.count * dims.places, dims.width
    near, far = pltpu.VMEM, pl.ANY
    pairs, planes, chunks, piece = dims.pairs, dims.planes, dims.chunks, dims.piece
    square = (width, width)
    own = (count, width)
    inputs = dict(
        x_hbm=(a.dec_states[0], far),
        go_hbm=(a.out_grad[0], far),
        gain_self=(a.gain_self, near),
        gain_cross=(a.gain_cross, near),
        gain_ffn=(a.gain_ffn, near),
        self_masses=(f.self_masses, near),
        cross_masses=(f.cross_masses, near),
        first_hbm=(f.first_out, far),
        second_hbm=(f.second_out, far),
        inner_hbm=(f.inner_out, far),
        win_hbm=(a.ffn_in, far),
        wout_hbm=(a.ffn_out.reshape(-1, *own), far),
        queries_hbm=(f.queries_t_out, far),
        cqueries_hbm=(f.cqueries_t_out, far),
        context_hbm=(f.context_t_out, far),
        ccontext_hbm=(f.ccontext_t_out, far),
        a2_hbm=(f.a2_out, far),
        across_hbm=(f.across_out, far),
        keys_hbm=(f.keys_out, far),
        values_hbm=(f.values_out, far),
        a1_hbm=(f.a1_out, far),
        ckeys_hbm=(f.ckeys_out, far),
        cvalues_hbm=(f.cvalues_out, far),
        es_hbm=(f.es_out, far),
        self_probs=(f.self_probs, far),
        cross_probs=(f.cross_probs, far),
        wo_hbm=(a.self_output, far),
        wq_hbm=(a.self_query, far),
        wk_hbm=(a.self_key, far),
        wv_hbm=(a.self_value, far),
        cwo_hbm=(a.cross_output, far),
        cwq_hbm=(a.cross_query, far),
        cwk_hbm=(a.cross_key, far),
        cwv_hbm=(a.cross_value, far),
    )
    outputs = dict(
        big=((2, 2, 4 * width, width), LOW, far),
        layer_out=(own, LOW, near),
        fin=((4 * width, width), LOW, near),
        dec_grad=(own, F32, near),
        enc_grad=(own, F32, near),
        small=((16, width), F32, near),
    )
    dma = pltpu.SemaphoreType.DMA
    rows = 4 * width
    scratch = dict(
        squares=pltpu.VMEM((4, *square), LOW),
        tall=pltpu.VMEM((16, *own), LOW),
        second=pltpu.VMEM(own, F32),
        keys_t=pltpu.VMEM((width, total), LOW),
        probs=pltpu.VMEM((2, total, 2 * count), LOW),
        grad_t=pltpu.VMEM((width, count), LOW),
        a3=pltpu.VMEM(own, LOW),
        x=pltpu.VMEM(own, LOW),
        go=pltpu.VMEM(own, LOW),
        a2=pltpu.VMEM(own, LOW),
        queries_t=pltpu.VMEM((width, count), LOW),
        cqueries_t=pltpu.VMEM((width, count), LOW),
        context_t=pltpu.VMEM((width, count), F32),
        ccontext_t=pltpu.VMEM((width, count), F32),
        query_grad_t=pltpu.VMEM((width, count), LOW),
        key_recv=pltpu.VMEM((2, 2, *own), LOW),
        value_recv=pltpu.VMEM((2, 2, *own), LOW),
        partial_low=pltpu.VMEM(own, LOW),
        partial_recv=pltpu.VMEM((2, *own), LOW),
        group=pltpu.VMEM((2, *own), LOW),
        group_t=pltpu.VMEM((width, 2 * count), LOW),
        before=pltpu.VMEM((NEAR, 2 * count), F32),
        own=pltpu.VMEM((count, 2 * count), F32),
        by_distance=pltpu.VMEM((128, 2 * NEAR), F32),
        stage=pltpu.VMEM((2, 2, 2, width // dims.places, width), LOW),
        fresh=pltpu.VMEM((2, dims.ring * dims.chunk_rows, width), LOW),
        sums=pltpu.VMEM((2, rows, width), LOW),
        x_recv=pltpu.VMEM((rows // 2, width), LOW),
        early_recv=pltpu.VMEM(
            (2, -(-dims.chunks // 6) * dims.chunk_rows // 2 if dims.line else dims.piece, width), LOW
        ),
        z_recv=pltpu.VMEM(
            (2, rows // 2, width) if dims.line else (planes - 1, chunks * piece, width), LOW
        ),
        tiny=pltpu.VMEM((4, 16, width), F32),
        tiny_recv=pltpu.VMEM((2 + planes, 16, width), F32),
        load_sem=dma((40,)),
        win_sem=dma((4,)),
        wout_sem=dma((4,)),
        head_sem=dma,
        probs_sem=dma((2,)),
        stage_sem=dma((2,)),
        link_sem=dma((2, 2)),
        swap_sem=dma((2, 2, 2, 2)),
        chunk_sem=dma((chunks,)),
        core_sem=dma((2, chunks)),
        y_sem=dma((2, chunks)),
        x_sem=dma((2, chunks)),
        z_sem=dma((2, chunks, planes - 1)),
        gz_sem=dma((2, chunks, planes - 1)),
        gx_sem=dma((2, chunks)),
        tiny_sem=dma((2, 2 + planes)),
    )
    return call(
        lambda names, *refs: backward_kernel(names, dims, *refs),
        "backward", 1, 63, inputs, outputs, scratch,
    )


def place_kernel(names, dims, *refs):
    r = SimpleNamespace(**dict(zip(names, refs)))
    width, fan = dims.width, dims.fan
    own = width // dims.places
    passed = (
        (r.layer_in, r.layer_held, r.layer),
        (r.dec_in, r.dec_held, r.dec),
        (r.enc_in, r.enc_held, r.enc),
    )
    inward = [
        pltpu.make_async_copy(src, held, r.pass_sem.at[0, slot])
        for slot, (src, held, _) in enumerate(passed)
    ]
    copies = [
        pltpu.make_async_copy(held, dst, r.pass_sem.at[1, slot])
        for slot, (_, held, dst) in enumerate(passed)
    ]
    groups = 4 * width // own
    loads, stores = [], []
    for index in range(4):
        rows = pl.ds(index * width, width)
        loads.append(pltpu.make_async_copy(r.fin.at[rows], r.low.at[rows], r.load_sem.at[index]))
        loads[-1].start()
    for copy in inward:
        copy.start()
    units = (
        r.cross_output, r.cross_query, r.cross_key, r.cross_value,
        r.self_output, r.self_query, r.self_key, r.self_value,
    )
    for index in range(groups):
        if index % (groups // 4) == 0:
            loads[index // (groups // 4)].wait()
        rows = pl.ds(index * own, own)
        r.wide[rows, :] = r.low[rows, :].astype(F32)
        if index < fan:
            dst = r.ffn_in.at[:, pl.ds(index * width, width)]
        elif index < 2 * fan:
            dst = r.ffn_out.at[pl.ds((index - fan) * own, own)]
        else:
            dst = units[index - 2 * fan]
        copy = pltpu.make_async_copy(r.wide.at[rows], dst, r.store_sem.at[index])
        copy.start()
        stores.append(copy)
    for arrival, copy in zip(inward, copies):
        arrival.wait()
        copy.start()
    at = lax.axis_index("seq")
    part = dims.buckets // dims.places
    for place in range(dims.places):
        @pl.when(at == place)
        def _():
            for index, grad in enumerate((r.gain_self, r.gain_cross, r.gain_ffn)):
                grad[...] = r.small[index : index + 1, place * own : (place + 1) * own]
            r.table_grad[...] = r.small[8 : 8 + part, 128 * place : 128 * place + dims.heads]
    for copy in stores + copies:
        copy.wait()


def run_place(dims, f, b):
    near, far = pltpu.VMEM, pl.ANY
    width, own = dims.width, dims.width // dims.places
    square, gain = ((own, width), F32, far), ((1, own), F32, near)
    rows = 4 * width
    inputs = dict(
        fin=(b.fin, far),
        small=(b.small, near),
        layer_in=(b.layer_out, far),
        dec_in=(b.dec_grad, far),
        enc_in=(b.enc_grad, far),
    )
    outputs = dict(
        layer=(b.layer_out.shape, LOW, far),
        dec=(b.dec_grad.shape, F32, far),
        enc=(b.enc_grad.shape, F32, far),
        ffn_out=((width, width), F32, far),
        ffn_in=((own, dims.fan * width), F32, far),
        cross_output=square,
        cross_query=square,
        cross_key=square,
        cross_value=square,
        self_output=square,
        self_query=square,
        self_key=square,
        self_value=square,
        gain_self=gain,
        gain_cross=gain,
        gain_ffn=gain,
        table_grad=((dims.buckets // dims.places, dims.heads), F32, near),
    )
    scratch = dict(
        low=pltpu.VMEM((rows, width), LOW),
        wide=pltpu.VMEM((rows, width), F32),
        layer_held=pltpu.VMEM(b.layer_out.shape, LOW),
        dec_held=pltpu.VMEM(b.dec_grad.shape, F32),
        enc_held=pltpu.VMEM(b.enc_grad.shape, F32),
        pass_sem=pltpu.SemaphoreType.DMA((2, 3)),
        load_sem=pltpu.SemaphoreType.DMA((4,)),
        store_sem=pltpu.SemaphoreType.DMA((rows // own,)),
    )
    names = (*inputs, *outputs, *scratch)
    results = pl.pallas_call(
        lambda *refs: place_kernel(names, dims, *refs),
        out_shape=tuple(jax.ShapeDtypeStruct(shape, kind) for shape, kind, _ in outputs.values()),
        in_specs=[pl.BlockSpec(memory_space=space) for _, space in inputs.values()],
        out_specs=tuple(pl.BlockSpec(memory_space=space) for _, _, space in outputs.values()),
        scratch_shapes=list(scratch.values()),
        compiler_params=pltpu.CompilerParams(vmem_limit_bytes=60 * 2**20),
        name="place",
    )(*(array for array, _ in inputs.values()))
    return SimpleNamespace(**dict(zip(outputs, results)))


def on_device(
    dec_states,
    enc_states,
    out_grad,
    dec_lengths,
    enc_lengths,
    self_query,
    self_key,
    self_value,
    self_output,
    cross_query,
    cross_key,
    cross_value,
    cross_output,
    ffn_in,
    ffn_out,
    gain_self,
    gain_cross,
    gain_ffn,
    position_bias,
):
    a = SimpleNamespace(
        dec_states=dec_states,
        enc_states=enc_states,
        out_grad=out_grad,
        dec_lengths=dec_lengths,
        enc_lengths=enc_lengths,
        self_query=self_query,
        self_key=self_key,
        self_value=self_value,
        self_output=self_output,
        cross_query=cross_query,
        cross_key=cross_key,
        cross_value=cross_value,
        cross_output=cross_output,
        ffn_in=ffn_in,
        ffn_out=ffn_out,
        gain_self=gain_self,
        gain_cross=gain_cross,
        gain_ffn=gain_ffn,
        position_bias=position_bias,
    )
    count, width = a.dec_states.shape[1:]
    buckets, heads = a.position_bias.shape
    planes, piece = lax.axis_size("dp") // 2, 16
    line = planes == 4
    chunk_rows = 128 if line else 2 * planes * piece
    chunks = 4 * width // chunk_rows
    dims = SimpleNamespace(
        count=count,
        width=width,
        places=lax.axis_size("seq"),
        heads=heads,
        head_dim=width // heads,
        pairs=heads // 2,
        fan=a.ffn_in.shape[1] // width,
        items=a.dec_lengths.shape[1],
        buckets=buckets,
        planes=planes,
        piece=piece,
        chunks=chunks,
        ring=4 if line else 1,
        line=line,
        chunk_rows=chunk_rows,
    )
    f = run_forward(dims, a)
    b = run_backward(dims, a, f)
    o = run_place(dims, f, b)
    return (
        o.layer[None],
        o.dec[None],
        o.enc[None],
        o.self_query,
        o.self_key,
        o.self_value,
        o.self_output,
        o.cross_query,
        o.cross_key,
        o.cross_value,
        o.cross_output,
        o.ffn_in,
        o.ffn_out,
        o.gain_self[0],
        o.gain_cross[0],
        o.gain_ffn[0],
        o.table_grad,
    )


def solution(mesh):
    split = P("dp", "seq", None)
    rows = P("seq", None)
    return jax.shard_map(
        on_device,
        mesh=mesh,
        in_specs=(split,) * 3 + (P("dp", None),) * 2 + (P(),) * 14,
        out_specs=(split,) * 3 + (rows,) * 10 + (P("seq"),) * 3 + (rows,),
        check_vma=False,
    )
```

```python
import functools
import math
from types import SimpleNamespace

import jax
import jax.numpy as jnp
from jax import lax
from jax.experimental import pallas as pl
from jax.experimental.pallas import tpu as pltpu
from jax.sharding import PartitionSpec as P

MESH = pl.DeviceIdType.MESH
EPS = 1e-06
NEG = -1000000000.0
NEAR = 128
F32 = jnp.float32
LOW = jnp.bfloat16


def dot(left, right):
    return jnp.dot(left, right, preferred_element_type=F32)


def dot_nt(left, right):
    return lax.dot_general(left, right, (((1,), (1,)), ((), ())), preferred_element_type=F32)


def add_low(left, right):
    return (left.astype(F32) + right.astype(F32)).astype(LOW)


def block(index, size):
    return pl.ds(pl.multiple_of(index * size, size), size)


def bucket_of(distance):
    farther = jnp.full(distance.shape, 16, jnp.int32)
    for level in range(1, 16):
        farther = farther + (distance >= math.ceil(16 * 8 ** (level / 16))).astype(jnp.int32)
    return jnp.where(distance < 16, distance, farther)


def bucket_terms(buckets):
    shape = (buckets, 2 * NEAR)
    lanes = lax.broadcasted_iota(jnp.int32, shape, 1)
    return (bucket_of(lanes) == lax.broadcasted_iota(jnp.int32, shape, 0)).astype(F32)


def scale_of(values):
    return lax.rsqrt(jnp.mean(values * values, axis=-1, keepdims=True) + EPS)


def norm_back(values, gain, grad):
    scale = scale_of(values)
    gain_grad = jnp.sum(grad * values * scale, axis=0, keepdims=True)
    inner = jnp.mean(values * gain * grad, axis=-1, keepdims=True)
    return scale * gain * grad - values * (scale * scale * scale) * inner, gain_grad


def head_blocks(pair):
    size = pair.shape[0] // 2
    zero = jnp.zeros((size, pair.shape[1]), pair.dtype)
    return jnp.concatenate(
        [
            jnp.concatenate([pair[:size], zero], axis=1),
            jnp.concatenate([zero, pair[size:]], axis=1),
        ],
        axis=0,
    )


def head_rows(both):
    size, count = both.shape[0] // 2, both.shape[1] // 2
    return jnp.concatenate([both[:size, :count], both[size:, count:]], axis=0)


def twice(values):
    return jnp.concatenate([values, values], axis=1)


def fold(values):
    return values.reshape(values.shape[0] // 8, 8, values.shape[1])


class Mesh2:
    def __init__(self):
        self.row = lax.axis_index("dp")
        self.place = lax.axis_index("seq")
        self.side, self.core = self.place // 2, lax.rem(self.place, 2)
        self.sibling = self.side * 2 + 1 - self.core
        self.across = (1 - self.side) * 2 + self.core
        self.diagonal = (1 - self.side) * 2 + 1 - self.core
        self.core_peer = (self.row, self.sibling)
        self.y_peer = (self.row, self.across)

    def call_out(self, peers):
        for peer in peers:
            pl.semaphore_signal(
                pltpu.get_barrier_semaphore(), inc=1, device_id=peer, device_id_type=MESH
            )

    def hear(self, peers):
        pl.semaphore_wait(pltpu.get_barrier_semaphore(), len(peers))

    def greet(self, peers):
        self.call_out(peers)
        self.hear(peers)


def send(src, dst, sems, slot, peer):
    return pltpu.make_async_remote_copy(
        src_ref=src,
        dst_ref=dst,
        send_sem=sems.at[(0, *slot)],
        recv_sem=sems.at[(1, *slot)],
        device_id=peer,
        device_id_type=MESH,
    )


def softmax_pair(pair, r, count, steps, keys, turned, terms, queries_t, masses, out_t, probs, place):
    lanes = block(pair, 2 * r.head_dim)
    queries = head_blocks(queries_t[lanes, :])
    near = place is not None
    if near:
        tiles = [
            pltpu.roll(
                jnp.broadcast_to(r.near_bias[pl.ds(pair * 2 + head, 1), :], (NEAR, 2 * NEAR)),
                0,
                1,
                stride=1,
                stride_axis=0,
            )
            for head in range(2)
        ]
        below = [tile[:, NEAR:] for tile in tiles]
        on = [tile[:, :NEAR] for tile in tiles]
        none = jnp.zeros((NEAR, NEAR), F32)
        before = jnp.concatenate([below[0], none, below[1], none], axis=1)
        first = jnp.concatenate([on[0], below[0], on[1], below[1]], axis=1)
        second = jnp.concatenate([none, on[0], none, on[1]], axis=1)

    top = jnp.full((8, 2 * count), -jnp.inf, F32)
    for index in range(steps):
        rows = block(index, count)
        raw = dot(keys[index, :, lanes], queries) + twice(terms[rows, :])
        r.scores[rows, :] = raw
        if not near:
            top = jnp.maximum(top, jnp.max(fold(raw), axis=0))
    if near:
        rows = block(place, count)
        r.scores[rows, :] = r.scores[rows, :] + jnp.concatenate([first, second], axis=0)

        @pl.when(place > 0)
        def _():
            last = block(place * (count // NEAR) - 1, NEAR)
            r.scores[last, :] = r.scores[last, :] + before

        for index in range(steps):
            top = jnp.maximum(top, jnp.max(fold(r.scores[block(index, count), :]), axis=0))
    top = jnp.max(top, axis=0, keepdims=True)
    mass = jnp.zeros((8, 2 * count), F32)
    context = jnp.zeros((2 * r.head_dim, 2 * count), F32)
    for index in range(steps):
        rows = block(index, count)
        weights = jnp.exp(r.scores[rows, :] - top)
        low = weights.astype(LOW)
        probs[rows, :] = low
        context = context + dot(turned[lanes, rows], low)
        mass = mass + jnp.sum(fold(weights), axis=0)
    inverse = 1.0 / jnp.sum(mass, axis=0, keepdims=True)
    masses[pair] = inverse
    out_t[lanes, :] = head_rows(context * inverse)


def forward_kernel(names, dims, *refs):
    r = SimpleNamespace(**dict(zip(names, refs)), head_dim=dims.head_dim)
    m = Mesh2()
    count, places, pairs, fan, width = dims.count, dims.places, dims.pairs, dims.fan, dims.width
    q_place = m.place

    def load(slot, src, dst):
        copy = pltpu.make_async_copy(src, dst, r.load_sem.at[slot])
        copy.start()
        return copy

    loads = SimpleNamespace(
        x=load(9, r.x_hbm, r.xs.at[m.place]),
        e=load(10, r.e_hbm, r.es.at[m.place]),
        go=load(11, r.go_hbm, r.go),
        wk=load(0, r.wk_hbm, r.wk),
        wv=load(1, r.wv_hbm, r.wv),
        wq=load(2, r.wq_hbm, r.wq),
        wout=load(3, r.wout_hbm, r.wout),
        cwk=load(4, r.cwk_hbm, r.cwk),
        cwv=load(5, r.cwv_hbm, r.cwv),
        wo=load(6, r.wo_hbm, r.wo),
        cwq=load(7, r.cwq_hbm, r.cwq),
        cwo=load(8, r.cwo_hbm, r.cwo),
    )

    m.greet([m.core_peer, m.y_peer])
    x_y = send(r.x_hbm, r.xs.at[m.place], r.link_sem, (0,), m.y_peer)
    x_core = send(r.x_hbm, r.xs.at[m.place], r.link_sem, (1,), m.core_peer)
    x_on = send(r.xs.at[m.across], r.xs.at[m.across], r.link_sem, (2,), m.core_peer)
    e_y = send(r.e_hbm, r.es.at[m.place], r.link_sem, (3,), m.y_peer)
    e_core = send(r.e_hbm, r.es.at[m.place], r.link_sem, (4,), m.core_peer)
    e_on = send(r.es.at[m.across], r.es.at[m.across], r.link_sem, (5,), m.core_peer)
    x_y.start()
    x_core.start()
    e_core.start()

    gain_self = r.gain_self[...].astype(F32).reshape(1, width)
    gain_cross = r.gain_cross[...].astype(F32).reshape(1, width)

    items = dims.items
    dec_starts, enc_starts = [0], [0]
    for index in range(items):
        dec_starts.append(dec_starts[-1] + r.dec_len[0, index])
        enc_starts.append(enc_starts[-1] + r.enc_len[0, index])
    query_at = q_place * count + lax.broadcasted_iota(jnp.int32, (1, count), 1)
    low_self = jnp.zeros((1, count), jnp.int32)
    low_cross = jnp.zeros((1, count), jnp.int32)
    high_cross = jnp.full((1, count), enc_starts[1], jnp.int32)
    for index in range(1, items):
        inside = query_at >= dec_starts[index]
        low_self = jnp.where(inside, dec_starts[index], low_self)
        low_cross = jnp.where(inside, enc_starts[index], low_cross)
        high_cross = jnp.where(inside, enc_starts[index + 1], high_cross)

    def masks(index, carry):
        rows = block(index, count)
        key_at = index * count + lax.broadcasted_iota(jnp.int32, (count, count), 0)
        r.self_terms[rows, :] = jnp.where((key_at >= low_self) & (key_at <= query_at), 0.0, NEG)
        r.cross_terms[rows, :] = jnp.where((key_at >= low_cross) & (key_at < high_cross), 0.0, NEG)
        return carry

    lax.fori_loop(0, places, masks, 0)

    buckets = r.table.shape[1]
    terms = bucket_terms(buckets)
    last = lax.broadcasted_iota(jnp.int32, terms.shape, 0) == buckets - 1
    terms = terms - last.astype(F32)
    r.near_bias[...] = dot(r.table[...], terms.astype(LOW))

    def self_block(place):
        rows = block(place, count)
        states = r.xs[place].astype(F32)
        normed = (states * scale_of(states) * gain_self).astype(LOW)
        r.a1[place] = normed
        r.keys[place] = dot(normed, r.wk[...]).astype(LOW)
        values = dot(normed, r.wv[...]).astype(LOW)
        r.values[place] = values
        r.values_t[:, rows] = jnp.transpose(values)

    def cross_block(place):
        rows = block(place, count)
        encoded = r.es[place]
        r.ckeys[place] = dot(encoded, r.cwk[...]).astype(LOW)
        values = dot(encoded, r.cwv[...]).astype(LOW)
        r.cvalues[place] = values
        r.cvalues_t[:, rows] = jnp.transpose(values)

    def nth_place(k):
        return lax.rem(m.side + k // 2, 2) * 2 + lax.rem(m.core + lax.rem(k, 2), 2)

    def cross_blocks(k, carry):
        @pl.when(k == 1)
        def _():
            e_core.wait()

        @pl.when(k == 3)
        def _():
            e_on.wait()

        cross_block(nth_place(k))
        return carry

    def inner_grad(index, carry):
        r.inner_grad[index] = dot_nt(r.go[...], r.wout[block(index, width), :]).astype(LOW)
        return carry

    def self_blocks(k, carry):
        @pl.when(k == 1)
        def _():
            x_core.wait()

        @pl.when(k == 2)
        def _():
            loads.wout.wait()
            loads.go.wait()
            loads.e.wait()
            lax.fori_loop(0, fan, inner_grad, 0)
            loads.cwk.wait()
            loads.cwv.wait()
            lax.fori_loop(0, 2, cross_blocks, 0)
            x_y.wait()
            x_on.start()
            e_y.start()

        @pl.when(k == 3)
        def _():
            x_on.wait()

        self_block(nth_place(k))

        @pl.when(k == 0)
        def _():
            loads.wq.wait()
            r.queries_t[...] = jnp.transpose(dot(r.a1[m.place], r.wq[...]).astype(LOW))

        return carry

    loads.x.wait()
    loads.wk.wait()
    loads.wv.wait()
    lax.fori_loop(0, 4, self_blocks, 0)

    def keep(src, dst, slot):
        copy = pltpu.make_async_copy(src, dst, r.keep_sem.at[slot])
        copy.start()
        return copy

    kept = [
        keep(r.keys, r.keys_out, 0),
        keep(r.values, r.values_out, 1),
        keep(r.a1, r.a1_out, 2),
        keep(r.inner_grad, r.inner_out, 6),
        keep(r.queries_t, r.queries_t_out, 7),
        keep(r.xs.at[m.across], r.across_out, 14),
    ]

    def probs_copy(slot, out, pair):
        return pltpu.make_async_copy(r.probs.at[slot], out.at[pair], r.probs_sem.at[slot])

    def attend(earlier, keys, turned, terms, queries_t, masses, out_t, out, place):
        def one(pair, carry):
            slot = lax.rem(pair, 2)
            if earlier:
                probs_copy(slot, out, pair).wait()
            else:
                @pl.when(pair >= 2)
                def _():
                    probs_copy(slot, out, pair).wait()

                @pl.when(pair == pairs - 2)
                def _():
                    e_y.wait()
                    e_on.start()
            softmax_pair(
                pair, r, count, places, keys, turned, terms, queries_t, masses, out_t,
                r.probs.at[slot], place,
            )
            probs_copy(slot, out, pair).start()
            return carry

        lax.fori_loop(0, pairs, one, 0)

    attend(
        False, r.keys, r.values_t, r.self_terms, r.queries_t, r.self_masses, r.context_t,
        r.self_probs, q_place,
    )
    loads.wo.wait()
    context = jnp.transpose(r.context_t[...]).astype(LOW)
    first = r.xs[m.place].astype(F32) + dot(context, r.wo[...])
    r.first[...] = first
    normed_cross = (first * scale_of(first) * gain_cross).astype(LOW)
    r.a2[...] = normed_cross
    loads.cwq.wait()
    r.cqueries_t[...] = jnp.transpose(dot(normed_cross, r.cwq[...]).astype(LOW))
    lax.fori_loop(2, 4, cross_blocks, 0)
    kept += [
        keep(r.ckeys, r.ckeys_out, 3),
        keep(r.cvalues, r.cvalues_out, 4),
        keep(r.es, r.es_out, 5),
        keep(r.context_t, r.context_t_out, 8),
        keep(r.first, r.first_out, 9),
        keep(r.a2, r.a2_out, 10),
        keep(r.cqueries_t, r.cqueries_t_out, 11),
    ]
    attend(
        True, r.ckeys, r.cvalues_t, r.cross_terms, r.cqueries_t, r.cross_masses, r.ccontext_t,
        r.cross_probs, None,
    )
    loads.cwo.wait()
    context = jnp.transpose(r.ccontext_t[...]).astype(LOW)
    kept.append(keep(r.ccontext_t, r.ccontext_t_out, 12))
    r.second[...] = r.first[...] + dot(context, r.cwo[...])
    kept.append(keep(r.second, r.second_out, 13))
    for slot in range(2):
        probs_copy(slot, r.cross_probs, pairs - 2 + slot).wait()
    for copy in kept:
        copy.wait()


def call(kernel, name, collective, limit, inputs, outputs, scratch, aliases=None):
    names = (*inputs, *outputs, *scratch)
    results = pl.pallas_call(
        functools.partial(kernel, names),
        out_shape=tuple(jax.ShapeDtypeStruct(shape, kind) for shape, kind, _ in outputs.values()),
        in_specs=[pl.BlockSpec(memory_space=space) for _, space in inputs.values()],
        out_specs=tuple(pl.BlockSpec(memory_space=space) for _, _, space in outputs.values()),
        scratch_shapes=list(scratch.values()),
        input_output_aliases=aliases or {},
        compiler_params=pltpu.CompilerParams(
            collective_id=collective, has_side_effects=True, vmem_limit_bytes=limit * 2**20
        ),
        name=name,
    )(*(array for array, _ in inputs.values()))
    return SimpleNamespace(**dict(zip(outputs, results)))


def run_forward(dims, a):
    count, total, width = dims.count, dims.count * dims.places, dims.width
    near, far, scalars = pltpu.VMEM, pl.ANY, pltpu.SMEM
    pairs, fan = dims.pairs, dims.fan
    square = (width, width)
    own = (count, width)
    inputs = dict(
        x_hbm=(a.dec_states[0], far),
        e_hbm=(a.enc_states[0], far),
        go_hbm=(a.out_grad[0], far),
        dec_len=(a.dec_lengths, scalars),
        enc_len=(a.enc_lengths, scalars),
        table=(a.position_bias.T, near),
        gain_self=(a.gain_self, near),
        gain_cross=(a.gain_cross, near),
        wk_hbm=(a.self_key, far),
        wv_hbm=(a.self_value, far),
        wq_hbm=(a.self_query, far),
        wout_hbm=(a.ffn_out, far),
        cwk_hbm=(a.cross_key, far),
        cwv_hbm=(a.cross_value, far),
        wo_hbm=(a.self_output, far),
        cwq_hbm=(a.cross_query, far),
        cwo_hbm=(a.cross_output, far),
    )
    outputs = dict(
        first_out=(own, F32, far),
        second_out=(own, F32, far),
        inner_out=((fan, *own), LOW, far),
        across_out=(own, LOW, far),
        queries_t_out=((width, count), LOW, far),
        cqueries_t_out=((width, count), LOW, far),
        context_t_out=((width, count), F32, far),
        ccontext_t_out=((width, count), F32, far),
        self_masses=((pairs, 1, 2 * count), F32, near),
        cross_masses=((pairs, 1, 2 * count), F32, near),
        a2_out=(own, LOW, far),
        keys_out=((dims.places, *own), LOW, far),
        values_out=((dims.places, *own), LOW, far),
        a1_out=((dims.places, *own), LOW, far),
        ckeys_out=((dims.places, *own), LOW, far),
        cvalues_out=((dims.places, *own), LOW, far),
        es_out=((dims.places, *own), LOW, far),
        self_probs=((pairs, total, 2 * count), LOW, far),
        cross_probs=((pairs, total, 2 * count), LOW, far),
    )
    scratch = dict(
        xs=pltpu.VMEM((dims.places, *own), LOW),
        go=pltpu.VMEM(own, LOW),
        first=pltpu.VMEM(own, F32),
        second=pltpu.VMEM(own, F32),
        queries_t=pltpu.VMEM((width, count), LOW),
        cqueries_t=pltpu.VMEM((width, count), LOW),
        context_t=pltpu.VMEM((width, count), F32),
        ccontext_t=pltpu.VMEM((width, count), F32),
        a2=pltpu.VMEM(own, LOW),
        es=pltpu.VMEM((dims.places, *own), LOW),
        wk=pltpu.VMEM(square, LOW),
        wv=pltpu.VMEM(square, LOW),
        wq=pltpu.VMEM(square, LOW),
        wout=pltpu.VMEM((fan * width, width), LOW),
        cwk=pltpu.VMEM(square, LOW),
        cwv=pltpu.VMEM(square, LOW),
        wo=pltpu.VMEM(square, LOW),
        cwq=pltpu.VMEM(square, LOW),
        cwo=pltpu.VMEM(square, LOW),
        a1=pltpu.VMEM((dims.places, *own), LOW),
        keys=pltpu.VMEM((dims.places, *own), LOW),
        values=pltpu.VMEM((dims.places, *own), LOW),
        values_t=pltpu.VMEM((width, total), LOW),
        ckeys=pltpu.VMEM((dims.places, *own), LOW),
        cvalues=pltpu.VMEM((dims.places, *own), LOW),
        cvalues_t=pltpu.VMEM((width, total), LOW),
        self_terms=pltpu.VMEM((total, count), F32),
        cross_terms=pltpu.VMEM((total, count), F32),
        near_bias=pltpu.VMEM((dims.heads, 2 * NEAR), F32),
        scores=pltpu.VMEM((total, 2 * count), F32),
        probs=pltpu.VMEM((2, total, 2 * count), LOW),
        inner_grad=pltpu.VMEM((fan, *own), LOW),
        load_sem=pltpu.SemaphoreType.DMA((12,)),
        link_sem=pltpu.SemaphoreType.DMA((2, 6)),
        keep_sem=pltpu.SemaphoreType.DMA((15,)),
        probs_sem=pltpu.SemaphoreType.DMA((2,)),
    )
    return call(
        lambda names, *refs: forward_kernel(names, dims, *refs),
        "forward", 0, 56, inputs, outputs, scratch,
    )


SWAPPED = (1, 4, 5, 7, 10, 11, 13, 16, 19)


class Reducer:
    LAGS = (0, 4, 7, 9, 12, 19)

    def __init__(self, r, m, dims):
        self.r, self.m = r, m
        self.planes = dims.planes
        self.line = dims.line
        self.piece = dims.piece
        self.chunk_rows = dims.chunk_rows
        self.half_rows = dims.chunk_rows // 2
        self.chunks = dims.chunks
        self.ring = dims.ring
        self.plane, self.half = m.row // 2, lax.rem(m.row, 2)
        self.x_peer = (self.plane * 2 + 1 - self.half, m.place)
        self.published = self.loaded = self.fed = self.moved = 0

    def z_peer(self, step):
        return (lax.rem(self.plane + step, self.planes) * 2 + self.half, self.m.place)

    def plane_peer(self, plane):
        return (plane * 2 + self.half, self.m.place)

    def peers(self):
        return [self.x_peer] + [self.z_peer(step) for step in range(1, self.planes)]

    def span(self, first, size):
        return pl.ds(pl.multiple_of(first, self.piece), size)

    def rows(self, index):
        return self.span(index * self.chunk_rows, self.chunk_rows)

    def by_planes(self, index):
        found = index == SWAPPED[0]
        for other in SWAPPED[1:]:
            found = found | (index == other)
        return found

    def by_halves(self, index):
        return lax.rem(index, 6) == 3

    def route(self, index, first, other, third=None):
        if not self.line:
            first(index)
            return
        special = self.by_planes(index)
        usual = jnp.logical_not(special)
        if third is not None:
            early = self.by_halves(index)
            usual = usual & jnp.logical_not(early)

            @pl.when(early)
            def _():
                third(index)

        @pl.when(usual)
        def _():
            first(index)

        @pl.when(special)
        def _():
            other(index)

    def half_of(self, index, half):
        return self.span(index * self.chunk_rows + half * self.half_rows, self.half_rows)

    def packed(self, index):
        return self.span(index * self.half_rows, self.half_rows)

    def fresh_rows(self, index):
        return self.span(lax.rem(index, self.ring) * self.chunk_rows, self.chunk_rows)

    def load(self, index):
        r = self.r
        return pltpu.make_async_copy(
            r.big.at[self.m.core, :, self.rows(index)],
            r.fresh.at[:, self.fresh_rows(index)],
            r.chunk_sem.at[index],
        )

    def core_copy(self, index):
        r, rows = self.r, self.rows(index)
        return send(
            r.big.at[1 - self.m.core, :, rows], r.sums.at[:, rows], r.core_sem, (index,),
            self.m.core_peer,
        )

    def y_copy(self, index):
        r, rows = self.r, self.rows(index)
        return send(
            r.sums.at[1 - self.m.side, rows], r.fin.at[rows], r.y_sem, (index,), self.m.y_peer
        )

    def x_copy(self, index):
        r = self.r
        return send(
            r.sums.at[self.m.side, self.half_of(index, 1 - self.half)],
            r.x_recv.at[self.packed(index)],
            r.x_sem, (index,), self.x_peer,
        )

    def in_copy(self, index, inner):
        r = self.r
        return send(
            r.sums.at[self.m.side, self.half_of(index, self.half)],
            r.z_recv.at[0, self.packed(index)],
            r.z_sem, (index, 0), self.plane_peer(inner),
        )

    def mid_copy(self, index):
        r = self.r
        return send(
            r.sums.at[self.m.side, self.half_of(index, self.half)],
            r.z_recv.at[1, self.packed(index)],
            r.z_sem, (index, 1), self.plane_peer(3 - self.plane),
        )

    def out_copy(self, index, outer):
        r, rows = self.r, self.half_of(index, self.half)
        return send(r.fin.at[rows], r.fin.at[rows], r.gz_sem, (index, 0), self.plane_peer(outer))

    def z_part(self, index, which):
        first = index * self.chunk_rows + self.half * self.half_rows + which * self.piece
        return self.span(first, self.piece)

    def z_copy(self, index, step):
        r = self.r
        target = lax.rem(self.plane + step, self.planes)
        return send(
            r.sums.at[self.m.side, self.z_part(index, target)],
            r.z_recv.at[step - 1, self.span(index * self.piece, self.piece)],
            r.z_sem, (index, step - 1), self.z_peer(step),
        )

    def gz_copy(self, index, step):
        r, rows = self.r, self.z_part(index, self.plane)
        return send(r.fin.at[rows], r.fin.at[rows], r.gz_sem, (index, step - 1), self.z_peer(step))

    def gx_copy(self, index):
        r, rows = self.r, self.half_of(index, self.half)
        return send(r.fin.at[rows], r.fin.at[rows], r.gx_sem, (index,), self.x_peer)

    def publish(self, rows):
        last = rows // self.chunk_rows

        def begin(index, carry):
            self.core_copy(index).start()
            return carry

        def fetch(index, carry):
            self.load(index).start()
            return carry

        lax.fori_loop(self.published, last, begin, 0)
        ahead = min(last, self.fed + self.ring)
        lax.fori_loop(self.loaded, ahead, fetch, 0)
        self.published, self.loaded = last, max(self.loaded, ahead)

    def publish_part(self, first, last):
        def begin(index, carry):
            self.core_copy(index).start()

            @pl.when(index < self.ring)
            def _():
                self.load(index).start()

            return carry

        lax.fori_loop(first, last, begin, 0)

    def parts_done(self, last, fed):
        self.published, self.fed = last, fed
        self.loaded = min(last, self.ring)

    def feed(self, index, prefetch=True):
        r = self.r
        self.load(index).wait()
        self.core_copy(index).wait()
        rows, fresh = self.rows(index), self.fresh_rows(index)
        for side in range(2):
            r.sums[side, rows, :] = add_low(r.sums[side, rows, :], r.fresh[side, fresh, :])
        self.route(
            index,
            lambda at: self.y_copy(at).start(),
            lambda at: self.swap_copy(at).start(),
            lambda at: self.early_copy(at).start(),
        )

        if not prefetch:
            return

        @pl.when(index + self.ring < self.published)
        def _():
            self.load(index + self.ring).start()

    def move(self, step):
        stages = (
            (self.after_y, self.after_swap, self.after_early),
            (self.after_x, self.swapped_y, self.early_y),
            (self.inward, self.swapped_x),
            (self.middle, self.swapped_pair),
            (self.outward, self.swapped_back),
            (self.finish, self.swapped_finish),
        )
        for lag, stage in reversed(tuple(zip(self.LAGS, stages))):
            index = step - lag

            @pl.when((index >= 0) & (index < self.chunks))
            def _():
                self.route(index, *stage)


    def early_rows(self, index):
        return self.span(index // 6 * self.half_rows, self.half_rows)

    def early_copy(self, index):
        r = self.r
        return send(
            r.sums.at[:, self.half_of(index, 1 - self.half)],
            r.early_recv.at[:, self.early_rows(index)],
            r.x_sem, (index,), self.x_peer,
        )

    def early_y_copy(self, index):
        r, rows = self.r, self.half_of(index, self.half)
        return send(
            r.sums.at[1 - self.m.side, rows], r.fin.at[rows], r.y_sem, (index,), self.m.y_peer
        )

    def after_early(self, index):
        r = self.r
        self.early_copy(index).wait()
        rows, packed = self.half_of(index, self.half), self.early_rows(index)
        for side in range(2):
            r.sums[side, rows, :] = add_low(r.sums[side, rows, :], r.early_recv[side, packed, :])
        self.early_y_copy(index).start()

    def early_y(self, index):
        r, m = self.r, self.m
        self.early_y_copy(index).wait()
        rows = self.half_of(index, self.half)
        r.sums[m.side, rows, :] = add_low(r.sums[m.side, rows, :], r.fin[rows, :])
        self.give_in(index)


    def parity(self):
        return lax.rem(self.plane, 2)

    def neighbour(self):
        return self.plane_peer(self.plane + 1 - 2 * self.parity())

    def quarter_of(self, index, half):
        size = self.half_rows // 2
        first = index * self.chunk_rows + self.parity() * self.half_rows + half * size
        return self.span(first, size)

    def packed_quarter(self, index, which):
        size = self.half_rows // 2
        return self.span(index * self.half_rows + which * size, size)

    def swap_copy(self, index):
        r = self.r
        return send(
            r.sums.at[:, self.half_of(index, 1 - self.parity())],
            r.z_recv.at[:, self.packed(index)],
            r.z_sem, (index, 0), self.neighbour(),
        )

    def swapped_y_copy(self, index):
        r, rows = self.r, self.half_of(index, self.parity())
        return send(
            r.sums.at[1 - self.m.side, rows], r.fin.at[rows], r.y_sem, (index,), self.m.y_peer
        )

    def swapped_x_copy(self, index):
        r = self.r
        return send(
            r.sums.at[self.m.side, self.quarter_of(index, 1 - self.half)],
            r.x_recv.at[self.packed_quarter(index, 0)],
            r.x_sem, (index,), self.x_peer,
        )

    def pair_copy(self, index):
        r = self.r
        return send(
            r.sums.at[self.m.side, self.quarter_of(index, self.half)],
            r.x_recv.at[self.packed_quarter(index, 1)],
            r.z_sem, (index, 1), self.z_peer(2),
        )

    def swapped_gx_copy(self, index):
        r, rows = self.r, self.quarter_of(index, self.half)
        return send(r.fin.at[rows], r.fin.at[rows], r.gx_sem, (index,), self.x_peer)

    def swapped_gz_copy(self, index):
        r, rows = self.r, self.half_of(index, self.parity())
        return send(r.fin.at[rows], r.fin.at[rows], r.gz_sem, (index, 0), self.neighbour())

    def after_swap(self, index):
        r = self.r
        self.swap_copy(index).wait()
        rows, packed = self.half_of(index, self.parity()), self.packed(index)
        for side in range(2):
            r.sums[side, rows, :] = add_low(r.sums[side, rows, :], r.z_recv[side, packed, :])
        self.swapped_y_copy(index).start()

    def swapped_y(self, index):
        r, m = self.r, self.m
        self.swapped_y_copy(index).wait()
        rows = self.half_of(index, self.parity())
        r.sums[m.side, rows, :] = add_low(r.sums[m.side, rows, :], r.fin[rows, :])
        self.swapped_x_copy(index).start()

    def swapped_x(self, index):
        r, m = self.r, self.m
        self.swapped_x_copy(index).wait()
        rows = self.quarter_of(index, self.half)
        arrived = r.x_recv[self.packed_quarter(index, 0), :]
        r.sums[m.side, rows, :] = add_low(r.sums[m.side, rows, :], arrived)
        self.pair_copy(index).start()

    def swapped_pair(self, index):
        r, m = self.r, self.m
        self.pair_copy(index).wait()
        rows = self.quarter_of(index, self.half)
        arrived = r.x_recv[self.packed_quarter(index, 1), :]
        r.fin[rows, :] = add_low(r.sums[m.side, rows, :], arrived)
        self.swapped_gx_copy(index).start()

    def swapped_back(self, index):
        self.swapped_gx_copy(index).wait()
        self.swapped_gz_copy(index).start()

    def swapped_finish(self, index):
        self.swapped_gz_copy(index).wait()

    def after_y(self, index):
        r, m = self.r, self.m
        self.y_copy(index).wait()
        rows = self.rows(index)
        r.sums[m.side, rows, :] = add_low(r.sums[m.side, rows, :], r.fin[rows, :])
        self.x_copy(index).start()

    def after_x(self, index):
        r, m = self.r, self.m
        self.x_copy(index).wait()
        rows = self.half_of(index, self.half)
        r.sums[m.side, rows, :] = add_low(r.sums[m.side, rows, :], r.x_recv[self.packed(index), :])
        if not self.line:
            for step in range(1, self.planes):
                self.z_copy(index, step).start()
            return
        self.give_in(index)

    def give_in(self, index):
        for outer, inner in ((0, 1), (3, 2)):
            @pl.when(self.plane == outer)
            def _():
                self.in_copy(index, inner).start()

    def inward(self, index):
        r, m = self.r, self.m
        if not self.line:
            return
        for outer, inner in ((0, 1), (3, 2)):
            @pl.when(self.plane == outer)
            def _():
                self.in_copy(index, inner).wait_send()

        @pl.when((self.plane == 1) | (self.plane == 2))
        def _():
            self.in_copy(index, self.plane).wait_recv()
            rows = self.half_of(index, self.half)
            arrived = r.z_recv[0, self.packed(index), :]
            r.sums[m.side, rows, :] = add_low(r.sums[m.side, rows, :], arrived)
            self.mid_copy(index).start()

    def middle(self, index):
        r, m = self.r, self.m
        if not self.line:
            part = self.z_part(index, self.plane)
            total = r.sums[m.side, part, :].astype(F32)
            for step in range(1, self.planes):
                self.z_copy(index, step).wait()
                arrived = r.z_recv[step - 1, self.span(index * self.piece, self.piece), :]
                total = total + arrived.astype(F32)
            r.fin[part, :] = total.astype(LOW)
            for step in range(1, self.planes):
                self.gz_copy(index, step).start()
            return

        @pl.when((self.plane == 1) | (self.plane == 2))
        def _():
            self.mid_copy(index).wait()
            rows = self.half_of(index, self.half)
            arrived = r.z_recv[1, self.packed(index), :]
            r.fin[rows, :] = add_low(r.sums[m.side, rows, :], arrived)
            for outer, inner in ((0, 1), (3, 2)):
                @pl.when(self.plane == inner)
                def _():
                    self.out_copy(index, outer).start()
            self.gx_copy(index).start()

    def outward(self, index):
        if not self.line:
            for step in range(1, self.planes):
                self.gz_copy(index, step).wait()
            self.gx_copy(index).start()
            return
        for outer, inner in ((0, 1), (3, 2)):
            @pl.when(self.plane == inner)
            def _():
                self.out_copy(index, outer).wait_send()

            @pl.when(self.plane == outer)
            def _():
                self.out_copy(index, inner).wait_recv()
                self.gx_copy(index).start()

    def finish(self, index):
        self.gx_copy(index).wait()

    def run(self, feeds, moves):
        loops = max(1, feeds, moves)
        one, after = self.beside(loops, feeds, moves)

        def body(index, carry):
            one(index)
            return carry

        lax.fori_loop(0, loops, body, 0)
        after()

    def beside(self, loops, feeds, moves):
        feeds = max(0, min(feeds, self.published - self.fed))
        fed = self.fed + feeds
        limit = self.chunks + self.LAGS[-1] if fed == self.chunks else fed
        moves = max(0, min(moves, limit - self.moved))
        first_feed, first_move = self.fed, self.moved

        each = -(-feeds // loops)

        def one(index):
            if feeds > 0:
                def feed(step, carry):
                    self.feed(first_feed + step)
                    return carry

                lax.fori_loop(
                    jnp.minimum(index * each, feeds), jnp.minimum((index + 1) * each, feeds), feed, 0
                )
            if moves > 0:
                def move(step, carry):
                    self.move(first_move + step)
                    return carry

                lax.fori_loop(index * moves // loops, (index + 1) * moves // loops, move, 0)

        def after():
            self.fed, self.moved = fed, first_move + moves
            self.loaded = max(self.loaded, min(self.published, self.fed + self.ring))

        return one, after

    def finish_all(self, each, events):
        feeds, moves = self.chunks - self.fed, self.left()
        first_feed, first_move = self.fed, self.moved
        events = [(min(step, moves - 1), event) for step, event in events]

        def body(step, carry):
            for at, event in events:
                @pl.when(step == at)
                def _():
                    event()

            def feed(index, carry):
                self.feed(first_feed + index)
                return carry

            lax.fori_loop(
                jnp.minimum(step * each, feeds), jnp.minimum((step + 1) * each, feeds), feed, 0
            )
            self.move(first_move + step)
            return carry

        lax.fori_loop(0, moves, body, 0)

    def left(self):
        return self.chunks + self.LAGS[-1] - self.moved


def attend_back(pair, r, count, keys, keys_t, values, queries_t, masses, context_t, grad_t, probs, place, places):
    lanes = block(pair, 2 * r.head_dim)
    inverse = masses[pair]
    grads = grad_t[lanes, :].astype(F32)
    product = grads * context_t[lanes, :]
    sums = [
        jnp.sum(product[: r.head_dim], axis=0, keepdims=True),
        jnp.sum(product[r.head_dim :], axis=0, keepdims=True),
    ]
    inner = jnp.concatenate(sums, axis=1) * inverse
    grads = (head_blocks(grads) * inverse).astype(LOW)
    queries = head_blocks(queries_t[lanes, :])

    total = jnp.zeros((2 * r.head_dim, 2 * count), F32)
    beyond = jnp.zeros((8, 2 * count), F32)
    split = count - NEAR
    if place is not None:
        r.before[...] = jnp.zeros_like(r.before)
    for index in range(places):
        rows = block(index, count)
        weights = probs[rows, :]
        score_grad = weights.astype(F32) * (dot(values[index, :, lanes], grads) - inner)
        low = score_grad.astype(LOW)
        r.value_grad[index, :, lanes] = dot_nt(weights, grads).astype(LOW)
        r.key_grad[index, :, lanes] = dot_nt(low, queries).astype(LOW)
        total = total + dot(keys_t[lanes, rows], low)
        if place is not None:
            early = jnp.sum(fold(score_grad[:split]), axis=0)
            late = jnp.sum(fold(score_grad[split:]), axis=0)
            beyond = beyond + jnp.where(index < place, early, 0.0)
            beyond = beyond + jnp.where(index < place - 1, late, 0.0)

            @pl.when(index == place - 1)
            def _():
                r.before[...] = score_grad[split:]

            @pl.when(index == place)
            def _():
                r.own[...] = score_grad

    if place is not None:
        own, before = r.own[...], r.before[...]
        parts = []
        for head in range(2):
            at = head * count
            on = own[:NEAR, at : at + NEAR] + own[NEAR:, at + NEAR : at + 2 * NEAR]
            below = before[:, at : at + NEAR] + own[:NEAR, at + NEAR : at + 2 * NEAR]
            both = jnp.concatenate([on, below], axis=1)
            summed = both[:8]
            for group in range(1, NEAR // 8):
                summed = summed + pltpu.roll(
                    both[8 * group : 8 * group + 8], 2 * NEAR - 8 * group, 1
                )
            parts.append(summed)
        summed = jnp.concatenate(parts, axis=0)
        sublane = lax.broadcasted_iota(jnp.int32, summed.shape, 0)
        for bit in (1, 2, 4):
            summed = jnp.where(
                (sublane & bit) != 0, pltpu.roll(summed, 2 * NEAR - bit, 1), summed
            )
        lane = lax.broadcasted_iota(jnp.int32, (1, 2 * NEAR), 1)
        for head in range(2):
            at = head * count
            line = jnp.sum(summed[8 * head : 8 * head + 8], axis=0, keepdims=True)
            rest = jnp.sum(beyond[:, at : at + count]) + jnp.sum(before[:, at + NEAR : at + 2 * NEAR])
            line = line + jnp.where(lane == 2 * NEAR - 1, rest, 0.0)
            r.by_distance[pl.ds(pair * 2 + head, 1), :] = line
    r.query_grad_t[lanes, :] = head_rows(total).astype(LOW)


FFN_FEEDS = 3
PLAN = (
    (0, 0), (6, 0), (2, 5), (14, 0), (19, 0), (17, 3),
    (0, 1), (1, 0), (36, 6), (21, 1), (44, 23),
)
TAIL_FEEDS = 4
TAIL = (3, 8, 13, 16, 21, 9, 27)


def backward_kernel(names, dims, *refs):
    r = SimpleNamespace(**dict(zip(names, refs)), head_dim=dims.head_dim)
    m = Mesh2()
    count, places, pairs, fan, width = dims.count, dims.places, dims.pairs, dims.fan, dims.width
    own = width // places
    engine = Reducer(r, m, dims)
    plan = iter(PLAN)
    r.wo, r.wq, r.wk, r.wv = (r.squares.at[index] for index in range(4))
    r.keys, r.values, r.key_grad, r.value_grad = (r.tall.at[pl.ds(4 * k, 4)] for k in range(4))

    loads = SimpleNamespace()
    slots = iter(range(r.load_sem.shape[0]))

    def later(src, dst):
        return pltpu.make_async_copy(src, dst, r.load_sem.at[next(slots)])

    def load(src, dst):
        copy = later(src, dst)
        copy.start()
        return copy

    def probs_copy(src, pair):
        slot = lax.rem(pair, 2)
        return pltpu.make_async_copy(src.at[pair], r.probs.at[slot], r.probs_sem.at[slot])

    third = width // count
    loads.second = load(r.second_hbm, r.second)
    loads.go = load(r.go_hbm, r.go)

    def ffn_copies(index):
        rows = pl.ds(index * third, third)
        win = r.win_hbm.at[:, block(index, width)]
        return (
            pltpu.make_async_copy(win, r.squares.at[index], r.win_sem.at[index]),
            pltpu.make_async_copy(r.wout_hbm.at[rows], r.tall.at[rows], r.wout_sem.at[index]),
        )

    for index in range(fan):
        win, wout = ffn_copies(index)
        win.start()
        if index == 0:
            loads.inner = load(r.inner_hbm, r.value_grad)
        wout.start()
    probs_copy(r.cross_probs, 0).start()
    probs_copy(r.cross_probs, 1).start()
    loads.es0 = load(r.es_hbm.at[m.core], r.group.at[0])
    loads.es1 = load(r.es_hbm.at[m.core + 2], r.group.at[1])
    loads.cqueries = load(r.cqueries_hbm, r.cqueries_t)
    loads.ccontext = load(r.ccontext_hbm, r.ccontext_t)
    loads.queries = load(r.queries_hbm, r.queries_t)
    loads.context = load(r.context_hbm, r.context_t)
    loads.a2 = load(r.a2_hbm, r.a2)
    loads.x = load(r.x_hbm, r.x)

    peers = [m.core_peer, m.y_peer] + engine.peers()
    m.call_out(peers)

    gain_self = r.gain_self[...].astype(F32).reshape(1, width)
    gain_cross = r.gain_cross[...].astype(F32).reshape(1, width)
    staged = {}

    def unit_copy(unit):
        rows = pl.ds(2 * width + unit * own, own)
        return pltpu.make_async_copy(
            r.stage.at[unit % 2], r.big.at[:, :, rows], r.stage_sem.at[unit % 2]
        )

    def give(unit, left_t, right):
        if unit - 2 in staged:
            staged.pop(unit - 2).wait()

        for place in range(places):
            grad = dot(left_t[place * own : (place + 1) * own, :], right)
            r.stage[unit % 2, place % 2, place // 2] = grad.astype(LOW)
        staged[unit] = unit_copy(unit)
        staged[unit].start()

    def settle(rows):
        for unit in sorted(staged):
            staged.pop(unit).wait()
        engine.publish(rows)

    def turn(src, dst):
        def one(index, carry):
            rows = block(index, count)
            dst[:, rows] = jnp.transpose(src[index])
            return carry

        lax.fori_loop(0, places, one, 0)

    def attend(src, queries_t, masses, context_t, grad_t, place):
        beside, after = engine.beside(pairs, *next(plan))

        def one(pair, carry):
            probs_copy(src, pair).wait()
            attend_back(
                pair, r, count, r.keys, r.keys_t, r.values, queries_t, masses, context_t, grad_t,
                r.probs.at[lax.rem(pair, 2)], place, places,
            )

            @pl.when(pair + 2 < pairs)
            def _():
                probs_copy(src, pair + 2).start()

            beside(pair)
            return carry

        lax.fori_loop(0, pairs, one, 0)
        after()

    def exchange(slot):
        copies = []
        for side in range(2):
            theirs = side * 2 + 1 - m.core
            for part, (src, dst) in enumerate(
                ((r.key_grad, r.key_recv), (r.value_grad, r.value_recv))
            ):
                copies.append(
                    send(
                        src.at[theirs], dst.at[slot, side], r.swap_sem, (slot, side, part),
                        m.core_peer,
                    )
                )
                copies[-1].start()
        return copies

    def chip_sum(grad, arrived):
        parts = [add_low(grad[side * 2 + m.core], arrived[side]) for side in range(2)]
        return jnp.concatenate(parts, axis=0)

    def partial(slot, side):
        key_grad = add_low(r.key_grad[side * 2 + m.core], r.key_recv[slot, side])
        value_grad = add_low(r.value_grad[side * 2 + m.core], r.value_recv[slot, side])
        return dot_nt(key_grad, r.wk[...]) + dot_nt(value_grad, r.wv[...])

    gain_ffn = r.gain_ffn[...].astype(F32).reshape(1, width)
    loads.second.wait()
    second = r.second[...]
    normed_ffn = (second * scale_of(second) * gain_ffn).astype(LOW)
    r.grad_t[...] = jnp.transpose(normed_ffn)
    r.a3[...] = normed_ffn
    r.dec_grad[...] = jnp.zeros_like(second)
    r.enc_grad[...] = jnp.zeros_like(second)
    loads.cwo, loads.cwq = later(r.cwo_hbm, r.wo), later(r.cwq_hbm, r.wq)
    loads.cwk, loads.cwv = later(r.cwk_hbm, r.wk), later(r.cwv_hbm, r.wv)
    loads.ckeys, loads.cvalues = later(r.ckeys_hbm, r.keys), later(r.cvalues_hbm, r.values)
    freed = ((loads.cwo,), (loads.cwq, loads.ckeys), (loads.cwk, loads.cvalues), (loads.cwv,))
    loads.inner.wait()
    loads.go.wait()

    def head_copy(index):
        return pltpu.make_async_copy(
            r.keys_t.at[:, pl.ds(0, width)],
            r.big.at[lax.rem(index, 2), index // 2, pl.ds(width, width)],
            r.head_sem,
        )

    def feed_forward(index, carry):
        slot = lax.rem(index, 2)
        win, wout = ffn_copies(index)
        win.wait()
        pre = dot(r.a3[...], r.squares[index])
        half = 0.5 + 0.5 * lax.erf(pre * (0.5**0.5))
        inner = (pre * half).astype(LOW)
        slope = half + pre * jnp.exp(-0.5 * pre * pre) * ((2.0 * math.pi) ** -0.5)
        pre_grad = (slope * r.value_grad[index].astype(F32)).astype(LOW)

        def rows_of(place, carry):
            grad = dot(r.grad_t[block(place, own), :], pre_grad)
            r.stage[slot, lax.rem(place, 2), place // 2] = grad.astype(LOW)
            return carry

        lax.fori_loop(0, places, rows_of, 0)
        tail = pltpu.make_async_copy(
            r.stage.at[slot], r.big.at[:, :, block(index, own)], r.stage_sem.at[slot]
        )
        tail.start()
        wout.wait()
        rows = r.tall[pl.ds(index * third, third)].reshape(width, width)
        r.dec_grad[...] += dot(inner, rows)
        r.enc_grad[...] += dot_nt(pre_grad, r.squares[index])

        @pl.when(index > 0)
        def _():
            head_copy(index - 1).wait()

        r.keys_t[:, :width] = dot(jnp.transpose(inner), r.go[...]).astype(LOW)
        head_copy(index).start()
        for step, copies in enumerate(freed):
            @pl.when(index == step)
            def _():
                for copy in copies:
                    copy.start()
        tail.wait()

        @pl.when(index == 0)
        def _():
            m.hear(peers)

        chunk_rows = engine.chunk_rows
        engine.publish_part(index * own // chunk_rows, (index + 1) * own // chunk_rows)

        def feed(step, carry):
            engine.feed(step, prefetch=False)
            return carry

        lax.fori_loop(index * ffn_feeds // fan, (index + 1) * ffn_feeds // fan, feed, 0)
        return carry

    ffn_feeds = min(FFN_FEEDS, fan * own // engine.chunk_rows)
    lax.fori_loop(0, fan, feed_forward, 0)
    engine.parts_done(fan * own // engine.chunk_rows, ffn_feeds)
    r.layer_out[...] = (second + r.dec_grad[...]).astype(LOW)
    second_part, gain_ffn_grad = norm_back(second, gain_ffn, r.enc_grad[...])
    loads.first = load(r.first_hbm, r.enc_grad)
    r.dec_grad[...] = r.go[...].astype(F32) + second_part
    r.tiny[0] = jnp.zeros(r.tiny.shape[1:], F32)
    r.tiny[0, 2:3] = gain_ffn_grad
    head_copy(fan - 1).wait()
    engine.publish(2 * width)
    engine.run(*next(plan))

    head_grad = r.dec_grad[...].astype(LOW)
    loads.cwo.wait()
    r.grad_t[...] = dot_nt(r.wo[...], head_grad).astype(LOW)
    loads.wo = load(r.wo_hbm, r.wo)
    engine.run(*next(plan))
    loads.ccontext.wait()
    r.query_grad_t[...] = r.ccontext_t[...].astype(LOW)
    give(0, r.query_grad_t, head_grad)
    loads.ckeys.wait()
    turn(r.keys, r.keys_t)
    loads.cvalues.wait()
    loads.cqueries.wait()
    attend(r.cross_probs, r.cqueries_t, r.cross_masses, r.ccontext_t, r.grad_t, None)
    copies = exchange(0)
    loads.keys = load(r.keys_hbm, r.keys)
    loads.values = load(r.values_hbm, r.values)
    probs_copy(r.self_probs, 0).start()
    probs_copy(r.self_probs, 1).start()
    query_grad = jnp.transpose(r.query_grad_t[...])
    engine.run(*next(plan))
    loads.cwq.wait()
    normed_grad = dot_nt(query_grad, r.wq[...])
    loads.wq = load(r.wq_hbm, r.wq)
    loads.first.wait()
    first_part, gain_cross_grad = norm_back(r.enc_grad[...], gain_cross, normed_grad)
    r.dec_grad[...] += first_part
    r.tiny[0, 1:2] = gain_cross_grad
    loads.a2.wait()
    r.query_grad_t[...] = jnp.transpose(r.a2[...])
    loads.across = load(r.across_hbm, r.a2)
    give(1, r.query_grad_t, query_grad)
    engine.run(*next(plan))
    loads.es0.wait()
    loads.es1.wait()
    for side in range(2):
        r.group_t[:, side * count : (side + 1) * count] = jnp.transpose(r.group[side])
    loads.a10 = load(r.a1_hbm.at[m.core], r.group.at[0])
    loads.a11 = load(r.a1_hbm.at[m.core + 2], r.group.at[1])
    for copy in copies:
        copy.wait()
    key_grad = chip_sum(r.key_grad, r.key_recv.at[0])
    value_grad = chip_sum(r.value_grad, r.value_recv.at[0])
    loads.cwk.wait()
    loads.cwv.wait()
    r.partial_low[...] = partial(0, 1 - m.side).astype(LOW)
    enc_copy = send(r.partial_low, r.partial_recv.at[0], r.link_sem, (0,), m.y_peer)
    enc_copy.start()
    r.enc_grad[...] = partial(0, m.side)
    loads.wk = load(r.wk_hbm, r.wk)
    loads.wv = load(r.wv_hbm, r.wv)
    engine.run(*next(plan))
    give(2, r.group_t, key_grad)
    give(3, r.group_t, value_grad)
    settle(3 * width)
    engine.run(*next(plan))

    first_grad = r.dec_grad[...]
    head_grad = first_grad.astype(LOW)
    loads.wo.wait()
    r.grad_t[...] = dot_nt(r.wo[...], head_grad).astype(LOW)
    loads.context.wait()
    engine.run(*next(plan))
    r.query_grad_t[...] = r.context_t[...].astype(LOW)
    give(4, r.query_grad_t, head_grad)
    loads.keys.wait()
    turn(r.keys, r.keys_t)
    loads.values.wait()
    loads.queries.wait()
    loads.x.wait()

    r.by_distance[...] = jnp.zeros_like(r.by_distance)
    attend(r.self_probs, r.queries_t, r.self_masses, r.context_t, r.grad_t, m.place)
    copies = exchange(1)
    query_grad = jnp.transpose(r.query_grad_t[...])
    engine.run(*next(plan))
    loads.wq.wait()
    normed_grad = dot_nt(query_grad, r.wq[...])
    loads.a10.wait()
    loads.a11.wait()
    for side in range(2):
        r.group_t[:, side * count : (side + 1) * count] = jnp.transpose(r.group[side])
    give(5, r.group_t.at[:, block(m.side, count)], query_grad)
    engine.run(*next(plan))
    for copy in copies:
        copy.wait()
    key_grad = chip_sum(r.key_grad, r.key_recv.at[1])
    value_grad = chip_sum(r.value_grad, r.value_recv.at[1])
    loads.wk.wait()
    loads.wv.wait()
    enc_copy.wait()
    r.enc_grad[...] += r.partial_recv[0].astype(F32)
    def gain_part(states, grad):
        return jnp.sum(grad * states * scale_of(states), axis=0, keepdims=True)

    loads.across.wait()
    theirs = partial(1, 1 - m.side)
    r.partial_low[...] = theirs.astype(LOW)
    dec_copy = send(r.partial_low, r.partial_recv.at[1], r.link_sem, (1,), m.y_peer)
    gain_self_grad = gain_part(r.a2[...].astype(F32), theirs)
    normed_grad = normed_grad + partial(1, m.side)
    gain_self_grad = gain_self_grad + gain_part(r.x[...].astype(F32), normed_grad)
    r.tiny[0, 0:1] = gain_self_grad
    give(6, r.group_t, key_grad)
    give(7, r.group_t, value_grad)
    settle(4 * width)
    r.second[...] = normed_grad

    def hop(slot):
        peer = (m.core_peer, m.y_peer, engine.x_peer)[slot]
        return send(r.tiny.at[slot], r.tiny_recv.at[slot], r.tiny_sem, (slot,), peer)

    def spread(step):
        return send(
            r.tiny.at[3], r.tiny_recv.at[2 + step], r.tiny_sem, (2 + step,), engine.z_peer(step)
        )

    def arrive(slot):
        hop(slot).wait()
        r.tiny[slot + 1] = r.tiny[slot] + r.tiny_recv[slot]
        if slot < 2:
            hop(slot + 1).start()
            return
        for step in range(1, dims.planes):
            spread(step).start()

    def states():
        dec_copy.wait()
        normed_grad = r.second[...] + r.partial_recv[1].astype(F32)
        state_part, _ = norm_back(r.x[...].astype(F32), gain_self, normed_grad)
        r.dec_grad[...] += state_part

    def smalls():
        buckets = dims.buckets
        table = lax.dot_general(
            bucket_terms(buckets), r.by_distance[...], (((1,), (1,)), ((), ())),
            precision=lax.Precision.HIGHEST, preferred_element_type=F32,
        )
        part = buckets // places
        for place in range(places):
            r.tiny[0, 8 : 8 + part, 128 * place : 128 * (place + 1)] = table[
                place * part : (place + 1) * part
            ]
        hop(0).start()

    def totals():
        total = r.tiny[3]
        for step in range(1, dims.planes):
            spread(step).wait()
            total = total + r.tiny_recv[2 + step]
        r.small[...] = total

    steps = (
        smalls, lambda: arrive(0), lambda: arrive(1), lambda: arrive(2), totals, dec_copy.start, states,
    )
    engine.finish_all(TAIL_FEEDS, tuple(zip(TAIL, steps)))


def run_backward(dims, a, f):
    count, total, width = dims.count, dims.count * dims.places, dims.width
    near, far = pltpu.VMEM, pl.ANY
    pairs, planes, chunks, piece = dims.pairs, dims.planes, dims.chunks, dims.piece
    square = (width, width)
    own = (count, width)
    inputs = dict(
        x_hbm=(a.dec_states[0], far),
        go_hbm=(a.out_grad[0], far),
        gain_self=(a.gain_self, near),
        gain_cross=(a.gain_cross, near),
        gain_ffn=(a.gain_ffn, near),
        self_masses=(f.self_masses, near),
        cross_masses=(f.cross_masses, near),
        first_hbm=(f.first_out, far),
        second_hbm=(f.second_out, far),
        inner_hbm=(f.inner_out, far),
        win_hbm=(a.ffn_in, far),
        wout_hbm=(a.ffn_out.reshape(-1, *own), far),
        queries_hbm=(f.queries_t_out, far),
        cqueries_hbm=(f.cqueries_t_out, far),
        context_hbm=(f.context_t_out, far),
        ccontext_hbm=(f.ccontext_t_out, far),
        a2_hbm=(f.a2_out, far),
        across_hbm=(f.across_out, far),
        keys_hbm=(f.keys_out, far),
        values_hbm=(f.values_out, far),
        a1_hbm=(f.a1_out, far),
        ckeys_hbm=(f.ckeys_out, far),
        cvalues_hbm=(f.cvalues_out, far),
        es_hbm=(f.es_out, far),
        self_probs=(f.self_probs, far),
        cross_probs=(f.cross_probs, far),
        wo_hbm=(a.self_output, far),
        wq_hbm=(a.self_query, far),
        wk_hbm=(a.self_key, far),
        wv_hbm=(a.self_value, far),
        cwo_hbm=(a.cross_output, far),
        cwq_hbm=(a.cross_query, far),
        cwk_hbm=(a.cross_key, far),
        cwv_hbm=(a.cross_value, far),
    )
    outputs = dict(
        big=((2, 2, 4 * width, width), LOW, far),
        layer_out=(own, LOW, near),
        fin=((4 * width, width), LOW, near),
        dec_grad=(own, F32, near),
        enc_grad=(own, F32, near),
        small=((16, width), F32, near),
    )
    dma = pltpu.SemaphoreType.DMA
    rows = 4 * width
    scratch = dict(
        squares=pltpu.VMEM((4, *square), LOW),
        tall=pltpu.VMEM((16, *own), LOW),
        second=pltpu.VMEM(own, F32),
        keys_t=pltpu.VMEM((width, total), LOW),
        probs=pltpu.VMEM((2, total, 2 * count), LOW),
        grad_t=pltpu.VMEM((width, count), LOW),
        a3=pltpu.VMEM(own, LOW),
        x=pltpu.VMEM(own, LOW),
        go=pltpu.VMEM(own, LOW),
        a2=pltpu.VMEM(own, LOW),
        queries_t=pltpu.VMEM((width, count), LOW),
        cqueries_t=pltpu.VMEM((width, count), LOW),
        context_t=pltpu.VMEM((width, count), F32),
        ccontext_t=pltpu.VMEM((width, count), F32),
        query_grad_t=pltpu.VMEM((width, count), LOW),
        key_recv=pltpu.VMEM((2, 2, *own), LOW),
        value_recv=pltpu.VMEM((2, 2, *own), LOW),
        partial_low=pltpu.VMEM(own, LOW),
        partial_recv=pltpu.VMEM((2, *own), LOW),
        group=pltpu.VMEM((2, *own), LOW),
        group_t=pltpu.VMEM((width, 2 * count), LOW),
        before=pltpu.VMEM((NEAR, 2 * count), F32),
        own=pltpu.VMEM((count, 2 * count), F32),
        by_distance=pltpu.VMEM((128, 2 * NEAR), F32),
        stage=pltpu.VMEM((2, 2, 2, width // dims.places, width), LOW),
        fresh=pltpu.VMEM((2, dims.ring * dims.chunk_rows, width), LOW),
        sums=pltpu.VMEM((2, rows, width), LOW),
        x_recv=pltpu.VMEM((rows // 2, width), LOW),
        early_recv=pltpu.VMEM(
            (2, -(-dims.chunks // 6) * dims.chunk_rows // 2 if dims.line else dims.piece, width), LOW
        ),
        z_recv=pltpu.VMEM(
            (2, rows // 2, width) if dims.line else (planes - 1, chunks * piece, width), LOW
        ),
        tiny=pltpu.VMEM((4, 16, width), F32),
        tiny_recv=pltpu.VMEM((2 + planes, 16, width), F32),
        load_sem=dma((40,)),
        win_sem=dma((4,)),
        wout_sem=dma((4,)),
        head_sem=dma,
        probs_sem=dma((2,)),
        stage_sem=dma((2,)),
        link_sem=dma((2, 2)),
        swap_sem=dma((2, 2, 2, 2)),
        chunk_sem=dma((chunks,)),
        core_sem=dma((2, chunks)),
        y_sem=dma((2, chunks)),
        x_sem=dma((2, chunks)),
        z_sem=dma((2, chunks, planes - 1)),
        gz_sem=dma((2, chunks, planes - 1)),
        gx_sem=dma((2, chunks)),
        tiny_sem=dma((2, 2 + planes)),
    )
    return call(
        lambda names, *refs: backward_kernel(names, dims, *refs),
        "backward", 1, 63, inputs, outputs, scratch,
    )


def place_kernel(names, dims, *refs):
    r = SimpleNamespace(**dict(zip(names, refs)))
    width, fan = dims.width, dims.fan
    own = width // dims.places
    passed = (
        (r.layer_in, r.layer_held, r.layer),
        (r.dec_in, r.dec_held, r.dec),
        (r.enc_in, r.enc_held, r.enc),
    )
    inward = [
        pltpu.make_async_copy(src, held, r.pass_sem.at[0, slot])
        for slot, (src, held, _) in enumerate(passed)
    ]
    copies = [
        pltpu.make_async_copy(held, dst, r.pass_sem.at[1, slot])
        for slot, (_, held, dst) in enumerate(passed)
    ]
    groups = 4 * width // own
    loads, stores = [], []
    for index in range(4):
        rows = pl.ds(index * width, width)
        loads.append(pltpu.make_async_copy(r.fin.at[rows], r.low.at[rows], r.load_sem.at[index]))
        loads[-1].start()
    for copy in inward:
        copy.start()
    units = (
        r.cross_output, r.cross_query, r.cross_key, r.cross_value,
        r.self_output, r.self_query, r.self_key, r.self_value,
    )
    for index in range(groups):
        if index % (groups // 4) == 0:
            loads[index // (groups // 4)].wait()
        rows = pl.ds(index * own, own)
        r.wide[rows, :] = r.low[rows, :].astype(F32)
        if index < fan:
            dst = r.ffn_in.at[:, pl.ds(index * width, width)]
        elif index < 2 * fan:
            dst = r.ffn_out.at[pl.ds((index - fan) * own, own)]
        else:
            dst = units[index - 2 * fan]
        copy = pltpu.make_async_copy(r.wide.at[rows], dst, r.store_sem.at[index])
        copy.start()
        stores.append(copy)
    for arrival, copy in zip(inward, copies):
        arrival.wait()
        copy.start()
    at = lax.axis_index("seq")
    part = dims.buckets // dims.places
    for place in range(dims.places):
        @pl.when(at == place)
        def _():
            for index, grad in enumerate((r.gain_self, r.gain_cross, r.gain_ffn)):
                grad[...] = r.small[index : index + 1, place * own : (place + 1) * own]
            r.table_grad[...] = r.small[8 : 8 + part, 128 * place : 128 * place + dims.heads]
    for copy in stores + copies:
        copy.wait()


def run_place(dims, f, b):
    near, far = pltpu.VMEM, pl.ANY
    width, own = dims.width, dims.width // dims.places
    square, gain = ((own, width), F32, far), ((1, own), F32, near)
    rows = 4 * width
    inputs = dict(
        fin=(b.fin, far),
        small=(b.small, near),
        layer_in=(b.layer_out, far),
        dec_in=(b.dec_grad, far),
        enc_in=(b.enc_grad, far),
    )
    outputs = dict(
        layer=(b.layer_out.shape, LOW, far),
        dec=(b.dec_grad.shape, F32, far),
        enc=(b.enc_grad.shape, F32, far),
        ffn_out=((width, width), F32, far),
        ffn_in=((own, dims.fan * width), F32, far),
        cross_output=square,
        cross_query=square,
        cross_key=square,
        cross_value=square,
        self_output=square,
        self_query=square,
        self_key=square,
        self_value=square,
        gain_self=gain,
        gain_cross=gain,
        gain_ffn=gain,
        table_grad=((dims.buckets // dims.places, dims.heads), F32, near),
    )
    scratch = dict(
        low=pltpu.VMEM((rows, width), LOW),
        wide=pltpu.VMEM((rows, width), F32),
        layer_held=pltpu.VMEM(b.layer_out.shape, LOW),
        dec_held=pltpu.VMEM(b.dec_grad.shape, F32),
        enc_held=pltpu.VMEM(b.enc_grad.shape, F32),
        pass_sem=pltpu.SemaphoreType.DMA((2, 3)),
        load_sem=pltpu.SemaphoreType.DMA((4,)),
        store_sem=pltpu.SemaphoreType.DMA((rows // own,)),
    )
    names = (*inputs, *outputs, *scratch)
    results = pl.pallas_call(
        lambda *refs: place_kernel(names, dims, *refs),
        out_shape=tuple(jax.ShapeDtypeStruct(shape, kind) for shape, kind, _ in outputs.values()),
        in_specs=[pl.BlockSpec(memory_space=space) for _, space in inputs.values()],
        out_specs=tuple(pl.BlockSpec(memory_space=space) for _, _, space in outputs.values()),
        scratch_shapes=list(scratch.values()),
        compiler_params=pltpu.CompilerParams(vmem_limit_bytes=60 * 2**20),
        name="place",
    )(*(array for array, _ in inputs.values()))
    return SimpleNamespace(**dict(zip(outputs, results)))


def on_device(
    dec_states,
    enc_states,
    out_grad,
    dec_lengths,
    enc_lengths,
    self_query,
    self_key,
    self_value,
    self_output,
    cross_query,
    cross_key,
    cross_value,
    cross_output,
    ffn_in,
    ffn_out,
    gain_self,
    gain_cross,
    gain_ffn,
    position_bias,
):
    a = SimpleNamespace(
        dec_states=dec_states,
        enc_states=enc_states,
        out_grad=out_grad,
        dec_lengths=dec_lengths,
        enc_lengths=enc_lengths,
        self_query=self_query,
        self_key=self_key,
        self_value=self_value,
        self_output=self_output,
        cross_query=cross_query,
        cross_key=cross_key,
        cross_value=cross_value,
        cross_output=cross_output,
        ffn_in=ffn_in,
        ffn_out=ffn_out,
        gain_self=gain_self,
        gain_cross=gain_cross,
        gain_ffn=gain_ffn,
        position_bias=position_bias,
    )
    count, width = a.dec_states.shape[1:]
    buckets, heads = a.position_bias.shape
    planes, piece = lax.axis_size("dp") // 2, 16
    line = planes == 4
    chunk_rows = 128 if line else 2 * planes * piece
    chunks = 4 * width // chunk_rows
    dims = SimpleNamespace(
        count=count,
        width=width,
        places=lax.axis_size("seq"),
        heads=heads,
        head_dim=width // heads,
        pairs=heads // 2,
        fan=a.ffn_in.shape[1] // width,
        items=a.dec_lengths.shape[1],
        buckets=buckets,
        planes=planes,
        piece=piece,
        chunks=chunks,
        ring=4 if line else 1,
        line=line,
        chunk_rows=chunk_rows,
    )
    f = run_forward(dims, a)
    b = run_backward(dims, a, f)
    o = run_place(dims, f, b)
    return (
        o.layer[None],
        o.dec[None],
        o.enc[None],
        o.self_query,
        o.self_key,
        o.self_value,
        o.self_output,
        o.cross_query,
        o.cross_key,
        o.cross_value,
        o.cross_output,
        o.ffn_in,
        o.ffn_out,
        o.gain_self[0],
        o.gain_cross[0],
        o.gain_ffn[0],
        o.table_grad,
    )


def solution(mesh):
    split = P("dp", "seq", None)
    rows = P("seq", None)
    return jax.shard_map(
        on_device,
        mesh=mesh,
        in_specs=(split,) * 3 + (P("dp", None),) * 2 + (P(),) * 14,
        out_specs=(split,) * 3 + (rows,) * 10 + (P("seq"),) * 3 + (rows,),
        check_vma=False,
    )
```
